32 devices in a mesh: row: 2 (over core), col: 16 (over z, y, x).
Axes of the slice: x: 2, y: 2, z: 4, core: 2. Of those that a mesh axis runs over, the one named last changes fastest.
Arguments:
- features: bfloat16 [16384, 128], P(('row', 'col')), may hold values from -6 to 6
- weight: bfloat16 [128, 128], replicated, may hold values from -0.5 to 0.5
- bias: float32 [128], replicated, may hold values from -3 to 3
- cotangent: bfloat16 [16384, 128], P(('row', 'col')), may hold values from -6 to 6
- block_count: int32 [2, 16], P('row', 'col'), may hold values from 64 to 512
- block_rows: int32 [2, 16, 512], P('row', 'col'), may hold values from 0 to 63
- block_cols: int32 [2, 16, 512], P('row', 'col'), may hold values from 0 to 7
- edge_offsets: int32 [2, 16, 512, 128], P('row', 'col'), may hold values from 0 to 16383, as said below
- edge_weight: bfloat16 [2, 16, 512, 128], P('row', 'col'), may hold values from 0.0099487305 to 0.099609375
Outputs:
- output: bfloat16 [16384, 128], P(('row', 'col'))
- grad_features: bfloat16 [16384, 128], P(('row', 'col'))
- grad_weight: float32 [128, 128], replicated
- grad_bias: float32 [128], replicated
The draws below stay inside these ranges and needn't reach their ends.
Inputs may be any that keep to these rules, and one draw needn't show every extreme that they name: `edge_offsets`: the offsets within one slot are distinct.
All inputs are finite; a program needn't handle non-finite values.
Results may differ from the reference program's by a relative error of at most 0.013.
The reference program's roundings to bfloat16 on the way count: a program that leaves them out, or rounds other values in their place, can miss the bound.
Values may be sent and summed in bfloat16 or wider, within the bound.
No kernel may reach another device: no remote copies, remote signals or barrier semaphores. Data moves between devices by JAX's collectives and lax.ppermute only.
A program may use at most 128 MiB of HBM per device.

```python
import math
import jax
import jax.numpy as jnp
from jax import lax

F = 128
NODE_DEV = 512
NBT = 512
E_BLK = 128
NODES = 16384
N_ROW = 2
N_COL = 16


def draw_block_count(key, part):
    levels = jnp.array([1, 2, 4, 8], dtype=jnp.int32)
    picks = jax.random.randint(jax.random.fold_in(key, 11), (N_ROW * N_COL,), 0, 4)
    fullest = jax.random.randint(jax.random.fold_in(key, 12), (), 0, N_ROW * N_COL)
    picks = jnp.where(jnp.arange(N_ROW * N_COL) == fullest, 0, picks)
    return (NBT // levels[picks]).reshape(N_ROW, N_COL).astype(jnp.int32)


def draw_edge_offsets(key, part):
    shape = (N_ROW, N_COL, NBT, E_BLK)
    stride = 16384 // E_BLK
    jitter = jax.random.randint(jax.random.fold_in(key, 21), shape, 0, stride)
    base = jnp.arange(E_BLK, dtype=jnp.int32) * stride + jitter
    factor = 2 * jax.random.randint(jax.random.fold_in(key, 22), (N_ROW, N_COL, NBT, 1), 0, 8192) + 1
    offset = jax.random.randint(jax.random.fold_in(key, 23), (N_ROW, N_COL, NBT, 1), 0, 16384)
    return ((factor * base + offset) % 16384).astype(jnp.int32)


def plant(result, own_key, smallest, top_value):
    longest = result.shape.index(max(result.shape))
    spots = []
    for shift in (0, 1):
        where = [jax.random.randint(jax.random.fold_in(own_key, axis), (), 0, length) for axis, length in enumerate(result.shape)]
        where[longest] = (where[longest] + shift) % result.shape[longest]
        spots.append(tuple(where))
    return result.at[spots[0]].set(smallest).at[spots[1]].set(top_value)


def steps_of(own_key, shape, cuts, least, largest):
    level = 1.0
    for dim, parts in cuts:
        steps = jax.random.uniform(jax.random.fold_in(jax.random.fold_in(own_key, 6), dim), (parts,), jnp.float32, least / len(cuts), largest / len(cuts))
        level = level * jnp.repeat(jnp.exp(steps), shape[dim] // parts).reshape((-1,) + (1,) * (len(shape) - 1 - dim))
    return level


def bell_draw(stream_key, shape, width, limit, pieces=(), held_as=jnp.bfloat16):
    loudness = steps_of(stream_key, shape, pieces, -0.22, 0.18) if pieces else 1.0
    entries = jax.random.normal(stream_key, shape, jnp.float32) * width * loudness
    return jnp.minimum(jnp.maximum(entries, -limit), limit).astype(held_as)


def setup_inputs(seed: int = 0) -> dict:
    keys = jax.random.split(jax.random.key(seed), 10)
    features = bell_draw(keys[0], (NODES, F), 1.0, 6.0, ((0, 32),))
    weight = bell_draw(keys[1], (F, F), F ** -0.5, 0.5)
    bias = bell_draw(keys[2], (F,), 0.5, 3.0, (), jnp.float32)
    cotangent = bell_draw(keys[3], (NODES, F), 1.0, 6.0, ((0, 32),))
    block_count = draw_block_count(jax.random.fold_in(keys[9], 71), 0)
    block_rows = plant(jax.random.randint(keys[5], (N_ROW, N_COL, NBT), 0, NODE_DEV * N_COL // 128), jax.random.fold_in(keys[5], 1), 0, (NODE_DEV * N_COL // 128) - 1).astype(jnp.int32)
    block_cols = plant(jax.random.randint(keys[6], (N_ROW, N_COL, NBT), 0, NODE_DEV * N_ROW // 128), jax.random.fold_in(keys[6], 1), 0, (NODE_DEV * N_ROW // 128) - 1).astype(jnp.int32)
    edge_offsets = draw_edge_offsets(jax.random.fold_in(keys[9], 71), 0)
    edge_weight = jnp.clip(jnp.exp(math.log(0.099609375) - 2.3038113 * jax.random.uniform(keys[8], (N_ROW, N_COL, NBT, E_BLK), jnp.float32) ** steps_of(keys[8], (N_ROW, N_COL, NBT, E_BLK), ((0, 2), (1, 16)), -0.2, 0.2)), 0.0099487305, 0.099609375).astype(jnp.bfloat16)
    return {"features": features, "weight": weight, "bias": bias, "cotangent": cotangent, "block_count": block_count, "block_rows": block_rows, "block_cols": block_cols, "edge_offsets": edge_offsets, "edge_weight": edge_weight}


def tile_edges(t, block_count, block_rows, block_cols, edge_offsets, edge_weight):
    r = t // N_COL
    c = t % N_COL
    count = block_count.reshape(-1)[t]
    brow = block_rows.reshape(-1, NBT)[t]
    bcol = block_cols.reshape(-1, NBT)[t]
    offs = edge_offsets.reshape(-1, NBT, E_BLK)[t]
    vals = edge_weight.reshape(-1, NBT, E_BLK)[t].astype(jnp.float32)
    live = jnp.arange(NBT, dtype=jnp.int32) < count
    vals = jnp.where(live[:, None], vals, jnp.zeros_like(vals))
    lrow = brow[:, None] * 128 + offs // 128
    lcol = bcol[:, None] * 128 + offs % 128
    grow = r * (NODE_DEV * N_COL) + lrow
    gcol = ((lcol // NODE_DEV) * N_COL + c) * NODE_DEV + lcol % NODE_DEV
    return grow.reshape(-1).astype(jnp.int32), gcol.reshape(-1).astype(jnp.int32), vals.reshape(-1)


def reference(features, weight, bias, cotangent, block_count, block_rows, block_cols, edge_offsets, edge_weight):
    tiles = jnp.arange(N_ROW * N_COL, dtype=jnp.int32)
    projected = jnp.dot(features, weight, preferred_element_type=jnp.float32).astype(jnp.bfloat16).astype(jnp.float32)

    def forward_step(total, t):
        rows, cols, vals = tile_edges(t, block_count, block_rows, block_cols, edge_offsets, edge_weight)
        return total.at[rows].add(vals[:, None] * projected[cols]), None

    aggregated, _ = lax.scan(forward_step, jnp.zeros((NODES, F), jnp.float32), tiles)
    pre = aggregated + bias
    output = jnp.maximum(pre, 0.0).astype(jnp.bfloat16)
    grad_pre = jnp.where(pre > 0, cotangent.astype(jnp.float32), 0.0).astype(jnp.bfloat16)
    grad_pre_f = grad_pre.astype(jnp.float32)

    def backward_step(total, t):
        rows, cols, vals = tile_edges(t, block_count, block_rows, block_cols, edge_offsets, edge_weight)
        return total.at[cols].add(vals[:, None] * grad_pre_f[rows]), None

    grad_proj, _ = lax.scan(backward_step, jnp.zeros((NODES, F), jnp.float32), tiles)
    grad_proj = grad_proj.astype(jnp.bfloat16)
    grad_features = jnp.dot(grad_proj, weight.T, preferred_element_type=jnp.float32).astype(jnp.bfloat16)
    scale = NODES ** -0.5
    grad_weight = jnp.dot(features.T, grad_proj, preferred_element_type=jnp.float32) * scale
    grad_bias = jnp.sum(grad_pre_f, axis=0) * scale
    return output, grad_features, grad_weight, grad_bias
```

```python
import jax
import jax.numpy as jnp
from jax import lax
from jax.sharding import PartitionSpec as P


def swap(x, axis, bit):
    n = lax.axis_size(axis)
    return lax.ppermute(x, axis, [(i, i ^ bit) for i in range(n)])


def bits_of(axis):
    n = lax.axis_size(axis)
    return [1 << k for k in range(n.bit_length() - 1)]


def scatter_sum(x, axis):
    for bit in bits_of(axis):
        pairs = x.reshape((x.shape[0] // 2, 2) + x.shape[1:])
        x = pairs[:, 0] + swap(pairs[:, 1], axis, bit)
    return x[0]


def gather_relative(x, axis):
    x = x[None]
    for bit in reversed(bits_of(axis)):
        x = jnp.stack([x, swap(x, axis, bit)], axis=1)
        x = x.reshape((x.shape[0] * 2,) + x.shape[2:])
    return x


def total_sum(x, axes):
    for axis in axes:
        for bit in bits_of(axis):
            x = x + swap(x, axis, bit)
    return x


def shards(
    features,
    weight,
    bias,
    cotangent,
    block_count,
    block_rows,
    block_cols,
    edge_offsets,
    edge_weight,
):
    node_dev, width = features.shape
    n_row = lax.axis_size("row")
    n_col = lax.axis_size("col")
    slots = block_rows.shape[2]
    batch = min(64, slots)
    count = block_count[0, 0]
    turns = (count + batch - 1) // batch
    mine = lax.axis_index("col")
    per = node_dev // 128
    brow = block_rows[0, 0]
    brow = ((brow // per) ^ mine) * per + brow % per
    bcol = block_cols[0, 0]
    offsets = edge_offsets[0, 0]
    weights = edge_weight[0, 0]
    lanes = jnp.arange(batch, dtype=jnp.int32)
    within = jnp.arange(128, dtype=jnp.int32)
    row_blocks = node_dev * n_col // 128
    col_blocks = node_dev * n_row // 128
    row_ids = jnp.arange(row_blocks, dtype=jnp.int32)
    col_ids = jnp.arange(col_blocks, dtype=jnp.int32)
    projected = jnp.dot(features, weight, preferred_element_type=jnp.float32).astype(jnp.bfloat16)
    panel = lax.all_gather(projected, "row", axis=0, tiled=True).reshape(-1, 128, width)

    def forward_step(i, carry):
        stored, totals = carry
        start = i * batch
        offs = lax.dynamic_slice_in_dim(offsets, start, batch, 0)
        vals = lax.dynamic_slice_in_dim(weights, start, batch, 0).astype(jnp.float32)
        vals = jnp.where((start + lanes < count)[:, None], vals, 0.0)
        left = jnp.where((offs // 128)[:, :, None] == within, vals[:, :, None], 0.0).astype(
            jnp.bfloat16
        )
        right = ((offs % 128)[:, :, None] == within).astype(jnp.bfloat16)
        dense = jnp.einsum("bei,bej->bij", left, right, preferred_element_type=jnp.float32).astype(
            jnp.bfloat16
        )
        stored = lax.dynamic_update_slice_in_dim(stored, dense, start, 0)
        rows_here = lax.dynamic_slice_in_dim(brow, start, batch, 0)
        cols_here = lax.dynamic_slice_in_dim(bcol, start, batch, 0)
        product = jnp.einsum(
            "bij,bjf->bif", dense, panel[cols_here], preferred_element_type=jnp.float32
        )
        select = (rows_here[:, None] == row_ids).astype(jnp.float32)
        added = jnp.einsum(
            "br,bif->rif",
            select,
            product,
            precision=lax.Precision.HIGHEST,
            preferred_element_type=jnp.float32,
        )
        return (stored, totals + added)

    stored0 = jnp.zeros((slots, 128, 128), jnp.bfloat16)
    totals0 = jnp.zeros((row_blocks, 128, width), jnp.float32)
    stored, totals = lax.fori_loop(0, turns, forward_step, (stored0, totals0))
    totals = totals.reshape(-1, width)
    own = scatter_sum(totals.reshape(n_col, node_dev, width), "col")
    pre = own + bias
    output = jnp.maximum(pre, 0.0).astype(jnp.bfloat16)
    grad_own = jnp.where(pre > 0, cotangent.astype(jnp.float32), 0.0).astype(jnp.bfloat16)
    grad_panel = gather_relative(grad_own, "col")
    grad_blocks = grad_panel.reshape(-1, 128, width)

    def backward_step(i, acc):
        start = i * batch
        dense = lax.dynamic_slice_in_dim(stored, start, batch, 0)
        rows_here = lax.dynamic_slice_in_dim(brow, start, batch, 0)
        cols_here = lax.dynamic_slice_in_dim(bcol, start, batch, 0)
        product = jnp.einsum(
            "bij,bif->bjf", dense, grad_blocks[rows_here], preferred_element_type=jnp.float32
        )
        select = (cols_here[:, None] == col_ids).astype(jnp.float32)
        added = jnp.einsum(
            "bc,bjf->cjf",
            select,
            product,
            precision=lax.Precision.HIGHEST,
            preferred_element_type=jnp.float32,
        )
        return acc + added

    acc0 = jnp.zeros((col_blocks, 128, width), jnp.float32)
    acc = lax.fori_loop(0, turns, backward_step, acc0)
    grad_proj = lax.psum_scatter(
        acc.reshape(-1, width), "row", scatter_dimension=0, tiled=True
    ).astype(jnp.bfloat16)
    grad_features = lax.dot_general(
        grad_proj, weight, (((1,), (1,)), ((), ())), preferred_element_type=jnp.float32
    ).astype(jnp.bfloat16)
    local_weight = lax.dot_general(
        features, grad_proj, (((0,), (0,)), ((), ())), preferred_element_type=jnp.float32
    )
    local_bias = jnp.sum(grad_own.astype(jnp.float32), axis=0)
    local = jnp.concatenate([local_weight, jnp.tile(local_bias[None], (8, 1))], axis=0)
    total = total_sum(local, ("row", "col"))
    total_weight, total_bias = total[: weight.shape[0]], total[weight.shape[0]]
    scale = (node_dev * n_row * n_col) ** (-0.5)
    return (output, grad_features, total_weight * scale, total_bias * scale)


def solution(mesh):
    return jax.shard_map(
        shards,
        mesh=mesh,
        in_specs=(
            P(("row", "col"), None),
            P(),
            P(),
            P(("row", "col"), None),
            P("row", "col"),
            P("row", "col", None),
            P("row", "col", None),
            P("row", "col", None, None),
            P("row", "col", None, None),
        ),
        out_specs=(P(("row", "col"), None), P(("row", "col"), None), P(), P()),
        check_vma=False,
    )
```

```python
import functools
import jax
import jax.numpy as jnp
from jax import lax
from jax.experimental import pallas as pl
from jax.experimental.pallas import tpu as pltpu
from jax.sharding import PartitionSpec as P


def swap(x, axis, bit):
    n = lax.axis_size(axis)
    return lax.ppermute(x, axis, [(i, i ^ bit) for i in range(n)])


def bits_of(axis):
    n = lax.axis_size(axis)
    return [1 << k for k in range(n.bit_length() - 1)]


def scatter_sum(x, axis):
    for bit in bits_of(axis):
        pairs = x.reshape((x.shape[0] // 2, 2) + x.shape[1:])
        x = pairs[:, 0] + swap(pairs[:, 1], axis, bit)
    return x[0]


def gather_relative(x, axis):
    x = x[None]
    for bit in reversed(bits_of(axis)):
        x = jnp.stack([x, swap(x, axis, bit)], axis=1)
        x = x.reshape((x.shape[0] * 2,) + x.shape[2:])
    return x


def total_sum(x, axes):
    for axis in axes:
        for bit in bits_of(axis):
            x = x + swap(x, axis, bit)
    return x


GROUP = 8


def forward_kernel(meta, order, dst, col, offs, wts, panel, totals, dense, dbuf, sems):
    turns = meta[0]
    rows = lax.broadcasted_iota(jnp.int32, (128, 128), 0)
    totals[...] = jnp.zeros_like(totals)

    def out_copy(i, slot):
        return pltpu.make_async_copy(
            dbuf.at[slot], dense.at[pl.ds(i * GROUP, GROUP)], sems.at[slot]
        )

    def turn(i, _):
        slot = lax.rem(i, 2)

        @pl.when(i >= 2)
        def _():
            out_copy(i - 2, slot).wait()

        for u in range(GROUP):
            p = i * GROUP + u
            s = order[p]
            o = offs[pl.ds(s, 1), :]
            w = wts[pl.ds(s, 1), :]
            left = jnp.where(rows == (o >> 7), w, 0.0).astype(jnp.bfloat16)
            right = jnp.where(rows == (o & 127), 1.0, 0.0).astype(jnp.bfloat16)
            block = lax.dot_general(
                left, right, (((1,), (1,)), ((), ())), preferred_element_type=jnp.float32
            ).astype(jnp.bfloat16)
            dbuf[slot, u] = block
            totals[dst[p]] += jnp.dot(block, panel[col[p]], preferred_element_type=jnp.float32)
        out_copy(i, slot).start()
        return 0

    lax.fori_loop(0, turns, turn, 0)

    @pl.when(turns >= 2)
    def _():
        out_copy(turns - 2, lax.rem(turns, 2)).wait()

    @pl.when(turns >= 1)
    def _():
        out_copy(turns - 1, lax.rem(turns + 1, 2)).wait()


def backward_kernel(meta, src, col, grad, dense, acc, dbuf, sems):
    turns = meta[0]
    acc[...] = jnp.zeros_like(acc)

    def in_copy(i, slot):
        return pltpu.make_async_copy(
            dense.at[pl.ds(i * GROUP, GROUP)], dbuf.at[slot], sems.at[slot]
        )

    for k in range(2):

        @pl.when(turns > k)
        def _():
            in_copy(k, k).start()

    def turn(i, _):
        slot = lax.rem(i, 3)

        @pl.when(i + 2 < turns)
        def _():
            in_copy(i + 2, lax.rem(i + 2, 3)).start()

        in_copy(i, slot).wait()
        for u in range(GROUP):
            p = i * GROUP + u
            acc[col[p]] += jnp.dot(
                grad[src[p]], dbuf[slot, u], preferred_element_type=jnp.float32
            )
        return 0

    lax.fori_loop(0, turns, turn, 0)


SMEM = pl.BlockSpec(memory_space=pltpu.SMEM)
VMEM = pl.BlockSpec(memory_space=pltpu.VMEM)
HBM = pl.BlockSpec(memory_space=pl.ANY)
LIMIT = 40 * 1024 * 1024


def run_forward(meta, order, dst, col, offs, wts, panel, row_blocks):
    slots = order.shape[0]
    width = panel.shape[-1]
    return pl.pallas_call(
        forward_kernel,
        out_shape=(
            jax.ShapeDtypeStruct((row_blocks, 128, width), jnp.float32),
            jax.ShapeDtypeStruct((slots, 128, 128), jnp.bfloat16),
        ),
        in_specs=[SMEM, SMEM, SMEM, SMEM, VMEM, VMEM, VMEM],
        out_specs=(VMEM, HBM),
        scratch_shapes=[
            pltpu.VMEM((2, GROUP, 128, 128), jnp.bfloat16),
            pltpu.SemaphoreType.DMA((2,)),
        ],
        compiler_params=pltpu.CompilerParams(vmem_limit_bytes=LIMIT),
    )(meta, order, dst, col, offs, wts, panel)


def run_backward(meta, src, col, grad, dense, col_blocks):
    width = grad.shape[1]
    return pl.pallas_call(
        backward_kernel,
        out_shape=jax.ShapeDtypeStruct((col_blocks, width, 128), jnp.float32),
        in_specs=[SMEM, SMEM, SMEM, VMEM, HBM],
        out_specs=VMEM,
        scratch_shapes=[
            pltpu.VMEM((3, GROUP, 128, 128), jnp.bfloat16),
            pltpu.SemaphoreType.DMA((3,)),
        ],
        compiler_params=pltpu.CompilerParams(vmem_limit_bytes=LIMIT),
    )(meta, src, col, grad, dense)


def shards(
    features,
    weight,
    bias,
    cotangent,
    block_count,
    block_rows,
    block_cols,
    edge_offsets,
    edge_weight,
):
    node_dev, width = features.shape
    n_row = lax.axis_size("row")
    n_col = lax.axis_size("col")
    slots = block_rows.shape[2]
    count = block_count[0, 0]
    mine = lax.axis_index("col")
    per = node_dev // 128
    row_blocks = per * n_col
    col_blocks = per * n_row

    brow = block_rows[0, 0]
    brow = ((brow // per) ^ mine) * per + brow % per
    bcol = block_cols[0, 0]
    ids = jnp.arange(slots, dtype=jnp.int32)
    order = jnp.where(ids < count, ids, slots)
    dst = jnp.where(ids < count, brow, 0)
    col = jnp.where(ids < count, bcol, 0)
    meta = ((count + GROUP - 1) // GROUP).reshape(1)
    offs = jnp.pad(edge_offsets[0, 0], ((0, 8), (0, 0)))
    wts = jnp.pad(edge_weight[0, 0].astype(jnp.float32), ((0, 8), (0, 0)))

    panel_in = lax.all_gather(features, "row", axis=0, tiled=True)
    panel = jnp.dot(panel_in, weight, preferred_element_type=jnp.float32).astype(jnp.bfloat16)
    totals, dense = run_forward(
        meta, order, dst, col, offs, wts, panel.reshape(col_blocks, 128, width), row_blocks
    )
    own = scatter_sum(totals.reshape(n_col, node_dev, width), "col")
    pre = own + bias
    output = jnp.maximum(pre, 0.0).astype(jnp.bfloat16)
    grad_own = jnp.where(pre > 0, cotangent.astype(jnp.float32), 0.0).astype(jnp.bfloat16)
    local_bias = jnp.sum(grad_own.astype(jnp.float32), axis=0)
    turned = jnp.swapaxes(grad_own.reshape(per, 128, width), 1, 2)
    grad = gather_relative(turned, "col").reshape(row_blocks, width, 128)

    acc = run_backward(meta, dst, col, grad, dense, col_blocks)
    back = jnp.swapaxes(acc, 1, 2).reshape(col_blocks * 128, width)
    local_weight = lax.dot_general(
        panel_in,
        back.astype(jnp.bfloat16),
        (((0,), (0,)), ((), ())),
        preferred_element_type=jnp.float32,
    )
    local = jnp.concatenate([local_weight, jnp.tile(local_bias[None], (8, 1))], axis=0)
    total = total_sum(local, ("row", "col"))
    mine_row = lax.axis_index("row")
    grad_proj = scatter_sum(
        jnp.stack(
            [
                lax.dynamic_slice_in_dim(back, (mine_row ^ k) * node_dev, node_dev, 0)
                for k in range(n_row)
            ]
        ),
        "row",
    ).astype(jnp.bfloat16)
    grad_features = lax.dot_general(
        grad_proj, weight, (((1,), (1,)), ((), ())), preferred_element_type=jnp.float32
    ).astype(jnp.bfloat16)
    scale = (node_dev * n_row * n_col) ** (-0.5)
    return (
        output,
        grad_features,
        total[: weight.shape[0]] * scale,
        total[weight.shape[0]] * scale,
    )


def solution(mesh):
    return jax.shard_map(
        shards,
        mesh=mesh,
        in_specs=(
            P(("row", "col"), None),
            P(),
            P(),
            P(("row", "col"), None),
            P("row", "col"),
            P("row", "col", None),
            P("row", "col", None),
            P("row", "col", None, None),
            P("row", "col", None, None),
        ),
        out_specs=(P(("row", "col"), None), P(("row", "col"), None), P(), P()),
        check_vma=False,
    )
```

```python
import functools
import jax
import jax.numpy as jnp
from jax import lax
from jax.experimental import pallas as pl
from jax.experimental.pallas import tpu as pltpu
from jax.sharding import PartitionSpec as P


def swap(x, axis, bit):
    n = lax.axis_size(axis)
    return lax.ppermute(x, axis, [(i, i ^ bit) for i in range(n)])


def bits_of(axis):
    n = lax.axis_size(axis)
    return [1 << k for k in range(n.bit_length() - 1)]


def scatter_sum(x, axis):
    for bit in bits_of(axis):
        pairs = x.reshape((x.shape[0] // 2, 2) + x.shape[1:])
        x = pairs[:, 0] + swap(pairs[:, 1], axis, bit)
    return x[0]


def gather_relative(x, axis):
    x = x[None]
    for bit in reversed(bits_of(axis)):
        x = jnp.stack([x, swap(x, axis, bit)], axis=1)
        x = x.reshape((x.shape[0] * 2,) + x.shape[2:])
    return x


def total_sum(x, axes):
    for axis in axes:
        for bit in bits_of(axis):
            x = x + swap(x, axis, bit)
    return x


GROUP = 8
ROOM = 64
SPARE = 8
FIELD = 1 << 16
UNIT = 2.0**-14


def block_of(code, rows):
    o = code >> 16
    w = (code & (FIELD - 1)).astype(jnp.float32) * UNIT
    left = jnp.where(rows == (o >> 7), w, 0.0).astype(jnp.bfloat16)
    right = jnp.where(rows == (o & 127), 1.0, 0.0).astype(jnp.bfloat16)
    return lax.dot_general(
        left, right, (((1,), (1,)), ((), ())), preferred_element_type=jnp.float32
    ).astype(jnp.bfloat16)


def pack_kernel(meta, pos, codes, labels, out):
    out[...] = jnp.zeros_like(out)
    stride = ROOM + SPARE
    for k in range(labels.shape[0]):
        out[pl.ds(k * stride + ROOM, 1), :] = labels[pl.ds(k, 1), :]

    def turn(i, _):
        for u in range(GROUP):
            s = i * GROUP + u
            out[pl.ds(pos[s], 1), :] = codes[pl.ds(s, 1), :]
        return 0

    lax.fori_loop(0, meta[0], turn, 0)


def build_kernel(meta, order, codes, dense, dbuf, sems):
    turns = meta[0]
    rows = lax.broadcasted_iota(jnp.int32, (128, 128), 0)

    def out_copy(i, slot):
        return pltpu.make_async_copy(
            dbuf.at[slot], dense.at[pl.ds(i * GROUP, GROUP)], sems.at[slot]
        )

    def turn(i, _):
        slot = lax.rem(i, 2)

        @pl.when(i >= 2)
        def _():
            out_copy(i - 2, slot).wait()

        lines = [codes[pl.ds(order[i * GROUP + u], 1), :] for u in range(GROUP)]
        blocks = [block_of(line, rows) for line in lines]
        for u in range(GROUP):
            dbuf[slot, u] = blocks[u]
        out_copy(i, slot).start()
        return 0

    lax.fori_loop(0, turns, turn, 0)

    @pl.when(turns >= 2)
    def _():
        out_copy(turns - 2, lax.rem(turns, 2)).wait()

    @pl.when(turns >= 1)
    def _():
        out_copy(turns - 1, lax.rem(turns + 1, 2)).wait()


def forward_kernel(meta, order, col, owner, codes, panel, totals, dbuf):
    turns = meta[0]
    rows = lax.broadcasted_iota(jnp.int32, (128, 128), 0)
    totals[...] = jnp.zeros_like(totals)

    def build(i, slot):
        lines = [codes[pl.ds(order[i * GROUP + u], 1), :] for u in range(GROUP)]
        blocks = [block_of(line, rows) for line in lines]
        for u in range(GROUP):
            dbuf[slot, :, u * 128 : (u + 1) * 128] = blocks[u]

    def product(i, slot):
        right = jnp.concatenate([panel[col[i * GROUP + u]] for u in range(GROUP)], axis=0)
        return jnp.dot(dbuf[slot], right, preferred_element_type=jnp.float32)

    @pl.when(turns > 0)
    def _():
        build(0, 0)

    def turn(i, _):
        slot = lax.rem(i, 2)
        added = product(i, slot)
        build(i + 1, 1 - slot)
        totals[owner[i]] += added
        return 0

    lax.fori_loop(0, turns, turn, 0)


def tile_kernel(meta, order, dst, col, codes, panel, totals):
    rows = lax.broadcasted_iota(jnp.int32, (128, 128), 0)
    totals[...] = jnp.zeros_like(totals)

    def turn(i, _):
        for u in range(GROUP):
            p = i * GROUP + u
            block = block_of(codes[pl.ds(order[p], 1), :], rows)
            totals[dst[p]] += jnp.dot(block, panel[col[p]], preferred_element_type=jnp.float32)
        return 0

    lax.fori_loop(0, meta[0], turn, 0)


def backward_kernel(meta, src, owner, grad, dense, acc, dbuf, sems):
    turns = meta[0]
    acc[...] = jnp.zeros_like(acc)

    def in_copy(i, slot):
        return pltpu.make_async_copy(
            dense.at[pl.ds(i * GROUP, GROUP)], dbuf.at[slot], sems.at[slot]
        )

    for k in range(2):

        @pl.when(turns > k)
        def _():
            in_copy(k, k).start()

    def turn(i, _):
        slot = lax.rem(i, 3)

        @pl.when(i + 2 < turns)
        def _():
            in_copy(i + 2, lax.rem(i + 2, 3)).start()

        in_copy(i, slot).wait()
        left = jnp.concatenate([grad[src[i * GROUP + u]] for u in range(GROUP)], axis=1)
        right = dbuf[slot].reshape(GROUP * 128, 128)
        acc[owner[i]] += jnp.dot(left, right, preferred_element_type=jnp.float32)
        return 0

    lax.fori_loop(0, turns, turn, 0)


SMEM = pl.BlockSpec(memory_space=pltpu.SMEM)
VMEM = pl.BlockSpec(memory_space=pltpu.VMEM)
HBM = pl.BlockSpec(memory_space=pl.ANY)
PARAMS = pltpu.CompilerParams(vmem_limit_bytes=48 * 1024 * 1024)


def cost(slots, products):
    flops = 2 * slots * products * 128**3
    return pl.CostEstimate(flops=flops, bytes_accessed=slots * 128 * 128 * 2, transcendentals=0)


def run_tile(meta, order, dst, col, codes, panel, row_blocks):
    return pl.pallas_call(
        tile_kernel,
        out_shape=jax.ShapeDtypeStruct((row_blocks, 128, panel.shape[-1]), jnp.float32),
        in_specs=[SMEM] * 4 + [VMEM] * 2,
        out_specs=VMEM,
        compiler_params=PARAMS,
    )(meta, order, dst, col, codes, panel)


def run_pack(meta, pos, codes, labels):
    length = labels.shape[0] * (ROOM + SPARE)
    return pl.pallas_call(
        pack_kernel,
        out_shape=jax.ShapeDtypeStruct((length, 128), jnp.int32),
        in_specs=[SMEM] * 2 + [VMEM] * 2,
        out_specs=VMEM,
        compiler_params=PARAMS,
    )(meta, pos, codes, labels)


def run_build(meta, order, codes):
    return pl.pallas_call(
        build_kernel,
        out_shape=jax.ShapeDtypeStruct((order.shape[0], 128, 128), jnp.bfloat16),
        in_specs=[SMEM] * 2 + [VMEM],
        out_specs=HBM,
        scratch_shapes=[
            pltpu.VMEM((2, GROUP, 128, 128), jnp.bfloat16),
            pltpu.SemaphoreType.DMA((2,)),
        ],
        compiler_params=PARAMS,
        cost_estimate=cost(order.shape[0], 4),
    )(meta, order, codes)


def run_forward(meta, order, col, owner, codes, panel, row_blocks):
    return pl.pallas_call(
        forward_kernel,
        out_shape=jax.ShapeDtypeStruct((row_blocks, 128, panel.shape[-1]), jnp.float32),
        in_specs=[SMEM] * 4 + [VMEM] * 2,
        out_specs=VMEM,
        scratch_shapes=[pltpu.VMEM((2, 128, GROUP * 128), jnp.bfloat16)],
        compiler_params=PARAMS,
        cost_estimate=cost(order.shape[0], 8),
    )(meta, order, col, owner, codes, panel)


def run_backward(meta, src, owner, grad, dense, col_blocks):
    return pl.pallas_call(
        backward_kernel,
        out_shape=jax.ShapeDtypeStruct((col_blocks, grad.shape[1], 128), jnp.float32),
        in_specs=[SMEM] * 3 + [VMEM, HBM],
        out_specs=VMEM,
        scratch_shapes=[
            pltpu.VMEM((3, GROUP, 128, 128), jnp.bfloat16),
            pltpu.SemaphoreType.DMA((3,)),
        ],
        compiler_params=PARAMS,
        cost_estimate=cost(src.shape[0], 4),
    )(meta, src, owner, grad, dense)


def grouped(key, live, keys):
    ids = jnp.arange(key.shape[0], dtype=jnp.int32)
    names = jnp.arange(keys, dtype=jnp.int32)
    key = jnp.where(live, key, keys)
    before = (key[None, :] == key[:, None]) & (ids[None, :] < ids[:, None])
    rank = jnp.sum(before.astype(jnp.int32), axis=1)
    counts = jnp.sum((key[None, :] == names[:, None]).astype(jnp.int32), axis=1)
    filled = (counts + GROUP - 1) // GROUP * GROUP
    base = jnp.sum(jnp.where(names[None, :] < key[:, None], filled[None, :], 0), axis=1)
    pos = jnp.where(live, base + rank, -1)
    ends = jnp.sum(jnp.where(names[None, :] <= names[:, None], filled[None, :], 0), axis=1)
    length = key.shape[0] + keys * GROUP
    first = jnp.arange(length // GROUP, dtype=jnp.int32) * GROUP
    group_key = jnp.sum((ends[None, :] <= first[:, None]).astype(jnp.int32), axis=1)
    return pos, jnp.minimum(group_key, keys - 1), jnp.sum(filled) // GROUP, length


def place(pos, value, length, fill):
    spots = jnp.arange(length, dtype=jnp.int32)
    hit = pos[None, :] == spots[:, None]
    return jnp.sum(jnp.where(hit, value[None, :] - fill, 0), axis=1) + fill


def shards(
    features,
    weight,
    bias,
    cotangent,
    block_count,
    block_rows,
    block_cols,
    edge_offsets,
    edge_weight,
):
    node_dev, width = features.shape
    n_row = lax.axis_size("row")
    n_col = lax.axis_size("col")
    slots = block_rows.shape[2]
    count = block_count[0, 0]
    mine = lax.axis_index("col")
    mine_row = lax.axis_index("row")
    per = node_dev // 128
    row_blocks = per * n_col
    col_blocks = per * n_row
    by_owner = n_row * n_col * node_dev * width * 2 <= 8 * 1024 * 1024

    brow = block_rows[0, 0]
    bcol = block_cols[0, 0]
    ids = jnp.arange(slots, dtype=jnp.int32)
    live = ids < count
    codes = edge_offsets[0, 0] * FIELD + (
        edge_weight[0, 0].astype(jnp.float32) * (1.0 / UNIT)
    ).astype(jnp.int32)
    codes = jnp.pad(codes, ((0, 8), (0, 0)))
    home = brow // per
    turns_plain = ((count + GROUP - 1) // GROUP).reshape(1)

    panel_in = lax.all_gather(features, "row", axis=0, tiled=True)

    def tile_plan(panel):
        order = jnp.where(live, ids, slots)
        dst = jnp.where(live, (home ^ mine) * per + brow % per, 0)
        totals = run_tile(turns_plain, order, dst, bcol, codes, panel, row_blocks)
        return scatter_sum(totals.reshape(n_col, node_dev, width), "col")

    if by_owner:
        same = live[None, :] & (home[None, :] == home[:, None]) & (ids[None, :] < ids[:, None])
        rank = jnp.sum(same.astype(jnp.int32), axis=1)
        over = jnp.any(live & (rank >= ROOM)).astype(jnp.int32)
        fits = live & (rank < ROOM)
        label = 1 + (brow % per) * col_blocks + bcol
        labels = place(jnp.where(fits, home * ROOM + rank, -1), label, n_col * ROOM, 0)
        labels = jnp.concatenate(
            [labels.reshape(n_col, ROOM), jnp.full((n_col, 128 - ROOM), over)], axis=1
        )
        stride = ROOM + SPARE
        pos = jnp.where(fits, home * stride + rank, ROOM + SPARE - 1)
        packed = run_pack(turns_plain, pos, codes, labels)
        came = lax.all_to_all(
            packed.reshape(n_col, stride, 128), "col", split_axis=0, concat_axis=0, tiled=True
        )
        spread = total_sum(jnp.max(came[:, ROOM, ROOM:], axis=0)[None], ("row",))
        any_over = jnp.max(spread) > 0

        projected = jnp.dot(features, weight, preferred_element_type=jnp.float32)
        everywhere = gather_relative(
            gather_relative(projected.astype(jnp.bfloat16), "col"), "row"
        )

        got = came[:, ROOM, :ROOM]
        sources = jnp.arange(n_col, dtype=jnp.int32)[:, None]
        places = jnp.arange(ROOM, dtype=jnp.int32)[None, :]
        row_here = ((got - 1) // col_blocks).reshape(-1)
        col_there = (got - 1) % col_blocks
        col_there = (
            ((col_there // per) ^ mine_row) * n_col + (sources ^ mine)
        ) * per + col_there % per
        pos, owner, turns, length = grouped(row_here, (got > 0).reshape(-1), per)
        line = (sources * stride + places).reshape(-1)
        order = place(pos, line, length + GROUP, ROOM + 1)
        cols = place(pos, col_there.reshape(-1), length + GROUP, 0)
        own = run_forward(
            turns.reshape(1),
            order,
            cols,
            owner,
            came.reshape(n_col * stride, 128),
            everywhere.reshape(-1, 128, width),
            per,
        ).reshape(node_dev, width)

        def slow():
            blocks = [
                lax.dynamic_index_in_dim(everywhere[:, 0], mine_row ^ k, 0, keepdims=False)
                for k in range(n_row)
            ]
            return tile_plan(jnp.stack(blocks).reshape(col_blocks, 128, width))

        own = lax.cond(any_over, slow, lambda: own)
    else:
        panel = jnp.dot(panel_in, weight, preferred_element_type=jnp.float32)
        own = tile_plan(panel.astype(jnp.bfloat16).reshape(col_blocks, 128, width))

    pos, back_owner, back_turns, length = grouped(bcol, live, col_blocks)
    back_order = place(pos, ids, length, slots)
    back_src = place(pos, (home ^ mine) * per + brow % per, length, 0)
    back_turns = back_turns.reshape(1)
    dense = run_build(back_turns, back_order, codes)

    pre = own + bias
    output = jnp.maximum(pre, 0.0).astype(jnp.bfloat16)
    grad_own = jnp.where(pre > 0, cotangent.astype(jnp.float32), 0.0).astype(jnp.bfloat16)
    local_bias = jnp.sum(grad_own.astype(jnp.float32), axis=0)
    turned = jnp.swapaxes(grad_own.reshape(per, 128, width), 1, 2)
    grad = gather_relative(turned, "col").reshape(row_blocks, width, 128)

    acc = run_backward(back_turns, back_src, back_owner, grad, dense, col_blocks)
    back = jnp.swapaxes(acc, 1, 2).reshape(col_blocks * 128, width)
    local_weight = lax.dot_general(
        panel_in,
        back.astype(jnp.bfloat16),
        (((0,), (0,)), ((), ())),
        preferred_element_type=jnp.float32,
    )
    local = jnp.concatenate([local_weight, jnp.tile(local_bias[None], (8, 1))], axis=0)
    total = total_sum(local, ("row", "col"))
    grad_proj = scatter_sum(
        jnp.stack(
            [
                lax.dynamic_slice_in_dim(back, (mine_row ^ k) * node_dev, node_dev, 0)
                for k in range(n_row)
            ]
        ),
        "row",
    ).astype(jnp.bfloat16)
    grad_features = lax.dot_general(
        grad_proj, weight, (((1,), (1,)), ((), ())), preferred_element_type=jnp.float32
    ).astype(jnp.bfloat16)
    scale = (node_dev * n_row * n_col) ** (-0.5)
    return (
        output,
        grad_features,
        total[: weight.shape[0]] * scale,
        total[weight.shape[0]] * scale,
    )


def solution(mesh):
    return jax.shard_map(
        shards,
        mesh=mesh,
        in_specs=(
            P(("row", "col"), None),
            P(),
            P(),
            P(("row", "col"), None),
            P("row", "col"),
            P("row", "col", None),
            P("row", "col", None),
            P("row", "col", None, None),
            P("row", "col", None, None),
        ),
        out_specs=(P(("row", "col"), None), P(("row", "col"), None), P(), P()),
        check_vma=False,
    )
```

```python
import functools
import functools
import jax
import jax.numpy as jnp
from jax import lax
from jax.experimental import pallas as pl
from jax.experimental.pallas import tpu as pltpu
from jax.sharding import PartitionSpec as P


def swap(x, axis, bit):
    n = lax.axis_size(axis)
    return lax.ppermute(x, axis, [(i, i ^ bit) for i in range(n)])


def bits_of(axis):
    n = lax.axis_size(axis)
    return [1 << k for k in range(n.bit_length() - 1)]


def scatter_sum(x, axis):
    for bit in bits_of(axis):
        pairs = x.reshape((x.shape[0] // 2, 2) + x.shape[1:])
        x = pairs[:, 0] + swap(pairs[:, 1], axis, bit)
    return x[0]


def part_orders(per):
    bits = bits_of("col")[::-1]
    turned = bits[:-2] + bits[-1:] + bits[-2:-1]
    return [bits, turned] if per % 2 == 0 and len(bits) > 1 else [bits]


def gather_pieces(blocks):
    orders = part_orders(blocks.shape[0])
    size = blocks.shape[0] // len(orders)
    held = [blocks[i * size : (i + 1) * size][None] for i in range(len(orders))]
    for step in range(len(orders[0]) - 1):
        came = [swap(x, "col", order[step]) for x, order in zip(held, orders)]
        held = [jnp.concatenate([x, y], axis=0) for x, y in zip(held, came)]
    came = [swap(x, "col", order[-1]) for x, order in zip(held, orders)]
    shape = (-1,) + blocks.shape[1:]
    return [[x.reshape(shape), y.reshape(shape)] for x, y in zip(held, came)]


def piece_index(per, far, block, rho=0, n_row=1):
    orders = part_orders(per)
    size = per // len(orders)
    half = lax.axis_size("col") // 2
    result = 0
    for i, order in enumerate(orders):
        spot = sum(((far & bit) > 0).astype(jnp.int32) << t for t, bit in enumerate(order))
        piece = (i * n_row + rho) * 2 + spot // half
        here = (piece * half + spot % half) * size + block % size
        result = jnp.where(block // size == i, here, result)
    return result


def total_sum(x, axes):
    for axis in axes:
        for bit in bits_of(axis):
            x = x + swap(x, axis, bit)
    return x


GROUP = 8
DEPTH = 8
ROOM = 64
SPARE = 8
FIELD = 1 << 16
UNIT = 2.0**-14


def block_of(code, rows):
    o = code >> 16
    w = (code & (FIELD - 1)).astype(jnp.float32) * UNIT
    left = jnp.where(rows == (o >> 7), w, 0.0).astype(jnp.bfloat16)
    right = jnp.where(rows == (o & 127), 1.0, 0.0).astype(jnp.bfloat16)
    return lax.dot_general(
        left, right, (((1,), (1,)), ((), ())), preferred_element_type=jnp.float32
    ).astype(jnp.bfloat16)


def pack_kernel(meta, pos, codes, labels, out):
    out[...] = jnp.zeros_like(out)
    stride = ROOM + SPARE
    for k in range(labels.shape[0]):
        out[pl.ds(k * stride + ROOM, 1), :] = labels[pl.ds(k, 1), :]

    def turn(i, _):
        for u in range(GROUP):
            s = i * GROUP + u
            out[pl.ds(pos[s], 1), :] = codes[pl.ds(s, 1), :]
        return 0

    lax.fori_loop(0, meta[0], turn, 0)


def build_kernel(meta, order, codes, dense, dbuf, sems):
    turns = meta[0]
    rows = lax.broadcasted_iota(jnp.int32, (128, 128), 0)

    def out_copy(i):
        slot = lax.rem(i, DEPTH)
        return pltpu.make_async_copy(
            dbuf.at[slot], dense.at[pl.ds(i * GROUP, GROUP)], sems.at[slot]
        )

    def turn(i, _):
        slot = lax.rem(i, DEPTH)

        @pl.when(i >= DEPTH)
        def _():
            out_copy(i - DEPTH).wait()

        lines = [codes[pl.ds(order[i * GROUP + u], 1), :] for u in range(GROUP)]
        blocks = [block_of(line, rows) for line in lines]
        for u in range(GROUP):
            dbuf[slot, u] = blocks[u]
        out_copy(i).start()
        return 0

    lax.fori_loop(0, turns, turn, 0)

    def finish(i, _):
        out_copy(i).wait()
        return 0

    lax.fori_loop(jnp.maximum(turns - DEPTH, 0), turns, finish, 0)


def fetch(pieces, into, sems):
    size = pieces[0].shape[0]
    copies = [
        pltpu.make_async_copy(piece, into.at[pl.ds(i * size, size)], sems.at[i])
        for i, piece in enumerate(pieces)
    ]
    for copy in copies:
        copy.start()
    return copies


def forward_kernel(n, meta, order, col, owner, codes, *refs):
    pieces, (totals, feat, proj, dbuf, sems) = refs[: 2 * n], refs[2 * n :]
    turns = meta[0]
    rows = lax.broadcasted_iota(jnp.int32, (128, 128), 0)
    copies = fetch(pieces[:n], feat, sems.at[0]) + fetch(pieces[n:], proj, sems.at[1])
    totals[...] = jnp.zeros_like(totals)

    def build(i, slot):
        lines = [codes[pl.ds(order[i * GROUP + u], 1), :] for u in range(GROUP)]
        blocks = [block_of(line, rows) for line in lines]
        for u in range(GROUP):
            dbuf[slot, :, u * 128 : (u + 1) * 128] = blocks[u]

    def product(i, slot):
        spots = [col[i * GROUP + u] for u in range(GROUP)]
        right = jnp.concatenate(
            [jnp.concatenate([proj[c], feat[c]], axis=1) for c in spots], axis=0
        )
        return jnp.dot(dbuf[slot], right, preferred_element_type=jnp.float32)

    @pl.when(turns > 0)
    def _():
        build(0, 0)

    for copy in copies:
        copy.wait()

    def turn(i, _):
        slot = lax.rem(i, 2)
        added = product(i, slot)
        build(i + 1, 1 - slot)
        totals[owner[i]] += added
        return 0

    lax.fori_loop(0, turns, turn, 0)


def tile_kernel(meta, order, dst, col, codes, panel, totals):
    rows = lax.broadcasted_iota(jnp.int32, (128, 128), 0)
    totals[...] = jnp.zeros_like(totals)

    def turn(i, _):
        for u in range(GROUP):
            p = i * GROUP + u
            block = block_of(codes[pl.ds(order[p], 1), :], rows)
            totals[dst[p]] += jnp.dot(block, panel[col[p]], preferred_element_type=jnp.float32)
        return 0

    lax.fori_loop(0, meta[0], turn, 0)


def backward_kernel(n, meta, src, owner, dense, *refs):
    pieces, (acc, grad, dbuf, grad_sems, sems) = refs[:n], refs[n:]
    turns = meta[0]
    copies = fetch(pieces, grad, grad_sems)

    def in_copy(i):
        slot = lax.rem(i, DEPTH)
        return pltpu.make_async_copy(
            dense.at[pl.ds(i * GROUP, GROUP)], dbuf.at[slot], sems.at[slot]
        )

    def begin(i, _):
        in_copy(i).start()
        return 0

    lax.fori_loop(0, jnp.minimum(turns, DEPTH - 1), begin, 0)
    acc[...] = jnp.zeros_like(acc)
    for copy in copies:
        copy.wait()

    def turn(i, _):
        @pl.when(i + DEPTH - 1 < turns)
        def _():
            in_copy(i + DEPTH - 1).start()

        in_copy(i).wait()
        left = jnp.concatenate([grad[src[i * GROUP + u]] for u in range(GROUP)], axis=1)
        right = dbuf[lax.rem(i, DEPTH)].reshape(GROUP * 128, 128)
        acc[owner[i]] += jnp.dot(left, right, preferred_element_type=jnp.float32)
        return 0

    lax.fori_loop(0, turns, turn, 0)


SMEM = pl.BlockSpec(memory_space=pltpu.SMEM)
VMEM = pl.BlockSpec(memory_space=pltpu.VMEM)
HBM = pl.BlockSpec(memory_space=pl.ANY)
PARAMS = pltpu.CompilerParams(vmem_limit_bytes=48 * 1024 * 1024)


def cost(slots, products):
    flops = 2 * slots * products * 128**3
    return pl.CostEstimate(flops=flops, bytes_accessed=slots * 128 * 128 * 2, transcendentals=0)


def run_tile(meta, order, dst, col, codes, panel, row_blocks):
    return pl.pallas_call(
        tile_kernel,
        out_shape=jax.ShapeDtypeStruct((row_blocks, 128, panel.shape[-1]), jnp.float32),
        in_specs=[SMEM] * 4 + [VMEM] * 2,
        out_specs=VMEM,
        compiler_params=PARAMS,
    )(meta, order, dst, col, codes, panel)


def run_pack(meta, pos, codes, labels):
    length = labels.shape[0] * (ROOM + SPARE)
    return pl.pallas_call(
        pack_kernel,
        out_shape=jax.ShapeDtypeStruct((length, 128), jnp.int32),
        in_specs=[SMEM] * 2 + [VMEM] * 2,
        out_specs=VMEM,
        compiler_params=PARAMS,
    )(meta, pos, codes, labels)


def run_build(meta, order, codes):
    return pl.pallas_call(
        build_kernel,
        out_shape=jax.ShapeDtypeStruct((order.shape[0], 128, 128), jnp.bfloat16),
        in_specs=[SMEM] * 2 + [VMEM],
        out_specs=HBM,
        scratch_shapes=[
            pltpu.VMEM((DEPTH, GROUP, 128, 128), jnp.bfloat16),
            pltpu.SemaphoreType.DMA((DEPTH,)),
        ],
        compiler_params=PARAMS,
        cost_estimate=cost(order.shape[0], 4),
    )(meta, order, codes)


def run_forward(meta, order, col, owner, codes, feat, proj, row_blocks):
    n = len(feat)
    size, _, width = feat[0].shape
    return pl.pallas_call(
        functools.partial(forward_kernel, n),
        out_shape=jax.ShapeDtypeStruct((row_blocks, 128, 2 * width), jnp.float32),
        in_specs=[SMEM] * 4 + [VMEM] + [HBM] * (2 * n),
        out_specs=VMEM,
        scratch_shapes=[
            pltpu.VMEM((n * size, 128, width), jnp.bfloat16),
            pltpu.VMEM((n * size, 128, width), jnp.bfloat16),
            pltpu.VMEM((2, 128, GROUP * 128), jnp.bfloat16),
            pltpu.SemaphoreType.DMA((2, n)),
        ],
        compiler_params=PARAMS,
        cost_estimate=cost(order.shape[0], 8),
    )(meta, order, col, owner, codes, *feat, *proj)


def run_backward(meta, src, owner, pieces, dense, col_blocks):
    n = len(pieces)
    size, width, _ = pieces[0].shape
    return pl.pallas_call(
        functools.partial(backward_kernel, n),
        out_shape=jax.ShapeDtypeStruct((col_blocks, width, 128), jnp.float32),
        in_specs=[SMEM] * 3 + [HBM] * (n + 1),
        out_specs=VMEM,
        scratch_shapes=[
            pltpu.VMEM((n * size, width, 128), jnp.bfloat16),
            pltpu.VMEM((DEPTH, GROUP, 128, 128), jnp.bfloat16),
            pltpu.SemaphoreType.DMA((n,)),
            pltpu.SemaphoreType.DMA((DEPTH,)),
        ],
        compiler_params=PARAMS,
        cost_estimate=cost(src.shape[0], 4),
    )(meta, src, owner, dense, *pieces)


def grouped(key, live, keys):
    ids = jnp.arange(key.shape[0], dtype=jnp.int32)
    names = jnp.arange(keys, dtype=jnp.int32)
    key = jnp.where(live, key, keys)
    before = (key[None, :] == key[:, None]) & (ids[None, :] < ids[:, None])
    rank = jnp.sum(before.astype(jnp.int32), axis=1)
    counts = jnp.sum((key[None, :] == names[:, None]).astype(jnp.int32), axis=1)
    filled = (counts + GROUP - 1) // GROUP * GROUP
    base = jnp.sum(jnp.where(names[None, :] < key[:, None], filled[None, :], 0), axis=1)
    pos = jnp.where(live, base + rank, -1)
    ends = jnp.sum(jnp.where(names[None, :] <= names[:, None], filled[None, :], 0), axis=1)
    length = key.shape[0] + keys * GROUP
    first = jnp.arange(length // GROUP, dtype=jnp.int32) * GROUP
    group_key = jnp.sum((ends[None, :] <= first[:, None]).astype(jnp.int32), axis=1)
    return pos, jnp.minimum(group_key, keys - 1), jnp.sum(filled) // GROUP, length


def place(pos, value, length, fill):
    spots = jnp.arange(length, dtype=jnp.int32)
    hit = pos[None, :] == spots[:, None]
    return jnp.sum(jnp.where(hit, value[None, :] - fill, 0), axis=1) + fill


def shards(
    features,
    weight,
    bias,
    cotangent,
    block_count,
    block_rows,
    block_cols,
    edge_offsets,
    edge_weight,
):
    node_dev, width = features.shape
    n_row = lax.axis_size("row")
    n_col = lax.axis_size("col")
    slots = block_rows.shape[2]
    count = block_count[0, 0]
    mine = lax.axis_index("col")
    mine_row = lax.axis_index("row")
    per = node_dev // 128
    row_blocks = per * n_col
    col_blocks = per * n_row
    by_owner = n_row * n_col * node_dev * width * 2 <= 8 * 1024 * 1024

    brow = block_rows[0, 0]
    bcol = block_cols[0, 0]
    ids = jnp.arange(slots, dtype=jnp.int32)
    live = ids < count
    codes = edge_offsets[0, 0] * FIELD + (
        edge_weight[0, 0].astype(jnp.float32) * (1.0 / UNIT)
    ).astype(jnp.int32)
    codes = jnp.pad(codes, ((0, 8), (0, 0)))
    home = brow // per
    turns_plain = ((count + GROUP - 1) // GROUP).reshape(1)

    def tile_plan():
        wide = lax.all_gather(features, "row", axis=0, tiled=True)
        low = jnp.dot(wide, weight, preferred_element_type=jnp.float32).astype(jnp.bfloat16)
        panel = jnp.concatenate([low, wide], axis=1).reshape(col_blocks, 128, 2 * width)
        order = jnp.where(live, ids, slots)
        dst = jnp.where(live, (home ^ mine) * per + brow % per, 0)
        totals = run_tile(turns_plain, order, dst, bcol, codes, panel, row_blocks)
        return scatter_sum(totals.reshape(n_col, node_dev, 2 * width), "col")

    if by_owner:
        same = live[None, :] & (home[None, :] == home[:, None]) & (ids[None, :] < ids[:, None])
        rank = jnp.sum(same.astype(jnp.int32), axis=1)
        over = jnp.any(live & (rank >= ROOM)).astype(jnp.int32)
        fits = live & (rank < ROOM)
        label = 1 + (brow % per) * col_blocks + bcol
        labels = place(jnp.where(fits, home * ROOM + rank, -1), label, n_col * ROOM, 0)
        labels = jnp.concatenate(
            [labels.reshape(n_col, ROOM), jnp.full((n_col, 128 - ROOM), over)], axis=1
        )
        stride = ROOM + SPARE
        pos = jnp.where(fits, home * stride + rank, ROOM + SPARE - 1)
        packed = run_pack(turns_plain, pos, codes, labels)
        came = lax.all_to_all(
            packed.reshape(n_col, stride, 128), "col", split_axis=0, concat_axis=0, tiled=True
        )
        spread = total_sum(jnp.max(came[:, ROOM, ROOM:], axis=0)[None], ("row",))
        any_over = jnp.max(spread) > 0

        feat = []
        for pair in gather_pieces(features.reshape(per, 128, width)):
            rows = [pair]
            for bit in bits_of("row"):
                rows = rows + [[swap(x, "row", bit) for x in pair] for pair in rows]
            feat += [x for pair in rows for x in pair]
        proj = [
            jnp.dot(x.reshape(-1, width), weight, preferred_element_type=jnp.float32)
            .astype(jnp.bfloat16)
            .reshape(x.shape)
            for x in feat
        ]

        got = came[:, ROOM, :ROOM]
        sources = jnp.arange(n_col, dtype=jnp.int32)[:, None]
        places = jnp.arange(ROOM, dtype=jnp.int32)[None, :]
        row_here = ((got - 1) // col_blocks).reshape(-1)
        col_there = (got - 1) % col_blocks
        col_there = piece_index(
            per, sources ^ mine, col_there % per, (col_there // per) ^ mine_row, n_row
        )
        pos, owner, turns, length = grouped(row_here, (got > 0).reshape(-1), per)
        line = (sources * stride + places).reshape(-1)
        order = place(pos, line, length + GROUP, ROOM + 1)
        cols = place(pos, col_there.reshape(-1), length + GROUP, 0)
        own = run_forward(
            turns.reshape(1),
            order,
            cols,
            owner,
            came.reshape(n_col * stride, 128),
            feat,
            proj,
            per,
        ).reshape(node_dev, 2 * width)
        own = lax.cond(any_over, tile_plan, lambda: own)
    else:
        own = tile_plan()

    pos, back_owner, back_turns, length = grouped(bcol, live, col_blocks)
    back_order = place(pos, ids, length, slots)
    back_src = place(pos, piece_index(per, home ^ mine, brow % per), length, 0)
    back_turns = back_turns.reshape(1)
    dense = run_build(back_turns, back_order, codes)

    pre = own[:, :width] + bias
    output = jnp.maximum(pre, 0.0).astype(jnp.bfloat16)
    grad_own = jnp.where(pre > 0, cotangent.astype(jnp.float32), 0.0).astype(jnp.bfloat16)
    local_bias = jnp.sum(grad_own.astype(jnp.float32), axis=0)
    turned = jnp.swapaxes(grad_own.reshape(per, 128, width), 1, 2)
    grad = [x for pair in gather_pieces(turned) for x in pair]
    local_weight = lax.dot_general(
        own[:, width:].astype(jnp.bfloat16),
        grad_own,
        (((0,), (0,)), ((), ())),
        preferred_element_type=jnp.float32,
    )
    local = jnp.concatenate([local_weight, jnp.tile(local_bias[None], (8, 1))], axis=0)
    total = total_sum(local, ("row", "col"))

    acc = run_backward(back_turns, back_src, back_owner, grad, dense, col_blocks)
    back = jnp.swapaxes(acc, 1, 2).reshape(col_blocks * 128, width)
    grad_proj = scatter_sum(
        jnp.stack(
            [
                lax.dynamic_slice_in_dim(back, (mine_row ^ k) * node_dev, node_dev, 0)
                for k in range(n_row)
            ]
        ),
        "row",
    ).astype(jnp.bfloat16)
    grad_features = lax.dot_general(
        grad_proj, weight, (((1,), (1,)), ((), ())), preferred_element_type=jnp.float32
    ).astype(jnp.bfloat16)
    scale = (node_dev * n_row * n_col) ** (-0.5)
    return (
        output,
        grad_features,
        total[: weight.shape[0]] * scale,
        total[weight.shape[0]] * scale,
    )


def solution(mesh):
    return jax.shard_map(
        shards,
        mesh=mesh,
        in_specs=(
            P(("row", "col"), None),
            P(),
            P(),
            P(("row", "col"), None),
            P("row", "col"),
            P("row", "col", None),
            P("row", "col", None),
            P("row", "col", None, None),
            P("row", "col", None, None),
        ),
        out_specs=(P(("row", "col"), None), P(("row", "col"), None), P(), P()),
        check_vma=False,
    )
```

```python
import functools
import functools
import jax
import jax.numpy as jnp
from jax import lax
from jax.experimental import pallas as pl
from jax.experimental.pallas import tpu as pltpu
from jax.sharding import PartitionSpec as P


def swap(x, axis, bit):
    n = lax.axis_size(axis)
    return lax.ppermute(x, axis, [(i, i ^ bit) for i in range(n)])


def bits_of(axis):
    n = lax.axis_size(axis)
    return [1 << k for k in range(n.bit_length() - 1)]


def scatter_sum(x, axis):
    for bit in bits_of(axis):
        pairs = x.reshape((x.shape[0] // 2, 2) + x.shape[1:])
        x = pairs[:, 0] + swap(pairs[:, 1], axis, bit)
    return x[0]


def part_orders(per):
    bits = bits_of("col")[::-1]
    turned = bits[:-2] + bits[-1:] + bits[-2:-1]
    return [bits, turned] if per % 2 == 0 and len(bits) > 1 else [bits]


def gather_pieces(blocks, beside=None):
    orders = part_orders(blocks.shape[0])
    size = blocks.shape[0] // len(orders)
    held = [blocks[i * size : (i + 1) * size][None] for i in range(len(orders))]
    for step in range(len(orders[0]) - 1):
        came = [swap(x, "col", order[step]) for x, order in zip(held, orders)]
        held = [jnp.concatenate([x, y], axis=0) for x, y in zip(held, came)]
        if beside is not None:
            beside(step, held)
    came = [swap(x, "col", order[-1]) for x, order in zip(held, orders)]
    shape = (-1,) + blocks.shape[1:]
    return [[x.reshape(shape), y.reshape(shape)] for x, y in zip(held, came)]


def piece_index(per, far, block, rho=0, n_row=1):
    orders = part_orders(per)
    size = per // len(orders)
    half = lax.axis_size("col") // 2
    result = 0
    for i, order in enumerate(orders):
        spot = sum(((far & bit) > 0).astype(jnp.int32) << t for t, bit in enumerate(order))
        piece = (i * n_row + rho) * 2 + spot // half
        here = (piece * half + spot % half) * size + block % size
        result = jnp.where(block // size == i, here, result)
    return result


def total_steps():
    return [("row", bit) for bit in bits_of("row")] + [("col", bit) for bit in bits_of("col")[::-1]]


GROUP = 8
DEPTH = 8
ROOM = 64
SPARE = 8
FIELD = 1 << 16
UNIT = 2.0**-14


def block_of(code, rows):
    o = code >> 16
    w = (code & (FIELD - 1)).astype(jnp.float32) * UNIT
    left = jnp.where(rows == (o >> 7), w, 0.0).astype(jnp.bfloat16)
    right = jnp.where(rows == (o & 127), 1.0, 0.0).astype(jnp.bfloat16)
    return lax.dot_general(
        left, right, (((1,), (1,)), ((), ())), preferred_element_type=jnp.float32
    ).astype(jnp.bfloat16)


def pack_kernel(meta, pos, codes, labels, after, out):
    out[...] = jnp.zeros_like(out)
    stride = ROOM + SPARE
    for k in range(labels.shape[0]):
        out[pl.ds(k * stride + ROOM, 1), :] = labels[pl.ds(k, 1), :]

    def turn(i, _):
        for u in range(GROUP):
            s = i * GROUP + u
            out[pl.ds(pos[s], 1), :] = codes[pl.ds(s, 1), :]
        return 0

    lax.fori_loop(0, meta[0], turn, 0)


def build_kernel(meta, order, codes, *refs):
    dense, dbuf, sems = refs[-3:]
    start, turns = meta[0], meta[1]
    rows = lax.broadcasted_iota(jnp.int32, (128, 128), 0)

    def out_copy(i):
        slot = lax.rem(i, DEPTH)
        return pltpu.make_async_copy(
            dbuf.at[slot], dense.at[pl.ds(i * GROUP, GROUP)], sems.at[slot]
        )

    def turn(i, _):
        slot = lax.rem(i, DEPTH)

        @pl.when(i >= start + DEPTH)
        def _():
            out_copy(i - DEPTH).wait()

        lines = [codes[pl.ds(order[i * GROUP + u], 1), :] for u in range(GROUP)]
        blocks = [block_of(line, rows) for line in lines]
        for u in range(GROUP):
            dbuf[slot, u] = blocks[u]
        out_copy(i).start()
        return 0

    lax.fori_loop(start, turns, turn, 0)

    def finish(i, _):
        out_copy(i).wait()
        return 0

    lax.fori_loop(jnp.maximum(turns - DEPTH, start), turns, finish, 0)


def fetch(pieces, into, sems):
    size = pieces[0].shape[0]
    copies = [
        pltpu.make_async_copy(piece, into.at[pl.ds(i * size, size)], sems.at[i])
        for i, piece in enumerate(pieces)
    ]
    for copy in copies:
        copy.start()
    return copies


def forward_kernel(n, meta, order, col, owner, codes, weight, *refs):
    pieces, (totals, feat, proj, dbuf, sems) = refs[:n], refs[n:]
    turns = meta[0]
    rows = lax.broadcasted_iota(jnp.int32, (128, 128), 0)
    copies = fetch(pieces, feat, sems)
    size, _, width = pieces[0].shape
    batch = 4 if size % 4 == 0 else 1
    totals[...] = jnp.zeros_like(totals)

    def build(i, slot):
        lines = [codes[pl.ds(order[i * GROUP + u], 1), :] for u in range(GROUP)]
        blocks = [block_of(line, rows) for line in lines]
        for u in range(GROUP):
            dbuf[slot, :, u * 128 : (u + 1) * 128] = blocks[u]

    def product(i, slot):
        spots = [col[i * GROUP + u] for u in range(GROUP)]
        right = jnp.concatenate(
            [jnp.concatenate([proj[c], feat[c]], axis=1) for c in spots], axis=0
        )
        return jnp.dot(dbuf[slot], right, preferred_element_type=jnp.float32)

    @pl.when(turns > 0)
    def _():
        build(0, 0)

    def project(t, _):
        spot = pl.ds(t * batch, batch)
        held = feat[spot].reshape(batch * 128, width)
        low = jnp.dot(held, weight[...], preferred_element_type=jnp.float32)
        proj[spot] = low.astype(jnp.bfloat16).reshape(batch, 128, width)
        return 0

    for i, copy in enumerate(copies):
        copy.wait()
        lax.fori_loop(i * size // batch, (i + 1) * size // batch, project, 0)

    def turn(i, _):
        slot = lax.rem(i, 2)
        added = product(i, slot)
        build(i + 1, 1 - slot)
        totals[owner[i]] += added
        return 0

    lax.fori_loop(0, turns, turn, 0)


def tile_kernel(meta, order, dst, col, codes, panel, totals):
    rows = lax.broadcasted_iota(jnp.int32, (128, 128), 0)
    totals[...] = jnp.zeros_like(totals)

    def turn(i, _):
        for u in range(GROUP):
            p = i * GROUP + u
            block = block_of(codes[pl.ds(order[p], 1), :], rows)
            totals[dst[p]] += jnp.dot(block, panel[col[p]], preferred_element_type=jnp.float32)
        return 0

    lax.fori_loop(0, meta[0], turn, 0)


def backward_kernel(n, meta, src, owner, dense, *refs):
    pieces, (acc, grad, dbuf, grad_sems, sems) = refs[:n], refs[n:]
    turns = meta[0]
    copies = fetch(pieces, grad, grad_sems)

    def in_copy(i):
        slot = lax.rem(i, DEPTH)
        return pltpu.make_async_copy(
            dense.at[pl.ds(i * GROUP, GROUP)], dbuf.at[slot], sems.at[slot]
        )

    def begin(i, _):
        in_copy(i).start()
        return 0

    lax.fori_loop(0, jnp.minimum(turns, DEPTH - 1), begin, 0)
    acc[...] = jnp.zeros_like(acc)
    for copy in copies:
        copy.wait()

    def turn(i, _):
        @pl.when(i + DEPTH - 1 < turns)
        def _():
            in_copy(i + DEPTH - 1).start()

        in_copy(i).wait()
        left = jnp.concatenate([grad[src[i * GROUP + u]] for u in range(GROUP)], axis=1)
        right = dbuf[lax.rem(i, DEPTH)].reshape(GROUP * 128, 128)
        acc[owner[i]] += jnp.dot(left, right, preferred_element_type=jnp.float32)
        return 0

    lax.fori_loop(0, turns, turn, 0)


SMEM = pl.BlockSpec(memory_space=pltpu.SMEM)
VMEM = pl.BlockSpec(memory_space=pltpu.VMEM)
HBM = pl.BlockSpec(memory_space=pl.ANY)
PARAMS = pltpu.CompilerParams(vmem_limit_bytes=48 * 1024 * 1024)


def cost(slots, products):
    flops = 2 * slots * products * 128**3
    return pl.CostEstimate(flops=flops, bytes_accessed=slots * 128 * 128 * 2, transcendentals=0)


def run_tile(meta, order, dst, col, codes, panel, row_blocks):
    return pl.pallas_call(
        tile_kernel,
        out_shape=jax.ShapeDtypeStruct((row_blocks, 128, panel.shape[-1]), jnp.float32),
        in_specs=[SMEM] * 4 + [VMEM] * 2,
        out_specs=VMEM,
        compiler_params=PARAMS,
    )(meta, order, dst, col, codes, panel)


def run_pack(meta, pos, codes, labels, after):
    length = labels.shape[0] * (ROOM + SPARE)
    return pl.pallas_call(
        pack_kernel,
        out_shape=jax.ShapeDtypeStruct((length, 128), jnp.int32),
        in_specs=[SMEM] * 2 + [VMEM] * 2 + [HBM],
        out_specs=VMEM,
        compiler_params=PARAMS,
    )(meta, pos, codes, labels, after)


def run_build(meta, order, codes, after, dense):
    others = after if dense is None else after + [dense]
    return pl.pallas_call(
        build_kernel,
        out_shape=jax.ShapeDtypeStruct((order.shape[0], 128, 128), jnp.bfloat16),
        in_specs=[SMEM] * 2 + [VMEM] + [HBM] * len(others),
        out_specs=HBM,
        scratch_shapes=[
            pltpu.VMEM((DEPTH, GROUP, 128, 128), jnp.bfloat16),
            pltpu.SemaphoreType.DMA((DEPTH,)),
        ],
        input_output_aliases={} if dense is None else {2 + len(others): 0},
        compiler_params=PARAMS,
        cost_estimate=cost(order.shape[0], 2),
    )(meta, order, codes, *others)


def run_forward(meta, order, col, owner, codes, weight, feat, row_blocks):
    n = len(feat)
    size, _, width = feat[0].shape
    return pl.pallas_call(
        functools.partial(forward_kernel, n),
        out_shape=jax.ShapeDtypeStruct((row_blocks, 128, 2 * width), jnp.float32),
        in_specs=[SMEM] * 4 + [VMEM] * 2 + [HBM] * n,
        out_specs=VMEM,
        scratch_shapes=[
            pltpu.VMEM((n * size, 128, width), jnp.bfloat16),
            pltpu.VMEM((n * size, 128, width), jnp.bfloat16),
            pltpu.VMEM((2, 128, GROUP * 128), jnp.bfloat16),
            pltpu.SemaphoreType.DMA((n,)),
        ],
        compiler_params=PARAMS,
        cost_estimate=cost(order.shape[0], 8),
    )(meta, order, col, owner, codes, weight, *feat)


def run_backward(meta, src, owner, pieces, dense, col_blocks):
    n = len(pieces)
    size, width, _ = pieces[0].shape
    return pl.pallas_call(
        functools.partial(backward_kernel, n),
        out_shape=jax.ShapeDtypeStruct((col_blocks, width, 128), jnp.float32),
        in_specs=[SMEM] * 3 + [HBM] * (n + 1),
        out_specs=VMEM,
        scratch_shapes=[
            pltpu.VMEM((n * size, width, 128), jnp.bfloat16),
            pltpu.VMEM((DEPTH, GROUP, 128, 128), jnp.bfloat16),
            pltpu.SemaphoreType.DMA((n,)),
            pltpu.SemaphoreType.DMA((DEPTH,)),
        ],
        compiler_params=PARAMS,
        cost_estimate=cost(src.shape[0], 4),
    )(meta, src, owner, dense, *pieces)


def grouped(key, live, keys):
    ids = jnp.arange(key.shape[0], dtype=jnp.int32)
    names = jnp.arange(keys, dtype=jnp.int32)
    key = jnp.where(live, key, keys)
    before = (key[None, :] == key[:, None]) & (ids[None, :] < ids[:, None])
    rank = jnp.sum(before.astype(jnp.int32), axis=1)
    counts = jnp.sum((key[None, :] == names[:, None]).astype(jnp.int32), axis=1)
    filled = (counts + GROUP - 1) // GROUP * GROUP
    base = jnp.sum(jnp.where(names[None, :] < key[:, None], filled[None, :], 0), axis=1)
    pos = jnp.where(live, base + rank, -1)
    ends = jnp.sum(jnp.where(names[None, :] <= names[:, None], filled[None, :], 0), axis=1)
    length = key.shape[0] + keys * GROUP
    first = jnp.arange(length // GROUP, dtype=jnp.int32) * GROUP
    group_key = jnp.sum((ends[None, :] <= first[:, None]).astype(jnp.int32), axis=1)
    return pos, jnp.minimum(group_key, keys - 1), jnp.sum(filled) // GROUP, length


def place(pos, value, length, fill):
    spots = jnp.arange(length, dtype=jnp.int32)
    hit = pos[None, :] == spots[:, None]
    return jnp.sum(jnp.where(hit, value[None, :] - fill, 0), axis=1) + fill


def shards(
    features,
    weight,
    bias,
    cotangent,
    block_count,
    block_rows,
    block_cols,
    edge_offsets,
    edge_weight,
):
    node_dev, width = features.shape
    n_row = lax.axis_size("row")
    n_col = lax.axis_size("col")
    slots = block_rows.shape[2]
    count = block_count[0, 0]
    mine = lax.axis_index("col")
    mine_row = lax.axis_index("row")
    per = node_dev // 128
    row_blocks = per * n_col
    col_blocks = per * n_row
    by_owner = n_row * n_col * node_dev * width * 2 <= 8 * 1024 * 1024

    brow = block_rows[0, 0]
    bcol = block_cols[0, 0]
    ids = jnp.arange(slots, dtype=jnp.int32)
    live = ids < count
    codes = edge_offsets[0, 0] * FIELD + (
        edge_weight[0, 0].astype(jnp.float32) * (1.0 / UNIT)
    ).astype(jnp.int32)
    codes = jnp.pad(codes, ((0, 8), (0, 0)))
    home = brow // per
    turns_plain = ((count + GROUP - 1) // GROUP).reshape(1)

    def tile_plan():
        wide = lax.all_gather(features, "row", axis=0, tiled=True)
        low = jnp.dot(wide, weight, preferred_element_type=jnp.float32).astype(jnp.bfloat16)
        panel = jnp.concatenate([low, wide], axis=1).reshape(col_blocks, 128, 2 * width)
        order = jnp.where(live, ids, slots)
        dst = jnp.where(live, (home ^ mine) * per + brow % per, 0)
        totals = run_tile(turns_plain, order, dst, bcol, codes, panel, row_blocks)
        return scatter_sum(totals.reshape(n_col, node_dev, 2 * width), "col")

    if by_owner:
        same = live[None, :] & (home[None, :] == home[:, None]) & (ids[None, :] < ids[:, None])
        rank = jnp.sum(same.astype(jnp.int32), axis=1)
        over = jnp.any(live & (rank >= ROOM)).astype(jnp.int32)
        fits = live & (rank < ROOM)
        label = 1 + (brow % per) * col_blocks + bcol
        labels = place(jnp.where(fits, home * ROOM + rank, -1), label, n_col * ROOM, 0)
        labels = jnp.concatenate(
            [labels.reshape(n_col, ROOM), jnp.full((n_col, 128 - ROOM), over)], axis=1
        )
        stride = ROOM + SPARE
        pos = jnp.where(fits, home * stride + rank, ROOM + SPARE - 1)
        state = {}

        def exchange(step, held):
            if step == 0:
                packed = run_pack(turns_plain, pos, codes, labels, held[0])
                state["came"] = lax.all_to_all(
                    packed.reshape(n_col, stride, 128),
                    "col",
                    split_axis=0,
                    concat_axis=0,
                    tiled=True,
                )

        feat = []
        for pair in gather_pieces(features.reshape(per, 128, width), exchange):
            rows = [pair]
            for bit in bits_of("row"):
                rows = rows + [[swap(x, "row", bit) for x in pair] for pair in rows]
            feat += [x for pair in rows for x in pair]
        came = state["came"]
        spread = jnp.max(came[:, ROOM, ROOM:], axis=0)[None]
        for bit in bits_of("row"):
            spread = spread + swap(spread, "row", bit)
        any_over = jnp.max(spread) > 0

        got = came[:, ROOM, :ROOM]
        sources = jnp.arange(n_col, dtype=jnp.int32)[:, None]
        places = jnp.arange(ROOM, dtype=jnp.int32)[None, :]
        row_here = ((got - 1) // col_blocks).reshape(-1)
        col_there = (got - 1) % col_blocks
        col_there = piece_index(
            per, sources ^ mine, col_there % per, (col_there // per) ^ mine_row, n_row
        )
        pos, owner, turns, length = grouped(row_here, (got > 0).reshape(-1), per)
        line = (sources * stride + places).reshape(-1)
        order = place(pos, line, length + GROUP, ROOM + 1)
        cols = place(pos, col_there.reshape(-1), length + GROUP, 0)
        own = run_forward(
            turns.reshape(1),
            order,
            cols,
            owner,
            came.reshape(n_col * stride, 128),
            weight,
            feat,
            per,
        ).reshape(node_dev, 2 * width)
        own = lax.cond(any_over, tile_plan, lambda: own)
    else:
        own = tile_plan()

    pos, back_owner, back_turns, length = grouped(bcol, live, col_blocks)
    back_order = place(pos, ids, length, slots)
    back_src = place(pos, piece_index(per, home ^ mine, brow % per), length, 0)
    parts = [0, 1, 2, 4]
    state = {"dense": None}

    def build(step, held):
        if step + 1 < len(parts):
            span = jnp.stack([back_turns * part // 4 for part in parts[step : step + 2]])
            state["dense"] = run_build(span, back_order, codes, held, state["dense"])

    pre = own[:, :width] + bias
    output = jnp.maximum(pre, 0.0).astype(jnp.bfloat16)
    grad_own = jnp.where(pre > 0, cotangent.astype(jnp.float32), 0.0).astype(jnp.bfloat16)
    local_bias = jnp.sum(grad_own.astype(jnp.float32), axis=0)
    turned = jnp.swapaxes(grad_own.reshape(per, 128, width), 1, 2)
    grad = [x for pair in gather_pieces(turned, build) for x in pair]
    local_weight = lax.dot_general(
        own[:, width:].astype(jnp.bfloat16),
        grad_own,
        (((0,), (0,)), ((), ())),
        preferred_element_type=jnp.float32,
    )
    local = jnp.concatenate([local_weight, jnp.tile(local_bias[None], (8, 1))], axis=0)
    steps = total_steps()
    for axis, bit in steps[:-1]:
        local = local + swap(local, axis, bit)
    acc = run_backward(
        back_turns.reshape(1), back_src, back_owner, grad, state["dense"], col_blocks
    )
    acc, local = lax.optimization_barrier((acc, local))
    total = local + swap(local, *steps[-1])
    back = jnp.swapaxes(acc, 1, 2).reshape(col_blocks * 128, width)
    grad_proj = scatter_sum(
        jnp.stack(
            [
                lax.dynamic_slice_in_dim(back, (mine_row ^ k) * node_dev, node_dev, 0)
                for k in range(n_row)
            ]
        ),
        "row",
    ).astype(jnp.bfloat16)
    grad_features = lax.dot_general(
        grad_proj, weight, (((1,), (1,)), ((), ())), preferred_element_type=jnp.float32
    ).astype(jnp.bfloat16)
    scale = (node_dev * n_row * n_col) ** (-0.5)
    return (
        output,
        grad_features,
        total[: weight.shape[0]] * scale,
        total[weight.shape[0]] * scale,
    )


def solution(mesh):
    return jax.shard_map(
        shards,
        mesh=mesh,
        in_specs=(
            P(("row", "col"), None),
            P(),
            P(),
            P(("row", "col"), None),
            P("row", "col"),
            P("row", "col", None),
            P("row", "col", None),
            P("row", "col", None, None),
            P("row", "col", None, None),
        ),
        out_specs=(P(("row", "col"), None), P(("row", "col"), None), P(), P()),
        check_vma=False,
    )
```

```python
import functools
import functools
import jax
import jax.numpy as jnp
from jax import lax
from jax.experimental import pallas as pl
from jax.experimental.pallas import tpu as pltpu
from jax.sharding import PartitionSpec as P


def swap(x, axis, bit):
    n = lax.axis_size(axis)
    return lax.ppermute(x, axis, [(i, i ^ bit) for i in range(n)])


def bits_of(axis):
    n = lax.axis_size(axis)
    return [1 << k for k in range(n.bit_length() - 1)]


def scatter_sum(x, axis):
    for bit in bits_of(axis):
        pairs = x.reshape((x.shape[0] // 2, 2) + x.shape[1:])
        x = pairs[:, 0] + swap(pairs[:, 1], axis, bit)
    return x[0]


def part_orders(per):
    bits = bits_of("col")[::-1]
    turned = bits[:-2] + bits[-1:] + bits[-2:-1]
    return [bits, turned] if per % 2 == 0 and len(bits) > 1 else [bits]


def gather_pieces(blocks, beside):
    orders = part_orders(blocks.shape[0])
    size = blocks.shape[0] // len(orders)
    held = [blocks[i * size : (i + 1) * size][None] for i in range(len(orders))]
    for step in range(len(orders[0]) - 1):
        came = [swap(x, "col", order[step]) for x, order in zip(held, orders)]
        held = [jnp.concatenate([x, y], axis=0) for x, y in zip(held, came)]
        held = beside(step, held)
    came = [swap(x, "col", order[-1]) for x, order in zip(held, orders)]
    shape = (-1,) + blocks.shape[1:]
    return [[x.reshape(shape), y.reshape(shape)] for x, y in zip(held, came)]


def piece_index(per, far, block, rho=0, n_row=1):
    orders = part_orders(per)
    size = per // len(orders)
    half = lax.axis_size("col") // 2
    result = 0
    for i, order in enumerate(orders):
        spot = sum(((far & bit) > 0).astype(jnp.int32) << t for t, bit in enumerate(order))
        piece = (i * n_row + rho) * 2 + spot // half
        here = (piece * half + spot % half) * size + block % size
        result = jnp.where(block // size == i, here, result)
    return result


def total_steps():
    bits = bits_of("col")[::-1]
    steps = [("row", [bit]) for bit in bits_of("row")]
    return steps + [("col", bits[i : i + 2]) for i in range(0, len(bits), 2)]


def total_step(x, axis, bits):
    if len(bits) == 1:
        return x + swap(x, axis, bits[0])
    near, far, both = [swap(x, axis, bit) for bit in (bits[0], bits[1], bits[0] ^ bits[1])]
    return (x + near) + (far + both)


GROUP = 8
DEPTH = 8
ROOM = 64
SPARE = 8
FIELD = 1 << 16
UNIT = 2.0**-14


def tile_rows():
    shape = (8, 16, 128)
    rows = 16 * lax.broadcasted_iota(jnp.int32, shape, 0) + lax.broadcasted_iota(jnp.int32, shape, 1)
    return rows.astype(jnp.float32).astype(jnp.bfloat16)


def block_of(code, rows):
    def tile(x):
        return jnp.broadcast_to(x.astype(jnp.float32), (16, 128)).astype(jnp.bfloat16)[None]

    o = code >> 16
    zero = jnp.zeros((), jnp.bfloat16)
    one = jnp.ones((), jnp.bfloat16)
    w = tile((code & (FIELD - 1)).astype(jnp.float32) * UNIT)
    left = jnp.where(rows == tile(o >> 7), w, zero).reshape(128, 128)
    right = jnp.where(rows == tile(o & 127), one, zero).reshape(128, 128)
    return lax.dot_general(
        left, right, (((1,), (1,)), ((), ())), preferred_element_type=jnp.float32
    ).astype(jnp.bfloat16)


def pack_kernel(meta, pos, codes, labels, after, out):
    out[...] = jnp.zeros_like(out)
    stride = ROOM + SPARE
    for k in range(labels.shape[0]):
        out[pl.ds(k * stride + ROOM, 1), :] = labels[pl.ds(k, 1), :]

    def turn(i, _):
        for u in range(GROUP):
            s = i * GROUP + u
            out[pl.ds(pos[s], 1), :] = codes[pl.ds(s, 1), :]
        return 0

    lax.fori_loop(0, meta[0], turn, 0)


def build_kernel(meta, order, codes, *refs):
    dense, dbuf, sems = refs[-3:]
    start, turns = meta[0], meta[1]
    rows = tile_rows()

    def out_copy(i):
        slot = lax.rem(i, DEPTH)
        return pltpu.make_async_copy(
            dbuf.at[slot], dense.at[pl.ds(i * GROUP, GROUP)], sems.at[slot]
        )

    def turn(i, _):
        slot = lax.rem(i, DEPTH)

        @pl.when(i >= start + DEPTH)
        def _():
            out_copy(i - DEPTH).wait()

        lines = [codes[pl.ds(order[i * GROUP + u], 1), :] for u in range(GROUP)]
        blocks = [block_of(line, rows) for line in lines]
        for u in range(GROUP):
            dbuf[slot, u] = blocks[u]
        out_copy(i).start()
        return 0

    lax.fori_loop(start, turns, turn, 0)

    def finish(i, _):
        out_copy(i).wait()
        return 0

    lax.fori_loop(jnp.maximum(turns - DEPTH, start), turns, finish, 0)


def fetch(pieces, into, sems):
    size = pieces[0].shape[0]
    copies = [
        pltpu.make_async_copy(piece, into.at[pl.ds(i * size, size)], sems.at[i])
        for i, piece in enumerate(pieces)
    ]
    for copy in copies:
        copy.start()
    return copies


def forward_kernel(n, meta, order, col, owner, codes, weight, *refs):
    pieces, (totals, feat, proj, dbuf, sems) = refs[:n], refs[n:]
    turns = meta[0]
    rows = tile_rows()
    copies = fetch(pieces, feat, sems)
    size, _, width = pieces[0].shape
    batch = 4 if size % 4 == 0 else 1
    totals[...] = jnp.zeros_like(totals)

    def build(i, slot):
        lines = [codes[pl.ds(order[i * GROUP + u], 1), :] for u in range(GROUP)]
        blocks = [block_of(line, rows) for line in lines]
        for u in range(GROUP):
            dbuf[slot, :, u * 128 : (u + 1) * 128] = blocks[u]

    def product(i, slot):
        spots = [col[i * GROUP + u] for u in range(GROUP)]
        right = jnp.concatenate(
            [jnp.concatenate([proj[c], feat[c]], axis=1) for c in spots], axis=0
        )
        return jnp.dot(dbuf[slot], right, preferred_element_type=jnp.float32)

    @pl.when(turns > 0)
    def _():
        build(0, 0)

    def project(t, _):
        spot = pl.ds(t * batch, batch)
        held = feat[spot].reshape(batch * 128, width)
        low = jnp.dot(held, weight[...], preferred_element_type=jnp.float32)
        proj[spot] = low.astype(jnp.bfloat16).reshape(batch, 128, width)
        return 0

    for i, copy in enumerate(copies):
        copy.wait()
        lax.fori_loop(i * size // batch, (i + 1) * size // batch, project, 0)

    def turn(i, _):
        slot = lax.rem(i, 2)
        added = product(i, slot)
        build(i + 1, 1 - slot)
        totals[owner[i]] += added
        return 0

    lax.fori_loop(0, turns, turn, 0)


def tile_kernel(meta, order, dst, col, codes, panel, totals):
    rows = tile_rows()
    totals[...] = jnp.zeros_like(totals)

    def turn(i, _):
        for u in range(GROUP):
            p = i * GROUP + u
            block = block_of(codes[pl.ds(order[p], 1), :], rows)
            totals[dst[p]] += jnp.dot(block, panel[col[p]], preferred_element_type=jnp.float32)
        return 0

    lax.fori_loop(0, meta[0], turn, 0)


def backward_kernel(n, meta, src, owner, dense, *refs):
    pieces, (acc, grad, dbuf, grad_sems, sems) = refs[:n], refs[n:]
    turns = meta[0]
    copies = fetch(pieces, grad, grad_sems)

    def in_copy(i):
        slot = lax.rem(i, DEPTH)
        return pltpu.make_async_copy(
            dense.at[pl.ds(i * GROUP, GROUP)], dbuf.at[slot], sems.at[slot]
        )

    def begin(i, _):
        in_copy(i).start()
        return 0

    lax.fori_loop(0, jnp.minimum(turns, DEPTH - 1), begin, 0)
    acc[...] = jnp.zeros_like(acc)
    for copy in copies:
        copy.wait()

    def turn(i, _):
        @pl.when(i + DEPTH - 1 < turns)
        def _():
            in_copy(i + DEPTH - 1).start()

        in_copy(i).wait()
        left = jnp.concatenate([grad[src[i * GROUP + u]] for u in range(GROUP)], axis=1)
        right = dbuf[lax.rem(i, DEPTH)].reshape(GROUP * 128, 128)
        acc[owner[i]] += jnp.dot(left, right, preferred_element_type=jnp.float32)
        return 0

    lax.fori_loop(0, turns, turn, 0)


SMEM = pl.BlockSpec(memory_space=pltpu.SMEM)
VMEM = pl.BlockSpec(memory_space=pltpu.VMEM)
HBM = pl.BlockSpec(memory_space=pl.ANY)
PARAMS = pltpu.CompilerParams(vmem_limit_bytes=16 * 1024 * 1024)
WIDE_PARAMS = pltpu.CompilerParams(vmem_limit_bytes=48 * 1024 * 1024)


def cost(slots, products):
    flops = 2 * slots * products * 128**3
    return pl.CostEstimate(flops=flops, bytes_accessed=slots * 128 * 128 * 2, transcendentals=0)


def run_tile(meta, order, dst, col, codes, panel, row_blocks):
    return pl.pallas_call(
        tile_kernel,
        out_shape=jax.ShapeDtypeStruct((row_blocks, 128, panel.shape[-1]), jnp.float32),
        in_specs=[SMEM] * 4 + [VMEM] * 2,
        out_specs=VMEM,
        compiler_params=WIDE_PARAMS,
    )(meta, order, dst, col, codes, panel)


def run_pack(meta, pos, codes, labels, after):
    length = labels.shape[0] * (ROOM + SPARE)
    return pl.pallas_call(
        pack_kernel,
        out_shape=jax.ShapeDtypeStruct((length, 128), jnp.int32),
        in_specs=[SMEM] * 2 + [VMEM] * 2 + [HBM],
        out_specs=VMEM,
        compiler_params=PARAMS,
    )(meta, pos, codes, labels, after)


def run_build(meta, order, codes, after, dense):
    others = after if dense is None else after + [dense]
    return pl.pallas_call(
        build_kernel,
        out_shape=jax.ShapeDtypeStruct((order.shape[0], 128, 128), jnp.bfloat16),
        in_specs=[SMEM] * 2 + [VMEM] + [HBM] * len(others),
        out_specs=HBM,
        scratch_shapes=[
            pltpu.VMEM((DEPTH, GROUP, 128, 128), jnp.bfloat16),
            pltpu.SemaphoreType.DMA((DEPTH,)),
        ],
        input_output_aliases={} if dense is None else {2 + len(others): 0},
        compiler_params=PARAMS,
        cost_estimate=cost(order.shape[0], 2),
    )(meta, order, codes, *others)


def run_forward(meta, order, col, owner, codes, weight, feat, row_blocks):
    n = len(feat)
    size, _, width = feat[0].shape
    return pl.pallas_call(
        functools.partial(forward_kernel, n),
        out_shape=jax.ShapeDtypeStruct((row_blocks, 128, 2 * width), jnp.float32),
        in_specs=[SMEM] * 4 + [VMEM] * 2 + [HBM] * n,
        out_specs=VMEM,
        scratch_shapes=[
            pltpu.VMEM((n * size, 128, width), jnp.bfloat16),
            pltpu.VMEM((n * size, 128, width), jnp.bfloat16),
            pltpu.VMEM((2, 128, GROUP * 128), jnp.bfloat16),
            pltpu.SemaphoreType.DMA((n,)),
        ],
        compiler_params=PARAMS,
        cost_estimate=cost(order.shape[0], 8),
    )(meta, order, col, owner, codes, weight, *feat)


def run_backward(meta, src, owner, pieces, dense, col_blocks):
    n = len(pieces)
    size, width, _ = pieces[0].shape
    return pl.pallas_call(
        functools.partial(backward_kernel, n),
        out_shape=jax.ShapeDtypeStruct((col_blocks, width, 128), jnp.float32),
        in_specs=[SMEM] * 3 + [HBM] * (n + 1),
        out_specs=VMEM,
        scratch_shapes=[
            pltpu.VMEM((n * size, width, 128), jnp.bfloat16),
            pltpu.VMEM((DEPTH, GROUP, 128, 128), jnp.bfloat16),
            pltpu.SemaphoreType.DMA((n,)),
            pltpu.SemaphoreType.DMA((DEPTH,)),
        ],
        compiler_params=PARAMS,
        cost_estimate=cost(src.shape[0], 4),
    )(meta, src, owner, dense, *pieces)


def grouped(key, live, keys):
    ids = jnp.arange(key.shape[0], dtype=jnp.int32)
    names = jnp.arange(keys, dtype=jnp.int32)
    key = jnp.where(live, key, keys)
    before = (key[None, :] == key[:, None]) & (ids[None, :] < ids[:, None])
    rank = jnp.sum(before.astype(jnp.int32), axis=1)
    counts = jnp.sum((key[None, :] == names[:, None]).astype(jnp.int32), axis=1)
    filled = (counts + GROUP - 1) // GROUP * GROUP
    base = jnp.sum(jnp.where(names[None, :] < key[:, None], filled[None, :], 0), axis=1)
    pos = jnp.where(live, base + rank, -1)
    ends = jnp.sum(jnp.where(names[None, :] <= names[:, None], filled[None, :], 0), axis=1)
    length = key.shape[0] + keys * GROUP
    first = jnp.arange(length // GROUP, dtype=jnp.int32) * GROUP
    group_key = jnp.sum((ends[None, :] <= first[:, None]).astype(jnp.int32), axis=1)
    return pos, jnp.minimum(group_key, keys - 1), jnp.sum(filled) // GROUP, length


def place(pos, value, length, fill):
    spots = jnp.arange(length, dtype=jnp.int32)
    hit = pos[None, :] == spots[:, None]
    return jnp.sum(jnp.where(hit, value[None, :] - fill, 0), axis=1) + fill


def shards(
    features,
    weight,
    bias,
    cotangent,
    block_count,
    block_rows,
    block_cols,
    edge_offsets,
    edge_weight,
):
    node_dev, width = features.shape
    n_row = lax.axis_size("row")
    n_col = lax.axis_size("col")
    slots = block_rows.shape[2]
    count = block_count[0, 0]
    mine = lax.axis_index("col")
    mine_row = lax.axis_index("row")
    per = node_dev // 128
    row_blocks = per * n_col
    col_blocks = per * n_row
    by_owner = n_row * n_col * node_dev * width * 2 <= 8 * 1024 * 1024

    brow = block_rows[0, 0]
    bcol = block_cols[0, 0]
    ids = jnp.arange(slots, dtype=jnp.int32)
    live = ids < count
    codes = edge_offsets[0, 0] * FIELD + (
        edge_weight[0, 0].astype(jnp.float32) * (1.0 / UNIT)
    ).astype(jnp.int32)
    codes = jnp.pad(codes, ((0, 8), (0, 0)))
    home = brow // per
    turns_plain = ((count + GROUP - 1) // GROUP).reshape(1)

    def tile_plan():
        wide = lax.all_gather(features, "row", axis=0, tiled=True)
        low = jnp.dot(wide, weight, preferred_element_type=jnp.float32).astype(jnp.bfloat16)
        panel = jnp.concatenate([low, wide], axis=1).reshape(col_blocks, 128, 2 * width)
        order = jnp.where(live, ids, slots)
        dst = jnp.where(live, (home ^ mine) * per + brow % per, 0)
        totals = run_tile(turns_plain, order, dst, bcol, codes, panel, row_blocks)
        return scatter_sum(totals.reshape(n_col, node_dev, 2 * width), "col")

    if by_owner:
        same = live[None, :] & (home[None, :] == home[:, None]) & (ids[None, :] < ids[:, None])
        rank = jnp.sum(same.astype(jnp.int32), axis=1)
        over = jnp.any(live & (rank >= ROOM)).astype(jnp.int32)
        fits = live & (rank < ROOM)
        label = 1 + (brow % per) * col_blocks + bcol
        labels = place(jnp.where(fits, home * ROOM + rank, -1), label, n_col * ROOM, 0)
        labels = jnp.concatenate(
            [labels.reshape(n_col, ROOM), jnp.full((n_col, 128 - ROOM), over)], axis=1
        )
        stride = ROOM + SPARE
        pos = jnp.where(fits, home * stride + rank, ROOM + SPARE - 1)
        state = {}

        def exchange(step, held):
            if step == 0:
                packed = run_pack(turns_plain, pos, codes, labels, held[0])
                state["came"] = lax.all_to_all(
                    packed.reshape(n_col, stride, 128),
                    "col",
                    split_axis=0,
                    concat_axis=0,
                    tiled=True,
                )
            return held

        pairs = gather_pieces(features.reshape(per, 128, width), exchange)
        came = state["came"]
        spread = jnp.max(came[:, ROOM, ROOM:], axis=0)[None]
        for bit in bits_of("row"):
            spread = spread + swap(spread, "row", bit)
        any_over = jnp.max(spread) > 0

        got = came[:, ROOM, :ROOM]
        sources = jnp.arange(n_col, dtype=jnp.int32)[:, None]
        places = jnp.arange(ROOM, dtype=jnp.int32)[None, :]
        row_here = ((got - 1) // col_blocks).reshape(-1)
        col_there = (got - 1) % col_blocks
        col_there = piece_index(
            per, sources ^ mine, col_there % per, (col_there // per) ^ mine_row, n_row
        )
        pos, owner, turns, length = grouped(row_here, (got > 0).reshape(-1), per)
        line = (sources * stride + places).reshape(-1)
        order = place(pos, line, length + GROUP, ROOM + 1)
        cols = place(pos, col_there.reshape(-1), length + GROUP, 0)
        last, order, cols, owner, turns = lax.optimization_barrier(
            ([pair[1] for pair in pairs], order, cols, owner, turns)
        )
        feat = []
        for pair in [[pair[0], x] for pair, x in zip(pairs, last)]:
            rows = [pair]
            for bit in bits_of("row"):
                rows = rows + [[swap(x, "row", bit) for x in pair] for pair in rows]
            feat += [x for pair in rows for x in pair]
        own = run_forward(
            turns.reshape(1),
            order,
            cols,
            owner,
            came.reshape(n_col * stride, 128),
            weight,
            feat,
            per,
        ).reshape(node_dev, 2 * width)
        own = lax.cond(any_over, tile_plan, lambda: own)
    else:
        own = tile_plan()

    pos, back_owner, back_turns, length = grouped(bcol, live, col_blocks)
    back_order = place(pos, ids, length, slots)
    back_src = place(pos, piece_index(per, home ^ mine, brow % per), length, 0)
    parts = [0, 1, 2, 4]
    state = {"dense": None}

    def build(step, held):
        if step + 1 < len(parts):
            span = jnp.stack([back_turns * part // 4 for part in parts[step : step + 2]])
            state["dense"] = run_build(span, back_order, codes, held, state["dense"])

    pre = own[:, :width] + bias
    output = jnp.maximum(pre, 0.0).astype(jnp.bfloat16)
    grad_own = jnp.where(pre > 0, cotangent.astype(jnp.float32), 0.0).astype(jnp.bfloat16)
    local_bias = jnp.sum(grad_own.astype(jnp.float32), axis=0)
    turned = jnp.swapaxes(grad_own.reshape(per, 128, width), 1, 2)
    local_weight = lax.dot_general(
        own[:, width:].astype(jnp.bfloat16),
        grad_own,
        (((0,), (0,)), ((), ())),
        preferred_element_type=jnp.float32,
    )
    total = jnp.concatenate([local_weight, jnp.tile(local_bias[None], (8, 1))], axis=0)
    steps = total_steps()
    for step in steps[: n_row.bit_length() - 1]:
        total = total_step(total, *step)
    steps = steps[n_row.bit_length() - 1 :]

    def beside(step, held):
        build(step, held)
        if step == 1:
            later, state["total"] = lax.optimization_barrier((held, state["total"]))
            for one in steps[:-1]:
                state["total"] = total_step(state["total"], *one)
            return later
        return held

    state["total"] = total
    grad = [x for pair in gather_pieces(turned, beside) for x in pair]
    grad, total = lax.optimization_barrier((grad, state["total"]))
    total = total_step(total, *steps[-1])
    acc = run_backward(
        back_turns.reshape(1), back_src, back_owner, grad, state["dense"], col_blocks
    )
    back = jnp.swapaxes(acc, 1, 2).reshape(col_blocks * 128, width)
    grad_proj = scatter_sum(
        jnp.stack(
            [
                lax.dynamic_slice_in_dim(back, (mine_row ^ k) * node_dev, node_dev, 0)
                for k in range(n_row)
            ]
        ),
        "row",
    ).astype(jnp.bfloat16)
    grad_features = lax.dot_general(
        grad_proj, weight, (((1,), (1,)), ((), ())), preferred_element_type=jnp.float32
    ).astype(jnp.bfloat16)
    scale = (node_dev * n_row * n_col) ** (-0.5)
    return (
        output,
        grad_features,
        total[: weight.shape[0]] * scale,
        total[weight.shape[0]] * scale,
    )


def solution(mesh):
    return jax.shard_map(
        shards,
        mesh=mesh,
        in_specs=(
            P(("row", "col"), None),
            P(),
            P(),
            P(("row", "col"), None),
            P("row", "col"),
            P("row", "col", None),
            P("row", "col", None),
            P("row", "col", None, None),
            P("row", "col", None, None),
        ),
        out_specs=(P(("row", "col"), None), P(("row", "col"), None), P(), P()),
        check_vma=False,
    )
```

```python
import functools
import functools
import jax
import jax.numpy as jnp
from jax import lax
from jax.experimental import pallas as pl
from jax.experimental.pallas import tpu as pltpu
from jax.sharding import PartitionSpec as P


def swap(x, axis, bit):
    n = lax.axis_size(axis)
    return lax.ppermute(x, axis, [(i, i ^ bit) for i in range(n)])


def bits_of(axis):
    n = lax.axis_size(axis)
    return [1 << k for k in range(n.bit_length() - 1)]


def scatter_sum(x, axis):
    for bit in bits_of(axis):
        pairs = x.reshape((x.shape[0] // 2, 2) + x.shape[1:])
        x = pairs[:, 0] + swap(pairs[:, 1], axis, bit)
    return x[0]


def part_orders(per):
    bits = bits_of("col")[::-1]
    turned = bits[:-2] + bits[-1:] + bits[-2:-1]
    return [bits, turned] if per % 2 == 0 and len(bits) > 1 else [bits]


def gather_pieces(blocks, beside):
    orders = part_orders(blocks.shape[0])
    size = blocks.shape[0] // len(orders)
    held = [blocks[i * size : (i + 1) * size][None] for i in range(len(orders))]
    for step in range(len(orders[0]) - 1):
        came = [swap(x, "col", order[step]) for x, order in zip(held, orders)]
        held = [jnp.concatenate([x, y], axis=0) for x, y in zip(held, came)]
        held = beside(step, held)
    came = [swap(x, "col", order[-1]) for x, order in zip(held, orders)]
    shape = (-1,) + blocks.shape[1:]
    return [[x.reshape(shape), y.reshape(shape)] for x, y in zip(held, came)]


def piece_index(per, far, block, rho=0, n_row=1):
    orders = part_orders(per)
    size = per // len(orders)
    half = lax.axis_size("col") // 2
    result = 0
    for i, order in enumerate(orders):
        spot = sum(((far & bit) > 0).astype(jnp.int32) << t for t, bit in enumerate(order))
        piece = (i * n_row + rho) * 2 + spot // half
        here = (piece * half + spot % half) * size + block % size
        result = jnp.where(block // size == i, here, result)
    return result


def total_steps():
    bits = bits_of("col")[::-1]
    steps = [("row", [bit]) for bit in bits_of("row")]
    return steps + [("col", bits[i : i + 2]) for i in range(0, len(bits), 2)]


def total_step(x, axis, bits):
    if len(bits) == 1:
        return x + swap(x, axis, bits[0])
    near, far, both = [swap(x, axis, bit) for bit in (bits[0], bits[1], bits[0] ^ bits[1])]
    return (x + near) + (far + both)


GROUP = 8
TURN = 4 * GROUP
DEPTH = 3
ROOM = 64
SPARE = 8
FIELD = 1 << 16
UNIT = 2.0**-14


def tile_rows():
    shape = (8, 16, 128)
    rows = 16 * lax.broadcasted_iota(jnp.int32, shape, 0) + lax.broadcasted_iota(jnp.int32, shape, 1)
    return rows.astype(jnp.float32).astype(jnp.bfloat16)


def block_of(code, rows):
    def tile(x):
        return jnp.broadcast_to(x.astype(jnp.float32), (16, 128)).astype(jnp.bfloat16)[None]

    o = code >> 16
    zero = jnp.zeros((), jnp.bfloat16)
    one = jnp.ones((), jnp.bfloat16)
    w = tile((code & (FIELD - 1)).astype(jnp.float32) * UNIT)
    left = jnp.where(rows == tile(o >> 7), w, zero).reshape(128, 128)
    right = jnp.where(rows == tile(o & 127), one, zero).reshape(128, 128)
    return lax.dot_general(
        left, right, (((1,), (1,)), ((), ())), preferred_element_type=jnp.float32
    ).astype(jnp.bfloat16)


def pack_kernel(meta, pos, codes, labels, after, out):
    out[...] = jnp.zeros_like(out)
    stride = ROOM + SPARE
    for k in range(labels.shape[0]):
        out[pl.ds(k * stride + ROOM, 1), :] = labels[pl.ds(k, 1), :]

    def turn(i, _):
        for u in range(GROUP):
            s = i * GROUP + u
            out[pl.ds(pos[s], 1), :] = codes[pl.ds(s, 1), :]
        return 0

    lax.fori_loop(0, meta[0], turn, 0)


def build_kernel(meta, order, codes, *refs):
    dense, dbuf, sems = refs[-3:]
    start, turns = meta[0], meta[1]
    rows = tile_rows()

    def out_copy(i):
        slot = lax.rem(i, DEPTH)
        return pltpu.make_async_copy(
            dbuf.at[slot], dense.at[pl.ds(i * TURN, TURN)], sems.at[slot]
        )

    def turn(i, _):
        slot = lax.rem(i, DEPTH)

        @pl.when(i >= start + DEPTH)
        def _():
            out_copy(i - DEPTH).wait()

        lines = [codes[pl.ds(order[i * TURN + u], 1), :] for u in range(TURN)]
        for u in range(0, TURN, GROUP):
            blocks = [block_of(line, rows) for line in lines[u : u + GROUP]]
            for k, block in enumerate(blocks):
                dbuf[slot, u + k] = block
        out_copy(i).start()
        return 0

    lax.fori_loop(start, turns, turn, 0)

    def finish(i, _):
        out_copy(i).wait()
        return 0

    lax.fori_loop(jnp.maximum(turns - DEPTH, start), turns, finish, 0)


def fetch(pieces, into, sems):
    size = pieces[0].shape[0]
    copies = [
        pltpu.make_async_copy(piece, into.at[pl.ds(i * size, size)], sems.at[i])
        for i, piece in enumerate(pieces)
    ]
    for copy in copies:
        copy.start()
    return copies


def read_dense(turns, dense, dbuf, sems, product, prepare):
    def in_copy(i):
        slot = lax.rem(i, DEPTH)
        return pltpu.make_async_copy(
            dense.at[pl.ds(i * TURN, TURN)], dbuf.at[slot], sems.at[slot]
        )

    def begin(i, _):
        in_copy(i).start()
        return 0

    lax.fori_loop(0, jnp.minimum(turns, DEPTH - 1), begin, 0)
    prepare()

    def turn(i, _):
        @pl.when(i + DEPTH - 1 < turns)
        def _():
            in_copy(i + DEPTH - 1).start()

        in_copy(i).wait()
        product(i, lax.rem(i, DEPTH))
        return 0

    lax.fori_loop(0, turns, turn, 0)


def add_pairs(i, owner, one, into):
    groups = TURN // GROUP
    for g in range(0, groups, 2):
        added = [one(g), one(g + 1)]
        for k in range(2):
            into[owner[i * groups + g + k]] += added[k]


def forward_kernel(n, meta, col, owner, weight, dense, *refs):
    pieces, (totals, feat, proj, dbuf, piece_sems, sems) = refs[:n], refs[n:]
    copies = fetch(pieces, feat, piece_sems)
    size, _, width = pieces[0].shape
    batch = 8 if size % 8 == 0 else 1

    def project(t, _):
        spot = pl.ds(t * batch, batch)
        held = feat[spot].reshape(batch * 128, width)
        low = jnp.dot(held, weight[...], preferred_element_type=jnp.float32)
        proj[spot] = low.astype(jnp.bfloat16).reshape(batch, 128, width)
        return 0

    def prepare():
        totals[...] = jnp.zeros_like(totals)
        for i, copy in enumerate(copies):
            copy.wait()
            lax.fori_loop(i * size // batch, (i + 1) * size // batch, project, 0)

    def product(i, slot):
        def one(g):
            spots = [col[i * TURN + g * GROUP + u] for u in range(GROUP)]
            left = jnp.concatenate([dbuf[slot, g * GROUP + u] for u in range(GROUP)], axis=1)
            right = jnp.concatenate(
                [jnp.concatenate([proj[c], feat[c]], axis=1) for c in spots], axis=0
            )
            return jnp.dot(left, right, preferred_element_type=jnp.float32)

        add_pairs(i, owner, one, totals)

    read_dense(meta[1], dense, dbuf, sems, product, prepare)


def tile_kernel(meta, order, dst, col, codes, panel, totals):
    rows = tile_rows()
    totals[...] = jnp.zeros_like(totals)

    def turn(i, _):
        for u in range(GROUP):
            p = i * GROUP + u
            block = block_of(codes[pl.ds(order[p], 1), :], rows)
            totals[dst[p]] += jnp.dot(block, panel[col[p]], preferred_element_type=jnp.float32)
        return 0

    lax.fori_loop(0, meta[0], turn, 0)


def backward_kernel(n, meta, src, owner, dense, *refs):
    pieces, (acc, grad, dbuf, piece_sems, sems) = refs[:n], refs[n:]
    copies = fetch(pieces, grad, piece_sems)

    def prepare():
        acc[...] = jnp.zeros_like(acc)
        for copy in copies:
            copy.wait()

    def product(i, slot):
        def one(g):
            spots = [src[i * TURN + g * GROUP + u] for u in range(GROUP)]
            left = jnp.concatenate([grad[c] for c in spots], axis=1)
            right = dbuf[slot, pl.ds(g * GROUP, GROUP)].reshape(GROUP * 128, 128)
            return jnp.dot(left, right, preferred_element_type=jnp.float32)

        add_pairs(i, owner, one, acc)

    read_dense(meta[1], dense, dbuf, sems, product, prepare)


SMEM = pl.BlockSpec(memory_space=pltpu.SMEM)
VMEM = pl.BlockSpec(memory_space=pltpu.VMEM)
HBM = pl.BlockSpec(memory_space=pl.ANY)
PARAMS = pltpu.CompilerParams(vmem_limit_bytes=20 * 1024 * 1024)
WIDE_PARAMS = pltpu.CompilerParams(vmem_limit_bytes=48 * 1024 * 1024)


def cost(slots, products):
    flops = 2 * slots * products * 128**3
    return pl.CostEstimate(flops=flops, bytes_accessed=slots * 128 * 128 * 2, transcendentals=0)


def run_tile(meta, order, dst, col, codes, panel, row_blocks):
    return pl.pallas_call(
        tile_kernel,
        out_shape=jax.ShapeDtypeStruct((row_blocks, 128, panel.shape[-1]), jnp.float32),
        in_specs=[SMEM] * 4 + [VMEM] * 2,
        out_specs=VMEM,
        compiler_params=WIDE_PARAMS,
    )(meta, order, dst, col, codes, panel)


def run_pack(meta, pos, codes, labels, after):
    length = labels.shape[0] * (ROOM + SPARE)
    return pl.pallas_call(
        pack_kernel,
        out_shape=jax.ShapeDtypeStruct((length, 128), jnp.int32),
        in_specs=[SMEM] * 2 + [VMEM] * 2 + [HBM],
        out_specs=VMEM,
        compiler_params=PARAMS,
    )(meta, pos, codes, labels, after)


def run_build(meta, order, codes, after, dense):
    others = after if dense is None else after + [dense]
    return pl.pallas_call(
        build_kernel,
        out_shape=jax.ShapeDtypeStruct((order.shape[0], 128, 128), jnp.bfloat16),
        in_specs=[SMEM] * 2 + [VMEM] + [HBM] * len(others),
        out_specs=HBM,
        scratch_shapes=[
            pltpu.VMEM((DEPTH, TURN, 128, 128), jnp.bfloat16),
            pltpu.SemaphoreType.DMA((DEPTH,)),
        ],
        input_output_aliases={} if dense is None else {2 + len(others): 0},
        compiler_params=PARAMS,
        cost_estimate=cost(order.shape[0], 2),
    )(meta, order, codes, *others)


def run_forward(meta, col, owner, weight, dense, feat, row_blocks):
    n = len(feat)
    size, _, width = feat[0].shape
    return pl.pallas_call(
        functools.partial(forward_kernel, n),
        out_shape=jax.ShapeDtypeStruct((row_blocks, 128, 2 * width), jnp.float32),
        in_specs=[SMEM] * 3 + [VMEM] + [HBM] * (n + 1),
        out_specs=VMEM,
        scratch_shapes=[
            pltpu.VMEM((n * size, 128, width), jnp.bfloat16),
            pltpu.VMEM((n * size, 128, width), jnp.bfloat16),
            pltpu.VMEM((DEPTH, TURN, 128, 128), jnp.bfloat16),
            pltpu.SemaphoreType.DMA((n,)),
            pltpu.SemaphoreType.DMA((DEPTH,)),
        ],
        compiler_params=PARAMS,
        cost_estimate=cost(col.shape[0], 4),
    )(meta, col, owner, weight, dense, *feat)


def run_backward(meta, src, owner, pieces, dense, col_blocks):
    n = len(pieces)
    size, width, _ = pieces[0].shape
    return pl.pallas_call(
        functools.partial(backward_kernel, n),
        out_shape=jax.ShapeDtypeStruct((col_blocks, width, 128), jnp.float32),
        in_specs=[SMEM] * 3 + [HBM] * (n + 1),
        out_specs=VMEM,
        scratch_shapes=[
            pltpu.VMEM((n * size, width, 128), jnp.bfloat16),
            pltpu.VMEM((DEPTH, TURN, 128, 128), jnp.bfloat16),
            pltpu.SemaphoreType.DMA((n,)),
            pltpu.SemaphoreType.DMA((DEPTH,)),
        ],
        compiler_params=PARAMS,
        cost_estimate=cost(src.shape[0], 4),
    )(meta, src, owner, dense, *pieces)


def grouped(key, live, value, fill, keys):
    ids = jnp.arange(key.shape[0], dtype=jnp.int32)
    names = jnp.arange(keys, dtype=jnp.int32)
    key = jnp.where(live, key, keys)
    before = (key[:, None] == key[None, :]) & (ids[:, None] < ids[None, :])
    rank = jnp.sum(before.astype(jnp.int32), axis=0)
    counts = jnp.sum((key[:, None] == names[None, :]).astype(jnp.int32), axis=0)
    filled = (counts + GROUP - 1) // GROUP * GROUP
    base = jnp.sum(jnp.where(names[:, None] < key[None, :], filled[:, None], 0), axis=0)
    pos = jnp.where(live, base + rank, -1)
    ends = jnp.sum(jnp.where(names[:, None] <= names[None, :], filled[:, None], 0), axis=0)
    length = -(-(key.shape[0] + keys * GROUP) // TURN) * TURN
    first = jnp.arange(length // GROUP, dtype=jnp.int32) * GROUP
    group_key = jnp.sum((ends[:, None] <= first[None, :]).astype(jnp.int32), axis=0)
    turns = (jnp.sum(filled) + TURN - 1) // TURN
    return place(pos, value, length, fill), jnp.minimum(group_key, keys - 1), turns


def place(pos, value, length, fill):
    spots = jnp.arange(length, dtype=jnp.int32)
    hit = pos[:, None] == spots[None, :]
    return jnp.sum(jnp.where(hit, value[:, None] - fill, 0), axis=0) + fill


def shards(
    features,
    weight,
    bias,
    cotangent,
    block_count,
    block_rows,
    block_cols,
    edge_offsets,
    edge_weight,
):
    node_dev, width = features.shape
    n_row = lax.axis_size("row")
    n_col = lax.axis_size("col")
    slots = block_rows.shape[2]
    count = block_count[0, 0]
    mine = lax.axis_index("col")
    mine_row = lax.axis_index("row")
    per = node_dev // 128
    row_blocks = per * n_col
    col_blocks = per * n_row
    by_owner = n_row * n_col * node_dev * width * 2 <= 8 * 1024 * 1024

    brow = block_rows[0, 0]
    bcol = block_cols[0, 0]
    ids = jnp.arange(slots, dtype=jnp.int32)
    live = ids < count
    codes = edge_offsets[0, 0] * FIELD + (
        edge_weight[0, 0].astype(jnp.float32) * (1.0 / UNIT)
    ).astype(jnp.int32)
    codes = jnp.pad(codes, ((0, 8), (0, 0)))
    home = brow // per
    turns_plain = ((count + GROUP - 1) // GROUP).reshape(1)

    def tile_plan():
        wide = lax.all_gather(features, "row", axis=0, tiled=True)
        low = jnp.dot(wide, weight, preferred_element_type=jnp.float32).astype(jnp.bfloat16)
        panel = jnp.concatenate([low, wide], axis=1).reshape(col_blocks, 128, 2 * width)
        order = jnp.where(live, ids, slots)
        dst = jnp.where(live, (home ^ mine) * per + brow % per, 0)
        totals = run_tile(turns_plain, order, dst, bcol, codes, panel, row_blocks)
        return scatter_sum(totals.reshape(n_col, node_dev, 2 * width), "col")

    if by_owner:
        same = live[:, None] & (home[:, None] == home[None, :]) & (ids[:, None] < ids[None, :])
        rank = jnp.sum(same.astype(jnp.int32), axis=0)
        over = jnp.any(live & (rank >= ROOM)).astype(jnp.int32)
        fits = live & (rank < ROOM)
        label = 1 + (brow % per) * col_blocks + bcol
        labels = place(jnp.where(fits, home * ROOM + rank, -1), label, n_col * ROOM, 0)
        labels = jnp.concatenate(
            [labels.reshape(n_col, ROOM), jnp.full((n_col, 128 - ROOM), over)], axis=1
        )
        stride = ROOM + SPARE
        pos = jnp.where(fits, home * stride + rank, ROOM + SPARE - 1)
        state = {}

        def exchange(step, held):
            if step == 0:
                packed = run_pack(turns_plain, pos, codes, labels, held[0])
                state["came"] = lax.all_to_all(
                    packed.reshape(n_col, stride, 128),
                    "col",
                    split_axis=0,
                    concat_axis=0,
                    tiled=True,
                )
            return held

        pairs = gather_pieces(features.reshape(per, 128, width), exchange)
        came = state["came"]
        spread = jnp.max(came[:, ROOM, ROOM:], axis=0)[None]
        for bit in bits_of("row"):
            spread = spread + swap(spread, "row", bit)
        any_over = jnp.max(spread) > 0

        got = came[:, ROOM, :ROOM]
        sources = jnp.arange(n_col, dtype=jnp.int32)[:, None]
        places = jnp.arange(ROOM, dtype=jnp.int32)[None, :]
        row_here = ((got - 1) // col_blocks).reshape(-1)
        col_there = (got - 1) % col_blocks
        col_there = piece_index(
            per, sources ^ mine, col_there % per, (col_there // per) ^ mine_row, n_row
        )
        line = sources * stride + places
        listed, owner, turns = grouped(
            row_here, (got > 0).reshape(-1), (line * FIELD + col_there).reshape(-1), (ROOM + 1) * FIELD, per
        )
        span = jnp.stack([jnp.zeros_like(turns), turns])
        here = run_build(span, listed // FIELD, came.reshape(n_col * stride, 128), [], None)
        last, here = lax.optimization_barrier(([pair[1] for pair in pairs], here))
        feat = []
        for pair in [[pair[0], x] for pair, x in zip(pairs, last)]:
            rows = [pair]
            for bit in bits_of("row"):
                rows = rows + [[swap(x, "row", bit) for x in pair] for pair in rows]
            feat += [x for pair in rows for x in pair]
        own = run_forward(span, listed % FIELD, owner, weight, here, feat, per)
        own = own.reshape(node_dev, 2 * width)
        own = lax.cond(any_over, tile_plan, lambda: own)
    else:
        own = tile_plan()

    source = piece_index(per, home ^ mine, brow % per)
    back_list, back_owner, back_turns = grouped(
        bcol, live, ids * FIELD + source, slots * FIELD, col_blocks
    )
    back_span = jnp.stack([jnp.zeros_like(back_turns), back_turns])
    parts = [0, 1, 2, 4]
    state = {"dense": None}

    def build(step, held):
        if step + 1 < len(parts):
            span = jnp.stack([back_turns * part // 4 for part in parts[step : step + 2]])
            state["dense"] = run_build(span, back_list // FIELD, codes, held, state["dense"])

    pre = own[:, :width] + bias
    output = jnp.maximum(pre, 0.0).astype(jnp.bfloat16)
    grad_own = jnp.where(pre > 0, cotangent.astype(jnp.float32), 0.0).astype(jnp.bfloat16)
    local_bias = jnp.sum(grad_own.astype(jnp.float32), axis=0)
    turned = jnp.swapaxes(grad_own.reshape(per, 128, width), 1, 2)
    local_weight = lax.dot_general(
        own[:, width:].astype(jnp.bfloat16),
        grad_own,
        (((0,), (0,)), ((), ())),
        preferred_element_type=jnp.float32,
    )
    total = jnp.concatenate([local_weight, jnp.tile(local_bias[None], (8, 1))], axis=0)
    steps = total_steps()
    for step in steps[: n_row.bit_length() - 1]:
        total = total_step(total, *step)
    steps = steps[n_row.bit_length() - 1 :]

    def beside(step, held):
        build(step, held)
        if step == 1:
            later, state["total"] = lax.optimization_barrier((held, state["total"]))
            for one in steps[:-1]:
                state["total"] = total_step(state["total"], *one)
            return later
        return held

    state["total"] = total
    grad = [x for pair in gather_pieces(turned, beside) for x in pair]
    grad, total = lax.optimization_barrier((grad, state["total"]))
    total = total_step(total, *steps[-1])
    acc = run_backward(
        back_span, back_list % FIELD, back_owner, grad, state["dense"], col_blocks
    )
    back = jnp.swapaxes(acc, 1, 2).reshape(col_blocks * 128, width)
    grad_proj = scatter_sum(
        jnp.stack(
            [
                lax.dynamic_slice_in_dim(back, (mine_row ^ k) * node_dev, node_dev, 0)
                for k in range(n_row)
            ]
        ),
        "row",
    ).astype(jnp.bfloat16)
    grad_features = lax.dot_general(
        grad_proj, weight, (((1,), (1,)), ((), ())), preferred_element_type=jnp.float32
    ).astype(jnp.bfloat16)
    scale = (node_dev * n_row * n_col) ** (-0.5)
    return (
        output,
        grad_features,
        total[: weight.shape[0]] * scale,
        total[weight.shape[0]] * scale,
    )


def solution(mesh):
    return jax.shard_map(
        shards,
        mesh=mesh,
        in_specs=(
            P(("row", "col"), None),
            P(),
            P(),
            P(("row", "col"), None),
            P("row", "col"),
            P("row", "col", None),
            P("row", "col", None),
            P("row", "col", None, None),
            P("row", "col", None, None),
        ),
        out_specs=(P(("row", "col"), None), P(("row", "col"), None), P(), P()),
        check_vma=False,
    )
```

```python
import functools
import functools
import jax
import jax.numpy as jnp
from jax import lax
from jax.experimental import pallas as pl
from jax.experimental.pallas import tpu as pltpu
from jax.sharding import PartitionSpec as P


def swap(x, axis, bit):
    n = lax.axis_size(axis)
    return lax.ppermute(x, axis, [(i, i ^ bit) for i in range(n)])


def bits_of(axis):
    n = lax.axis_size(axis)
    return [1 << k for k in range(n.bit_length() - 1)]


def scatter_sum(x, axis):
    for bit in bits_of(axis):
        pairs = x.reshape((x.shape[0] // 2, 2) + x.shape[1:])
        x = pairs[:, 0] + swap(pairs[:, 1], axis, bit)
    return x[0]


def part_orders(per):
    bits = bits_of("col")[::-1]
    turned = bits[:-2] + bits[-1:] + bits[-2:-1]
    return [bits, turned] if per % 2 == 0 and len(bits) > 1 else [bits]


def gather_pieces(blocks, beside):
    orders = part_orders(blocks.shape[0])
    size = blocks.shape[0] // len(orders)
    held = [blocks[None]]
    for step in range(len(orders[0]) - 1):
        if len(held) < len(orders) and step >= len(orders[0]) - 2:
            held = [held[0][:, i * size : (i + 1) * size] for i in range(len(orders))]
        came = [swap(x, "col", order[step]) for x, order in zip(held, orders)]
        held = [jnp.concatenate([x, y], axis=0) for x, y in zip(held, came)]
        held = beside(step, held)
    came = [swap(x, "col", order[-1]) for x, order in zip(held, orders)]
    shape = (-1,) + blocks.shape[1:]
    return [[x.reshape(shape), y.reshape(shape)] for x, y in zip(held, came)]


def piece_index(per, far, block, rho=0, n_row=1):
    orders = part_orders(per)
    size = per // len(orders)
    half = lax.axis_size("col") // 2
    result = 0
    for i, order in enumerate(orders):
        spot = sum(((far & bit) > 0).astype(jnp.int32) << t for t, bit in enumerate(order))
        piece = (i * n_row + rho) * 2 + spot // half
        here = (piece * half + spot % half) * size + block % size
        result = jnp.where(block // size == i, here, result)
    return result


def total_steps():
    return [("row", bit) for bit in bits_of("row")] + [("col", bit) for bit in bits_of("col")[::-1]]


GROUP = 8
TURN = 4 * GROUP
DEPTH = 3
ROOM = 64
SPARE = 8
FIELD = 1 << 16
UNIT = 2.0**-14


def tile_rows():
    shape = (8, 16, 128)
    rows = 16 * lax.broadcasted_iota(jnp.int32, shape, 0) + lax.broadcasted_iota(jnp.int32, shape, 1)
    return rows.astype(jnp.float32).astype(jnp.bfloat16)


def block_of(code, rows):
    def tile(x):
        return jnp.broadcast_to(x.astype(jnp.float32), (16, 128)).astype(jnp.bfloat16)[None]

    o = code >> 16
    zero = jnp.zeros((), jnp.bfloat16)
    one = jnp.ones((), jnp.bfloat16)
    w = tile((code & (FIELD - 1)).astype(jnp.float32) * UNIT)
    left = jnp.where(rows == tile(o >> 7), w, zero).reshape(128, 128)
    right = jnp.where(rows == tile(o & 127), one, zero).reshape(128, 128)
    return lax.dot_general(
        left, right, (((1,), (1,)), ((), ())), preferred_element_type=jnp.float32
    ).astype(jnp.bfloat16)


def pack_kernel(meta, pos, codes, labels, after, out):
    out[...] = jnp.zeros_like(out)
    stride = ROOM + SPARE
    for k in range(labels.shape[0]):
        out[pl.ds(k * stride + ROOM, 1), :] = labels[pl.ds(k, 1), :]

    def turn(i, _):
        for u in range(GROUP):
            s = i * GROUP + u
            out[pl.ds(pos[s], 1), :] = codes[pl.ds(s, 1), :]
        return 0

    lax.fori_loop(0, meta[0], turn, 0)


def build_kernel(meta, order, codes, *refs):
    dense, dbuf, sems = refs[-3:]
    start, turns = meta[0], meta[1]
    rows = tile_rows()

    def out_copy(i):
        slot = lax.rem(i, DEPTH)
        return pltpu.make_async_copy(
            dbuf.at[slot], dense.at[pl.ds(i * TURN, TURN)], sems.at[slot]
        )

    def turn(i, _):
        slot = lax.rem(i, DEPTH)

        @pl.when(i >= start + DEPTH)
        def _():
            out_copy(i - DEPTH).wait()

        lines = [codes[pl.ds(order[i * TURN + u], 1), :] for u in range(TURN)]
        for u in range(0, TURN, GROUP):
            blocks = [block_of(line, rows) for line in lines[u : u + GROUP]]
            for k, block in enumerate(blocks):
                dbuf[slot, u + k] = block
        out_copy(i).start()
        return 0

    lax.fori_loop(start, turns, turn, 0)

    def finish(i, _):
        out_copy(i).wait()
        return 0

    lax.fori_loop(jnp.maximum(turns - DEPTH, start), turns, finish, 0)


def fetch(pieces, into, sems):
    size = pieces[0].shape[0]
    copies = [
        pltpu.make_async_copy(piece, into.at[pl.ds(i * size, size)], sems.at[i])
        for i, piece in enumerate(pieces)
    ]
    for copy in copies:
        copy.start()
    return copies


def read_dense(turns, dense, dbuf, sems, product, prepare):
    def in_copy(i):
        slot = lax.rem(i, DEPTH)
        return pltpu.make_async_copy(
            dense.at[pl.ds(i * TURN, TURN)], dbuf.at[slot], sems.at[slot]
        )

    def begin(i, _):
        in_copy(i).start()
        return 0

    lax.fori_loop(0, jnp.minimum(turns, DEPTH - 1), begin, 0)
    prepare()

    def turn(i, _):
        @pl.when(i + DEPTH - 1 < turns)
        def _():
            in_copy(i + DEPTH - 1).start()

        in_copy(i).wait()
        product(i, lax.rem(i, DEPTH))
        return 0

    lax.fori_loop(0, turns, turn, 0)


def add_pairs(i, owner, one, into):
    groups = TURN // GROUP
    for g in range(0, groups, 2):
        added = [one(g), one(g + 1)]
        for k in range(2):
            into[owner[i * groups + g + k]] += added[k]


def forward_kernel(n, meta, col, owner, weight, bias, cotangent, dense, *refs):
    pieces, refs = refs[:n], refs[n:]
    output, turned, local, totals, feat, proj, dbuf, piece_sems, sems = refs
    copies = fetch(pieces, feat, piece_sems)
    size, _, width = pieces[0].shape
    batch = 8 if size % 8 == 0 else 1

    def project(t, _):
        spot = pl.ds(t * batch, batch)
        held = feat[spot].reshape(batch * 128, width)
        low = jnp.dot(held, weight[...], preferred_element_type=jnp.float32)
        proj[spot] = low.astype(jnp.bfloat16).reshape(batch, 128, width)
        return 0

    def prepare():
        totals[...] = jnp.zeros_like(totals)
        for i, copy in enumerate(copies):
            copy.wait()
            lax.fori_loop(i * size // batch, (i + 1) * size // batch, project, 0)

    def product(i, slot):
        def one(g):
            spots = [col[i * TURN + g * GROUP + u] for u in range(GROUP)]
            left = jnp.concatenate([dbuf[slot, g * GROUP + u] for u in range(GROUP)], axis=1)
            right = jnp.concatenate(
                [jnp.concatenate([proj[c], feat[c]], axis=1) for c in spots], axis=0
            )
            return jnp.dot(left, right, preferred_element_type=jnp.float32)

        add_pairs(i, owner, one, totals)

    read_dense(meta[1], dense, dbuf, sems, product, prepare)

    weight_sum, bias_sum = 0.0, 0.0
    for q in range(totals.shape[0]):
        lines = pl.ds(q * 128, 128)
        pre = totals[q, :, :width] + bias[...]
        output[lines, :] = jnp.maximum(pre, 0.0).astype(jnp.bfloat16)
        grad = jnp.where(pre > 0, cotangent[lines, :].astype(jnp.float32), 0.0)
        turned[q] = grad.T.astype(jnp.bfloat16)
        weight_sum += lax.dot_general(
            totals[q, :, width:].astype(jnp.bfloat16),
            grad.astype(jnp.bfloat16),
            (((0,), (0,)), ((), ())),
            preferred_element_type=jnp.float32,
        )
        bias_sum += jnp.sum(grad, axis=0, keepdims=True)
    local[pl.ds(0, width), :] = weight_sum
    local[pl.ds(width, 8), :] = jnp.broadcast_to(bias_sum, (8, width))


def tile_kernel(meta, order, dst, col, codes, panel, totals):
    rows = tile_rows()
    totals[...] = jnp.zeros_like(totals)

    def turn(i, _):
        for u in range(GROUP):
            p = i * GROUP + u
            block = block_of(codes[pl.ds(order[p], 1), :], rows)
            totals[dst[p]] += jnp.dot(block, panel[col[p]], preferred_element_type=jnp.float32)
        return 0

    lax.fori_loop(0, meta[0], turn, 0)


def backward_kernel(n, meta, src, owner, dense, *refs):
    pieces, (acc, grad, dbuf, piece_sems, sems) = refs[:n], refs[n:]
    copies = fetch(pieces, grad, piece_sems)

    def prepare():
        acc[...] = jnp.zeros_like(acc)
        for copy in copies:
            copy.wait()

    def product(i, slot):
        def one(g):
            spots = [src[i * TURN + g * GROUP + u] for u in range(GROUP)]
            left = jnp.concatenate([grad[c] for c in spots], axis=1)
            right = dbuf[slot, pl.ds(g * GROUP, GROUP)].reshape(GROUP * 128, 128)
            return jnp.dot(left, right, preferred_element_type=jnp.float32)

        add_pairs(i, owner, one, acc)

    read_dense(meta[1], dense, dbuf, sems, product, prepare)


SMEM = pl.BlockSpec(memory_space=pltpu.SMEM)
VMEM = pl.BlockSpec(memory_space=pltpu.VMEM)
HBM = pl.BlockSpec(memory_space=pl.ANY)
PARAMS = pltpu.CompilerParams(vmem_limit_bytes=48 * 1024 * 1024)


def cost(slots, products):
    flops = 2 * slots * products * 128**3
    return pl.CostEstimate(flops=flops, bytes_accessed=slots * 128 * 128 * 2, transcendentals=0)


def run_tile(meta, order, dst, col, codes, panel, row_blocks):
    return pl.pallas_call(
        tile_kernel,
        out_shape=jax.ShapeDtypeStruct((row_blocks, 128, panel.shape[-1]), jnp.float32),
        in_specs=[SMEM] * 4 + [VMEM] * 2,
        out_specs=VMEM,
        compiler_params=PARAMS,
    )(meta, order, dst, col, codes, panel)


def run_pack(meta, pos, codes, labels, after):
    length = labels.shape[0] * (ROOM + SPARE)
    return pl.pallas_call(
        pack_kernel,
        out_shape=jax.ShapeDtypeStruct((length, 128), jnp.int32),
        in_specs=[SMEM] * 2 + [VMEM] * 2 + [HBM],
        out_specs=VMEM,
        compiler_params=PARAMS,
    )(meta, pos, codes, labels, after)


def run_build(meta, order, codes, after, dense):
    others = after if dense is None else after + [dense]
    return pl.pallas_call(
        build_kernel,
        out_shape=jax.ShapeDtypeStruct((order.shape[0], 128, 128), jnp.bfloat16),
        in_specs=[SMEM] * 2 + [VMEM] + [HBM] * len(others),
        out_specs=HBM,
        scratch_shapes=[
            pltpu.VMEM((DEPTH, TURN, 128, 128), jnp.bfloat16),
            pltpu.SemaphoreType.DMA((DEPTH,)),
        ],
        input_output_aliases={} if dense is None else {2 + len(others): 0},
        compiler_params=PARAMS,
        cost_estimate=cost(order.shape[0], 2),
    )(meta, order, codes, *others)


def run_forward(meta, col, owner, weight, bias, cotangent, dense, feat):
    n = len(feat)
    size, _, width = feat[0].shape
    row_blocks = cotangent.shape[0] // 128
    return pl.pallas_call(
        functools.partial(forward_kernel, n),
        out_shape=(
            jax.ShapeDtypeStruct(cotangent.shape, jnp.bfloat16),
            jax.ShapeDtypeStruct((row_blocks, width, 128), jnp.bfloat16),
            jax.ShapeDtypeStruct((width + 8, width), jnp.float32),
        ),
        in_specs=[SMEM] * 3 + [VMEM] * 3 + [HBM] * (n + 1),
        out_specs=[VMEM] * 3,
        scratch_shapes=[
            pltpu.VMEM((row_blocks, 128, 2 * width), jnp.float32),
            pltpu.VMEM((n * size, 128, width), jnp.bfloat16),
            pltpu.VMEM((n * size, 128, width), jnp.bfloat16),
            pltpu.VMEM((DEPTH, TURN, 128, 128), jnp.bfloat16),
            pltpu.SemaphoreType.DMA((n,)),
            pltpu.SemaphoreType.DMA((DEPTH,)),
        ],
        compiler_params=PARAMS,
        cost_estimate=cost(col.shape[0], 4),
    )(meta, col, owner, weight, bias, cotangent, dense, *feat)


def run_backward(meta, src, owner, pieces, dense, col_blocks):
    n = len(pieces)
    size, width, _ = pieces[0].shape
    return pl.pallas_call(
        functools.partial(backward_kernel, n),
        out_shape=jax.ShapeDtypeStruct((col_blocks, width, 128), jnp.float32),
        in_specs=[SMEM] * 3 + [HBM] * (n + 1),
        out_specs=VMEM,
        scratch_shapes=[
            pltpu.VMEM((n * size, width, 128), jnp.bfloat16),
            pltpu.VMEM((DEPTH, TURN, 128, 128), jnp.bfloat16),
            pltpu.SemaphoreType.DMA((n,)),
            pltpu.SemaphoreType.DMA((DEPTH,)),
        ],
        compiler_params=PARAMS,
        cost_estimate=cost(src.shape[0], 4),
    )(meta, src, owner, dense, *pieces)


def grouped(key, live, value, fill, keys):
    ids = jnp.arange(key.shape[0], dtype=jnp.int32)
    names = jnp.arange(keys, dtype=jnp.int32)
    key = jnp.where(live, key, keys)
    before = (key[:, None] == key[None, :]) & (ids[:, None] < ids[None, :])
    rank = jnp.sum(before.astype(jnp.int32), axis=0)
    counts = jnp.sum((key[:, None] == names[None, :]).astype(jnp.int32), axis=0)
    filled = (counts + GROUP - 1) // GROUP * GROUP
    base = jnp.sum(jnp.where(names[:, None] < key[None, :], filled[:, None], 0), axis=0)
    pos = jnp.where(live, base + rank, -1)
    ends = jnp.sum(jnp.where(names[:, None] <= names[None, :], filled[:, None], 0), axis=0)
    length = -(-(key.shape[0] + keys * GROUP) // TURN) * TURN
    first = jnp.arange(length // GROUP, dtype=jnp.int32) * GROUP
    group_key = jnp.sum((ends[:, None] <= first[None, :]).astype(jnp.int32), axis=0)
    turns = (jnp.sum(filled) + TURN - 1) // TURN
    return place(pos, value, length, fill), jnp.minimum(group_key, keys - 1), turns


def place(pos, value, length, fill):
    spots = jnp.arange(length, dtype=jnp.int32)
    hit = pos[:, None] == spots[None, :]
    return jnp.sum(jnp.where(hit, value[:, None] - fill, 0), axis=0) + fill


def shards(
    features,
    weight,
    bias,
    cotangent,
    block_count,
    block_rows,
    block_cols,
    edge_offsets,
    edge_weight,
):
    node_dev, width = features.shape
    n_row = lax.axis_size("row")
    n_col = lax.axis_size("col")
    slots = block_rows.shape[2]
    count = block_count[0, 0]
    mine = lax.axis_index("col")
    mine_row = lax.axis_index("row")
    per = node_dev // 128
    row_blocks = per * n_col
    col_blocks = per * n_row
    by_owner = n_row * n_col * node_dev * width * 2 <= 8 * 1024 * 1024

    brow = block_rows[0, 0]
    bcol = block_cols[0, 0]
    ids = jnp.arange(slots, dtype=jnp.int32)
    live = ids < count
    codes = edge_offsets[0, 0] * FIELD + (
        edge_weight[0, 0].astype(jnp.float32) * (1.0 / UNIT)
    ).astype(jnp.int32)
    codes = jnp.pad(codes, ((0, 8), (0, 0)))
    home = brow // per
    turns_plain = ((count + GROUP - 1) // GROUP).reshape(1)

    def tile_plan():
        wide = lax.all_gather(features, "row", axis=0, tiled=True)
        low = jnp.dot(wide, weight, preferred_element_type=jnp.float32).astype(jnp.bfloat16)
        panel = jnp.concatenate([low, wide], axis=1).reshape(col_blocks, 128, 2 * width)
        order = jnp.where(live, ids, slots)
        dst = jnp.where(live, (home ^ mine) * per + brow % per, 0)
        totals = run_tile(turns_plain, order, dst, bcol, codes, panel, row_blocks)
        own = scatter_sum(totals.reshape(n_col, node_dev, 2 * width), "col")
        pre = own[:, :width] + bias
        output = jnp.maximum(pre, 0.0).astype(jnp.bfloat16)
        grad = jnp.where(pre > 0, cotangent.astype(jnp.float32), 0.0)
        turned = jnp.swapaxes(grad.astype(jnp.bfloat16).reshape(per, 128, width), 1, 2)
        weight_sum = lax.dot_general(
            own[:, width:].astype(jnp.bfloat16),
            grad.astype(jnp.bfloat16),
            (((0,), (0,)), ((), ())),
            preferred_element_type=jnp.float32,
        )
        bias_sum = jnp.broadcast_to(jnp.sum(grad, axis=0), (8, width))
        return output, turned, jnp.concatenate([weight_sum, bias_sum], axis=0)

    source = piece_index(per, home ^ mine, brow % per)
    back_list, back_owner, back_turns = grouped(
        bcol, live, ids * FIELD + source, slots * FIELD, col_blocks
    )
    back_span = jnp.stack([jnp.zeros_like(back_turns), back_turns])
    state = {"dense": None}

    def build(held, start, end):
        span = jnp.stack([back_turns * start // 8, back_turns * end // 8])
        state["dense"] = run_build(
            span, back_list // FIELD, codes, held, state["dense"]
        )

    if by_owner:
        same = live[:, None] & (home[:, None] == home[None, :]) & (ids[:, None] < ids[None, :])
        rank = jnp.sum(same.astype(jnp.int32), axis=0)
        over = jnp.any(live & (rank >= ROOM)).astype(jnp.int32)
        fits = live & (rank < ROOM)
        label = 1 + (brow % per) * col_blocks + bcol
        labels = place(jnp.where(fits, home * ROOM + rank, -1), label, n_col * ROOM, 0)
        labels = jnp.concatenate(
            [labels.reshape(n_col, ROOM), jnp.full((n_col, 128 - ROOM), over)], axis=1
        )
        stride = ROOM + SPARE
        pos = jnp.where(fits, home * stride + rank, ROOM + SPARE - 1)
        def exchange(step, held):
            if step == 1:
                packed = run_pack(turns_plain, pos, codes, labels, held[0])
                state["came"] = lax.all_to_all(
                    packed.reshape(n_col, stride, 128),
                    "col",
                    split_axis=0,
                    concat_axis=0,
                    tiled=True,
                )
                build(held, 0, 4)
            if step == 2:
                held, state["dense"] = lax.optimization_barrier((held, state["dense"]))
            return held

        pairs = gather_pieces(features.reshape(per, 128, width), exchange)
        came = state["came"]
        spread = jnp.max(came[:, ROOM, ROOM:], axis=0)[None]
        for bit in bits_of("row"):
            spread = spread + swap(spread, "row", bit)
        any_over = jnp.max(spread) > 0

        got = came[:, ROOM, :ROOM]
        sources = jnp.arange(n_col, dtype=jnp.int32)[:, None]
        places = jnp.arange(ROOM, dtype=jnp.int32)[None, :]
        row_here = ((got - 1) // col_blocks).reshape(-1)
        col_there = (got - 1) % col_blocks
        col_there = piece_index(
            per, sources ^ mine, col_there % per, (col_there // per) ^ mine_row, n_row
        )
        line = sources * stride + places
        listed, owner, turns = grouped(
            row_here, (got > 0).reshape(-1), (line * FIELD + col_there).reshape(-1), (ROOM + 1) * FIELD, per
        )
        span = jnp.stack([jnp.zeros_like(turns), turns])
        here = run_build(span, listed // FIELD, came.reshape(n_col * stride, 128), [], None)
        last, here = lax.optimization_barrier(([pair[1] for pair in pairs], here))
        feat = []
        for pair in [[pair[0], x] for pair, x in zip(pairs, last)]:
            rows = [pair]
            for bit in bits_of("row"):
                rows = rows + [[swap(x, "row", bit) for x in pair] for pair in rows]
            feat += [x for pair in rows for x in pair]
        done = run_forward(
            span, listed % FIELD, owner, weight, bias[None], cotangent, here, feat
        )
        done = lax.cond(any_over, tile_plan, lambda: tuple(done))
    else:
        build([features], 0, 4)
        done = tile_plan()

    output, turned, total = done
    steps = total_steps()

    def add_total():
        state["total"] = state["total"] + swap(state["total"], *steps.pop(0))

    def beside(step, held):
        held, state["total"], state["dense"] = lax.optimization_barrier(
            (held, state["total"], state["dense"])
        )
        add_total()
        if step in (1, 2):
            build(held, 2 + 2 * step, 4 + 2 * step)
        return held

    state["total"] = total
    for _ in range(n_row.bit_length() - 1):
        add_total()
    grad = [x for pair in gather_pieces(turned, beside) for x in pair]
    grad, state["total"] = lax.optimization_barrier((grad, state["total"]))
    while steps:
        add_total()
    total = state["total"]
    acc = run_backward(
        back_span, back_list % FIELD, back_owner, grad, state["dense"], col_blocks
    )
    back = jnp.swapaxes(acc, 1, 2).reshape(col_blocks * 128, width)
    grad_proj = scatter_sum(
        jnp.stack(
            [
                lax.dynamic_slice_in_dim(back, (mine_row ^ k) * node_dev, node_dev, 0)
                for k in range(n_row)
            ]
        ),
        "row",
    ).astype(jnp.bfloat16)
    grad_features = lax.dot_general(
        grad_proj, weight, (((1,), (1,)), ((), ())), preferred_element_type=jnp.float32
    ).astype(jnp.bfloat16)
    scale = (node_dev * n_row * n_col) ** (-0.5)
    return (
        output,
        grad_features,
        total[: weight.shape[0]] * scale,
        total[weight.shape[0]] * scale,
    )


def solution(mesh):
    return jax.shard_map(
        shards,
        mesh=mesh,
        in_specs=(
            P(("row", "col"), None),
            P(),
            P(),
            P(("row", "col"), None),
            P("row", "col"),
            P("row", "col", None),
            P("row", "col", None),
            P("row", "col", None, None),
            P("row", "col", None, None),
        ),
        out_specs=(P(("row", "col"), None), P(("row", "col"), None), P(), P()),
        check_vma=False,
    )
```

```python
import functools
import functools
import jax
import jax.numpy as jnp
from jax import lax
from jax.experimental import pallas as pl
from jax.experimental.pallas import tpu as pltpu
from jax.sharding import PartitionSpec as P


def swap(x, axis, bit):
    n = lax.axis_size(axis)
    return lax.ppermute(x, axis, [(i, i ^ bit) for i in range(n)])


def bits_of(axis):
    n = lax.axis_size(axis)
    return [1 << k for k in range(n.bit_length() - 1)]


def scatter_sum(x, axis):
    for bit in bits_of(axis):
        pairs = x.reshape((x.shape[0] // 2, 2) + x.shape[1:])
        x = pairs[:, 0] + swap(pairs[:, 1], axis, bit)
    return x[0]


def part_orders(per):
    bits = bits_of("col")[::-1]
    turned = bits[:-2] + bits[-1:] + bits[-2:-1]
    return [bits, turned] if per % 2 == 0 and len(bits) > 1 else [bits]


def gather_pieces(blocks, beside):
    orders = part_orders(blocks.shape[0])
    size = blocks.shape[0] // len(orders)
    near = [0]
    for bit in orders[0][:-2]:
        near = near + [far | bit for far in near]
    whole = [blocks if far == 0 else swap(blocks, "col", far) for far in near]
    (whole,) = beside(0, [jnp.stack(whole)])
    held = [whole[:, i * size : (i + 1) * size] for i in range(len(orders))]
    if len(orders[0]) > 1:
        came = [swap(x, "col", order[-2]) for x, order in zip(held, orders)]
        held = beside(1, [jnp.concatenate([x, y], axis=0) for x, y in zip(held, came)])
    came = [swap(x, "col", order[-1]) for x, order in zip(held, orders)]
    shape = (-1,) + blocks.shape[1:]
    return [[x.reshape(shape), y.reshape(shape)] for x, y in zip(held, came)]


def piece_index(per, far, block, rho=0, n_row=1):
    orders = part_orders(per)
    size = per // len(orders)
    half = lax.axis_size("col") // 2
    result = 0
    for i, order in enumerate(orders):
        spot = sum(((far & bit) > 0).astype(jnp.int32) << t for t, bit in enumerate(order))
        piece = (i * n_row + rho) * 2 + spot // half
        here = (piece * half + spot % half) * size + block % size
        result = jnp.where(block // size == i, here, result)
    return result


def split_rows(x):
    n, mine = lax.axis_size("row"), lax.axis_index("row")
    size = -(-x.shape[0] // (8 * n)) * 8
    x = jnp.pad(x, ((0, n * size - x.shape[0]), (0, 0)))
    parts = [lax.dynamic_slice_in_dim(x, (mine ^ k) * size, size, 0) for k in range(n)]
    return scatter_sum(jnp.stack(parts), "row")


def join_rows(x):
    n, mine = lax.axis_size("row"), lax.axis_index("row")
    parts = [x]
    for bit in bits_of("row"):
        parts = parts + [swap(part, "row", bit) for part in parts]
    parts = jnp.stack(parts)
    return jnp.concatenate(
        [lax.dynamic_index_in_dim(parts, mine ^ k, 0, keepdims=False) for k in range(n)]
    )


GROUP = 8
TURN = 4 * GROUP
DEPTH = 5
ROOM = 64
SPARE = 8
FIELD = 1 << 16
UNIT = 2.0**-14


def tile_rows():
    shape = (8, 16, 128)
    rows = 16 * lax.broadcasted_iota(jnp.int32, shape, 0) + lax.broadcasted_iota(jnp.int32, shape, 1)
    return rows.astype(jnp.float32).astype(jnp.bfloat16)


def block_of(code, rows):
    def tile(x):
        return jnp.broadcast_to(x.astype(jnp.float32), (16, 128)).astype(jnp.bfloat16)[None]

    o = code >> 16
    zero = jnp.zeros((), jnp.bfloat16)
    one = jnp.ones((), jnp.bfloat16)
    w = tile((code & (FIELD - 1)).astype(jnp.float32) * UNIT)
    left = jnp.where(rows == tile(o >> 7), w, zero).reshape(128, 128)
    right = jnp.where(rows == tile(o & 127), one, zero).reshape(128, 128)
    return lax.dot_general(
        left, right, (((1,), (1,)), ((), ())), preferred_element_type=jnp.float32
    ).astype(jnp.bfloat16)


def pack_kernel(meta, pos, codes, labels, out):
    out[...] = jnp.zeros_like(out)
    stride = ROOM + SPARE
    for k in range(labels.shape[0]):
        out[pl.ds(k * stride + ROOM, 1), :] = labels[pl.ds(k, 1), :]

    def turn(i, _):
        for u in range(GROUP):
            s = i * GROUP + u
            out[pl.ds(pos[s], 1), :] = codes[pl.ds(s, 1), :]
        return 0

    lax.fori_loop(0, meta[0], turn, 0)


def build_kernel(meta, order, codes, *refs):
    dense, dbuf, sems = refs[-3:]
    start, turns = meta[0], meta[1]
    rows = tile_rows()

    def out_copy(i):
        slot = lax.rem(i, DEPTH)
        return pltpu.make_async_copy(
            dbuf.at[slot], dense.at[pl.ds(i * TURN, TURN)], sems.at[slot]
        )

    def turn(i, _):
        slot = lax.rem(i, DEPTH)

        @pl.when(i >= start + DEPTH)
        def _():
            out_copy(i - DEPTH).wait()

        lines = [codes[pl.ds(order[i * TURN + u], 1), :] for u in range(TURN)]
        for u in range(0, TURN, GROUP):
            blocks = [block_of(line, rows) for line in lines[u : u + GROUP]]
            for k, block in enumerate(blocks):
                dbuf[slot, u + k] = block
        out_copy(i).start()
        return 0

    lax.fori_loop(start, turns, turn, 0)

    def finish(i, _):
        out_copy(i).wait()
        return 0

    lax.fori_loop(jnp.maximum(turns - DEPTH, start), turns, finish, 0)


def fetch(pieces, into, sems):
    size = pieces[0].shape[0]
    copies = [
        pltpu.make_async_copy(piece, into.at[pl.ds(i * size, size)], sems.at[i])
        for i, piece in enumerate(pieces)
    ]
    for copy in copies:
        copy.start()
    return copies


def read_dense(turns, dense, dbuf, sems, product, prepare):
    def in_copy(i):
        slot = lax.rem(i, DEPTH)
        return pltpu.make_async_copy(
            dense.at[pl.ds(i * TURN, TURN)], dbuf.at[slot], sems.at[slot]
        )

    def begin(i, _):
        in_copy(i).start()
        return 0

    lax.fori_loop(0, jnp.minimum(turns, DEPTH - 1), begin, 0)
    prepare()

    def turn(i, _):
        @pl.when(i + DEPTH - 1 < turns)
        def _():
            in_copy(i + DEPTH - 1).start()

        in_copy(i).wait()
        product(i, lax.rem(i, DEPTH))
        return 0

    lax.fori_loop(0, turns, turn, 0)


def add_pairs(i, owner, one, into):
    groups = TURN // GROUP
    for g in range(0, groups, 2):
        added = [one(g), one(g + 1)]
        for k in range(2):
            into[owner[i * groups + g + k]] += added[k]


def forward_kernel(n, meta, col, owner, weight, bias, cotangent, dense, *refs):
    pieces, refs = refs[:n], refs[n:]
    output, turned, local, totals, feat, proj, dbuf, piece_sems, sems = refs
    copies = fetch(pieces, feat, piece_sems)
    size, _, width = pieces[0].shape
    batch = 8 if size % 8 == 0 else 1

    def project(t, _):
        spot = pl.ds(t * batch, batch)
        held = feat[spot].reshape(batch * 128, width)
        low = jnp.dot(held, weight[...], preferred_element_type=jnp.float32)
        proj[spot] = low.astype(jnp.bfloat16).reshape(batch, 128, width)
        return 0

    def prepare():
        totals[...] = jnp.zeros_like(totals)
        for i, copy in enumerate(copies):
            copy.wait()
            lax.fori_loop(i * size // batch, (i + 1) * size // batch, project, 0)

    def product(i, slot):
        def one(g):
            spots = [col[i * TURN + g * GROUP + u] for u in range(GROUP)]
            left = jnp.concatenate([dbuf[slot, g * GROUP + u] for u in range(GROUP)], axis=1)
            right = jnp.concatenate(
                [jnp.concatenate([proj[c], feat[c]], axis=1) for c in spots], axis=0
            )
            return jnp.dot(left, right, preferred_element_type=jnp.float32)

        add_pairs(i, owner, one, totals)

    read_dense(meta[1], dense, dbuf, sems, product, prepare)

    weight_sum, bias_sum = 0.0, 0.0
    for q in range(totals.shape[0]):
        lines = pl.ds(q * 128, 128)
        pre = totals[q, :, :width] + bias[...]
        output[lines, :] = jnp.maximum(pre, 0.0).astype(jnp.bfloat16)
        grad = jnp.where(pre > 0, cotangent[lines, :].astype(jnp.float32), 0.0)
        turned[q] = grad.T.astype(jnp.bfloat16)
        weight_sum += lax.dot_general(
            totals[q, :, width:].astype(jnp.bfloat16),
            grad.astype(jnp.bfloat16),
            (((0,), (0,)), ((), ())),
            preferred_element_type=jnp.float32,
        )
        bias_sum += jnp.sum(grad, axis=0, keepdims=True)
    local[pl.ds(0, width), :] = weight_sum
    local[pl.ds(width, 8), :] = jnp.broadcast_to(bias_sum, (8, width))


def tile_kernel(meta, order, dst, col, codes, panel, totals):
    rows = tile_rows()
    totals[...] = jnp.zeros_like(totals)

    def turn(i, _):
        for u in range(GROUP):
            p = i * GROUP + u
            block = block_of(codes[pl.ds(order[p], 1), :], rows)
            totals[dst[p]] += jnp.dot(block, panel[col[p]], preferred_element_type=jnp.float32)
        return 0

    lax.fori_loop(0, meta[0], turn, 0)


def backward_kernel(n, meta, src, owner, dense, *refs):
    pieces, (acc, grad, dbuf, piece_sems, sems) = refs[:n], refs[n:]
    copies = fetch(pieces, grad, piece_sems)

    def prepare():
        acc[...] = jnp.zeros_like(acc)
        for copy in copies:
            copy.wait()

    def product(i, slot):
        def one(g):
            spots = [src[i * TURN + g * GROUP + u] for u in range(GROUP)]
            left = jnp.concatenate([grad[c] for c in spots], axis=1)
            right = dbuf[slot, pl.ds(g * GROUP, GROUP)].reshape(GROUP * 128, 128)
            return jnp.dot(left, right, preferred_element_type=jnp.float32)

        add_pairs(i, owner, one, acc)

    read_dense(meta[1], dense, dbuf, sems, product, prepare)


SMEM = pl.BlockSpec(memory_space=pltpu.SMEM)
VMEM = pl.BlockSpec(memory_space=pltpu.VMEM)
HBM = pl.BlockSpec(memory_space=pl.ANY)
PARAMS = pltpu.CompilerParams(vmem_limit_bytes=48 * 1024 * 1024)


def cost(slots, products):
    flops = 2 * slots * products * 128**3
    return pl.CostEstimate(flops=flops, bytes_accessed=slots * 128 * 128 * 2, transcendentals=0)


def run_tile(meta, order, dst, col, codes, panel, row_blocks):
    return pl.pallas_call(
        tile_kernel,
        out_shape=jax.ShapeDtypeStruct((row_blocks, 128, panel.shape[-1]), jnp.float32),
        in_specs=[SMEM] * 4 + [VMEM] * 2,
        out_specs=VMEM,
        compiler_params=PARAMS,
    )(meta, order, dst, col, codes, panel)


def run_pack(meta, pos, codes, labels):
    length = labels.shape[0] * (ROOM + SPARE)
    return pl.pallas_call(
        pack_kernel,
        out_shape=jax.ShapeDtypeStruct((length, 128), jnp.int32),
        in_specs=[SMEM] * 2 + [VMEM] * 2,
        out_specs=VMEM,
        compiler_params=PARAMS,
    )(meta, pos, codes, labels)


def run_build(meta, order, codes, after, dense):
    others = after if dense is None else after + [dense]
    return pl.pallas_call(
        build_kernel,
        out_shape=jax.ShapeDtypeStruct((order.shape[0], 128, 128), jnp.bfloat16),
        in_specs=[SMEM] * 2 + [VMEM] + [HBM] * len(others),
        out_specs=HBM,
        scratch_shapes=[
            pltpu.VMEM((DEPTH, TURN, 128, 128), jnp.bfloat16),
            pltpu.SemaphoreType.DMA((DEPTH,)),
        ],
        input_output_aliases={} if dense is None else {2 + len(others): 0},
        compiler_params=PARAMS,
        cost_estimate=cost(order.shape[0], 2),
    )(meta, order, codes, *others)


def run_forward(meta, col, owner, weight, bias, cotangent, dense, feat):
    n = len(feat)
    size, _, width = feat[0].shape
    row_blocks = cotangent.shape[0] // 128
    return pl.pallas_call(
        functools.partial(forward_kernel, n),
        out_shape=(
            jax.ShapeDtypeStruct(cotangent.shape, jnp.bfloat16),
            jax.ShapeDtypeStruct((row_blocks, width, 128), jnp.bfloat16),
            jax.ShapeDtypeStruct((width + 8, width), jnp.float32),
        ),
        in_specs=[SMEM] * 3 + [VMEM] * 3 + [HBM] * (n + 1),
        out_specs=[VMEM] * 3,
        scratch_shapes=[
            pltpu.VMEM((row_blocks, 128, 2 * width), jnp.float32),
            pltpu.VMEM((n * size, 128, width), jnp.bfloat16),
            pltpu.VMEM((n * size, 128, width), jnp.bfloat16),
            pltpu.VMEM((DEPTH, TURN, 128, 128), jnp.bfloat16),
            pltpu.SemaphoreType.DMA((n,)),
            pltpu.SemaphoreType.DMA((DEPTH,)),
        ],
        compiler_params=PARAMS,
        cost_estimate=cost(col.shape[0], 4),
    )(meta, col, owner, weight, bias, cotangent, dense, *feat)


def run_backward(meta, src, owner, pieces, dense, col_blocks):
    n = len(pieces)
    size, width, _ = pieces[0].shape
    return pl.pallas_call(
        functools.partial(backward_kernel, n),
        out_shape=jax.ShapeDtypeStruct((col_blocks, width, 128), jnp.float32),
        in_specs=[SMEM] * 3 + [HBM] * (n + 1),
        out_specs=VMEM,
        scratch_shapes=[
            pltpu.VMEM((n * size, width, 128), jnp.bfloat16),
            pltpu.VMEM((DEPTH, TURN, 128, 128), jnp.bfloat16),
            pltpu.SemaphoreType.DMA((n,)),
            pltpu.SemaphoreType.DMA((DEPTH,)),
        ],
        compiler_params=PARAMS,
        cost_estimate=cost(src.shape[0], 4),
    )(meta, src, owner, dense, *pieces)


def grouped(key, live, value, fill, keys):
    ids = jnp.arange(key.shape[0], dtype=jnp.int32)
    names = jnp.arange(keys, dtype=jnp.int32)
    key = jnp.where(live, key, keys)
    before = (key[:, None] == key[None, :]) & (ids[:, None] < ids[None, :])
    rank = jnp.sum(before.astype(jnp.int32), axis=0)
    counts = jnp.sum((key[:, None] == names[None, :]).astype(jnp.int32), axis=0)
    filled = (counts + GROUP - 1) // GROUP * GROUP
    base = jnp.sum(jnp.where(names[:, None] < key[None, :], filled[:, None], 0), axis=0)
    pos = jnp.where(live, base + rank, -1)
    ends = jnp.sum(jnp.where(names[:, None] <= names[None, :], filled[:, None], 0), axis=0)
    length = -(-(key.shape[0] + keys * GROUP) // TURN) * TURN
    first = jnp.arange(length // GROUP, dtype=jnp.int32) * GROUP
    group_key = jnp.sum((ends[:, None] <= first[None, :]).astype(jnp.int32), axis=0)
    turns = (jnp.sum(filled) + TURN - 1) // TURN
    return place(pos, value, length, fill), jnp.minimum(group_key, keys - 1), turns


def place(pos, value, length, fill):
    spots = jnp.arange(length, dtype=jnp.int32)
    hit = pos[:, None] == spots[None, :]
    return jnp.sum(jnp.where(hit, value[:, None] - fill, 0), axis=0) + fill


def shards(
    features,
    weight,
    bias,
    cotangent,
    block_count,
    block_rows,
    block_cols,
    edge_offsets,
    edge_weight,
):
    node_dev, width = features.shape
    n_row = lax.axis_size("row")
    n_col = lax.axis_size("col")
    slots = block_rows.shape[2]
    count = block_count[0, 0]
    mine = lax.axis_index("col")
    mine_row = lax.axis_index("row")
    per = node_dev // 128
    row_blocks = per * n_col
    col_blocks = per * n_row
    by_owner = n_row * n_col * node_dev * width * 2 <= 8 * 1024 * 1024

    brow = block_rows[0, 0]
    bcol = block_cols[0, 0]
    ids = jnp.arange(slots, dtype=jnp.int32)
    live = ids < count
    codes = edge_offsets[0, 0] * FIELD + (
        edge_weight[0, 0].astype(jnp.float32) * (1.0 / UNIT)
    ).astype(jnp.int32)
    codes = jnp.pad(codes, ((0, 8), (0, 0)))
    home = brow // per
    turns_plain = ((count + GROUP - 1) // GROUP).reshape(1)

    def tile_plan():
        wide = lax.all_gather(features, "row", axis=0, tiled=True)
        low = jnp.dot(wide, weight, preferred_element_type=jnp.float32).astype(jnp.bfloat16)
        panel = jnp.concatenate([low, wide], axis=1).reshape(col_blocks, 128, 2 * width)
        order = jnp.where(live, ids, slots)
        dst = jnp.where(live, (home ^ mine) * per + brow % per, 0)
        totals = run_tile(turns_plain, order, dst, bcol, codes, panel, row_blocks)
        own = scatter_sum(totals.reshape(n_col, node_dev, 2 * width), "col")
        pre = own[:, :width] + bias
        output = jnp.maximum(pre, 0.0).astype(jnp.bfloat16)
        grad = jnp.where(pre > 0, cotangent.astype(jnp.float32), 0.0)
        turned = jnp.swapaxes(grad.astype(jnp.bfloat16).reshape(per, 128, width), 1, 2)
        weight_sum = lax.dot_general(
            own[:, width:].astype(jnp.bfloat16),
            grad.astype(jnp.bfloat16),
            (((0,), (0,)), ((), ())),
            preferred_element_type=jnp.float32,
        )
        bias_sum = jnp.broadcast_to(jnp.sum(grad, axis=0), (8, width))
        return output, turned, jnp.concatenate([weight_sum, bias_sum], axis=0)

    source = piece_index(per, home ^ mine, brow % per)
    back_list, back_owner, back_turns = grouped(
        bcol, live, ids * FIELD + source, slots * FIELD, col_blocks
    )
    back_span = jnp.stack([jnp.zeros_like(back_turns), back_turns])
    state = {"dense": None}

    def build(held, start, end):
        span = jnp.stack([back_turns * start // 8, back_turns * end // 8])
        state["dense"] = run_build(
            span, back_list // FIELD, codes, held, state["dense"]
        )

    if by_owner:
        same = live[:, None] & (home[:, None] == home[None, :]) & (ids[:, None] < ids[None, :])
        rank = jnp.sum(same.astype(jnp.int32), axis=0)
        over = jnp.any(live & (rank >= ROOM)).astype(jnp.int32)
        fits = live & (rank < ROOM)
        label = 1 + (brow % per) * col_blocks + bcol
        labels = place(jnp.where(fits, home * ROOM + rank, -1), label, n_col * ROOM, 0)
        labels = jnp.concatenate(
            [labels.reshape(n_col, ROOM), jnp.full((n_col, 128 - ROOM), over)], axis=1
        )
        stride = ROOM + SPARE
        pos = jnp.where(fits, home * stride + rank, ROOM + SPARE - 1)
        packed = run_pack(turns_plain, pos, codes, labels)
        came = lax.all_to_all(
            packed.reshape(n_col, stride, 128), "col", split_axis=0, concat_axis=0, tiled=True
        )
        spread = jnp.max(came[:, ROOM, ROOM:], axis=0)[None]
        for bit in bits_of("row"):
            spread = spread + swap(spread, "row", bit)
        any_over = jnp.max(spread) > 0

        got = came[:, ROOM, :ROOM]
        sources = jnp.arange(n_col, dtype=jnp.int32)[:, None]
        places = jnp.arange(ROOM, dtype=jnp.int32)[None, :]
        row_here = ((got - 1) // col_blocks).reshape(-1)
        col_there = (got - 1) % col_blocks
        col_there = piece_index(
            per, sources ^ mine, col_there % per, (col_there // per) ^ mine_row, n_row
        )
        line = sources * stride + places
        listed, owner, turns = grouped(
            row_here, (got > 0).reshape(-1), (line * FIELD + col_there).reshape(-1), (ROOM + 1) * FIELD, per
        )
        span = jnp.stack([jnp.zeros_like(turns), turns])
        lists = [listed, owner, span]

        def prepare(step, held):
            nonlocal lists
            if step == 0:
                build(held, 0, 4)
            if step == 1:
                held, lists, state["dense"] = lax.optimization_barrier(
                    (held, lists, state["dense"])
                )
            return held

        pairs = gather_pieces(features.reshape(per, 128, width), prepare)
        listed, owner, span = lists
        here = run_build(span, listed // FIELD, came.reshape(n_col * stride, 128), [], None)
        last, here = lax.optimization_barrier(([pair[1] for pair in pairs], here))
        feat = []
        for pair in [[pair[0], x] for pair, x in zip(pairs, last)]:
            rows = [pair]
            for bit in bits_of("row"):
                rows = rows + [[swap(x, "row", bit) for x in pair] for pair in rows]
            feat += [x for pair in rows for x in pair]
        done = run_forward(
            span, listed % FIELD, owner, weight, bias[None], cotangent, here, feat
        )
        done = lax.cond(any_over, tile_plan, lambda: tuple(done))
    else:
        build([features], 0, 4)
        done = tile_plan()

    output, turned, total = done
    steps = bits_of("col")[::-1]

    def add_total():
        state["total"] = state["total"] + swap(state["total"], "col", steps.pop(0))

    def beside(step, held):
        held, state["total"], state["dense"] = lax.optimization_barrier(
            (held, state["total"], state["dense"])
        )
        if steps:
            add_total()
        build(held, 4 + 2 * step, 6 + 2 * step)
        return held

    state["total"] = split_rows(total)
    while len(steps) > 3:
        add_total()
    grad = [x for pair in gather_pieces(turned, beside) for x in pair]
    grad, state["total"] = lax.optimization_barrier((grad, state["total"]))
    while steps:
        add_total()
    acc = run_backward(
        back_span, back_list % FIELD, back_owner, grad, state["dense"], col_blocks
    )
    acc, total = lax.optimization_barrier((acc, state["total"]))
    total = join_rows(total)
    back = jnp.swapaxes(acc, 1, 2).reshape(col_blocks * 128, width)
    grad_proj = scatter_sum(
        jnp.stack(
            [
                lax.dynamic_slice_in_dim(back, (mine_row ^ k) * node_dev, node_dev, 0)
                for k in range(n_row)
            ]
        ),
        "row",
    ).astype(jnp.bfloat16)
    grad_features = lax.dot_general(
        grad_proj, weight, (((1,), (1,)), ((), ())), preferred_element_type=jnp.float32
    ).astype(jnp.bfloat16)
    scale = (node_dev * n_row * n_col) ** (-0.5)
    return (
        output,
        grad_features,
        total[: weight.shape[0]] * scale,
        total[weight.shape[0]] * scale,
    )


def solution(mesh):
    return jax.shard_map(
        shards,
        mesh=mesh,
        in_specs=(
            P(("row", "col"), None),
            P(),
            P(),
            P(("row", "col"), None),
            P("row", "col"),
            P("row", "col", None),
            P("row", "col", None),
            P("row", "col", None, None),
            P("row", "col", None, None),
        ),
        out_specs=(P(("row", "col"), None), P(("row", "col"), None), P(), P()),
        check_vma=False,
    )
```

```python
import functools
import functools
import jax
import jax.numpy as jnp
from jax import lax
from jax.experimental import pallas as pl
from jax.experimental.pallas import tpu as pltpu
from jax.sharding import PartitionSpec as P


def swap(x, axis, bit):
    n = lax.axis_size(axis)
    return lax.ppermute(x, axis, [(i, i ^ bit) for i in range(n)])


def bits_of(axis):
    n = lax.axis_size(axis)
    return [1 << k for k in range(n.bit_length() - 1)]


def scatter_sum(x, axis):
    for bit in bits_of(axis):
        pairs = x.reshape((x.shape[0] // 2, 2) + x.shape[1:])
        x = pairs[:, 0] + swap(pairs[:, 1], axis, bit)
    return x[0]


def part_orders(per):
    bits = bits_of("col")[::-1]
    turned = bits[:-2] + bits[-1:] + bits[-2:-1]
    return [bits, turned] if per % 2 == 0 and len(bits) > 1 else [bits]


def gather_pieces(blocks, beside):
    orders = part_orders(blocks.shape[0])
    size = blocks.shape[0] // len(orders)
    near = [0]
    for bit in orders[0][:-2]:
        near = near + [far | bit for far in near]
    whole = [blocks if far == 0 else swap(blocks, "col", far) for far in near]
    (whole,) = beside(0, [jnp.stack(whole)])
    held = [whole[:, i * size : (i + 1) * size] for i in range(len(orders))]
    if len(orders[0]) > 1:
        came = [swap(x, "col", order[-2]) for x, order in zip(held, orders)]
        held = beside(1, [jnp.concatenate([x, y], axis=0) for x, y in zip(held, came)])
    came = [swap(x, "col", order[-1]) for x, order in zip(held, orders)]
    shape = (-1,) + blocks.shape[1:]
    return [[x.reshape(shape), y.reshape(shape)] for x, y in zip(held, came)]


def piece_index(per, far, block, rho=0, n_row=1):
    orders = part_orders(per)
    size = per // len(orders)
    half = lax.axis_size("col") // 2
    result = 0
    for i, order in enumerate(orders):
        spot = sum(((far & bit) > 0).astype(jnp.int32) << t for t, bit in enumerate(order))
        piece = (i * n_row + rho) * 2 + spot // half
        here = (piece * half + spot % half) * size + block % size
        result = jnp.where(block // size == i, here, result)
    return result


def split_rows(x):
    n, mine = lax.axis_size("row"), lax.axis_index("row")
    size = -(-x.shape[0] // (8 * n)) * 8
    x = jnp.pad(x, ((0, n * size - x.shape[0]), (0, 0)))
    parts = [lax.dynamic_slice_in_dim(x, (mine ^ k) * size, size, 0) for k in range(n)]
    return scatter_sum(jnp.stack(parts), "row")


def join_rows(x):
    n, mine = lax.axis_size("row"), lax.axis_index("row")
    parts = [x]
    for bit in bits_of("row"):
        parts = parts + [swap(part, "row", bit) for part in parts]
    parts = jnp.stack(parts)
    return jnp.concatenate(
        [lax.dynamic_index_in_dim(parts, mine ^ k, 0, keepdims=False) for k in range(n)]
    )


GROUP = 8
TURN = 4 * GROUP
DEPTH = 5
ROOM = 64
SPARE = 8
FIELD = 1 << 16
UNIT = 2.0**-14


def tile_rows():
    shape = (8, 16, 128)
    rows = 16 * lax.broadcasted_iota(jnp.int32, shape, 0) + lax.broadcasted_iota(jnp.int32, shape, 1)
    return rows.astype(jnp.float32).astype(jnp.bfloat16)


def block_of(code, rows):
    def tile(x):
        return jnp.broadcast_to(x.astype(jnp.float32), (16, 128)).astype(jnp.bfloat16)[None]

    o = code >> 16
    zero = jnp.zeros((), jnp.bfloat16)
    one = jnp.ones((), jnp.bfloat16)
    w = tile((code & (FIELD - 1)).astype(jnp.float32) * UNIT)
    left = jnp.where(rows == tile(o >> 7), w, zero).reshape(128, 128)
    right = jnp.where(rows == tile(o & 127), one, zero).reshape(128, 128)
    return lax.dot_general(
        left, right, (((1,), (1,)), ((), ())), preferred_element_type=jnp.float32
    ).astype(jnp.bfloat16)


def pack_kernel(meta, pos, codes, labels, out):
    out[...] = jnp.zeros_like(out)
    stride = ROOM + SPARE
    for k in range(labels.shape[0]):
        out[pl.ds(k * stride + ROOM, 1), :] = labels[pl.ds(k, 1), :]

    def turn(i, _):
        for u in range(GROUP):
            s = i * GROUP + u
            out[pl.ds(pos[s], 1), :] = codes[pl.ds(s, 1), :]
        return 0

    lax.fori_loop(0, meta[0], turn, 0)


def build_kernel(meta, order, codes, *refs):
    dense, dbuf, sems = refs[-3:]
    start, turns = meta[0], meta[1]
    rows = tile_rows()

    def out_copy(i):
        slot = lax.rem(i, DEPTH)
        return pltpu.make_async_copy(
            dbuf.at[slot], dense.at[pl.ds(i * TURN, TURN)], sems.at[slot]
        )

    def turn(i, _):
        slot = lax.rem(i, DEPTH)

        @pl.when(i >= start + DEPTH)
        def _():
            out_copy(i - DEPTH).wait()

        lines = [codes[pl.ds(order[i * TURN + u], 1), :] for u in range(TURN)]
        for u in range(0, TURN, GROUP):
            blocks = [block_of(line, rows) for line in lines[u : u + GROUP]]
            for k, block in enumerate(blocks):
                dbuf[slot, u + k] = block
        out_copy(i).start()
        return 0

    lax.fori_loop(start, turns, turn, 0)

    def finish(i, _):
        out_copy(i).wait()
        return 0

    lax.fori_loop(jnp.maximum(turns - DEPTH, start), turns, finish, 0)


def fetch(pieces, into, sems):
    size = pieces[0].shape[0]
    copies = [
        pltpu.make_async_copy(piece, into.at[pl.ds(i * size, size)], sems.at[i])
        for i, piece in enumerate(pieces)
    ]
    for copy in copies:
        copy.start()
    return copies


def read_dense(turns, dense, dbuf, sems, product, prepare):
    def in_copy(i):
        slot = lax.rem(i, DEPTH)
        return pltpu.make_async_copy(
            dense.at[pl.ds(i * TURN, TURN)], dbuf.at[slot], sems.at[slot]
        )

    def begin(i, _):
        in_copy(i).start()
        return 0

    lax.fori_loop(0, jnp.minimum(turns, DEPTH - 1), begin, 0)
    prepare()

    def turn(i, _):
        @pl.when(i + DEPTH - 1 < turns)
        def _():
            in_copy(i + DEPTH - 1).start()

        in_copy(i).wait()
        product(i, lax.rem(i, DEPTH))
        return 0

    lax.fori_loop(0, turns, turn, 0)


def add_pairs(i, owner, one, into):
    groups = TURN // GROUP
    for g in range(0, groups, 2):
        added = [one(g), one(g + 1)]
        for k in range(2):
            into[owner[i * groups + g + k]] += added[k]


def forward_kernel(n, scale, meta, col, owner, weight, bias, cotangent, dense, *refs):
    pieces, refs = refs[:n], refs[n:]
    output, turned, local, totals, feat, proj, dbuf, piece_sems, sems = refs
    copies = fetch(pieces, feat, piece_sems)
    size, _, width = pieces[0].shape
    batch = 8 if size % 8 == 0 else 1

    def project(t, _):
        spot = pl.ds(t * batch, batch)
        held = feat[spot].reshape(batch * 128, width)
        low = jnp.dot(held, weight[...], preferred_element_type=jnp.float32)
        proj[spot] = low.astype(jnp.bfloat16).reshape(batch, 128, width)
        return 0

    def prepare():
        totals[...] = jnp.zeros_like(totals)
        for i, copy in enumerate(copies):
            copy.wait()
            lax.fori_loop(i * size // batch, (i + 1) * size // batch, project, 0)

    def product(i, slot):
        def one(g):
            spots = [col[i * TURN + g * GROUP + u] for u in range(GROUP)]
            left = jnp.concatenate([dbuf[slot, g * GROUP + u] for u in range(GROUP)], axis=1)
            right = jnp.concatenate(
                [jnp.concatenate([proj[c], feat[c]], axis=1) for c in spots], axis=0
            )
            return jnp.dot(left, right, preferred_element_type=jnp.float32)

        add_pairs(i, owner, one, totals)

    read_dense(meta[1], dense, dbuf, sems, product, prepare)

    weight_sum, bias_sum = 0.0, 0.0
    for q in range(totals.shape[0]):
        lines = pl.ds(q * 128, 128)
        pre = totals[q, :, :width] + bias[...]
        output[lines, :] = jnp.maximum(pre, 0.0).astype(jnp.bfloat16)
        grad = jnp.where(pre > 0, cotangent[lines, :].astype(jnp.float32), 0.0)
        turned[q] = grad.T.astype(jnp.bfloat16)
        weight_sum += lax.dot_general(
            totals[q, :, width:].astype(jnp.bfloat16),
            grad.astype(jnp.bfloat16),
            (((0,), (0,)), ((), ())),
            preferred_element_type=jnp.float32,
        )
        bias_sum += jnp.sum(grad, axis=0, keepdims=True)
    local[pl.ds(0, width), :] = weight_sum * scale
    local[pl.ds(width, 8), :] = jnp.broadcast_to(bias_sum * scale, (8, width))


def tile_kernel(meta, order, dst, col, codes, panel, totals):
    rows = tile_rows()
    totals[...] = jnp.zeros_like(totals)

    def turn(i, _):
        for u in range(GROUP):
            p = i * GROUP + u
            block = block_of(codes[pl.ds(order[p], 1), :], rows)
            totals[dst[p]] += jnp.dot(block, panel[col[p]], preferred_element_type=jnp.float32)
        return 0

    lax.fori_loop(0, meta[0], turn, 0)


def backward_kernel(n, meta, src, owner, dense, *refs):
    pieces, (acc, grad, dbuf, piece_sems, sems) = refs[:n], refs[n:]
    copies = fetch(pieces, grad, piece_sems)

    def prepare():
        acc[...] = jnp.zeros_like(acc)
        for copy in copies:
            copy.wait()

    def product(i, slot):
        def one(g):
            spots = [src[i * TURN + g * GROUP + u] for u in range(GROUP)]
            left = jnp.concatenate([grad[c] for c in spots], axis=1)
            right = dbuf[slot, pl.ds(g * GROUP, GROUP)].reshape(GROUP * 128, 128)
            return jnp.dot(left, right, preferred_element_type=jnp.float32)

        add_pairs(i, owner, one, acc)

    read_dense(meta[1], dense, dbuf, sems, product, prepare)


SMEM = pl.BlockSpec(memory_space=pltpu.SMEM)
VMEM = pl.BlockSpec(memory_space=pltpu.VMEM)
HBM = pl.BlockSpec(memory_space=pl.ANY)
PARAMS = pltpu.CompilerParams(vmem_limit_bytes=48 * 1024 * 1024)


def cost(slots, products):
    flops = 2 * slots * products * 128**3
    return pl.CostEstimate(flops=flops, bytes_accessed=slots * 128 * 128 * 2, transcendentals=0)


def run_tile(meta, order, dst, col, codes, panel, row_blocks):
    return pl.pallas_call(
        tile_kernel,
        out_shape=jax.ShapeDtypeStruct((row_blocks, 128, panel.shape[-1]), jnp.float32),
        in_specs=[SMEM] * 4 + [VMEM] * 2,
        out_specs=VMEM,
        compiler_params=PARAMS,
    )(meta, order, dst, col, codes, panel)


def run_pack(meta, pos, codes, labels):
    length = labels.shape[0] * (ROOM + SPARE)
    return pl.pallas_call(
        pack_kernel,
        out_shape=jax.ShapeDtypeStruct((length, 128), jnp.int32),
        in_specs=[SMEM] * 2 + [VMEM] * 2,
        out_specs=VMEM,
        compiler_params=PARAMS,
    )(meta, pos, codes, labels)


def run_build(meta, order, codes, after, dense):
    others = after if dense is None else after + [dense]
    return pl.pallas_call(
        build_kernel,
        out_shape=jax.ShapeDtypeStruct((order.shape[0], 128, 128), jnp.bfloat16),
        in_specs=[SMEM] * 2 + [VMEM] + [HBM] * len(others),
        out_specs=HBM,
        scratch_shapes=[
            pltpu.VMEM((DEPTH, TURN, 128, 128), jnp.bfloat16),
            pltpu.SemaphoreType.DMA((DEPTH,)),
        ],
        input_output_aliases={} if dense is None else {2 + len(others): 0},
        compiler_params=PARAMS,
        cost_estimate=cost(order.shape[0], 2),
    )(meta, order, codes, *others)


def run_forward(scale, meta, col, owner, weight, bias, cotangent, dense, feat):
    n = len(feat)
    size, _, width = feat[0].shape
    row_blocks = cotangent.shape[0] // 128
    return pl.pallas_call(
        functools.partial(forward_kernel, n, scale),
        out_shape=(
            jax.ShapeDtypeStruct(cotangent.shape, jnp.bfloat16),
            jax.ShapeDtypeStruct((row_blocks, width, 128), jnp.bfloat16),
            jax.ShapeDtypeStruct((width + 8, width), jnp.float32),
        ),
        in_specs=[SMEM] * 3 + [VMEM] * 3 + [HBM] * (n + 1),
        out_specs=[VMEM] * 3,
        scratch_shapes=[
            pltpu.VMEM((row_blocks, 128, 2 * width), jnp.float32),
            pltpu.VMEM((n * size, 128, width), jnp.bfloat16),
            pltpu.VMEM((n * size, 128, width), jnp.bfloat16),
            pltpu.VMEM((DEPTH, TURN, 128, 128), jnp.bfloat16),
            pltpu.SemaphoreType.DMA((n,)),
            pltpu.SemaphoreType.DMA((DEPTH,)),
        ],
        compiler_params=PARAMS,
        cost_estimate=cost(col.shape[0], 4),
    )(meta, col, owner, weight, bias, cotangent, dense, *feat)


def run_backward(meta, src, owner, pieces, dense, col_blocks):
    n = len(pieces)
    size, width, _ = pieces[0].shape
    return pl.pallas_call(
        functools.partial(backward_kernel, n),
        out_shape=jax.ShapeDtypeStruct((col_blocks, width, 128), jnp.float32),
        in_specs=[SMEM] * 3 + [HBM] * (n + 1),
        out_specs=VMEM,
        scratch_shapes=[
            pltpu.VMEM((n * size, width, 128), jnp.bfloat16),
            pltpu.VMEM((DEPTH, TURN, 128, 128), jnp.bfloat16),
            pltpu.SemaphoreType.DMA((n,)),
            pltpu.SemaphoreType.DMA((DEPTH,)),
        ],
        compiler_params=PARAMS,
        cost_estimate=cost(src.shape[0], 4),
    )(meta, src, owner, dense, *pieces)


def grouped(key, live, value, fill, keys):
    ids = jnp.arange(key.shape[0], dtype=jnp.int32)
    names = jnp.arange(keys, dtype=jnp.int32)
    key = jnp.where(live, key, keys)
    before = (key[:, None] == key[None, :]) & (ids[:, None] < ids[None, :])
    rank = jnp.sum(before.astype(jnp.int32), axis=0)
    counts = jnp.sum((key[:, None] == names[None, :]).astype(jnp.int32), axis=0)
    filled = (counts + GROUP - 1) // GROUP * GROUP
    base = jnp.sum(jnp.where(names[:, None] < key[None, :], filled[:, None], 0), axis=0)
    pos = jnp.where(live, base + rank, -1)
    ends = jnp.sum(jnp.where(names[:, None] <= names[None, :], filled[:, None], 0), axis=0)
    length = -(-(key.shape[0] + keys * GROUP) // TURN) * TURN
    first = jnp.arange(length // GROUP, dtype=jnp.int32) * GROUP
    group_key = jnp.sum((ends[:, None] <= first[None, :]).astype(jnp.int32), axis=0)
    turns = (jnp.sum(filled) + TURN - 1) // TURN
    return place(pos, value, length, fill), jnp.minimum(group_key, keys - 1), turns


def place(pos, value, length, fill):
    spots = jnp.arange(length, dtype=jnp.int32)
    hit = pos[:, None] == spots[None, :]
    return jnp.sum(jnp.where(hit, value[:, None] - fill, 0), axis=0) + fill


def shards(
    features,
    weight,
    bias,
    cotangent,
    block_count,
    block_rows,
    block_cols,
    edge_offsets,
    edge_weight,
):
    node_dev, width = features.shape
    n_row = lax.axis_size("row")
    n_col = lax.axis_size("col")
    slots = block_rows.shape[2]
    count = block_count[0, 0]
    mine = lax.axis_index("col")
    mine_row = lax.axis_index("row")
    per = node_dev // 128
    row_blocks = per * n_col
    col_blocks = per * n_row
    scale = (node_dev * n_row * n_col) ** (-0.5)
    by_owner = n_row * n_col * node_dev * width * 2 <= 8 * 1024 * 1024

    brow = block_rows[0, 0]
    bcol = block_cols[0, 0]
    ids = jnp.arange(slots, dtype=jnp.int32)
    live = ids < count
    codes = edge_offsets[0, 0] * FIELD + (
        edge_weight[0, 0].astype(jnp.float32) * (1.0 / UNIT)
    ).astype(jnp.int32)
    codes = jnp.pad(codes, ((0, 8), (0, 0)))
    home = brow // per
    turns_plain = ((count + GROUP - 1) // GROUP).reshape(1)

    def tile_plan():
        wide = lax.all_gather(features, "row", axis=0, tiled=True)
        low = jnp.dot(wide, weight, preferred_element_type=jnp.float32).astype(jnp.bfloat16)
        panel = jnp.concatenate([low, wide], axis=1).reshape(col_blocks, 128, 2 * width)
        order = jnp.where(live, ids, slots)
        dst = jnp.where(live, (home ^ mine) * per + brow % per, 0)
        totals = run_tile(turns_plain, order, dst, bcol, codes, panel, row_blocks)
        own = scatter_sum(totals.reshape(n_col, node_dev, 2 * width), "col")
        pre = own[:, :width] + bias
        output = jnp.maximum(pre, 0.0).astype(jnp.bfloat16)
        grad = jnp.where(pre > 0, cotangent.astype(jnp.float32), 0.0)
        turned = jnp.swapaxes(grad.astype(jnp.bfloat16).reshape(per, 128, width), 1, 2)
        weight_sum = lax.dot_general(
            own[:, width:].astype(jnp.bfloat16),
            grad.astype(jnp.bfloat16),
            (((0,), (0,)), ((), ())),
            preferred_element_type=jnp.float32,
        )
        bias_sum = jnp.broadcast_to(jnp.sum(grad, axis=0), (8, width))
        return output, turned, jnp.concatenate([weight_sum, bias_sum], axis=0) * scale

    source = piece_index(per, home ^ mine, brow % per)
    back_list, back_owner, back_turns = grouped(
        bcol, live, ids * FIELD + source, slots * FIELD, col_blocks
    )
    back_span = jnp.stack([jnp.zeros_like(back_turns), back_turns])
    state = {"dense": None}

    def build(held, start, end):
        span = jnp.stack([back_turns * start // 4, back_turns * end // 4])
        state["dense"] = run_build(
            span, back_list // FIELD, codes, held, state["dense"]
        )

    if by_owner:
        same = live[:, None] & (home[:, None] == home[None, :]) & (ids[:, None] < ids[None, :])
        rank = jnp.sum(same.astype(jnp.int32), axis=0)
        over = jnp.any(live & (rank >= ROOM)).astype(jnp.int32)
        fits = live & (rank < ROOM)
        label = 1 + (brow % per) * col_blocks + bcol
        labels = place(jnp.where(fits, home * ROOM + rank, -1), label, n_col * ROOM, 0)
        labels = jnp.concatenate(
            [labels.reshape(n_col, ROOM), jnp.full((n_col, 128 - ROOM), over)], axis=1
        )
        stride = ROOM + SPARE
        pos = jnp.where(fits, home * stride + rank, ROOM + SPARE - 1)
        packed = run_pack(turns_plain, pos, codes, labels)
        came = lax.all_to_all(
            packed.reshape(n_col, stride, 128), "col", split_axis=0, concat_axis=0, tiled=True
        )
        spread = jnp.max(came[:, ROOM, ROOM:], axis=0)[None]
        for bit in bits_of("row"):
            spread = spread + swap(spread, "row", bit)
        any_over = jnp.max(spread, axis=1)

        got = came[:, ROOM, :ROOM]
        sources = jnp.arange(n_col, dtype=jnp.int32)[:, None]
        places = jnp.arange(ROOM, dtype=jnp.int32)[None, :]
        row_here = ((got - 1) // col_blocks).reshape(-1)
        col_there = (got - 1) % col_blocks
        col_there = piece_index(
            per, sources ^ mine, col_there % per, (col_there // per) ^ mine_row, n_row
        )
        line = sources * stride + places
        listed, owner, turns = grouped(
            row_here, (got > 0).reshape(-1), (line * FIELD + col_there).reshape(-1), (ROOM + 1) * FIELD, per
        )
        span = jnp.stack([jnp.zeros_like(turns), turns])
        lists = [listed, owner, span, any_over]
        lines = came.reshape(n_col * stride, 128)
        here = None

        def prepare(step, held):
            nonlocal lists, here
            if step == 1:
                held, lists, here = lax.optimization_barrier((held, lists, here))
            half = jnp.stack([turns * step // 2, turns * (step + 1) // 2])
            here = run_build(half, listed // FIELD, lines, held + lists[3:], here)
            return held

        pairs = gather_pieces(features.reshape(per, 128, width), prepare)
        listed, owner, span, any_over = lists
        last, here = lax.optimization_barrier(([pair[1] for pair in pairs], here))
        feat = []
        for pair in [[pair[0], x] for pair, x in zip(pairs, last)]:
            rows = [pair]
            for bit in bits_of("row"):
                rows = rows + [[swap(x, "row", bit) for x in pair] for pair in rows]
            feat += [x for pair in rows for x in pair]
        done = run_forward(
            scale, span, listed % FIELD, owner, weight, bias[None], cotangent, here, feat
        )
        done = lax.cond(any_over[0] > 0, tile_plan, lambda: tuple(done))
    else:
        done = tile_plan()

    output, turned, total = done
    steps = bits_of("col")[::-1]

    def add_total():
        state["total"] = state["total"] + swap(state["total"], "col", steps.pop(0))

    def beside(step, held):
        held, state["total"], state["dense"] = lax.optimization_barrier(
            (held, state["total"], state["dense"])
        )
        if steps:
            add_total()
        build(held, 2 + step, 3 + step)
        return held

    state["total"] = split_rows(total)
    while len(steps) > 3:
        add_total()
    build([turned], 0, 2)
    grad = [x for pair in gather_pieces(turned, beside) for x in pair]
    grad, state["total"] = lax.optimization_barrier((grad, state["total"]))
    while steps:
        add_total()
    acc = run_backward(
        back_span, back_list % FIELD, back_owner, grad, state["dense"], col_blocks
    )
    acc, total = lax.optimization_barrier((acc, state["total"]))
    total = join_rows(total)
    back = jnp.swapaxes(acc, 1, 2).reshape(col_blocks * 128, width)
    grad_proj = scatter_sum(
        jnp.stack(
            [
                lax.dynamic_slice_in_dim(back, (mine_row ^ k) * node_dev, node_dev, 0)
                for k in range(n_row)
            ]
        ),
        "row",
    ).astype(jnp.bfloat16)
    grad_features = lax.dot_general(
        grad_proj, weight, (((1,), (1,)), ((), ())), preferred_element_type=jnp.float32
    ).astype(jnp.bfloat16)
    return (
        output,
        grad_features,
        total[: weight.shape[0]],
        total[weight.shape[0]],
    )


def solution(mesh):
    return jax.shard_map(
        shards,
        mesh=mesh,
        in_specs=(
            P(("row", "col"), None),
            P(),
            P(),
            P(("row", "col"), None),
            P("row", "col"),
            P("row", "col", None),
            P("row", "col", None),
            P("row", "col", None, None),
            P("row", "col", None, None),
        ),
        out_specs=(P(("row", "col"), None), P(("row", "col"), None), P(), P()),
        check_vma=False,
    )
```

```python
import functools
import functools
import jax
import jax.numpy as jnp
from jax import lax
from jax.experimental import pallas as pl
from jax.experimental.pallas import tpu as pltpu
from jax.experimental.layout import Layout, with_layout_constraint
from jax.sharding import PartitionSpec as P


def swap(x, axis, bit):
    n = lax.axis_size(axis)
    return lax.ppermute(x, axis, [(i, i ^ bit) for i in range(n)])


def bits_of(axis):
    n = lax.axis_size(axis)
    return [1 << k for k in range(n.bit_length() - 1)]


def scatter_sum(x, axis):
    for bit in bits_of(axis):
        pairs = x.reshape((x.shape[0] // 2, 2) + x.shape[1:])
        x = pairs[:, 0] + swap(pairs[:, 1], axis, bit)
    return x[0]


def part_orders(per):
    bits = bits_of("col")[::-1]
    turned = bits[:-2] + bits[-1:] + bits[-2:-1]
    return [bits, turned] if per % 2 == 0 and len(bits) > 1 else [bits]


def gather_pieces(blocks, beside):
    orders = part_orders(blocks.shape[0])
    size = blocks.shape[0] // len(orders)
    near = [0]
    for bit in orders[0][:-2]:
        near = near + [far | bit for far in near]
    whole = [blocks if far == 0 else swap(blocks, "col", far) for far in near]
    (whole,) = beside(0, [jnp.stack(whole)])
    held = [whole[:, i * size : (i + 1) * size] for i in range(len(orders))]
    if len(orders[0]) > 1:
        came = [swap(x, "col", order[-2]) for x, order in zip(held, orders)]
        held = beside(1, [jnp.concatenate([x, y], axis=0) for x, y in zip(held, came)])
    came = [swap(x, "col", order[-1]) for x, order in zip(held, orders)]
    shape = (-1,) + blocks.shape[1:]
    return [[x.reshape(shape), y.reshape(shape)] for x, y in zip(held, came)]


def piece_index(per, far, block, rho=0, n_row=1):
    orders = part_orders(per)
    size = per // len(orders)
    half = lax.axis_size("col") // 2
    result = 0
    for i, order in enumerate(orders):
        spot = sum(((far & bit) > 0).astype(jnp.int32) << t for t, bit in enumerate(order))
        piece = (i * n_row + rho) * 2 + spot // half
        here = (piece * half + spot % half) * size + block % size
        result = jnp.where(block // size == i, here, result)
    return result


def split_rows(x):
    n, mine = lax.axis_size("row"), lax.axis_index("row")
    size = -(-x.shape[0] // (8 * n)) * 8
    x = jnp.pad(x, ((0, n * size - x.shape[0]), (0, 0)))
    parts = [lax.dynamic_slice_in_dim(x, (mine ^ k) * size, size, 0) for k in range(n)]
    return scatter_sum(jnp.stack(parts), "row")


def join_rows(x):
    n, mine = lax.axis_size("row"), lax.axis_index("row")
    parts = [x]
    for bit in bits_of("row"):
        parts = parts + [swap(part, "row", bit) for part in parts]
    parts = jnp.stack(parts)
    return jnp.concatenate(
        [lax.dynamic_index_in_dim(parts, mine ^ k, 0, keepdims=False) for k in range(n)]
    )


GROUP = 8
TURN = 4 * GROUP
DEPTH = 5
ROOM = 64
SPARE = 8
FIELD = 1 << 16
UNIT = 2.0**-14


def tile_rows():
    shape = (8, 16, 128)
    rows = 16 * lax.broadcasted_iota(jnp.int32, shape, 0) + lax.broadcasted_iota(jnp.int32, shape, 1)
    return rows.astype(jnp.float32).astype(jnp.bfloat16)


def block_of(code, rows):
    def tile(x):
        return jnp.broadcast_to(x.astype(jnp.float32), (16, 128)).astype(jnp.bfloat16)[None]

    o = code >> 16
    zero = jnp.zeros((), jnp.bfloat16)
    one = jnp.ones((), jnp.bfloat16)
    w = tile((code & (FIELD - 1)).astype(jnp.float32) * UNIT)
    left = jnp.where(rows == tile(o >> 7), w, zero).reshape(128, 128)
    right = jnp.where(rows == tile(o & 127), one, zero).reshape(128, 128)
    return lax.dot_general(
        left, right, (((1,), (1,)), ((), ())), preferred_element_type=jnp.float32
    ).astype(jnp.bfloat16)


def pack_kernel(meta, pos, codes, labels, out):
    out[...] = jnp.zeros_like(out)
    stride = ROOM + SPARE
    for k in range(labels.shape[0]):
        out[pl.ds(k * stride + ROOM, 1), :] = labels[pl.ds(k, 1), :]

    def turn(i, _):
        for u in range(GROUP):
            s = i * GROUP + u
            out[pl.ds(pos[s], 1), :] = codes[pl.ds(s, 1), :]
        return 0

    lax.fori_loop(0, meta[0], turn, 0)


def build_kernel(meta, order, codes, *refs):
    dense, dbuf, sems = refs[-3:]
    start, turns = meta[0], meta[1]
    rows = tile_rows()

    def out_copy(i):
        slot = lax.rem(i, DEPTH)
        return pltpu.make_async_copy(
            dbuf.at[slot], dense.at[pl.ds(i * TURN, TURN)], sems.at[slot]
        )

    def turn(i, _):
        slot = lax.rem(i, DEPTH)

        @pl.when(i >= start + DEPTH)
        def _():
            out_copy(i - DEPTH).wait()

        lines = [codes[pl.ds(order[i * TURN + u], 1), :] for u in range(TURN)]
        for u in range(0, TURN, GROUP):
            blocks = [block_of(line, rows) for line in lines[u : u + GROUP]]
            for k, block in enumerate(blocks):
                dbuf[slot, u + k] = block
        out_copy(i).start()
        return 0

    lax.fori_loop(start, turns, turn, 0)

    def finish(i, _):
        out_copy(i).wait()
        return 0

    lax.fori_loop(jnp.maximum(turns - DEPTH, start), turns, finish, 0)


def fetch(pieces, into, sems):
    size = pieces[0].shape[0]
    copies = [
        pltpu.make_async_copy(piece, into.at[pl.ds(i * size, size)], sems.at[i])
        for i, piece in enumerate(pieces)
    ]
    for copy in copies:
        copy.start()
    return copies


def read_dense(start, turns, dense, dbuf, sems, product, prepare):
    def in_copy(i):
        slot = lax.rem(i, DEPTH)
        return pltpu.make_async_copy(
            dense.at[pl.ds(i * TURN, TURN)], dbuf.at[slot], sems.at[slot]
        )

    def begin(i, _):
        in_copy(i).start()
        return 0

    lax.fori_loop(start, jnp.minimum(turns, start + DEPTH - 1), begin, 0)
    prepare()

    def turn(i, _):
        @pl.when(i + DEPTH - 1 < turns)
        def _():
            in_copy(i + DEPTH - 1).start()

        in_copy(i).wait()
        product(i, lax.rem(i, DEPTH))
        return 0

    lax.fori_loop(start, turns, turn, 0)


def add_pairs(i, owner, one, into):
    groups = TURN // GROUP
    for g in range(0, groups, 2):
        added = [one(g), one(g + 1)]
        for k in range(2):
            into[owner[i * groups + g + k]] += added[k]


def forward_kernel(n, scale, meta, col, owner, weight, bias, cotangent, dense, *refs):
    pieces, refs = refs[:n], refs[n:]
    output, turned, local, totals, feat, proj, dbuf, piece_sems, sems = refs
    copies = fetch(pieces, feat, piece_sems)
    size, _, width = pieces[0].shape
    batch = 8 if size % 8 == 0 else 1

    def project(t, _):
        spot = pl.ds(t * batch, batch)
        held = feat[spot].reshape(batch * 128, width)
        low = jnp.dot(held, weight[...], preferred_element_type=jnp.float32)
        proj[spot] = low.astype(jnp.bfloat16).reshape(batch, 128, width)
        return 0

    def prepare():
        totals[...] = jnp.zeros_like(totals)
        for i, copy in enumerate(copies):
            copy.wait()
            lax.fori_loop(i * size // batch, (i + 1) * size // batch, project, 0)

    def product(i, slot):
        def one(g):
            spots = [col[i * TURN + g * GROUP + u] for u in range(GROUP)]
            left = jnp.concatenate([dbuf[slot, g * GROUP + u] for u in range(GROUP)], axis=1)
            right = jnp.concatenate(
                [jnp.concatenate([proj[c], feat[c]], axis=1) for c in spots], axis=0
            )
            return jnp.dot(left, right, preferred_element_type=jnp.float32)

        add_pairs(i, owner, one, totals)

    read_dense(meta[0], meta[1], dense, dbuf, sems, product, prepare)

    weight_sum, bias_sum = 0.0, 0.0
    for q in range(totals.shape[0]):
        lines = pl.ds(q * 128, 128)
        pre = totals[q, :, :width] + bias[...]
        output[lines, :] = jnp.maximum(pre, 0.0).astype(jnp.bfloat16)
        grad = jnp.where(pre > 0, cotangent[lines, :].astype(jnp.float32), 0.0)
        turned[q] = grad.T.astype(jnp.bfloat16)
        weight_sum += lax.dot_general(
            totals[q, :, width:].astype(jnp.bfloat16),
            grad.astype(jnp.bfloat16),
            (((0,), (0,)), ((), ())),
            preferred_element_type=jnp.float32,
        )
        bias_sum += jnp.sum(grad, axis=0, keepdims=True)
    local[pl.ds(0, width), :] = weight_sum * scale
    local[pl.ds(width, 8), :] = jnp.broadcast_to(bias_sum * scale, (8, width))


def tile_kernel(meta, order, dst, col, codes, panel, totals):
    rows = tile_rows()
    totals[...] = jnp.zeros_like(totals)

    def turn(i, _):
        for u in range(GROUP):
            p = i * GROUP + u
            block = block_of(codes[pl.ds(order[p], 1), :], rows)
            totals[dst[p]] += jnp.dot(block, panel[col[p]], preferred_element_type=jnp.float32)
        return 0

    lax.fori_loop(0, meta[0], turn, 0)


def backward_kernel(n, meta, src, owner, before, dense, *refs):
    pieces, (acc, grad, dbuf, piece_sems, sems) = refs[:n], refs[n:]
    copies = fetch(pieces, grad, piece_sems)

    def prepare():
        acc[...] = before[...]
        for copy in copies:
            copy.wait()

    def product(i, slot):
        def one(g):
            spots = [src[i * TURN + g * GROUP + u] for u in range(GROUP)]
            left = jnp.concatenate([grad[c] for c in spots], axis=1)
            right = dbuf[slot, pl.ds(g * GROUP, GROUP)].reshape(GROUP * 128, 128)
            return jnp.dot(left, right, preferred_element_type=jnp.float32)

        add_pairs(i, owner, one, acc)

    read_dense(meta[0], meta[1], dense, dbuf, sems, product, prepare)


SMEM = pl.BlockSpec(memory_space=pltpu.SMEM)
VMEM = pl.BlockSpec(memory_space=pltpu.VMEM)
HBM = pl.BlockSpec(memory_space=pl.ANY)
PARAMS = pltpu.CompilerParams(vmem_limit_bytes=48 * 1024 * 1024)


def cost(slots, products):
    flops = 2 * slots * products * 128**3
    return pl.CostEstimate(flops=flops, bytes_accessed=slots * 128 * 128 * 2, transcendentals=0)


def run_tile(meta, order, dst, col, codes, panel, row_blocks):
    return pl.pallas_call(
        tile_kernel,
        out_shape=jax.ShapeDtypeStruct((row_blocks, 128, panel.shape[-1]), jnp.float32),
        in_specs=[SMEM] * 4 + [VMEM] * 2,
        out_specs=VMEM,
        compiler_params=PARAMS,
    )(meta, order, dst, col, codes, panel)


def run_pack(meta, pos, codes, labels):
    length = labels.shape[0] * (ROOM + SPARE)
    return pl.pallas_call(
        pack_kernel,
        out_shape=jax.ShapeDtypeStruct((length, 128), jnp.int32),
        in_specs=[SMEM] * 2 + [VMEM] * 2,
        out_specs=VMEM,
        compiler_params=PARAMS,
    )(meta, pos, codes, labels)


def run_build(meta, order, codes, after, dense):
    others = after if dense is None else after + [dense]
    return pl.pallas_call(
        build_kernel,
        out_shape=jax.ShapeDtypeStruct((order.shape[0], 128, 128), jnp.bfloat16),
        in_specs=[SMEM] * 2 + [VMEM] + [HBM] * len(others),
        out_specs=HBM,
        scratch_shapes=[
            pltpu.VMEM((DEPTH, TURN, 128, 128), jnp.bfloat16),
            pltpu.SemaphoreType.DMA((DEPTH,)),
        ],
        input_output_aliases={} if dense is None else {2 + len(others): 0},
        compiler_params=PARAMS,
        cost_estimate=cost(order.shape[0], 2),
    )(meta, order, codes, *others)


def run_forward(scale, meta, col, owner, weight, bias, cotangent, dense, feat):
    n = len(feat)
    size, _, width = feat[0].shape
    row_blocks = cotangent.shape[0] // 128
    return pl.pallas_call(
        functools.partial(forward_kernel, n, scale),
        out_shape=(
            jax.ShapeDtypeStruct(cotangent.shape, jnp.bfloat16),
            jax.ShapeDtypeStruct((row_blocks, width, 128), jnp.bfloat16),
            jax.ShapeDtypeStruct((width + 8, width), jnp.float32),
        ),
        in_specs=[SMEM] * 3 + [VMEM] * 3 + [HBM] * (n + 1),
        out_specs=[VMEM] * 3,
        scratch_shapes=[
            pltpu.VMEM((row_blocks, 128, 2 * width), jnp.float32),
            pltpu.VMEM((n * size, 128, width), jnp.bfloat16),
            pltpu.VMEM((n * size, 128, width), jnp.bfloat16),
            pltpu.VMEM((DEPTH, TURN, 128, 128), jnp.bfloat16),
            pltpu.SemaphoreType.DMA((n,)),
            pltpu.SemaphoreType.DMA((DEPTH,)),
        ],
        compiler_params=PARAMS,
        cost_estimate=cost(col.shape[0], 4),
    )(meta, col, owner, weight, bias, cotangent, dense, *feat)


def run_backward(meta, src, owner, before, dense, pieces):
    n = len(pieces)
    size, width, _ = pieces[0].shape
    return pl.pallas_call(
        functools.partial(backward_kernel, n),
        out_shape=jax.ShapeDtypeStruct(before.shape, jnp.float32),
        in_specs=[SMEM] * 3 + [VMEM] + [HBM] * (n + 1),
        out_specs=VMEM,
        scratch_shapes=[
            pltpu.VMEM((n * size, width, 128), jnp.bfloat16),
            pltpu.VMEM((DEPTH, TURN, 128, 128), jnp.bfloat16),
            pltpu.SemaphoreType.DMA((n,)),
            pltpu.SemaphoreType.DMA((DEPTH,)),
        ],
        compiler_params=PARAMS,
        cost_estimate=cost(src.shape[0], 4),
    )(meta, src, owner, before, dense, *pieces)


def grouped(key, live, value, fill, keys, split):
    ids = jnp.arange(key.shape[0], dtype=jnp.int32)
    names = jnp.arange(keys, dtype=jnp.int32)
    key = jnp.where(live, key, keys)
    before = (key[:, None] == key[None, :]) & (ids[:, None] < ids[None, :])
    rank = jnp.sum(before.astype(jnp.int32), axis=0)
    counts = jnp.sum((key[:, None] == names[None, :]).astype(jnp.int32), axis=0)
    filled = (counts + GROUP - 1) // GROUP * GROUP
    below = jnp.sum(jnp.where(names < split, filled, 0))
    first_turns = (below + TURN - 1) // TURN
    filled = filled + jnp.where(names == split - 1, first_turns * TURN - below, 0)
    base = jnp.sum(jnp.where(names[:, None] < key[None, :], filled[:, None], 0), axis=0)
    pos = jnp.where(live, base + rank, -1)
    ends = jnp.sum(jnp.where(names[:, None] <= names[None, :], filled[:, None], 0), axis=0)
    length = (-(-(key.shape[0] + keys * GROUP) // TURN) + 1) * TURN
    first = jnp.arange(length // GROUP, dtype=jnp.int32) * GROUP
    group_key = jnp.sum((ends[:, None] <= first[None, :]).astype(jnp.int32), axis=0)
    turns = (jnp.sum(filled) + TURN - 1) // TURN
    return place(pos, value, length, fill), jnp.minimum(group_key, keys - 1), turns, first_turns


def place(pos, value, length, fill):
    spots = jnp.arange(length, dtype=jnp.int32)
    hit = pos[:, None] == spots[None, :]
    return jnp.sum(jnp.where(hit, value[:, None] - fill, 0), axis=0) + fill


def shards(
    features,
    weight,
    bias,
    cotangent,
    block_count,
    block_rows,
    block_cols,
    edge_offsets,
    edge_weight,
):
    node_dev, width = features.shape
    n_row = lax.axis_size("row")
    n_col = lax.axis_size("col")
    slots = block_rows.shape[2]
    count = block_count[0, 0]
    mine = lax.axis_index("col")
    mine_row = lax.axis_index("row")
    per = node_dev // 128
    row_blocks = per * n_col
    col_blocks = per * n_row
    scale = (node_dev * n_row * n_col) ** (-0.5)
    by_owner = n_row * n_col * node_dev * width * 2 <= 8 * 1024 * 1024

    brow = block_rows[0, 0]
    bcol = block_cols[0, 0]
    ids = jnp.arange(slots, dtype=jnp.int32)
    live = ids < count
    codes = edge_offsets[0, 0] * FIELD + (
        edge_weight[0, 0].astype(jnp.float32) * (1.0 / UNIT)
    ).astype(jnp.int32)
    codes = jnp.pad(codes, ((0, 8), (0, 0)))
    home = brow // per
    turns_plain = ((count + GROUP - 1) // GROUP).reshape(1)

    def tile_plan():
        wide = lax.all_gather(features, "row", axis=0, tiled=True)
        low = jnp.dot(wide, weight, preferred_element_type=jnp.float32).astype(jnp.bfloat16)
        panel = jnp.concatenate([low, wide], axis=1).reshape(col_blocks, 128, 2 * width)
        order = jnp.where(live, ids, slots)
        dst = jnp.where(live, (home ^ mine) * per + brow % per, 0)
        totals = run_tile(turns_plain, order, dst, bcol, codes, panel, row_blocks)
        own = scatter_sum(totals.reshape(n_col, node_dev, 2 * width), "col")
        pre = own[:, :width] + bias
        output = jnp.maximum(pre, 0.0).astype(jnp.bfloat16)
        grad = jnp.where(pre > 0, cotangent.astype(jnp.float32), 0.0)
        turned = jnp.swapaxes(grad.astype(jnp.bfloat16).reshape(per, 128, width), 1, 2)
        weight_sum = lax.dot_general(
            own[:, width:].astype(jnp.bfloat16),
            grad.astype(jnp.bfloat16),
            (((0,), (0,)), ((), ())),
            preferred_element_type=jnp.float32,
        )
        bias_sum = jnp.broadcast_to(jnp.sum(grad, axis=0), (8, width))
        return output, turned, jnp.concatenate([weight_sum, bias_sum], axis=0) * scale

    source = piece_index(per, home ^ mine, brow % per)
    unit = row_blocks // (2 * len(part_orders(per)))
    late = source // unit % 2
    source = source // (2 * unit) * unit + source % unit
    back_list, back_owner, back_turns, early_turns = grouped(
        late * col_blocks + bcol,
        live,
        ids * FIELD + source,
        slots * FIELD,
        2 * col_blocks,
        col_blocks,
    )
    back_owner = back_owner % col_blocks
    spans = [
        jnp.stack([jnp.zeros_like(early_turns), early_turns]),
        jnp.stack([early_turns, back_turns]),
    ]
    state = {"dense": None}

    def build(held, half):
        state["dense"] = run_build(
            spans[half], back_list // FIELD, codes, held, state["dense"]
        )

    if by_owner:
        same = live[:, None] & (home[:, None] == home[None, :]) & (ids[:, None] < ids[None, :])
        rank = jnp.sum(same.astype(jnp.int32), axis=0)
        over = jnp.any(live & (rank >= ROOM)).astype(jnp.int32)
        fits = live & (rank < ROOM)
        label = 1 + (brow % per) * col_blocks + bcol
        labels = place(jnp.where(fits, home * ROOM + rank, -1), label, n_col * ROOM, 0)
        labels = jnp.concatenate(
            [labels.reshape(n_col, ROOM), jnp.full((n_col, 128 - ROOM), over)], axis=1
        )
        stride = ROOM + SPARE
        pos = jnp.where(fits, home * stride + rank, ROOM + SPARE - 1)
        packed = run_pack(turns_plain, pos, codes, labels)
        came = lax.all_to_all(
            packed.reshape(n_col, stride, 128), "col", split_axis=0, concat_axis=0, tiled=True
        )
        spread = jnp.max(came[:, ROOM, ROOM:], axis=0)[None]
        for bit in bits_of("row"):
            spread = spread + swap(spread, "row", bit)
        any_over = jnp.max(spread, axis=1)

        got = came[:, ROOM, :ROOM]
        sources = jnp.arange(n_col, dtype=jnp.int32)[:, None]
        places = jnp.arange(ROOM, dtype=jnp.int32)[None, :]
        row_here = ((got - 1) // col_blocks).reshape(-1)
        col_there = (got - 1) % col_blocks
        col_there = piece_index(
            per, sources ^ mine, col_there % per, (col_there // per) ^ mine_row, n_row
        )
        line = sources * stride + places
        listed, owner, turns, _ = grouped(
            row_here,
            (got > 0).reshape(-1),
            (line * FIELD + col_there).reshape(-1),
            (ROOM + 1) * FIELD,
            per,
            per,
        )
        span = jnp.stack([jnp.zeros_like(turns), turns])

        def prepare(step, held):
            if step == 0:
                build(held, 0)
            if step == 1:
                held, state["dense"] = lax.optimization_barrier((held, state["dense"]))
            return held

        pairs = gather_pieces(features.reshape(per, 128, width), prepare)
        lines = came.reshape(n_col * stride, 128)
        here = run_build(span, listed // FIELD, lines, [], None)
        last, here, any_over = lax.optimization_barrier(
            ([pair[1] for pair in pairs], here, any_over)
        )
        feat = []
        for pair in [[pair[0], x] for pair, x in zip(pairs, last)]:
            rows = [pair]
            for bit in bits_of("row"):
                rows = rows + [[swap(x, "row", bit) for x in pair] for pair in rows]
            feat += [x for pair in rows for x in pair]
        done = run_forward(
            scale, span, listed % FIELD, owner, weight, bias[None], cotangent, here, feat
        )
        done = lax.cond(any_over[0] > 0, tile_plan, lambda: tuple(done))
    else:
        done = tile_plan()

    output, turned, total = done
    turned = with_layout_constraint(turned, Layout(major_to_minor=(0, 1, 2)))
    steps = bits_of("col")[::-1]

    def add_total():
        state["total"] = state["total"] + swap(state["total"], "col", steps.pop(0))

    def beside(step, held):
        held, state["total"], state["dense"] = lax.optimization_barrier(
            (held, state["total"], state["dense"])
        )
        if steps:
            add_total()
        if step == 1:
            add_products(0, held)
        return held

    def add_products(half, pieces):
        pieces = [x.reshape((-1,) + x.shape[2:]) if x.ndim == 4 else x for x in pieces]
        state["acc"] = run_backward(
            spans[half], back_list % FIELD, back_owner, state["acc"], state["dense"], pieces
        )

    state["acc"] = jnp.zeros((col_blocks, width, 128), jnp.float32)
    state["total"] = split_rows(total)
    while len(steps) > 3:
        add_total()
    build([turned], 1)
    grad = gather_pieces(turned, beside)
    late_pieces, state["total"] = lax.optimization_barrier(
        ([pair[1] for pair in grad], state["total"])
    )
    while steps:
        add_total()
    total = join_rows(state["total"])
    add_products(1, late_pieces)
    acc = state["acc"]
    back = jnp.swapaxes(acc, 1, 2).reshape(col_blocks * 128, width)
    grad_proj = scatter_sum(
        jnp.stack(
            [
                lax.dynamic_slice_in_dim(back, (mine_row ^ k) * node_dev, node_dev, 0)
                for k in range(n_row)
            ]
        ),
        "row",
    ).astype(jnp.bfloat16)
    grad_features = lax.dot_general(
        grad_proj, weight, (((1,), (1,)), ((), ())), preferred_element_type=jnp.float32
    ).astype(jnp.bfloat16)
    return (
        output,
        grad_features,
        total[: weight.shape[0]],
        total[weight.shape[0]],
    )


def solution(mesh):
    return jax.shard_map(
        shards,
        mesh=mesh,
        in_specs=(
            P(("row", "col"), None),
            P(),
            P(),
            P(("row", "col"), None),
            P("row", "col"),
            P("row", "col", None),
            P("row", "col", None),
            P("row", "col", None, None),
            P("row", "col", None, None),
        ),
        out_specs=(P(("row", "col"), None), P(("row", "col"), None), P(), P()),
        check_vma=False,
    )
```

```python
import functools
import functools
import jax
import jax.numpy as jnp
from jax import lax
from jax.experimental import pallas as pl
from jax.experimental.pallas import tpu as pltpu
from jax.experimental.layout import Layout, with_layout_constraint
from jax.sharding import PartitionSpec as P


def swap(x, axis, bit):
    n = lax.axis_size(axis)
    return lax.ppermute(x, axis, [(i, i ^ bit) for i in range(n)])


def bits_of(axis):
    n = lax.axis_size(axis)
    return [1 << k for k in range(n.bit_length() - 1)]


def scatter_sum(x, axis):
    for bit in bits_of(axis):
        pairs = x.reshape((x.shape[0] // 2, 2) + x.shape[1:])
        x = pairs[:, 0] + swap(pairs[:, 1], axis, bit)
    return x[0]


def part_orders(per):
    bits = bits_of("col")[::-1]
    turned = bits[:-2] + bits[-1:] + bits[-2:-1]
    return [bits, turned] if per % 2 == 0 and len(bits) > 1 else [bits]


def gather_pieces(blocks, beside):
    orders = part_orders(blocks.shape[0])
    size = blocks.shape[0] // len(orders)
    near = [0]
    for bit in orders[0][:-2]:
        near = near + [far | bit for far in near]
    whole = [blocks if far == 0 else swap(blocks, "col", far) for far in near]
    (whole,) = beside(0, [jnp.stack(whole)])
    held = [whole[:, i * size : (i + 1) * size] for i in range(len(orders))]
    if len(orders[0]) > 1:
        came = [swap(x, "col", order[-2]) for x, order in zip(held, orders)]
        held = beside(1, [jnp.concatenate([x, y], axis=0) for x, y in zip(held, came)])
    came = [swap(x, "col", order[-1]) for x, order in zip(held, orders)]
    shape = (-1,) + blocks.shape[1:]
    return [[x.reshape(shape), y.reshape(shape)] for x, y in zip(held, came)]


def piece_index(per, far, block, rho=0, n_row=1):
    orders = part_orders(per)
    size = per // len(orders)
    half = lax.axis_size("col") // 2
    result = 0
    for i, order in enumerate(orders):
        spot = sum(((far & bit) > 0).astype(jnp.int32) << t for t, bit in enumerate(order))
        piece = (i * n_row + rho) * 2 + spot // half
        here = (piece * half + spot % half) * size + block % size
        result = jnp.where(block // size == i, here, result)
    return result


def split_rows(x):
    n, mine = lax.axis_size("row"), lax.axis_index("row")
    size = -(-x.shape[0] // (8 * n)) * 8
    x = jnp.pad(x, ((0, n * size - x.shape[0]), (0, 0)))
    parts = [lax.dynamic_slice_in_dim(x, (mine ^ k) * size, size, 0) for k in range(n)]
    return scatter_sum(jnp.stack(parts), "row")


def join_rows(x):
    n, mine = lax.axis_size("row"), lax.axis_index("row")
    parts = [x]
    for bit in bits_of("row"):
        parts = parts + [swap(part, "row", bit) for part in parts]
    parts = jnp.stack(parts)
    return jnp.concatenate(
        [lax.dynamic_index_in_dim(parts, mine ^ k, 0, keepdims=False) for k in range(n)]
    )


GROUP = 8
TURN = 4 * GROUP
DEPTH = 5
ROOM = 64
SPARE = 8
FIELD = 1 << 16
UNIT = 2.0**-14


def tile_rows():
    shape = (8, 16, 128)
    rows = 16 * lax.broadcasted_iota(jnp.int32, shape, 0) + lax.broadcasted_iota(jnp.int32, shape, 1)
    return rows.astype(jnp.float32).astype(jnp.bfloat16)


def block_of(code, rows):
    def tile(x):
        return jnp.broadcast_to(x.astype(jnp.float32), (16, 128)).astype(jnp.bfloat16)[None]

    o = code >> 16
    zero = jnp.zeros((), jnp.bfloat16)
    one = jnp.ones((), jnp.bfloat16)
    w = tile((code & (FIELD - 1)).astype(jnp.float32) * UNIT)
    left = jnp.where(rows == tile(o >> 7), w, zero).reshape(128, 128)
    right = jnp.where(rows == tile(o & 127), one, zero).reshape(128, 128)
    return lax.dot_general(
        left, right, (((1,), (1,)), ((), ())), preferred_element_type=jnp.float32
    ).astype(jnp.bfloat16)


def pack_kernel(meta, pos, codes, labels, out):
    out[...] = jnp.zeros_like(out)
    stride = ROOM + SPARE
    for k in range(labels.shape[0]):
        out[pl.ds(k * stride + ROOM, 1), :] = labels[pl.ds(k, 1), :]

    def turn(i, _):
        for u in range(GROUP):
            s = i * GROUP + u
            out[pl.ds(pos[s], 1), :] = codes[pl.ds(s, 1), :]
        return 0

    lax.fori_loop(0, meta[0], turn, 0)


def build_kernel(span, marks, lists, codes, *refs):
    dense, dbuf, sems = refs[-3:]
    start, turns = marks[0, span[0]], marks[0, span[1]]
    rows = tile_rows()

    def out_copy(i):
        slot = lax.rem(i, DEPTH)
        return pltpu.make_async_copy(
            dbuf.at[slot], dense.at[pl.ds(i * TURN, TURN)], sems.at[slot]
        )

    def turn(i, _):
        slot = lax.rem(i, DEPTH)

        @pl.when(i >= start + DEPTH)
        def _():
            out_copy(i - DEPTH).wait()

        lines = [codes[pl.ds(lists[0, i * TURN + u], 1), :] for u in range(TURN)]
        for u in range(0, TURN, GROUP):
            blocks = [block_of(line, rows) for line in lines[u : u + GROUP]]
            for k, block in enumerate(blocks):
                dbuf[slot, u + k] = block
        out_copy(i).start()
        return 0

    lax.fori_loop(start, turns, turn, 0)

    def finish(i, _):
        out_copy(i).wait()
        return 0

    lax.fori_loop(jnp.maximum(turns - DEPTH, start), turns, finish, 0)


def fetch(pieces, into, sems):
    size = pieces[0].shape[0]
    copies = [
        pltpu.make_async_copy(piece, into.at[pl.ds(i * size, size)], sems.at[i])
        for i, piece in enumerate(pieces)
    ]
    for copy in copies:
        copy.start()
    return copies


def read_dense(start, turns, dense, dbuf, sems, product, prepare):
    def in_copy(i):
        slot = lax.rem(i, DEPTH)
        return pltpu.make_async_copy(
            dense.at[pl.ds(i * TURN, TURN)], dbuf.at[slot], sems.at[slot]
        )

    def begin(i, _):
        in_copy(i).start()
        return 0

    lax.fori_loop(start, jnp.minimum(turns, start + DEPTH - 1), begin, 0)
    prepare()

    def turn(i, _):
        @pl.when(i + DEPTH - 1 < turns)
        def _():
            in_copy(i + DEPTH - 1).start()

        in_copy(i).wait()
        product(i, lax.rem(i, DEPTH))
        return 0

    lax.fori_loop(start, turns, turn, 0)


def add_pairs(i, owner, one, into):
    groups = TURN // GROUP
    for g in range(0, groups, 2):
        added = [one(g), one(g + 1)]
        for k in range(2):
            into[owner[0, i * groups + g + k]] += added[k]


def forward_kernel(n, scale, span, marks, lists, owner, weight, bias, cotangent, dense, *refs):
    pieces, refs = refs[:n], refs[n:]
    output, turned, local, totals, feat, proj, dbuf, piece_sems, sems = refs
    copies = fetch(pieces, feat, piece_sems)
    size, _, width = pieces[0].shape
    batch = 8 if size % 8 == 0 else 1

    def project(t, _):
        spot = pl.ds(t * batch, batch)
        held = feat[spot].reshape(batch * 128, width)
        low = jnp.dot(held, weight[...], preferred_element_type=jnp.float32)
        proj[spot] = low.astype(jnp.bfloat16).reshape(batch, 128, width)
        return 0

    def prepare():
        totals[...] = jnp.zeros_like(totals)
        for i, copy in enumerate(copies):
            copy.wait()
            lax.fori_loop(i * size // batch, (i + 1) * size // batch, project, 0)

    def product(i, slot):
        def one(g):
            spots = [lists[1, i * TURN + g * GROUP + u] for u in range(GROUP)]
            left = jnp.concatenate([dbuf[slot, g * GROUP + u] for u in range(GROUP)], axis=1)
            right = jnp.concatenate(
                [jnp.concatenate([proj[c], feat[c]], axis=1) for c in spots], axis=0
            )
            return jnp.dot(left, right, preferred_element_type=jnp.float32)

        add_pairs(i, owner, one, totals)

    read_dense(marks[0, span[0]], marks[0, span[1]], dense, dbuf, sems, product, prepare)

    weight_sum, bias_sum = 0.0, 0.0
    for q in range(totals.shape[0]):
        lines = pl.ds(q * 128, 128)
        pre = totals[q, :, :width] + bias[...]
        output[lines, :] = jnp.maximum(pre, 0.0).astype(jnp.bfloat16)
        grad = jnp.where(pre > 0, cotangent[lines, :].astype(jnp.float32), 0.0)
        turned[q] = grad.T.astype(jnp.bfloat16)
        weight_sum += lax.dot_general(
            totals[q, :, width:].astype(jnp.bfloat16),
            grad.astype(jnp.bfloat16),
            (((0,), (0,)), ((), ())),
            preferred_element_type=jnp.float32,
        )
        bias_sum += jnp.sum(grad, axis=0, keepdims=True)
    local[pl.ds(0, width), :] = weight_sum * scale
    local[pl.ds(width, 8), :] = jnp.broadcast_to(bias_sum * scale, (8, width))


def tile_kernel(meta, order, dst, col, codes, panel, totals):
    rows = tile_rows()
    totals[...] = jnp.zeros_like(totals)

    def turn(i, _):
        for u in range(GROUP):
            p = i * GROUP + u
            block = block_of(codes[pl.ds(order[p], 1), :], rows)
            totals[dst[p]] += jnp.dot(block, panel[col[p]], preferred_element_type=jnp.float32)
        return 0

    lax.fori_loop(0, meta[0], turn, 0)


def backward_kernel(n, span, marks, lists, owner, before, dense, *refs):
    pieces, (acc, grad, dbuf, piece_sems, sems) = refs[:n], refs[n:]
    copies = fetch(pieces, grad, piece_sems)

    def prepare():
        acc[...] = before[...]
        for copy in copies:
            copy.wait()

    def product(i, slot):
        def one(g):
            spots = [lists[1, i * TURN + g * GROUP + u] for u in range(GROUP)]
            left = jnp.concatenate([grad[c] for c in spots], axis=1)
            right = dbuf[slot, pl.ds(g * GROUP, GROUP)].reshape(GROUP * 128, 128)
            return jnp.dot(left, right, preferred_element_type=jnp.float32)

        add_pairs(i, owner, one, acc)

    read_dense(marks[0, span[0]], marks[0, span[1]], dense, dbuf, sems, product, prepare)


SMEM = pl.BlockSpec(memory_space=pltpu.SMEM)
VMEM = pl.BlockSpec(memory_space=pltpu.VMEM)
HBM = pl.BlockSpec(memory_space=pl.ANY)
PARAMS = pltpu.CompilerParams(vmem_limit_bytes=48 * 1024 * 1024)


def cost(slots, products):
    flops = 2 * slots * products * 128**3
    return pl.CostEstimate(flops=flops, bytes_accessed=slots * 128 * 128 * 2, transcendentals=0)


def run_tile(meta, order, dst, col, codes, panel, row_blocks):
    return pl.pallas_call(
        tile_kernel,
        out_shape=jax.ShapeDtypeStruct((row_blocks, 128, panel.shape[-1]), jnp.float32),
        in_specs=[SMEM] * 4 + [VMEM] * 2,
        out_specs=VMEM,
        compiler_params=PARAMS,
    )(meta, order, dst, col, codes, panel)


def run_pack(meta, pos, codes, labels):
    length = labels.shape[0] * (ROOM + SPARE)
    return pl.pallas_call(
        pack_kernel,
        out_shape=jax.ShapeDtypeStruct((length, 128), jnp.int32),
        in_specs=[SMEM] * 2 + [VMEM] * 2,
        out_specs=VMEM,
        compiler_params=PARAMS,
    )(meta, pos, codes, labels)


def run_build(span, listed, codes, after, dense):
    lists, _, marks = listed
    others = after if dense is None else after + [dense]
    return pl.pallas_call(
        functools.partial(build_kernel, span),
        out_shape=jax.ShapeDtypeStruct((lists.shape[1], 128, 128), jnp.bfloat16),
        in_specs=[SMEM] * 2 + [VMEM] + [HBM] * len(others),
        out_specs=HBM,
        scratch_shapes=[
            pltpu.VMEM((DEPTH, TURN, 128, 128), jnp.bfloat16),
            pltpu.SemaphoreType.DMA((DEPTH,)),
        ],
        input_output_aliases={} if dense is None else {2 + len(others): 0},
        compiler_params=PARAMS,
        cost_estimate=cost(lists.shape[1], 2),
    )(marks, lists, codes, *others)


def run_forward(scale, span, listed, weight, bias, cotangent, dense, feat):
    lists, owner, marks = listed
    n = len(feat)
    size, _, width = feat[0].shape
    row_blocks = cotangent.shape[0] // 128
    return pl.pallas_call(
        functools.partial(forward_kernel, n, scale, span),
        out_shape=(
            jax.ShapeDtypeStruct(cotangent.shape, jnp.bfloat16),
            jax.ShapeDtypeStruct((row_blocks, width, 128), jnp.bfloat16),
            jax.ShapeDtypeStruct((width + 8, width), jnp.float32),
        ),
        in_specs=[SMEM] * 3 + [VMEM] * 3 + [HBM] * (n + 1),
        out_specs=[VMEM] * 3,
        scratch_shapes=[
            pltpu.VMEM((row_blocks, 128, 2 * width), jnp.float32),
            pltpu.VMEM((n * size, 128, width), jnp.bfloat16),
            pltpu.VMEM((n * size, 128, width), jnp.bfloat16),
            pltpu.VMEM((DEPTH, TURN, 128, 128), jnp.bfloat16),
            pltpu.SemaphoreType.DMA((n,)),
            pltpu.SemaphoreType.DMA((DEPTH,)),
        ],
        compiler_params=PARAMS,
        cost_estimate=cost(lists.shape[1], 4),
    )(marks, lists, owner, weight, bias, cotangent, dense, *feat)


def run_backward(span, listed, before, dense, pieces):
    lists, owner, marks = listed
    n = len(pieces)
    size, width, _ = pieces[0].shape
    return pl.pallas_call(
        functools.partial(backward_kernel, n, span),
        out_shape=jax.ShapeDtypeStruct(before.shape, jnp.float32),
        in_specs=[SMEM] * 3 + [VMEM] + [HBM] * (n + 1),
        out_specs=VMEM,
        scratch_shapes=[
            pltpu.VMEM((n * size, width, 128), jnp.bfloat16),
            pltpu.VMEM((DEPTH, TURN, 128, 128), jnp.bfloat16),
            pltpu.SemaphoreType.DMA((n,)),
            pltpu.SemaphoreType.DMA((DEPTH,)),
        ],
        compiler_params=PARAMS,
        cost_estimate=cost(lists.shape[1], 4),
    )(marks, lists, owner, before, dense, *pieces)


def column(row):
    return jnp.broadcast_to(row, (8, row.shape[1])).T[:, :1]


def list_kernel(keys, split, fills, key_ref, *refs):
    value_refs, (lists, owner_ref, marks_ref) = refs[: len(fills)], refs[len(fills) :]
    n, length = key_ref.shape[1], lists.shape[1]
    key = key_ref[...].astype(jnp.float32)
    key_column = column(key)
    lanes = lax.broadcasted_iota(jnp.int32, (128, n), 1)
    lines = lax.broadcasted_iota(jnp.int32, (128, n), 0)
    rank = jnp.zeros((1, n), jnp.float32)
    for t in range(0, n, 128):
        before = (key_column[t : t + 128] == key) & (lines + t < lanes)
        rank += jnp.sum(jnp.where(before, 1.0, 0.0), axis=0, keepdims=True)

    rows = -(-keys // 8) * 8
    names = lax.broadcasted_iota(jnp.int32, (rows, n), 0).astype(jnp.float32)
    name = lax.broadcasted_iota(jnp.int32, (rows, 1), 0).astype(jnp.float32)
    counts = jnp.sum(jnp.where(names == key, 1.0, 0.0), axis=1, keepdims=True)
    filled = jnp.where(name < keys, jnp.floor((counts + (GROUP - 1)) * (1.0 / GROUP)) * GROUP, 0.0)
    below = jnp.sum(jnp.where(name < split, filled, 0.0), axis=0, keepdims=True)
    first = jnp.floor((below + (TURN - 1)) * (1.0 / TURN))
    filled = filled + jnp.where(name == split - 1, first * TURN - below, 0.0)
    turns = jnp.floor((jnp.sum(filled, axis=0, keepdims=True) + (TURN - 1)) * (1.0 / TURN))
    base = jnp.sum(jnp.where(names < key, filled, 0.0), axis=0, keepdims=True)
    pos_column = column(jnp.where(key < keys, base + rank, -1.0))

    spots = lax.broadcasted_iota(jnp.int32, (1, length), 1).astype(jnp.float32)
    columns = [column(ref[...].astype(jnp.float32)) for ref in value_refs]
    sums = [jnp.zeros((1, length), jnp.float32) for _ in fills]
    for t in range(0, n, 128):
        hit = pos_column[t : t + 128] == spots
        for k, fill in enumerate(fills):
            value = columns[k][t : t + 128] - fill
            sums[k] += jnp.sum(jnp.where(hit, value, 0.0), axis=0, keepdims=True)
    for k, fill in enumerate(fills):
        lists[pl.ds(k, 1), :] = (sums[k] + fill).astype(jnp.int32)

    other = lax.broadcasted_iota(jnp.int32, (rows, 128), 1).astype(jnp.float32)
    ends = column(jnp.sum(jnp.where(name <= other, filled, 0.0), axis=0, keepdims=True))[:rows]
    starts = lax.broadcasted_iota(jnp.int32, owner_ref.shape, 1).astype(jnp.float32) * GROUP
    passed = (ends <= starts) & (name < keys)
    owner = jnp.sum(jnp.where(passed, 1.0, 0.0), axis=0, keepdims=True)
    owner = jnp.minimum(owner, keys - 1.0)
    owner_ref[...] = jnp.where(owner >= split, owner - split, owner).astype(jnp.int32)

    spot = lax.broadcasted_iota(jnp.int32, (1, 128), 1)
    marks = jnp.where(spot == FIRST, first, 0.0)
    for k in range(1, 5):
        marks = jnp.where(spot == FIRST + k, jnp.floor(turns * (k / 4)), marks)
    marks_ref[...] = marks.astype(jnp.int32)


FIRST = 1
QUARTERS = [0, 2, 3, 4, 5]


def make_lists(key, values, fills, keys, split):
    n = key.size
    length = (-(-(n + keys * GROUP) // TURN) + 1) * TURN
    groups = -(-length // GROUP // 128) * 128
    lists, owner, marks = pl.pallas_call(
        functools.partial(list_kernel, keys, split, fills),
        out_shape=(
            jax.ShapeDtypeStruct((len(fills), length), jnp.int32),
            jax.ShapeDtypeStruct((1, groups), jnp.int32),
            jax.ShapeDtypeStruct((1, 128), jnp.int32),
        ),
        in_specs=[VMEM] * (1 + len(fills)),
        out_specs=[VMEM] * 3,
        compiler_params=PARAMS,
        cost_estimate=cost(32, 2),
    )(key.reshape(1, n), *[value.reshape(1, n) for value in values])
    return lists, owner, marks


def place(pos, value, length, fill):
    spots = jnp.arange(length, dtype=jnp.int32)
    hit = pos[:, None] == spots[None, :]
    return jnp.sum(jnp.where(hit, value[:, None] - fill, 0), axis=0) + fill


def shards(
    features,
    weight,
    bias,
    cotangent,
    block_count,
    block_rows,
    block_cols,
    edge_offsets,
    edge_weight,
):
    node_dev, width = features.shape
    n_row = lax.axis_size("row")
    n_col = lax.axis_size("col")
    slots = block_rows.shape[2]
    count = block_count[0, 0]
    mine = lax.axis_index("col")
    mine_row = lax.axis_index("row")
    per = node_dev // 128
    row_blocks = per * n_col
    col_blocks = per * n_row
    scale = (node_dev * n_row * n_col) ** (-0.5)
    by_owner = n_row * n_col * node_dev * width * 2 <= 8 * 1024 * 1024

    brow = block_rows[0, 0]
    bcol = block_cols[0, 0]
    ids = jnp.arange(slots, dtype=jnp.int32)
    live = ids < count
    codes = edge_offsets[0, 0] * FIELD + (
        edge_weight[0, 0].astype(jnp.float32) * (1.0 / UNIT)
    ).astype(jnp.int32)
    codes = jnp.pad(codes, ((0, 8), (0, 0)))
    home = brow // per
    turns_plain = ((count + GROUP - 1) // GROUP).reshape(1)

    def tile_plan():
        wide = lax.all_gather(features, "row", axis=0, tiled=True)
        low = jnp.dot(wide, weight, preferred_element_type=jnp.float32).astype(jnp.bfloat16)
        panel = jnp.concatenate([low, wide], axis=1).reshape(col_blocks, 128, 2 * width)
        order = jnp.where(live, ids, slots)
        dst = jnp.where(live, (home ^ mine) * per + brow % per, 0)
        totals = run_tile(turns_plain, order, dst, bcol, codes, panel, row_blocks)
        own = scatter_sum(totals.reshape(n_col, node_dev, 2 * width), "col")
        pre = own[:, :width] + bias
        output = jnp.maximum(pre, 0.0).astype(jnp.bfloat16)
        grad = jnp.where(pre > 0, cotangent.astype(jnp.float32), 0.0)
        turned = jnp.swapaxes(grad.astype(jnp.bfloat16).reshape(per, 128, width), 1, 2)
        weight_sum = lax.dot_general(
            own[:, width:].astype(jnp.bfloat16),
            grad.astype(jnp.bfloat16),
            (((0,), (0,)), ((), ())),
            preferred_element_type=jnp.float32,
        )
        bias_sum = jnp.broadcast_to(jnp.sum(grad, axis=0), (8, width))
        return output, turned, jnp.concatenate([weight_sum, bias_sum], axis=0) * scale

    source = piece_index(per, home ^ mine, brow % per)
    unit = row_blocks // (2 * len(part_orders(per)))
    late = source // unit % 2
    source = source // (2 * unit) * unit + source % unit
    back = make_lists(
        jnp.where(live, late * col_blocks + bcol, 2 * col_blocks),
        [ids, source],
        [slots, 0],
        2 * col_blocks,
        col_blocks,
    )
    state = {"dense": None}

    def build(held, start, end):
        span = (QUARTERS[start], QUARTERS[end])
        state["dense"] = run_build(span, back, codes, held, state["dense"])

    if by_owner:
        same = live[:, None] & (home[:, None] == home[None, :]) & (ids[:, None] < ids[None, :])
        rank = jnp.sum(same.astype(jnp.int32), axis=0)
        over = jnp.any(live & (rank >= ROOM)).astype(jnp.int32)
        fits = live & (rank < ROOM)
        label = 1 + (brow % per) * col_blocks + bcol
        labels = place(jnp.where(fits, home * ROOM + rank, -1), label, n_col * ROOM, 0)
        labels = jnp.concatenate(
            [labels.reshape(n_col, ROOM), jnp.full((n_col, 128 - ROOM), over)], axis=1
        )
        stride = ROOM + SPARE
        pos = jnp.where(fits, home * stride + rank, ROOM + SPARE - 1)
        packed = run_pack(turns_plain, pos, codes, labels)
        came = lax.all_to_all(
            packed.reshape(n_col, stride, 128), "col", split_axis=0, concat_axis=0, tiled=True
        )
        spread = jnp.max(came[:, ROOM, ROOM:], axis=0)[None]
        for bit in bits_of("row"):
            spread = spread + swap(spread, "row", bit)
        any_over = jnp.max(spread, axis=1)

        got = came[:, ROOM, :ROOM]
        sources = jnp.arange(n_col, dtype=jnp.int32)[:, None]
        places = jnp.arange(ROOM, dtype=jnp.int32)[None, :]
        row_here = ((got - 1) // col_blocks).reshape(-1)
        col_there = (got - 1) % col_blocks
        col_there = piece_index(
            per, sources ^ mine, col_there % per, (col_there // per) ^ mine_row, n_row
        )
        line = sources * stride + places
        listed = make_lists(
            jnp.where(got > 0, row_here.reshape(got.shape), per),
            [jnp.broadcast_to(line, got.shape), col_there],
            [ROOM + 1, 0],
            per,
            per,
        )

        def prepare(step, held):
            if step == 0:
                build(held, 0, 1)
            if step == 1:
                held, state["dense"] = lax.optimization_barrier((held, state["dense"]))
            return held

        pairs = gather_pieces(features.reshape(per, 128, width), prepare)
        lines = came.reshape(n_col * stride, 128)
        here = run_build((0, QUARTERS[4]), listed, lines, [], None)
        last, here, any_over = lax.optimization_barrier(
            ([pair[1] for pair in pairs], here, any_over)
        )
        feat = []
        for pair in [[pair[0], x] for pair, x in zip(pairs, last)]:
            rows = [pair]
            for bit in bits_of("row"):
                rows = rows + [[swap(x, "row", bit) for x in pair] for pair in rows]
            feat += [x for pair in rows for x in pair]
        done = run_forward(
            scale, (0, QUARTERS[4]), listed, weight, bias[None], cotangent, here, feat
        )
        done = lax.cond(any_over[0] > 0, tile_plan, lambda: tuple(done))
    else:
        done = tile_plan()

    output, turned, total = done
    turned = with_layout_constraint(turned, Layout(major_to_minor=(0, 1, 2)))
    steps = bits_of("col")[::-1]

    def add_total():
        state["total"] = state["total"] + swap(state["total"], "col", steps.pop(0))

    def beside(step, held):
        held, state["total"], state["dense"] = lax.optimization_barrier(
            (held, state["total"], state["dense"])
        )
        if steps:
            add_total()
        if step == 0:
            build(held, 3, 4)
        if step == 1:
            add_products(0, held)
        return held

    def add_products(half, pieces):
        pieces = [x.reshape((-1,) + x.shape[2:]) if x.ndim == 4 else x for x in pieces]
        state["acc"] = run_backward(
            [(0, FIRST), (FIRST, QUARTERS[4])][half], back, state["acc"], state["dense"], pieces
        )

    state["acc"] = jnp.zeros((col_blocks, width, 128), jnp.float32)
    state["total"] = split_rows(total)
    while len(steps) > 3:
        add_total()
    build([turned], 1, 3)
    grad = gather_pieces(turned, beside)
    late_pieces, state["total"] = lax.optimization_barrier(
        ([pair[1] for pair in grad], state["total"])
    )
    while steps:
        add_total()
    add_products(1, late_pieces)
    acc, total = lax.optimization_barrier((state["acc"], state["total"]))
    total = join_rows(total)
    back = jnp.swapaxes(acc, 1, 2).reshape(col_blocks * 128, width)
    grad_proj = scatter_sum(
        jnp.stack(
            [
                lax.dynamic_slice_in_dim(back, (mine_row ^ k) * node_dev, node_dev, 0)
                for k in range(n_row)
            ]
        ),
        "row",
    ).astype(jnp.bfloat16)
    grad_features = lax.dot_general(
        grad_proj, weight, (((1,), (1,)), ((), ())), preferred_element_type=jnp.float32
    ).astype(jnp.bfloat16)
    return (
        output,
        grad_features,
        total[: weight.shape[0]],
        total[weight.shape[0]],
    )


def solution(mesh):
    return jax.shard_map(
        shards,
        mesh=mesh,
        in_specs=(
            P(("row", "col"), None),
            P(),
            P(),
            P(("row", "col"), None),
            P("row", "col"),
            P("row", "col", None),
            P("row", "col", None),
            P("row", "col", None, None),
            P("row", "col", None, None),
        ),
        out_specs=(P(("row", "col"), None), P(("row", "col"), None), P(), P()),
        check_vma=False,
    )
```

```python
import functools
import functools
import jax
import jax.numpy as jnp
from jax import lax
from jax.experimental import pallas as pl
from jax.experimental.pallas import tpu as pltpu
from jax.experimental.layout import Layout, with_layout_constraint
from jax.sharding import PartitionSpec as P


def swap(x, axis, bit):
    n = lax.axis_size(axis)
    return lax.ppermute(x, axis, [(i, i ^ bit) for i in range(n)])


def bits_of(axis):
    n = lax.axis_size(axis)
    return [1 << k for k in range(n.bit_length() - 1)]


def scatter_sum(x, axis):
    for bit in bits_of(axis):
        pairs = x.reshape((x.shape[0] // 2, 2) + x.shape[1:])
        x = pairs[:, 0] + swap(pairs[:, 1], axis, bit)
    return x[0]


def part_orders(per):
    bits = bits_of("col")[::-1]
    turned = bits[:-2] + bits[-1:] + bits[-2:-1]
    return [bits, turned] if per % 2 == 0 and len(bits) > 1 else [bits]


def gather_pieces(blocks, beside):
    orders = part_orders(blocks.shape[0])
    size = blocks.shape[0] // len(orders)
    near = [0]
    for bit in orders[0][:-2]:
        near = near + [far | bit for far in near]
    whole = [blocks if far == 0 else swap(blocks, "col", far) for far in near]
    (whole,) = beside(0, [jnp.stack(whole)])
    held = [whole[:, i * size : (i + 1) * size] for i in range(len(orders))]
    if len(orders[0]) > 1:
        came = [swap(x, "col", order[-2]) for x, order in zip(held, orders)]
        held = beside(1, [jnp.concatenate([x, y], axis=0) for x, y in zip(held, came)])
    came = [swap(x, "col", order[-1]) for x, order in zip(held, orders)]
    shape = (-1,) + blocks.shape[1:]
    return [[x.reshape(shape), y.reshape(shape)] for x, y in zip(held, came)]


def piece_index(per, far, block, rho=0, n_row=1):
    orders = part_orders(per)
    size = per // len(orders)
    half = lax.axis_size("col") // 2
    result = 0
    for i, order in enumerate(orders):
        spot = sum(((far & bit) > 0).astype(jnp.int32) << t for t, bit in enumerate(order))
        piece = (i * n_row + rho) * 2 + spot // half
        here = (piece * half + spot % half) * size + block % size
        result = jnp.where(block // size == i, here, result)
    return result


def split_rows(x):
    n, mine = lax.axis_size("row"), lax.axis_index("row")
    size = -(-x.shape[0] // (8 * n)) * 8
    x = jnp.pad(x, ((0, n * size - x.shape[0]), (0, 0)))
    parts = [lax.dynamic_slice_in_dim(x, (mine ^ k) * size, size, 0) for k in range(n)]
    return scatter_sum(jnp.stack(parts), "row")


def join_rows(x):
    n, mine = lax.axis_size("row"), lax.axis_index("row")
    parts = [x]
    for bit in bits_of("row"):
        parts = parts + [swap(part, "row", bit) for part in parts]
    parts = jnp.stack(parts)
    return jnp.concatenate(
        [lax.dynamic_index_in_dim(parts, mine ^ k, 0, keepdims=False) for k in range(n)]
    )


GROUP = 8
TURN = 4 * GROUP
DEPTH = 5
ROOM = 64
SPARE = 8
FIELD = 1 << 16
UNIT = 2.0**-14


def tile_rows():
    shape = (8, 16, 128)
    rows = 16 * lax.broadcasted_iota(jnp.int32, shape, 0) + lax.broadcasted_iota(jnp.int32, shape, 1)
    return rows.astype(jnp.float32).astype(jnp.bfloat16)


def blocks_of(lines, rows):
    codes = jnp.concatenate(lines, axis=0)
    inner = ((codes >> 16) & 127).astype(jnp.float32).T
    outer = (codes >> 23).astype(jnp.float32)
    weight = (codes & (FIELD - 1)).astype(jnp.float32) * UNIT
    lanes = lax.broadcasted_iota(jnp.int32, (128, 128), 1).astype(jnp.float32)
    zero = jnp.zeros((), jnp.bfloat16)

    def tile(x):
        return jnp.broadcast_to(x, (16, 128)).astype(jnp.bfloat16)[None]

    blocks = []
    for u in range(GROUP):
        left = jnp.where(rows == tile(outer[u : u + 1]), tile(weight[u : u + 1]), zero)
        right = jnp.where(inner[:, u : u + 1] == lanes, 1.0, 0.0).astype(jnp.bfloat16)
        block = jnp.dot(left.reshape(128, 128), right, preferred_element_type=jnp.float32)
        blocks.append(block.astype(jnp.bfloat16))
    return blocks


def pack_kernel(meta, pos, codes, labels, out):
    out[...] = jnp.zeros_like(out)
    stride = ROOM + SPARE
    for k in range(labels.shape[0]):
        out[pl.ds(k * stride + ROOM, 1), :] = labels[pl.ds(k, 1), :]

    def turn(i, _):
        for u in range(GROUP):
            s = i * GROUP + u
            out[pl.ds(pos[s], 1), :] = codes[pl.ds(s, 1), :]
        return 0

    lax.fori_loop(0, meta[0], turn, 0)


def build_kernel(span, marks, lists, codes, *refs):
    dense, dbuf, sems = refs[-3:]
    start, turns = marks[0, span[0]], marks[0, span[1]]
    rows = tile_rows()

    def out_copy(i):
        slot = lax.rem(i, DEPTH)
        return pltpu.make_async_copy(
            dbuf.at[slot], dense.at[pl.ds(i * TURN, TURN)], sems.at[slot]
        )

    def turn(i, _):
        slot = lax.rem(i, DEPTH)

        @pl.when(i >= start + DEPTH)
        def _():
            out_copy(i - DEPTH).wait()

        lines = [codes[pl.ds(lists[0, i * TURN + u], 1), :] for u in range(TURN)]
        for u in range(0, TURN, GROUP):
            blocks = blocks_of(lines[u : u + GROUP], rows)
            for k, block in enumerate(blocks):
                dbuf[slot, u + k] = block
        out_copy(i).start()
        return 0

    lax.fori_loop(start, turns, turn, 0)

    def finish(i, _):
        out_copy(i).wait()
        return 0

    lax.fori_loop(jnp.maximum(turns - DEPTH, start), turns, finish, 0)


def fetch(pieces, into, sems):
    size = pieces[0].shape[0]
    copies = [
        pltpu.make_async_copy(piece, into.at[pl.ds(i * size, size)], sems.at[i])
        for i, piece in enumerate(pieces)
    ]
    for copy in copies:
        copy.start()
    return copies


def read_dense(start, turns, dense, dbuf, sems, product, prepare):
    def in_copy(i):
        slot = lax.rem(i, DEPTH)
        return pltpu.make_async_copy(
            dense.at[pl.ds(i * TURN, TURN)], dbuf.at[slot], sems.at[slot]
        )

    def begin(i, _):
        in_copy(i).start()
        return 0

    lax.fori_loop(start, jnp.minimum(turns, start + DEPTH - 1), begin, 0)
    prepare()

    def turn(i, _):
        @pl.when(i + DEPTH - 1 < turns)
        def _():
            in_copy(i + DEPTH - 1).start()

        in_copy(i).wait()
        product(i, lax.rem(i, DEPTH))
        return 0

    lax.fori_loop(start, turns, turn, 0)


def add_pairs(i, owner, one, into):
    groups = TURN // GROUP
    for g in range(0, groups, 2):
        added = [one(g), one(g + 1)]
        for k in range(2):
            into[owner[0, i * groups + g + k]] += added[k]


def forward_kernel(n, scale, span, marks, lists, owner, weight, bias, cotangent, dense, *refs):
    pieces, refs = refs[:n], refs[n:]
    output, turned, local, totals, feat, proj, dbuf, piece_sems, sems = refs
    copies = fetch(pieces, feat, piece_sems)
    size, _, width = pieces[0].shape
    batch = 8 if size % 8 == 0 else 2
    zero = jnp.zeros_like(weight[...])
    twice = jnp.concatenate(
        [jnp.concatenate([weight[...], zero], 1), jnp.concatenate([zero, weight[...]], 1)], 0
    )

    def project(t, _):
        halves = [pl.ds(t * batch + k * batch // 2, batch // 2) for k in range(2)]
        held = [feat[half].reshape(batch * 64, width) for half in halves]
        low = jnp.dot(
            jnp.concatenate(held, axis=1), twice, preferred_element_type=jnp.float32
        ).astype(jnp.bfloat16)
        for k, half in enumerate(halves):
            proj[half] = low[:, k * width : (k + 1) * width].reshape(batch // 2, 128, width)
        return 0

    def prepare():
        totals[...] = jnp.zeros_like(totals)
        for i, copy in enumerate(copies):
            copy.wait()
            lax.fori_loop(i * size // batch, (i + 1) * size // batch, project, 0)

    def product(i, slot):
        def one(g):
            spots = [lists[1, i * TURN + g * GROUP + u] for u in range(GROUP)]
            left = jnp.concatenate([dbuf[slot, g * GROUP + u] for u in range(GROUP)], axis=1)
            right = jnp.concatenate(
                [jnp.concatenate([proj[c], feat[c]], axis=1) for c in spots], axis=0
            )
            return jnp.dot(left, right, preferred_element_type=jnp.float32)

        add_pairs(i, owner, one, totals)

    read_dense(marks[0, span[0]], marks[0, span[1]], dense, dbuf, sems, product, prepare)

    weight_sum, bias_sum = 0.0, 0.0
    for q in range(totals.shape[0]):
        lines = pl.ds(q * 128, 128)
        pre = totals[q, :, :width] + bias[...]
        output[lines, :] = jnp.maximum(pre, 0.0).astype(jnp.bfloat16)
        grad = jnp.where(pre > 0, cotangent[lines, :].astype(jnp.float32), 0.0)
        turned[q] = grad.T.astype(jnp.bfloat16)
        weight_sum += lax.dot_general(
            totals[q, :, width:].astype(jnp.bfloat16),
            grad.astype(jnp.bfloat16),
            (((0,), (0,)), ((), ())),
            preferred_element_type=jnp.float32,
        )
        bias_sum += jnp.sum(grad, axis=0, keepdims=True)
    local[pl.ds(0, width), :] = weight_sum * scale
    local[pl.ds(width, 8), :] = jnp.broadcast_to(bias_sum * scale, (8, width))


def tile_kernel(meta, order, dst, col, codes, panel, totals):
    rows = tile_rows()
    totals[...] = jnp.zeros_like(totals)

    def turn(i, _):
        lines = [codes[pl.ds(order[i * GROUP + u], 1), :] for u in range(GROUP)]
        for u, block in enumerate(blocks_of(lines, rows)):
            p = i * GROUP + u
            totals[dst[p]] += jnp.dot(block, panel[col[p]], preferred_element_type=jnp.float32)
        return 0

    lax.fori_loop(0, meta[0], turn, 0)


def backward_kernel(n, span, marks, lists, owner, before, dense, *refs):
    pieces, (acc, grad, dbuf, piece_sems, sems) = refs[:n], refs[n:]
    copies = fetch(pieces, grad, piece_sems)

    def prepare():
        acc[...] = before[...]
        for copy in copies:
            copy.wait()

    def product(i, slot):
        def one(g):
            spots = [lists[1, i * TURN + g * GROUP + u] for u in range(GROUP)]
            left = jnp.concatenate([grad[c] for c in spots], axis=1)
            right = dbuf[slot, pl.ds(g * GROUP, GROUP)].reshape(GROUP * 128, 128)
            return jnp.dot(left, right, preferred_element_type=jnp.float32)

        add_pairs(i, owner, one, acc)

    read_dense(marks[0, span[0]], marks[0, span[1]], dense, dbuf, sems, product, prepare)


SMEM = pl.BlockSpec(memory_space=pltpu.SMEM)
VMEM = pl.BlockSpec(memory_space=pltpu.VMEM)
HBM = pl.BlockSpec(memory_space=pl.ANY)
PARAMS = pltpu.CompilerParams(vmem_limit_bytes=48 * 1024 * 1024)


def cost(slots, products):
    flops = 2 * slots * products * 128**3
    return pl.CostEstimate(flops=flops, bytes_accessed=slots * 128 * 128 * 2, transcendentals=0)


def run_tile(meta, order, dst, col, codes, panel, row_blocks):
    return pl.pallas_call(
        tile_kernel,
        out_shape=jax.ShapeDtypeStruct((row_blocks, 128, panel.shape[-1]), jnp.float32),
        in_specs=[SMEM] * 4 + [VMEM] * 2,
        out_specs=VMEM,
        compiler_params=PARAMS,
    )(meta, order, dst, col, codes, panel)


def run_pack(meta, pos, codes, labels):
    length = labels.shape[0] * (ROOM + SPARE)
    return pl.pallas_call(
        pack_kernel,
        out_shape=jax.ShapeDtypeStruct((length, 128), jnp.int32),
        in_specs=[SMEM] * 2 + [VMEM] * 2,
        out_specs=VMEM,
        compiler_params=PARAMS,
    )(meta, pos, codes, labels)


def run_build(span, listed, codes, after, dense):
    lists, _, marks = listed
    others = after if dense is None else after + [dense]
    return pl.pallas_call(
        functools.partial(build_kernel, span),
        out_shape=jax.ShapeDtypeStruct((lists.shape[1], 128, 128), jnp.bfloat16),
        in_specs=[SMEM] * 2 + [VMEM] + [HBM] * len(others),
        out_specs=HBM,
        scratch_shapes=[
            pltpu.VMEM((DEPTH, TURN, 128, 128), jnp.bfloat16),
            pltpu.SemaphoreType.DMA((DEPTH,)),
        ],
        input_output_aliases={} if dense is None else {2 + len(others): 0},
        compiler_params=PARAMS,
        cost_estimate=cost(lists.shape[1], 2),
    )(marks, lists, codes, *others)


def run_forward(scale, span, listed, weight, bias, cotangent, dense, feat):
    lists, owner, marks = listed
    n = len(feat)
    size, _, width = feat[0].shape
    row_blocks = cotangent.shape[0] // 128
    return pl.pallas_call(
        functools.partial(forward_kernel, n, scale, span),
        out_shape=(
            jax.ShapeDtypeStruct(cotangent.shape, jnp.bfloat16),
            jax.ShapeDtypeStruct((row_blocks, width, 128), jnp.bfloat16),
            jax.ShapeDtypeStruct((width + 8, width), jnp.float32),
        ),
        in_specs=[SMEM] * 3 + [VMEM] * 3 + [HBM] * (n + 1),
        out_specs=[VMEM] * 3,
        scratch_shapes=[
            pltpu.VMEM((row_blocks, 128, 2 * width), jnp.float32),
            pltpu.VMEM((n * size, 128, width), jnp.bfloat16),
            pltpu.VMEM((n * size, 128, width), jnp.bfloat16),
            pltpu.VMEM((DEPTH, TURN, 128, 128), jnp.bfloat16),
            pltpu.SemaphoreType.DMA((n,)),
            pltpu.SemaphoreType.DMA((DEPTH,)),
        ],
        compiler_params=PARAMS,
        cost_estimate=cost(lists.shape[1], 4),
    )(marks, lists, owner, weight, bias, cotangent, dense, *feat)


def run_backward(span, listed, before, dense, pieces):
    lists, owner, marks = listed
    n = len(pieces)
    size, width, _ = pieces[0].shape
    return pl.pallas_call(
        functools.partial(backward_kernel, n, span),
        out_shape=jax.ShapeDtypeStruct(before.shape, jnp.float32),
        in_specs=[SMEM] * 3 + [VMEM] + [HBM] * (n + 1),
        out_specs=VMEM,
        scratch_shapes=[
            pltpu.VMEM((n * size, width, 128), jnp.bfloat16),
            pltpu.VMEM((DEPTH, TURN, 128, 128), jnp.bfloat16),
            pltpu.SemaphoreType.DMA((n,)),
            pltpu.SemaphoreType.DMA((DEPTH,)),
        ],
        compiler_params=PARAMS,
        cost_estimate=cost(lists.shape[1], 4),
    )(marks, lists, owner, before, dense, *pieces)


def column(row):
    return jnp.broadcast_to(row, (8, row.shape[1])).T[:, :1]


def list_kernel(keys, split, fills, key_ref, *refs):
    value_refs, (lists, owner_ref, marks_ref) = refs[: len(fills)], refs[len(fills) :]
    n, length = key_ref.shape[1], lists.shape[1]
    key = key_ref[...].astype(jnp.float32)
    key_column = column(key)
    lanes = lax.broadcasted_iota(jnp.int32, (128, n), 1)
    lines = lax.broadcasted_iota(jnp.int32, (128, n), 0)
    rank = jnp.zeros((1, n), jnp.float32)
    for t in range(0, n, 128):
        before = (key_column[t : t + 128] == key) & (lines + t < lanes)
        rank += jnp.sum(jnp.where(before, 1.0, 0.0), axis=0, keepdims=True)

    rows = -(-keys // 8) * 8
    names = lax.broadcasted_iota(jnp.int32, (rows, n), 0).astype(jnp.float32)
    name = lax.broadcasted_iota(jnp.int32, (rows, 1), 0).astype(jnp.float32)
    counts = jnp.sum(jnp.where(names == key, 1.0, 0.0), axis=1, keepdims=True)
    filled = jnp.where(name < keys, jnp.floor((counts + (GROUP - 1)) * (1.0 / GROUP)) * GROUP, 0.0)
    below = jnp.sum(jnp.where(name < split, filled, 0.0), axis=0, keepdims=True)
    first = jnp.floor((below + (TURN - 1)) * (1.0 / TURN))
    filled = filled + jnp.where(name == split - 1, first * TURN - below, 0.0)
    turns = jnp.floor((jnp.sum(filled, axis=0, keepdims=True) + (TURN - 1)) * (1.0 / TURN))
    base = jnp.sum(jnp.where(names < key, filled, 0.0), axis=0, keepdims=True)
    pos_column = column(jnp.where(key < keys, base + rank, -1.0))

    spots = lax.broadcasted_iota(jnp.int32, (1, length), 1).astype(jnp.float32)
    columns = [column(ref[...].astype(jnp.float32)) for ref in value_refs]
    sums = [jnp.zeros((1, length), jnp.float32) for _ in fills]
    for t in range(0, n, 128):
        hit = pos_column[t : t + 128] == spots
        for k, fill in enumerate(fills):
            value = columns[k][t : t + 128] - fill
            sums[k] += jnp.sum(jnp.where(hit, value, 0.0), axis=0, keepdims=True)
    for k, fill in enumerate(fills):
        lists[pl.ds(k, 1), :] = (sums[k] + fill).astype(jnp.int32)

    other = lax.broadcasted_iota(jnp.int32, (rows, 128), 1).astype(jnp.float32)
    ends = column(jnp.sum(jnp.where(name <= other, filled, 0.0), axis=0, keepdims=True))[:rows]
    starts = lax.broadcasted_iota(jnp.int32, owner_ref.shape, 1).astype(jnp.float32) * GROUP
    passed = (ends <= starts) & (name < keys)
    owner = jnp.sum(jnp.where(passed, 1.0, 0.0), axis=0, keepdims=True)
    owner = jnp.minimum(owner, keys - 1.0)
    owner_ref[...] = jnp.where(owner >= split, owner - split, owner).astype(jnp.int32)

    spot = lax.broadcasted_iota(jnp.int32, (1, 128), 1)
    marks = jnp.where(spot == FIRST, first, 0.0)
    marks = jnp.where(spot == MIDDLE, jnp.floor((first + turns) * 0.5), marks)
    marks = jnp.where(spot == ALL, turns, marks)
    marks_ref[...] = marks.astype(jnp.int32)


NONE, FIRST, MIDDLE, ALL = range(4)


def make_lists(key, values, fills, keys, split):
    n = key.size
    length = (-(-(n + keys * GROUP) // TURN) + 1) * TURN
    groups = -(-length // GROUP // 128) * 128
    lists, owner, marks = pl.pallas_call(
        functools.partial(list_kernel, keys, split, fills),
        out_shape=(
            jax.ShapeDtypeStruct((len(fills), length), jnp.int32),
            jax.ShapeDtypeStruct((1, groups), jnp.int32),
            jax.ShapeDtypeStruct((1, 128), jnp.int32),
        ),
        in_specs=[VMEM] * (1 + len(fills)),
        out_specs=[VMEM] * 3,
        compiler_params=PARAMS,
        cost_estimate=cost(32, 2),
    )(key.reshape(1, n), *[value.reshape(1, n) for value in values])
    return lists, owner, marks


def place(pos, value, length, fill):
    spots = jnp.arange(length, dtype=jnp.int32)
    hit = pos[:, None] == spots[None, :]
    return jnp.sum(jnp.where(hit, value[:, None] - fill, 0), axis=0) + fill


def shards(
    features,
    weight,
    bias,
    cotangent,
    block_count,
    block_rows,
    block_cols,
    edge_offsets,
    edge_weight,
):
    node_dev, width = features.shape
    n_row = lax.axis_size("row")
    n_col = lax.axis_size("col")
    slots = block_rows.shape[2]
    count = block_count[0, 0]
    mine = lax.axis_index("col")
    mine_row = lax.axis_index("row")
    per = node_dev // 128
    row_blocks = per * n_col
    col_blocks = per * n_row
    scale = (node_dev * n_row * n_col) ** (-0.5)
    by_owner = n_row * n_col * node_dev * width * 2 <= 8 * 1024 * 1024

    brow = block_rows[0, 0]
    bcol = block_cols[0, 0]
    ids = jnp.arange(slots, dtype=jnp.int32)
    live = ids < count
    codes = edge_offsets[0, 0] * FIELD + (
        edge_weight[0, 0].astype(jnp.float32) * (1.0 / UNIT)
    ).astype(jnp.int32)
    codes = jnp.pad(codes, ((0, 8), (0, 0)))
    home = brow // per
    turns_plain = ((count + GROUP - 1) // GROUP).reshape(1)

    def tile_plan():
        wide = lax.all_gather(features, "row", axis=0, tiled=True)
        low = jnp.dot(wide, weight, preferred_element_type=jnp.float32).astype(jnp.bfloat16)
        panel = jnp.concatenate([low, wide], axis=1).reshape(col_blocks, 128, 2 * width)
        order = jnp.where(live, ids, slots)
        dst = jnp.where(live, (home ^ mine) * per + brow % per, 0)
        totals = run_tile(turns_plain, order, dst, bcol, codes, panel, row_blocks)
        own = scatter_sum(totals.reshape(n_col, node_dev, 2 * width), "col")
        pre = own[:, :width] + bias
        output = jnp.maximum(pre, 0.0).astype(jnp.bfloat16)
        grad = jnp.where(pre > 0, cotangent.astype(jnp.float32), 0.0)
        turned = jnp.swapaxes(grad.astype(jnp.bfloat16).reshape(per, 128, width), 1, 2)
        weight_sum = lax.dot_general(
            own[:, width:].astype(jnp.bfloat16),
            grad.astype(jnp.bfloat16),
            (((0,), (0,)), ((), ())),
            preferred_element_type=jnp.float32,
        )
        bias_sum = jnp.broadcast_to(jnp.sum(grad, axis=0), (8, width))
        return output, turned, jnp.concatenate([weight_sum, bias_sum], axis=0) * scale

    source = piece_index(per, home ^ mine, brow % per)
    unit = row_blocks // (2 * len(part_orders(per)))
    late = source // unit % 2
    source = source // (2 * unit) * unit + source % unit
    back = make_lists(
        jnp.where(live, late * col_blocks + bcol, 2 * col_blocks),
        [ids, source],
        [slots, 0],
        2 * col_blocks,
        col_blocks,
    )
    state = {"dense": None}

    def build(held, start, end):
        state["dense"] = run_build((start, end), back, codes, held, state["dense"])

    if by_owner:
        same = live[:, None] & (home[:, None] == home[None, :]) & (ids[:, None] < ids[None, :])
        rank = jnp.sum(same.astype(jnp.int32), axis=0)
        over = jnp.any(live & (rank >= ROOM)).astype(jnp.int32)
        fits = live & (rank < ROOM)
        label = 1 + (brow % per) * col_blocks + bcol
        labels = place(jnp.where(fits, home * ROOM + rank, -1), label, n_col * ROOM, 0)
        labels = jnp.concatenate(
            [labels.reshape(n_col, ROOM), jnp.full((n_col, 128 - ROOM), over)], axis=1
        )
        stride = ROOM + SPARE
        pos = jnp.where(fits, home * stride + rank, ROOM + SPARE - 1)
        packed = run_pack(turns_plain, pos, codes, labels)
        came = lax.all_to_all(
            packed.reshape(n_col, stride, 128), "col", split_axis=0, concat_axis=0, tiled=True
        )
        spread = jnp.max(came[:, ROOM, ROOM:], axis=0)[None]
        for bit in bits_of("row"):
            spread = spread + swap(spread, "row", bit)
        any_over = jnp.max(spread, axis=1)

        got = came[:, ROOM, :ROOM]
        sources = jnp.arange(n_col, dtype=jnp.int32)[:, None]
        places = jnp.arange(ROOM, dtype=jnp.int32)[None, :]
        row_here = ((got - 1) // col_blocks).reshape(-1)
        col_there = (got - 1) % col_blocks
        col_there = piece_index(
            per, sources ^ mine, col_there % per, (col_there // per) ^ mine_row, n_row
        )
        line = sources * stride + places
        listed = make_lists(
            jnp.where(got > 0, row_here.reshape(got.shape), per),
            [jnp.broadcast_to(line, got.shape), col_there],
            [ROOM + 1, 0],
            per,
            per,
        )

        pairs = gather_pieces(features.reshape(per, 128, width), lambda step, held: held)
        lines = came.reshape(n_col * stride, 128)
        here = run_build((NONE, ALL), listed, lines, [], None)
        last, here, back = lax.optimization_barrier(([pair[1] for pair in pairs], here, back))
        feat = []
        for pair in [[pair[0], x] for pair, x in zip(pairs, last)]:
            rows = [pair]
            for bit in bits_of("row"):
                rows = rows + [[swap(x, "row", bit) for x in pair] for pair in rows]
            feat += [x for pair in rows for x in pair]
        done = run_forward(
            scale, (NONE, ALL), listed, weight, bias[None], cotangent, here, feat
        )
        done = lax.cond(any_over[0] > 0, tile_plan, lambda: tuple(done))
    else:
        done = tile_plan()

    output, turned, total = done
    turned = with_layout_constraint(turned, Layout(major_to_minor=(0, 1, 2)))
    steps = bits_of("col")[::-1]

    def add_total():
        state["total"] = state["total"] + swap(state["total"], "col", steps.pop(0))

    def beside(step, held):
        held, state["total"], state["dense"] = lax.optimization_barrier(
            (held, state["total"], state["dense"])
        )
        if steps:
            add_total()
        if step == 0:
            build(held, FIRST, MIDDLE)
        if step == 1:
            add_products(0, held)
            build(held, MIDDLE, ALL)
        return held

    def add_products(half, pieces):
        pieces = [x.reshape((-1,) + x.shape[2:]) if x.ndim == 4 else x for x in pieces]
        state["acc"] = run_backward(
            [(NONE, FIRST), (FIRST, ALL)][half], back, state["acc"], state["dense"], pieces
        )

    state["acc"] = jnp.zeros((col_blocks, width, 128), jnp.float32)
    state["total"] = split_rows(total)
    while len(steps) > 3:
        add_total()
    build([turned], NONE, FIRST)
    grad = gather_pieces(turned, beside)
    late_pieces, state["total"] = lax.optimization_barrier(
        ([pair[1] for pair in grad], state["total"])
    )
    while steps:
        add_total()
    add_products(1, late_pieces)
    acc, total = lax.optimization_barrier((state["acc"], state["total"]))
    total = join_rows(total)
    back = jnp.swapaxes(acc, 1, 2).reshape(col_blocks * 128, width)
    grad_proj = scatter_sum(
        jnp.stack(
            [
                lax.dynamic_slice_in_dim(back, (mine_row ^ k) * node_dev, node_dev, 0)
                for k in range(n_row)
            ]
        ),
        "row",
    ).astype(jnp.bfloat16)
    grad_features = lax.dot_general(
        grad_proj, weight, (((1,), (1,)), ((), ())), preferred_element_type=jnp.float32
    ).astype(jnp.bfloat16)
    return (
        output,
        grad_features,
        total[: weight.shape[0]],
        total[weight.shape[0]],
    )


def solution(mesh):
    return jax.shard_map(
        shards,
        mesh=mesh,
        in_specs=(
            P(("row", "col"), None),
            P(),
            P(),
            P(("row", "col"), None),
            P("row", "col"),
            P("row", "col", None),
            P("row", "col", None),
            P("row", "col", None, None),
            P("row", "col", None, None),
        ),
        out_specs=(P(("row", "col"), None), P(("row", "col"), None), P(), P()),
        check_vma=False,
    )
```

```python
import functools
import functools
import jax
import jax.numpy as jnp
from jax import lax
from jax.experimental import pallas as pl
from jax.experimental.pallas import tpu as pltpu
from jax.experimental.layout import Layout, with_layout_constraint
from jax.sharding import PartitionSpec as P


def swap(x, axis, bit):
    n = lax.axis_size(axis)
    return lax.ppermute(x, axis, [(i, i ^ bit) for i in range(n)])


def bits_of(axis):
    n = lax.axis_size(axis)
    return [1 << k for k in range(n.bit_length() - 1)]


def scatter_sum(x, axis):
    for bit in bits_of(axis):
        pairs = x.reshape((x.shape[0] // 2, 2) + x.shape[1:])
        x = pairs[:, 0] + swap(pairs[:, 1], axis, bit)
    return x[0]


def part_orders(per):
    bits = bits_of("col")[::-1]
    turned = bits[:-2] + bits[-1:] + bits[-2:-1]
    return [bits, turned] if per % 2 == 0 and len(bits) > 1 else [bits]


def gather_pieces(blocks, beside):
    orders = part_orders(blocks.shape[0])
    size = blocks.shape[0] // len(orders)
    near = [0]
    for bit in orders[0][:-2]:
        near = near + [far | bit for far in near]
    whole = [blocks if far == 0 else swap(blocks, "col", far) for far in near]
    (whole,) = beside(0, [jnp.stack(whole)])
    held = [whole[:, i * size : (i + 1) * size] for i in range(len(orders))]
    if len(orders[0]) > 1:
        came = [swap(x, "col", order[-2]) for x, order in zip(held, orders)]
        held = beside(1, [jnp.concatenate([x, y], axis=0) for x, y in zip(held, came)])
    came = [swap(x, "col", order[-1]) for x, order in zip(held, orders)]
    shape = (-1,) + blocks.shape[1:]
    return [[x.reshape(shape), y.reshape(shape)] for x, y in zip(held, came)]


def piece_index(per, far, block, rho=0, n_row=1):
    orders = part_orders(per)
    size = per // len(orders)
    half = lax.axis_size("col") // 2
    result = 0
    for i, order in enumerate(orders):
        spot = sum(((far & bit) > 0).astype(jnp.int32) << t for t, bit in enumerate(order))
        piece = (i * n_row + rho) * 2 + spot // half
        here = (piece * half + spot % half) * size + block % size
        result = jnp.where(block // size == i, here, result)
    return result


def split_rows(x):
    n, mine = lax.axis_size("row"), lax.axis_index("row")
    size = -(-x.shape[0] // (8 * n)) * 8
    x = jnp.pad(x, ((0, n * size - x.shape[0]), (0, 0)))
    parts = [lax.dynamic_slice_in_dim(x, (mine ^ k) * size, size, 0) for k in range(n)]
    return scatter_sum(jnp.stack(parts), "row")


def join_rows(x):
    n, mine = lax.axis_size("row"), lax.axis_index("row")
    parts = [x]
    for bit in bits_of("row"):
        parts = parts + [swap(part, "row", bit) for part in parts]
    parts = jnp.stack(parts)
    return jnp.concatenate(
        [lax.dynamic_index_in_dim(parts, mine ^ k, 0, keepdims=False) for k in range(n)]
    )


GROUP = 8
TURN = 4 * GROUP
DEPTH = 5
ROOM = 64
SPARE = 8
FIELD = 1 << 16
UNIT = 2.0**-14


def tile_rows():
    shape = (8, 16, 128)
    rows = 16 * lax.broadcasted_iota(jnp.int32, shape, 0) + lax.broadcasted_iota(jnp.int32, shape, 1)
    return rows.astype(jnp.float32).astype(jnp.bfloat16)


def blocks_of(lines, rows):
    zero = jnp.zeros((), jnp.bfloat16)
    one = jnp.ones((), jnp.bfloat16)
    empty = jnp.zeros((128, 128), jnp.bfloat16)

    def tile(x):
        return jnp.broadcast_to(x.astype(jnp.float32), (16, 128)).astype(jnp.bfloat16)[None]

    def factors(code):
        o = code >> 16
        w = tile((code & (FIELD - 1)).astype(jnp.float32) * UNIT)
        left = jnp.where(rows == tile(o >> 7), w, zero).reshape(128, 128)
        right = jnp.where(rows == tile(o & 127), one, zero).reshape(128, 128)
        return left, right

    blocks = []
    for u in range(0, len(lines), 2):
        (left, right), (left_too, right_too) = factors(lines[u]), factors(lines[u + 1])
        both = lax.dot_general(
            jnp.concatenate([left, left_too], axis=1),
            jnp.concatenate(
                [
                    jnp.concatenate([right, empty], axis=1),
                    jnp.concatenate([empty, right_too], axis=1),
                ],
                axis=0,
            ),
            (((1,), (1,)), ((), ())),
            preferred_element_type=jnp.float32,
        ).astype(jnp.bfloat16)
        blocks += [both[:, :128], both[:, 128:]]
    return blocks


def pack_kernel(meta, pos, codes, labels, out):
    out[...] = jnp.zeros_like(out)
    stride = ROOM + SPARE
    for k in range(labels.shape[0]):
        out[pl.ds(k * stride + ROOM, 1), :] = labels[pl.ds(k, 1), :]

    def turn(i, _):
        for u in range(GROUP):
            s = i * GROUP + u
            out[pl.ds(pos[s], 1), :] = codes[pl.ds(s, 1), :]
        return 0

    lax.fori_loop(0, meta[0], turn, 0)


def build_kernel(span, marks, lists, codes, *refs):
    dense, dbuf, sems = refs[-3:]
    start, turns = marks[0, span[0]], marks[0, span[1]]
    rows = tile_rows()

    def out_copy(i):
        slot = lax.rem(i, DEPTH)
        return pltpu.make_async_copy(
            dbuf.at[slot], dense.at[pl.ds(i * TURN, TURN)], sems.at[slot]
        )

    def turn(i, _):
        slot = lax.rem(i, DEPTH)

        @pl.when(i >= start + DEPTH)
        def _():
            out_copy(i - DEPTH).wait()

        lines = [codes[pl.ds(lists[0, i * TURN + u], 1), :] for u in range(TURN)]
        for u in range(0, TURN, GROUP):
            blocks = blocks_of(lines[u : u + GROUP], rows)
            for k, block in enumerate(blocks):
                dbuf[slot, u + k] = block
        out_copy(i).start()
        return 0

    lax.fori_loop(start, turns, turn, 0)

    def finish(i, _):
        out_copy(i).wait()
        return 0

    lax.fori_loop(jnp.maximum(turns - DEPTH, start), turns, finish, 0)


def fetch(pieces, into, sems):
    size = pieces[0].shape[0]
    copies = [
        pltpu.make_async_copy(piece, into.at[pl.ds(i * size, size)], sems.at[i])
        for i, piece in enumerate(pieces)
    ]
    for copy in copies:
        copy.start()
    return copies


def read_dense(start, turns, dense, dbuf, sems, product, prepare):
    def in_copy(i):
        slot = lax.rem(i, DEPTH)
        return pltpu.make_async_copy(
            dense.at[pl.ds(i * TURN, TURN)], dbuf.at[slot], sems.at[slot]
        )

    def begin(i, _):
        in_copy(i).start()
        return 0

    lax.fori_loop(start, jnp.minimum(turns, start + DEPTH - 1), begin, 0)
    prepare()

    def turn(i, _):
        @pl.when(i + DEPTH - 1 < turns)
        def _():
            in_copy(i + DEPTH - 1).start()

        in_copy(i).wait()
        product(i, lax.rem(i, DEPTH))
        return 0

    lax.fori_loop(start, turns, turn, 0)


def add_pairs(i, owner, one, into):
    groups = TURN // GROUP
    for g in range(0, groups, 2):
        added = [one(g), one(g + 1)]
        for k in range(2):
            into[owner[0, i * groups + g + k]] += added[k]


def forward_kernel(n, scale, span, marks, lists, owner, weight, bias, cotangent, dense, *refs):
    pieces, refs = refs[:n], refs[n:]
    output, turned, local, totals, feat, proj, dbuf, piece_sems, sems = refs
    copies = fetch(pieces, feat, piece_sems)
    size, _, width = pieces[0].shape
    batch = 8 if size % 8 == 0 else 1

    def project(t, _):
        spot = pl.ds(t * batch, batch)
        held = feat[spot].reshape(batch * 128, width)
        low = jnp.dot(held, weight[...], preferred_element_type=jnp.float32)
        proj[spot] = low.astype(jnp.bfloat16).reshape(batch, 128, width)
        return 0

    def prepare():
        totals[...] = jnp.zeros_like(totals)
        for i, copy in enumerate(copies):
            copy.wait()
            lax.fori_loop(i * size // batch, (i + 1) * size // batch, project, 0)

    def product(i, slot):
        def one(g):
            spots = [lists[1, i * TURN + g * GROUP + u] for u in range(GROUP)]
            left = jnp.concatenate([dbuf[slot, g * GROUP + u] for u in range(GROUP)], axis=1)
            right = jnp.concatenate(
                [jnp.concatenate([proj[c], feat[c]], axis=1) for c in spots], axis=0
            )
            return jnp.dot(left, right, preferred_element_type=jnp.float32)

        add_pairs(i, owner, one, totals)

    read_dense(marks[0, span[0]], marks[0, span[1]], dense, dbuf, sems, product, prepare)

    weight_sum, bias_sum = 0.0, 0.0
    for q in range(totals.shape[0]):
        lines = pl.ds(q * 128, 128)
        pre = totals[q, :, :width] + bias[...]
        output[lines, :] = jnp.maximum(pre, 0.0).astype(jnp.bfloat16)
        grad = jnp.where(pre > 0, cotangent[lines, :].astype(jnp.float32), 0.0)
        turned[q] = grad.T.astype(jnp.bfloat16)
        weight_sum += lax.dot_general(
            totals[q, :, width:].astype(jnp.bfloat16),
            grad.astype(jnp.bfloat16),
            (((0,), (0,)), ((), ())),
            preferred_element_type=jnp.float32,
        )
        bias_sum += jnp.sum(grad, axis=0, keepdims=True)
    local[pl.ds(0, width), :] = weight_sum * scale
    local[pl.ds(width, 8), :] = jnp.broadcast_to(bias_sum * scale, (8, width))


def tile_kernel(meta, order, dst, col, codes, panel, totals):
    rows = tile_rows()
    totals[...] = jnp.zeros_like(totals)

    def turn(i, _):
        lines = [codes[pl.ds(order[i * GROUP + u], 1), :] for u in range(GROUP)]
        for u, block in enumerate(blocks_of(lines, rows)):
            p = i * GROUP + u
            totals[dst[p]] += jnp.dot(block, panel[col[p]], preferred_element_type=jnp.float32)
        return 0

    lax.fori_loop(0, meta[0], turn, 0)


def backward_kernel(n, span, marks, lists, owner, before, dense, *refs):
    pieces, (acc, grad, dbuf, piece_sems, sems) = refs[:n], refs[n:]
    copies = fetch(pieces, grad, piece_sems)

    def prepare():
        acc[...] = before[...]
        for copy in copies:
            copy.wait()

    def product(i, slot):
        def one(g):
            spots = [lists[1, i * TURN + g * GROUP + u] for u in range(GROUP)]
            left = jnp.concatenate([grad[c] for c in spots], axis=1)
            right = dbuf[slot, pl.ds(g * GROUP, GROUP)].reshape(GROUP * 128, 128)
            return jnp.dot(left, right, preferred_element_type=jnp.float32)

        add_pairs(i, owner, one, acc)

    read_dense(marks[0, span[0]], marks[0, span[1]], dense, dbuf, sems, product, prepare)


SMEM = pl.BlockSpec(memory_space=pltpu.SMEM)
VMEM = pl.BlockSpec(memory_space=pltpu.VMEM)
HBM = pl.BlockSpec(memory_space=pl.ANY)
PARAMS = pltpu.CompilerParams(vmem_limit_bytes=48 * 1024 * 1024)


def cost(slots, products):
    flops = 2 * slots * products * 128**3
    return pl.CostEstimate(flops=flops, bytes_accessed=slots * 128 * 128 * 2, transcendentals=0)


def run_tile(meta, order, dst, col, codes, panel, row_blocks):
    return pl.pallas_call(
        tile_kernel,
        out_shape=jax.ShapeDtypeStruct((row_blocks, 128, panel.shape[-1]), jnp.float32),
        in_specs=[SMEM] * 4 + [VMEM] * 2,
        out_specs=VMEM,
        compiler_params=PARAMS,
    )(meta, order, dst, col, codes, panel)


def run_pack(meta, pos, codes, labels):
    length = labels.shape[0] * (ROOM + SPARE)
    return pl.pallas_call(
        pack_kernel,
        out_shape=jax.ShapeDtypeStruct((length, 128), jnp.int32),
        in_specs=[SMEM] * 2 + [VMEM] * 2,
        out_specs=VMEM,
        compiler_params=PARAMS,
    )(meta, pos, codes, labels)


def run_build(span, listed, codes, after, dense):
    lists, _, marks = listed
    others = after if dense is None else after + [dense]
    return pl.pallas_call(
        functools.partial(build_kernel, span),
        out_shape=jax.ShapeDtypeStruct((lists.shape[1], 128, 128), jnp.bfloat16),
        in_specs=[SMEM] * 2 + [VMEM] + [HBM] * len(others),
        out_specs=HBM,
        scratch_shapes=[
            pltpu.VMEM((DEPTH, TURN, 128, 128), jnp.bfloat16),
            pltpu.SemaphoreType.DMA((DEPTH,)),
        ],
        input_output_aliases={} if dense is None else {2 + len(others): 0},
        compiler_params=PARAMS,
        cost_estimate=cost(lists.shape[1], 2),
    )(marks, lists, codes, *others)


def run_forward(scale, span, listed, weight, bias, cotangent, dense, feat):
    lists, owner, marks = listed
    n = len(feat)
    size, _, width = feat[0].shape
    row_blocks = cotangent.shape[0] // 128
    return pl.pallas_call(
        functools.partial(forward_kernel, n, scale, span),
        out_shape=(
            jax.ShapeDtypeStruct(cotangent.shape, jnp.bfloat16),
            jax.ShapeDtypeStruct((row_blocks, width, 128), jnp.bfloat16),
            jax.ShapeDtypeStruct((width + 8, width), jnp.float32),
        ),
        in_specs=[SMEM] * 3 + [VMEM] * 3 + [HBM] * (n + 1),
        out_specs=[VMEM] * 3,
        scratch_shapes=[
            pltpu.VMEM((row_blocks, 128, 2 * width), jnp.float32),
            pltpu.VMEM((n * size, 128, width), jnp.bfloat16),
            pltpu.VMEM((n * size, 128, width), jnp.bfloat16),
            pltpu.VMEM((DEPTH, TURN, 128, 128), jnp.bfloat16),
            pltpu.SemaphoreType.DMA((n,)),
            pltpu.SemaphoreType.DMA((DEPTH,)),
        ],
        compiler_params=PARAMS,
        cost_estimate=cost(lists.shape[1], 4),
    )(marks, lists, owner, weight, bias, cotangent, dense, *feat)


def run_backward(span, listed, before, dense, pieces):
    lists, owner, marks = listed
    n = len(pieces)
    size, width, _ = pieces[0].shape
    return pl.pallas_call(
        functools.partial(backward_kernel, n, span),
        out_shape=jax.ShapeDtypeStruct(before.shape, jnp.float32),
        in_specs=[SMEM] * 3 + [VMEM] + [HBM] * (n + 1),
        out_specs=VMEM,
        scratch_shapes=[
            pltpu.VMEM((n * size, width, 128), jnp.bfloat16),
            pltpu.VMEM((DEPTH, TURN, 128, 128), jnp.bfloat16),
            pltpu.SemaphoreType.DMA((n,)),
            pltpu.SemaphoreType.DMA((DEPTH,)),
        ],
        compiler_params=PARAMS,
        cost_estimate=cost(lists.shape[1], 4),
    )(marks, lists, owner, before, dense, *pieces)


def column(row):
    return jnp.broadcast_to(row, (8, row.shape[1])).T[:, :1]


def list_kernel(keys, split, fills, key_ref, *refs):
    value_refs, (lists, owner_ref, marks_ref) = refs[: len(fills)], refs[len(fills) :]
    n, length = key_ref.shape[1], lists.shape[1]
    key = key_ref[...].astype(jnp.float32)
    key_column = column(key)
    lanes = lax.broadcasted_iota(jnp.int32, (128, n), 1)
    lines = lax.broadcasted_iota(jnp.int32, (128, n), 0)
    rank = jnp.zeros((1, n), jnp.float32)
    for t in range(0, n, 128):
        before = (key_column[t : t + 128] == key) & (lines + t < lanes)
        rank += jnp.sum(jnp.where(before, 1.0, 0.0), axis=0, keepdims=True)

    rows = -(-keys // 8) * 8
    names = lax.broadcasted_iota(jnp.int32, (rows, n), 0).astype(jnp.float32)
    name = lax.broadcasted_iota(jnp.int32, (rows, 1), 0).astype(jnp.float32)
    counts = jnp.sum(jnp.where(names == key, 1.0, 0.0), axis=1, keepdims=True)
    filled = jnp.where(name < keys, jnp.floor((counts + (GROUP - 1)) * (1.0 / GROUP)) * GROUP, 0.0)
    below = jnp.sum(jnp.where(name < split, filled, 0.0), axis=0, keepdims=True)
    first = jnp.floor((below + (TURN - 1)) * (1.0 / TURN))
    filled = filled + jnp.where(name == split - 1, first * TURN - below, 0.0)
    turns = jnp.floor((jnp.sum(filled, axis=0, keepdims=True) + (TURN - 1)) * (1.0 / TURN))
    base = jnp.sum(jnp.where(names < key, filled, 0.0), axis=0, keepdims=True)
    pos_column = column(jnp.where(key < keys, base + rank, -1.0))

    spots = lax.broadcasted_iota(jnp.int32, (1, length), 1).astype(jnp.float32)
    columns = [column(ref[...].astype(jnp.float32)) for ref in value_refs]
    sums = [jnp.zeros((1, length), jnp.float32) for _ in fills]
    for t in range(0, n, 128):
        hit = pos_column[t : t + 128] == spots
        for k, fill in enumerate(fills):
            value = columns[k][t : t + 128] - fill
            sums[k] += jnp.sum(jnp.where(hit, value, 0.0), axis=0, keepdims=True)
    for k, fill in enumerate(fills):
        lists[pl.ds(k, 1), :] = (sums[k] + fill).astype(jnp.int32)

    other = lax.broadcasted_iota(jnp.int32, (rows, 128), 1).astype(jnp.float32)
    ends = column(jnp.sum(jnp.where(name <= other, filled, 0.0), axis=0, keepdims=True))[:rows]
    starts = lax.broadcasted_iota(jnp.int32, owner_ref.shape, 1).astype(jnp.float32) * GROUP
    passed = (ends <= starts) & (name < keys)
    owner = jnp.sum(jnp.where(passed, 1.0, 0.0), axis=0, keepdims=True)
    owner = jnp.minimum(owner, keys - 1.0)
    owner_ref[...] = jnp.where(owner >= split, owner - split, owner).astype(jnp.int32)

    spot = lax.broadcasted_iota(jnp.int32, (1, 128), 1)
    marks = jnp.where(spot == FIRST, first, 0.0)
    for k in range(1, 5):
        marks = jnp.where(spot == FIRST + k, jnp.floor(turns * (k / 4)), marks)
    marks_ref[...] = marks.astype(jnp.int32)


FIRST = 1
QUARTERS = [0, 2, 3, 4, 5]


def make_lists(key, values, fills, keys, split):
    n = key.size
    length = (-(-(n + keys * GROUP) // TURN) + 1) * TURN
    groups = -(-length // GROUP // 128) * 128
    lists, owner, marks = pl.pallas_call(
        functools.partial(list_kernel, keys, split, fills),
        out_shape=(
            jax.ShapeDtypeStruct((len(fills), length), jnp.int32),
            jax.ShapeDtypeStruct((1, groups), jnp.int32),
            jax.ShapeDtypeStruct((1, 128), jnp.int32),
        ),
        in_specs=[VMEM] * (1 + len(fills)),
        out_specs=[VMEM] * 3,
        compiler_params=PARAMS,
        cost_estimate=cost(32, 2),
    )(key.reshape(1, n), *[value.reshape(1, n) for value in values])
    return lists, owner, marks


def place(pos, value, length, fill):
    spots = jnp.arange(length, dtype=jnp.int32)
    hit = pos[:, None] == spots[None, :]
    return jnp.sum(jnp.where(hit, value[:, None] - fill, 0), axis=0) + fill


def shards(
    features,
    weight,
    bias,
    cotangent,
    block_count,
    block_rows,
    block_cols,
    edge_offsets,
    edge_weight,
):
    node_dev, width = features.shape
    n_row = lax.axis_size("row")
    n_col = lax.axis_size("col")
    slots = block_rows.shape[2]
    count = block_count[0, 0]
    mine = lax.axis_index("col")
    mine_row = lax.axis_index("row")
    per = node_dev // 128
    row_blocks = per * n_col
    col_blocks = per * n_row
    scale = (node_dev * n_row * n_col) ** (-0.5)
    by_owner = n_row * n_col * node_dev * width * 2 <= 8 * 1024 * 1024

    brow = block_rows[0, 0]
    bcol = block_cols[0, 0]
    ids = jnp.arange(slots, dtype=jnp.int32)
    live = ids < count
    codes = edge_offsets[0, 0] * FIELD + (
        edge_weight[0, 0].astype(jnp.float32) * (1.0 / UNIT)
    ).astype(jnp.int32)
    codes = jnp.pad(codes, ((0, 8), (0, 0)))
    home = brow // per
    turns_plain = ((count + GROUP - 1) // GROUP).reshape(1)

    def tile_plan():
        wide = lax.all_gather(features, "row", axis=0, tiled=True)
        low = jnp.dot(wide, weight, preferred_element_type=jnp.float32).astype(jnp.bfloat16)
        panel = jnp.concatenate([low, wide], axis=1).reshape(col_blocks, 128, 2 * width)
        order = jnp.where(live, ids, slots)
        dst = jnp.where(live, (home ^ mine) * per + brow % per, 0)
        totals = run_tile(turns_plain, order, dst, bcol, codes, panel, row_blocks)
        own = scatter_sum(totals.reshape(n_col, node_dev, 2 * width), "col")
        pre = own[:, :width] + bias
        output = jnp.maximum(pre, 0.0).astype(jnp.bfloat16)
        grad = jnp.where(pre > 0, cotangent.astype(jnp.float32), 0.0)
        turned = jnp.swapaxes(grad.astype(jnp.bfloat16).reshape(per, 128, width), 1, 2)
        weight_sum = lax.dot_general(
            own[:, width:].astype(jnp.bfloat16),
            grad.astype(jnp.bfloat16),
            (((0,), (0,)), ((), ())),
            preferred_element_type=jnp.float32,
        )
        bias_sum = jnp.broadcast_to(jnp.sum(grad, axis=0), (8, width))
        return output, turned, jnp.concatenate([weight_sum, bias_sum], axis=0) * scale

    source = piece_index(per, home ^ mine, brow % per)
    unit = row_blocks // (2 * len(part_orders(per)))
    late = source // unit % 2
    source = source // (2 * unit) * unit + source % unit
    back = make_lists(
        jnp.where(live, late * col_blocks + bcol, 2 * col_blocks),
        [ids, source],
        [slots, 0],
        2 * col_blocks,
        col_blocks,
    )
    state = {"dense": None}

    def build(held, start, end):
        span = (QUARTERS[start], QUARTERS[end])
        state["dense"] = run_build(span, back, codes, held, state["dense"])

    if by_owner:
        same = live[:, None] & (home[:, None] == home[None, :]) & (ids[:, None] < ids[None, :])
        rank = jnp.sum(same.astype(jnp.int32), axis=0)
        over = jnp.any(live & (rank >= ROOM)).astype(jnp.int32)
        fits = live & (rank < ROOM)
        label = 1 + (brow % per) * col_blocks + bcol
        labels = place(jnp.where(fits, home * ROOM + rank, -1), label, n_col * ROOM, 0)
        labels = jnp.concatenate(
            [labels.reshape(n_col, ROOM), jnp.full((n_col, 128 - ROOM), over)], axis=1
        )
        stride = ROOM + SPARE
        pos = jnp.where(fits, home * stride + rank, ROOM + SPARE - 1)
        packed = run_pack(turns_plain, pos, codes, labels)
        came = lax.all_to_all(
            packed.reshape(n_col, stride, 128), "col", split_axis=0, concat_axis=0, tiled=True
        )
        spread = jnp.max(came[:, ROOM, ROOM:], axis=0)[None]
        for bit in bits_of("row"):
            spread = spread + swap(spread, "row", bit)
        any_over = jnp.max(spread, axis=1)

        got = came[:, ROOM, :ROOM]
        sources = jnp.arange(n_col, dtype=jnp.int32)[:, None]
        places = jnp.arange(ROOM, dtype=jnp.int32)[None, :]
        row_here = ((got - 1) // col_blocks).reshape(-1)
        col_there = (got - 1) % col_blocks
        col_there = piece_index(
            per, sources ^ mine, col_there % per, (col_there // per) ^ mine_row, n_row
        )
        line = sources * stride + places
        listed = make_lists(
            jnp.where(got > 0, row_here.reshape(got.shape), per),
            [jnp.broadcast_to(line, got.shape), col_there],
            [ROOM + 1, 0],
            per,
            per,
        )

        def prepare(step, held):
            if step == 0:
                build(held, 0, 1)
            if step == 1:
                held, state["dense"] = lax.optimization_barrier((held, state["dense"]))
            return held

        pairs = gather_pieces(features.reshape(per, 128, width), prepare)
        lines = came.reshape(n_col * stride, 128)
        here = run_build((0, QUARTERS[4]), listed, lines, [], None)
        last, here = lax.optimization_barrier(([pair[1] for pair in pairs], here))
        feat = []
        for pair in [[pair[0], x] for pair, x in zip(pairs, last)]:
            rows = [pair]
            for bit in bits_of("row"):
                rows = rows + [[swap(x, "row", bit) for x in pair] for pair in rows]
            feat += [x for pair in rows for x in pair]
        done = run_forward(
            scale, (0, QUARTERS[4]), listed, weight, bias[None], cotangent, here, feat
        )
        done = lax.cond(any_over[0] > 0, tile_plan, lambda: tuple(done))
    else:
        done = tile_plan()

    output, turned, total = done
    turned = with_layout_constraint(turned, Layout(major_to_minor=(0, 1, 2)))
    steps = bits_of("col")[::-1]

    def add_total():
        state["total"] = state["total"] + swap(state["total"], "col", steps.pop(0))

    def beside(step, held):
        held, state["total"], state["dense"] = lax.optimization_barrier(
            (held, state["total"], state["dense"])
        )
        if steps:
            add_total()
        if step == 0:
            build(held, 3, 4)
        if step == 1:
            add_products(0, held)
        return held

    def add_products(half, pieces):
        pieces = [x.reshape((-1,) + x.shape[2:]) if x.ndim == 4 else x for x in pieces]
        state["acc"] = run_backward(
            [(0, FIRST), (FIRST, QUARTERS[4])][half], back, state["acc"], state["dense"], pieces
        )

    state["acc"] = jnp.zeros((col_blocks, width, 128), jnp.float32)
    state["total"] = split_rows(total)
    while len(steps) > 3:
        add_total()
    build([turned], 1, 3)
    grad = gather_pieces(turned, beside)
    late_pieces, state["total"] = lax.optimization_barrier(
        ([pair[1] for pair in grad], state["total"])
    )
    while steps:
        add_total()
    add_products(1, late_pieces)
    acc, total = lax.optimization_barrier((state["acc"], state["total"]))
    total = join_rows(total)
    back = jnp.swapaxes(acc, 1, 2).reshape(col_blocks * 128, width)
    grad_proj = scatter_sum(
        jnp.stack(
            [
                lax.dynamic_slice_in_dim(back, (mine_row ^ k) * node_dev, node_dev, 0)
                for k in range(n_row)
            ]
        ),
        "row",
    ).astype(jnp.bfloat16)
    grad_features = lax.dot_general(
        grad_proj, weight, (((1,), (1,)), ((), ())), preferred_element_type=jnp.float32
    ).astype(jnp.bfloat16)
    return (
        output,
        grad_features,
        total[: weight.shape[0]],
        total[weight.shape[0]],
    )


def solution(mesh):
    return jax.shard_map(
        shards,
        mesh=mesh,
        in_specs=(
            P(("row", "col"), None),
            P(),
            P(),
            P(("row", "col"), None),
            P("row", "col"),
            P("row", "col", None),
            P("row", "col", None),
            P("row", "col", None, None),
            P("row", "col", None, None),
        ),
        out_specs=(P(("row", "col"), None), P(("row", "col"), None), P(), P()),
        check_vma=False,
    )
```

```python
import functools
import functools
import jax
import jax.numpy as jnp
from jax import lax
from jax.experimental import pallas as pl
from jax.experimental.pallas import tpu as pltpu
from jax.experimental.layout import Layout, with_layout_constraint
from jax.sharding import PartitionSpec as P


def swap(x, axis, bit):
    n = lax.axis_size(axis)
    return lax.ppermute(x, axis, [(i, i ^ bit) for i in range(n)])


def bits_of(axis):
    n = lax.axis_size(axis)
    return [1 << k for k in range(n.bit_length() - 1)]


def scatter_sum(x, axis):
    for bit in bits_of(axis):
        pairs = x.reshape((x.shape[0] // 2, 2) + x.shape[1:])
        x = pairs[:, 0] + swap(pairs[:, 1], axis, bit)
    return x[0]


def part_orders(per):
    bits = bits_of("col")[::-1]
    turned = bits[:-2] + bits[-1:] + bits[-2:-1]
    return [bits, turned] if per % 2 == 0 and len(bits) > 1 else [bits]


def gather_pieces(blocks, beside):
    orders = part_orders(blocks.shape[0])
    size = blocks.shape[0] // len(orders)
    near = [0]
    for bit in orders[0][:-2]:
        near = near + [far | bit for far in near]
    whole = [blocks if far == 0 else swap(blocks, "col", far) for far in near]
    (whole,) = beside(0, [jnp.stack(whole)])
    held = [whole[:, i * size : (i + 1) * size] for i in range(len(orders))]
    if len(orders[0]) > 1:
        came = [swap(x, "col", order[-2]) for x, order in zip(held, orders)]
        held = beside(1, [jnp.concatenate([x, y], axis=0) for x, y in zip(held, came)])
    came = [swap(x, "col", order[-1]) for x, order in zip(held, orders)]
    shape = (-1,) + blocks.shape[1:]
    return [[x.reshape(shape), y.reshape(shape)] for x, y in zip(held, came)]


def piece_index(per, far, block, rho=0, n_row=1):
    orders = part_orders(per)
    size = per // len(orders)
    half = lax.axis_size("col") // 2
    result = 0
    for i, order in enumerate(orders):
        spot = sum(((far & bit) > 0).astype(jnp.int32) << t for t, bit in enumerate(order))
        piece = (i * n_row + rho) * 2 + spot // half
        here = (piece * half + spot % half) * size + block % size
        result = jnp.where(block // size == i, here, result)
    return result


def split_rows(x):
    n, mine = lax.axis_size("row"), lax.axis_index("row")
    size = -(-x.shape[0] // (8 * n)) * 8
    x = jnp.pad(x, ((0, n * size - x.shape[0]), (0, 0)))
    parts = [lax.dynamic_slice_in_dim(x, (mine ^ k) * size, size, 0) for k in range(n)]
    return scatter_sum(jnp.stack(parts), "row")


def join_rows(x):
    n, mine = lax.axis_size("row"), lax.axis_index("row")
    parts = [x]
    for bit in bits_of("row"):
        parts = parts + [swap(part, "row", bit) for part in parts]
    parts = jnp.stack(parts)
    return jnp.concatenate(
        [lax.dynamic_index_in_dim(parts, mine ^ k, 0, keepdims=False) for k in range(n)]
    )


GROUP = 8
TURN = 4 * GROUP
DEPTH = 5
ROOM = 64
SPARE = 8
FIELD = 1 << 16
UNIT = 2.0**-14


def tile_rows():
    shape = (8, 16, 128)
    rows = 16 * lax.broadcasted_iota(jnp.int32, shape, 0) + lax.broadcasted_iota(jnp.int32, shape, 1)
    return rows.astype(jnp.float32).astype(jnp.bfloat16)


def blocks_of(lines, rows):
    zero = jnp.zeros((), jnp.bfloat16)
    one = jnp.ones((), jnp.bfloat16)
    empty = jnp.zeros((128, 128), jnp.bfloat16)

    def tile(x):
        return jnp.broadcast_to(x.astype(jnp.float32), (16, 128)).astype(jnp.bfloat16)[None]

    def factors(code):
        o = code >> 16
        w = tile((code & (FIELD - 1)).astype(jnp.float32) * UNIT)
        left = jnp.where(rows == tile(o >> 7), w, zero).reshape(128, 128)
        right = jnp.where(rows == tile(o & 127), one, zero).reshape(128, 128)
        return left, right

    blocks = []
    for u in range(0, len(lines), 2):
        (left, right), (left_too, right_too) = factors(lines[u]), factors(lines[u + 1])
        both = lax.dot_general(
            jnp.concatenate([left, left_too], axis=1),
            jnp.concatenate(
                [
                    jnp.concatenate([right, empty], axis=1),
                    jnp.concatenate([empty, right_too], axis=1),
                ],
                axis=0,
            ),
            (((1,), (1,)), ((), ())),
            preferred_element_type=jnp.float32,
        ).astype(jnp.bfloat16)
        blocks += [both[:, :128], both[:, 128:]]
    return blocks


def pack_kernel(meta, pos, codes, labels, out):
    out[...] = jnp.zeros_like(out)
    stride = ROOM + SPARE
    for k in range(labels.shape[0]):
        out[pl.ds(k * stride + ROOM, 1), :] = labels[pl.ds(k, 1), :]

    def turn(i, _):
        for u in range(GROUP):
            s = i * GROUP + u
            out[pl.ds(pos[s], 1), :] = codes[pl.ds(s, 1), :]
        return 0

    lax.fori_loop(0, meta[0], turn, 0)


def build_kernel(span, marks, lists, codes, *refs):
    dense, dbuf, sems = refs[-3:]
    start, turns = marks[0, span[0]], marks[0, span[1]]
    rows = tile_rows()

    def out_copy(i):
        slot = lax.rem(i, DEPTH)
        return pltpu.make_async_copy(
            dbuf.at[slot], dense.at[pl.ds(i * TURN, TURN)], sems.at[slot]
        )

    def turn(i, _):
        slot = lax.rem(i, DEPTH)

        @pl.when(i >= start + DEPTH)
        def _():
            out_copy(i - DEPTH).wait()

        lines = [codes[pl.ds(lists[0, i * TURN + u], 1), :] for u in range(TURN)]
        for u in range(0, TURN, GROUP):
            blocks = blocks_of(lines[u : u + GROUP], rows)
            for k, block in enumerate(blocks):
                dbuf[slot, u + k] = block
        out_copy(i).start()
        return 0

    lax.fori_loop(start, turns, turn, 0)

    def finish(i, _):
        out_copy(i).wait()
        return 0

    lax.fori_loop(jnp.maximum(turns - DEPTH, start), turns, finish, 0)


def fetch(pieces, into, sems):
    size = pieces[0].shape[0]
    copies = [
        pltpu.make_async_copy(piece, into.at[pl.ds(i * size, size)], sems.at[i])
        for i, piece in enumerate(pieces)
    ]
    for copy in copies:
        copy.start()
    return copies


def read_dense(start, turns, dense, dbuf, sems, product, prepare):
    def in_copy(i):
        slot = lax.rem(i, DEPTH)
        return pltpu.make_async_copy(
            dense.at[pl.ds(i * TURN, TURN)], dbuf.at[slot], sems.at[slot]
        )

    def begin(i, _):
        in_copy(i).start()
        return 0

    lax.fori_loop(start, jnp.minimum(turns, start + DEPTH - 1), begin, 0)
    prepare()

    def turn(i, _):
        @pl.when(i + DEPTH - 1 < turns)
        def _():
            in_copy(i + DEPTH - 1).start()

        in_copy(i).wait()
        product(i, lax.rem(i, DEPTH))
        return 0

    lax.fori_loop(start, turns, turn, 0)


def add_pairs(i, owner, one, into):
    groups = TURN // GROUP
    for g in range(0, groups, 2):
        added = [one(g), one(g + 1)]
        for k in range(2):
            into[owner[0, i * groups + g + k]] += added[k]


def forward_kernel(n, scale, span, marks, lists, owner, weight, bias, cotangent, dense, *refs):
    pieces, refs = refs[:n], refs[n:]
    output, turned, local, totals, feat, proj, dbuf, piece_sems, sems = refs
    copies = fetch(pieces, feat, piece_sems)
    size, _, width = pieces[0].shape
    batch = 8 if size % 8 == 0 else 1

    def project(t, _):
        spot = pl.ds(t * batch, batch)
        held = feat[spot].reshape(batch * 128, width)
        low = jnp.dot(held, weight[...], preferred_element_type=jnp.float32)
        proj[spot] = low.astype(jnp.bfloat16).reshape(batch, 128, width)
        return 0

    def prepare():
        totals[...] = jnp.zeros_like(totals)
        for i, copy in enumerate(copies):
            copy.wait()
            lax.fori_loop(i * size // batch, (i + 1) * size // batch, project, 0)

    def product(i, slot):
        def one(g):
            spots = [lists[1, i * TURN + g * GROUP + u] for u in range(GROUP)]
            left = jnp.concatenate([dbuf[slot, g * GROUP + u] for u in range(GROUP)], axis=1)
            right = jnp.concatenate(
                [jnp.concatenate([proj[c], feat[c]], axis=1) for c in spots], axis=0
            )
            return jnp.dot(left, right, preferred_element_type=jnp.float32)

        add_pairs(i, owner, one, totals)

    read_dense(marks[0, span[0]], marks[0, span[1]], dense, dbuf, sems, product, prepare)

    weight_sum, bias_sum = 0.0, 0.0
    for q in range(totals.shape[0]):
        lines = pl.ds(q * 128, 128)
        pre = totals[q, :, :width] + bias[...]
        output[lines, :] = jnp.maximum(pre, 0.0).astype(jnp.bfloat16)
        grad = jnp.where(pre > 0, cotangent[lines, :].astype(jnp.float32), 0.0)
        turned[q] = grad.T.astype(jnp.bfloat16)
        weight_sum += lax.dot_general(
            totals[q, :, width:].astype(jnp.bfloat16),
            grad.astype(jnp.bfloat16),
            (((0,), (0,)), ((), ())),
            preferred_element_type=jnp.float32,
        )
        bias_sum += jnp.sum(grad, axis=0, keepdims=True)
    local[pl.ds(0, width), :] = weight_sum * scale
    local[pl.ds(width, 8), :] = jnp.broadcast_to(bias_sum * scale, (8, width))


def tile_kernel(meta, order, dst, col, codes, panel, totals):
    rows = tile_rows()
    totals[...] = jnp.zeros_like(totals)

    def turn(i, _):
        lines = [codes[pl.ds(order[i * GROUP + u], 1), :] for u in range(GROUP)]
        for u, block in enumerate(blocks_of(lines, rows)):
            p = i * GROUP + u
            totals[dst[p]] += jnp.dot(block, panel[col[p]], preferred_element_type=jnp.float32)
        return 0

    lax.fori_loop(0, meta[0], turn, 0)


def backward_kernel(n, span, marks, lists, owner, before, dense, *refs):
    pieces, (acc, grad, dbuf, piece_sems, sems) = refs[:n], refs[n:]
    copies = fetch(pieces, grad, piece_sems)

    def prepare():
        acc[...] = before[...]
        for copy in copies:
            copy.wait()

    def product(i, slot):
        def one(g):
            spots = [lists[1, i * TURN + g * GROUP + u] for u in range(GROUP)]
            left = jnp.concatenate([grad[c] for c in spots], axis=1)
            right = dbuf[slot, pl.ds(g * GROUP, GROUP)].reshape(GROUP * 128, 128)
            return jnp.dot(left, right, preferred_element_type=jnp.float32)

        add_pairs(i, owner, one, acc)

    read_dense(marks[0, span[0]], marks[0, span[1]], dense, dbuf, sems, product, prepare)


SMEM = pl.BlockSpec(memory_space=pltpu.SMEM)
VMEM = pl.BlockSpec(memory_space=pltpu.VMEM)
HBM = pl.BlockSpec(memory_space=pl.ANY)
PARAMS = pltpu.CompilerParams(vmem_limit_bytes=48 * 1024 * 1024)


def cost(slots, products):
    flops = 2 * slots * products * 128**3
    return pl.CostEstimate(flops=flops, bytes_accessed=slots * 128 * 128 * 2, transcendentals=0)


def run_tile(meta, order, dst, col, codes, panel, row_blocks):
    return pl.pallas_call(
        tile_kernel,
        out_shape=jax.ShapeDtypeStruct((row_blocks, 128, panel.shape[-1]), jnp.float32),
        in_specs=[SMEM] * 4 + [VMEM] * 2,
        out_specs=VMEM,
        compiler_params=PARAMS,
    )(meta, order, dst, col, codes, panel)


def run_pack(meta, pos, codes, labels):
    length = labels.shape[0] * (ROOM + SPARE)
    return pl.pallas_call(
        pack_kernel,
        out_shape=jax.ShapeDtypeStruct((length, 128), jnp.int32),
        in_specs=[SMEM] * 2 + [VMEM] * 2,
        out_specs=VMEM,
        compiler_params=PARAMS,
    )(meta, pos, codes, labels)


def run_build(span, listed, codes, after, dense):
    lists, _, marks = listed
    others = after if dense is None else after + [dense]
    return pl.pallas_call(
        functools.partial(build_kernel, span),
        out_shape=jax.ShapeDtypeStruct((lists.shape[1], 128, 128), jnp.bfloat16),
        in_specs=[SMEM] * 2 + [VMEM] + [HBM] * len(others),
        out_specs=HBM,
        scratch_shapes=[
            pltpu.VMEM((DEPTH, TURN, 128, 128), jnp.bfloat16),
            pltpu.SemaphoreType.DMA((DEPTH,)),
        ],
        input_output_aliases={} if dense is None else {2 + len(others): 0},
        compiler_params=PARAMS,
        cost_estimate=cost(lists.shape[1], 2),
    )(marks, lists, codes, *others)


def run_forward(scale, span, listed, weight, bias, cotangent, dense, feat):
    lists, owner, marks = listed
    n = len(feat)
    size, _, width = feat[0].shape
    row_blocks = cotangent.shape[0] // 128
    return pl.pallas_call(
        functools.partial(forward_kernel, n, scale, span),
        out_shape=(
            jax.ShapeDtypeStruct(cotangent.shape, jnp.bfloat16),
            jax.ShapeDtypeStruct((row_blocks, width, 128), jnp.bfloat16),
            jax.ShapeDtypeStruct((width + 8, width), jnp.float32),
        ),
        in_specs=[SMEM] * 3 + [VMEM] * 3 + [HBM] * (n + 1),
        out_specs=[VMEM] * 3,
        scratch_shapes=[
            pltpu.VMEM((row_blocks, 128, 2 * width), jnp.float32),
            pltpu.VMEM((n * size, 128, width), jnp.bfloat16),
            pltpu.VMEM((n * size, 128, width), jnp.bfloat16),
            pltpu.VMEM((DEPTH, TURN, 128, 128), jnp.bfloat16),
            pltpu.SemaphoreType.DMA((n,)),
            pltpu.SemaphoreType.DMA((DEPTH,)),
        ],
        compiler_params=PARAMS,
        cost_estimate=cost(lists.shape[1], 4),
    )(marks, lists, owner, weight, bias, cotangent, dense, *feat)


def run_backward(span, listed, before, dense, pieces):
    lists, owner, marks = listed
    n = len(pieces)
    size, width, _ = pieces[0].shape
    return pl.pallas_call(
        functools.partial(backward_kernel, n, span),
        out_shape=jax.ShapeDtypeStruct(before.shape, jnp.float32),
        in_specs=[SMEM] * 3 + [VMEM] + [HBM] * (n + 1),
        out_specs=VMEM,
        scratch_shapes=[
            pltpu.VMEM((n * size, width, 128), jnp.bfloat16),
            pltpu.VMEM((DEPTH, TURN, 128, 128), jnp.bfloat16),
            pltpu.SemaphoreType.DMA((n,)),
            pltpu.SemaphoreType.DMA((DEPTH,)),
        ],
        compiler_params=PARAMS,
        cost_estimate=cost(lists.shape[1], 4),
    )(marks, lists, owner, before, dense, *pieces)


def column(row):
    return jnp.broadcast_to(row, (8, row.shape[1])).T[:, :1]


def list_kernel(keys, split, fills, key_ref, *refs):
    value_refs, (lists, owner_ref, marks_ref) = refs[: len(fills)], refs[len(fills) :]
    n, length = key_ref.shape[1], lists.shape[1]
    key = key_ref[...].astype(jnp.float32)
    key_column = column(key)
    lanes = lax.broadcasted_iota(jnp.int32, (128, n), 1)
    lines = lax.broadcasted_iota(jnp.int32, (128, n), 0)
    rank = jnp.zeros((1, n), jnp.float32)
    for t in range(0, n, 128):
        before = (key_column[t : t + 128] == key) & (lines + t < lanes)
        rank += jnp.sum(jnp.where(before, 1.0, 0.0), axis=0, keepdims=True)

    rows = -(-keys // 8) * 8
    names = lax.broadcasted_iota(jnp.int32, (rows, n), 0).astype(jnp.float32)
    name = lax.broadcasted_iota(jnp.int32, (rows, 1), 0).astype(jnp.float32)
    counts = jnp.sum(jnp.where(names == key, 1.0, 0.0), axis=1, keepdims=True)
    filled = jnp.where(name < keys, jnp.floor((counts + (GROUP - 1)) * (1.0 / GROUP)) * GROUP, 0.0)
    below = jnp.sum(jnp.where(name < split, filled, 0.0), axis=0, keepdims=True)
    first = jnp.floor((below + (TURN - 1)) * (1.0 / TURN))
    filled = filled + jnp.where(name == split - 1, first * TURN - below, 0.0)
    turns = jnp.floor((jnp.sum(filled, axis=0, keepdims=True) + (TURN - 1)) * (1.0 / TURN))
    base = jnp.sum(jnp.where(names < key, filled, 0.0), axis=0, keepdims=True)
    pos_column = column(jnp.where(key < keys, base + rank, -1.0))

    spots = lax.broadcasted_iota(jnp.int32, (1, length), 1).astype(jnp.float32)
    columns = [column(ref[...].astype(jnp.float32)) for ref in value_refs]
    sums = [jnp.zeros((1, length), jnp.float32) for _ in fills]
    for t in range(0, n, 128):
        hit = pos_column[t : t + 128] == spots
        for k, fill in enumerate(fills):
            value = columns[k][t : t + 128] - fill
            sums[k] += jnp.sum(jnp.where(hit, value, 0.0), axis=0, keepdims=True)
    for k, fill in enumerate(fills):
        lists[pl.ds(k, 1), :] = (sums[k] + fill).astype(jnp.int32)

    other = lax.broadcasted_iota(jnp.int32, (rows, 128), 1).astype(jnp.float32)
    ends = column(jnp.sum(jnp.where(name <= other, filled, 0.0), axis=0, keepdims=True))[:rows]
    starts = lax.broadcasted_iota(jnp.int32, owner_ref.shape, 1).astype(jnp.float32) * GROUP
    passed = (ends <= starts) & (name < keys)
    owner = jnp.sum(jnp.where(passed, 1.0, 0.0), axis=0, keepdims=True)
    owner = jnp.minimum(owner, keys - 1.0)
    owner_ref[...] = jnp.where(owner >= split, owner - split, owner).astype(jnp.int32)

    spot = lax.broadcasted_iota(jnp.int32, (1, 128), 1)
    marks = jnp.where(spot == FIRST, first, 0.0)
    for k in range(1, 5):
        marks = jnp.where(spot == FIRST + k, jnp.floor(turns * (k / 4)), marks)
    marks_ref[...] = marks.astype(jnp.int32)


FIRST = 1
QUARTERS = [0, 2, 3, 4, 5]


def make_lists(key, values, fills, keys, split):
    n = key.size
    length = (-(-(n + keys * GROUP) // TURN) + 1) * TURN
    groups = -(-length // GROUP // 128) * 128
    lists, owner, marks = pl.pallas_call(
        functools.partial(list_kernel, keys, split, fills),
        out_shape=(
            jax.ShapeDtypeStruct((len(fills), length), jnp.int32),
            jax.ShapeDtypeStruct((1, groups), jnp.int32),
            jax.ShapeDtypeStruct((1, 128), jnp.int32),
        ),
        in_specs=[VMEM] * (1 + len(fills)),
        out_specs=[VMEM] * 3,
        compiler_params=PARAMS,
        cost_estimate=cost(32, 2),
    )(key.reshape(1, n), *[value.reshape(1, n) for value in values])
    return lists, owner, marks


def place(pos, value, length, fill):
    spots = jnp.arange(length, dtype=jnp.int32)
    hit = pos[:, None] == spots[None, :]
    return jnp.sum(jnp.where(hit, value[:, None] - fill, 0), axis=0) + fill


def shards(
    features,
    weight,
    bias,
    cotangent,
    block_count,
    block_rows,
    block_cols,
    edge_offsets,
    edge_weight,
):
    node_dev, width = features.shape
    n_row = lax.axis_size("row")
    n_col = lax.axis_size("col")
    slots = block_rows.shape[2]
    count = block_count[0, 0]
    mine = lax.axis_index("col")
    mine_row = lax.axis_index("row")
    per = node_dev // 128
    row_blocks = per * n_col
    col_blocks = per * n_row
    scale = (node_dev * n_row * n_col) ** (-0.5)
    by_owner = n_row * n_col * node_dev * width * 2 <= 8 * 1024 * 1024

    brow = block_rows[0, 0]
    bcol = block_cols[0, 0]
    ids = jnp.arange(slots, dtype=jnp.int32)
    live = ids < count
    codes = edge_offsets[0, 0] * FIELD + (
        edge_weight[0, 0].astype(jnp.float32) * (1.0 / UNIT)
    ).astype(jnp.int32)
    codes = jnp.pad(codes, ((0, 8), (0, 0)))
    home = brow // per
    turns_plain = ((count + GROUP - 1) // GROUP).reshape(1)

    def tile_plan():
        wide = lax.all_gather(features, "row", axis=0, tiled=True)
        low = jnp.dot(wide, weight, preferred_element_type=jnp.float32).astype(jnp.bfloat16)
        panel = jnp.concatenate([low, wide], axis=1).reshape(col_blocks, 128, 2 * width)
        order = jnp.where(live, ids, slots)
        dst = jnp.where(live, (home ^ mine) * per + brow % per, 0)
        totals = run_tile(turns_plain, order, dst, bcol, codes, panel, row_blocks)
        own = scatter_sum(totals.reshape(n_col, node_dev, 2 * width), "col")
        pre = own[:, :width] + bias
        output = jnp.maximum(pre, 0.0).astype(jnp.bfloat16)
        grad = jnp.where(pre > 0, cotangent.astype(jnp.float32), 0.0)
        turned = jnp.swapaxes(grad.astype(jnp.bfloat16).reshape(per, 128, width), 1, 2)
        weight_sum = lax.dot_general(
            own[:, width:].astype(jnp.bfloat16),
            grad.astype(jnp.bfloat16),
            (((0,), (0,)), ((), ())),
            preferred_element_type=jnp.float32,
        )
        bias_sum = jnp.broadcast_to(jnp.sum(grad, axis=0), (8, width))
        return output, turned, jnp.concatenate([weight_sum, bias_sum], axis=0) * scale

    source = piece_index(per, home ^ mine, brow % per)
    unit = row_blocks // (2 * len(part_orders(per)))
    late = source // unit % 2
    source = source // (2 * unit) * unit + source % unit
    back_key = jnp.where(live, late * col_blocks + bcol, 2 * col_blocks)
    state = {"dense": None}

    def list_backward(key, value):
        return make_lists(key, [ids, value], [slots, 0], 2 * col_blocks, col_blocks)

    def build(held, start, end):
        span = (QUARTERS[start], QUARTERS[end])
        state["dense"] = run_build(span, state["back"], codes, held, state["dense"])

    if by_owner:
        same = live[:, None] & (home[:, None] == home[None, :]) & (ids[:, None] < ids[None, :])
        rank = jnp.sum(same.astype(jnp.int32), axis=0)
        over = jnp.any(live & (rank >= ROOM)).astype(jnp.int32)
        fits = live & (rank < ROOM)
        label = 1 + (brow % per) * col_blocks + bcol
        labels = place(jnp.where(fits, home * ROOM + rank, -1), label, n_col * ROOM, 0)
        labels = jnp.concatenate(
            [labels.reshape(n_col, ROOM), jnp.full((n_col, 128 - ROOM), over)], axis=1
        )
        stride = ROOM + SPARE
        pos = jnp.where(fits, home * stride + rank, ROOM + SPARE - 1)
        packed = run_pack(turns_plain, pos, codes, labels)
        came = lax.all_to_all(
            packed.reshape(n_col, stride, 128), "col", split_axis=0, concat_axis=0, tiled=True
        )
        spread = jnp.max(came[:, ROOM, ROOM:], axis=0)[None]
        for bit in bits_of("row"):
            spread = spread + swap(spread, "row", bit)
        any_over = jnp.max(spread, axis=1)

        got = came[:, ROOM, :ROOM]
        sources = jnp.arange(n_col, dtype=jnp.int32)[:, None]
        places = jnp.arange(ROOM, dtype=jnp.int32)[None, :]
        row_here = ((got - 1) // col_blocks).reshape(-1)
        col_there = (got - 1) % col_blocks
        col_there = piece_index(
            per, sources ^ mine, col_there % per, (col_there // per) ^ mine_row, n_row
        )
        line = sources * stride + places
        listed = make_lists(
            jnp.where(got > 0, row_here.reshape(got.shape), per),
            [jnp.broadcast_to(line, got.shape), col_there],
            [ROOM + 1, 0],
            per,
            per,
        )

        def prepare(step, held):
            if step == 0:
                held, inputs = lax.optimization_barrier((held, (back_key, source)))
                state["back"] = list_backward(*inputs)
                build(held, 0, 1)
            if step == 1:
                held, state["dense"] = lax.optimization_barrier((held, state["dense"]))
            return held

        pairs = gather_pieces(features.reshape(per, 128, width), prepare)
        lines = came.reshape(n_col * stride, 128)
        here = run_build((0, QUARTERS[4]), listed, lines, [], None)
        last, here = lax.optimization_barrier(([pair[1] for pair in pairs], here))
        feat = []
        for pair in [[pair[0], x] for pair, x in zip(pairs, last)]:
            rows = [pair]
            for bit in bits_of("row"):
                rows = rows + [[swap(x, "row", bit) for x in pair] for pair in rows]
            feat += [x for pair in rows for x in pair]
        done = run_forward(
            scale, (0, QUARTERS[4]), listed, weight, bias[None], cotangent, here, feat
        )
        done = lax.cond(any_over[0] > 0, tile_plan, lambda: tuple(done))
    else:
        state["back"] = list_backward(back_key, source)
        build([features], 0, 1)
        done = tile_plan()

    output, turned, total = done
    turned = with_layout_constraint(turned, Layout(major_to_minor=(0, 1, 2)))
    steps = bits_of("col")

    def add_total():
        state["total"] = state["total"] + swap(state["total"], "col", steps.pop(0))

    def beside(step, held):
        held, state["total"], state["dense"] = lax.optimization_barrier(
            (held, state["total"], state["dense"])
        )
        if steps:
            add_total()
        if step == 0:
            build(held, 3, 4)
        if step == 1:
            add_products(0, held)
        return held

    def add_products(half, pieces):
        pieces = [x.reshape((-1,) + x.shape[2:]) if x.ndim == 4 else x for x in pieces]
        state["acc"] = run_backward(
            [(0, FIRST), (FIRST, QUARTERS[4])][half], state["back"], state["acc"], state["dense"], pieces
        )

    state["acc"] = jnp.zeros((col_blocks, width, 128), jnp.float32)
    state["total"] = split_rows(total)
    while len(steps) > 3:
        add_total()
    build([turned], 1, 3)
    if len(steps) > 2:
        state["dense"], state["total"] = lax.optimization_barrier(
            (state["dense"], state["total"])
        )
        add_total()
    grad = gather_pieces(turned, beside)
    late_pieces, state["total"] = lax.optimization_barrier(
        ([pair[1] for pair in grad], state["total"])
    )
    while steps:
        add_total()
    total = join_rows(state["total"])
    add_products(1, late_pieces)
    acc = state["acc"]
    back = jnp.swapaxes(acc, 1, 2).reshape(col_blocks * 128, width)
    grad_proj = scatter_sum(
        jnp.stack(
            [
                lax.dynamic_slice_in_dim(back, (mine_row ^ k) * node_dev, node_dev, 0)
                for k in range(n_row)
            ]
        ),
        "row",
    ).astype(jnp.bfloat16)
    grad_features = lax.dot_general(
        grad_proj, weight, (((1,), (1,)), ((), ())), preferred_element_type=jnp.float32
    ).astype(jnp.bfloat16)
    return (
        output,
        grad_features,
        total[: weight.shape[0]],
        total[weight.shape[0]],
    )


def solution(mesh):
    return jax.shard_map(
        shards,
        mesh=mesh,
        in_specs=(
            P(("row", "col"), None),
            P(),
            P(),
            P(("row", "col"), None),
            P("row", "col"),
            P("row", "col", None),
            P("row", "col", None),
            P("row", "col", None, None),
            P("row", "col", None, None),
        ),
        out_specs=(P(("row", "col"), None), P(("row", "col"), None), P(), P()),
        check_vma=False,
    )
```

```python
import functools
import functools
import jax
import jax.numpy as jnp
from jax import lax
from jax.experimental import pallas as pl
from jax.experimental.pallas import tpu as pltpu
from jax.experimental.layout import Layout, with_layout_constraint
from jax.sharding import PartitionSpec as P


def swap(x, axis, bit):
    n = lax.axis_size(axis)
    return lax.ppermute(x, axis, [(i, i ^ bit) for i in range(n)])


def bits_of(axis):
    n = lax.axis_size(axis)
    return [1 << k for k in range(n.bit_length() - 1)]


def scatter_sum(x, axis):
    for bit in bits_of(axis):
        pairs = x.reshape((x.shape[0] // 2, 2) + x.shape[1:])
        x = pairs[:, 0] + swap(pairs[:, 1], axis, bit)
    return x[0]


def part_orders(per):
    bits = bits_of("col")[::-1]
    turned = bits[:-2] + bits[-1:] + bits[-2:-1]
    return [bits, turned] if per % 2 == 0 and len(bits) > 1 else [bits]


def gather_pieces(blocks, beside):
    orders = part_orders(blocks.shape[0])
    size = blocks.shape[0] // len(orders)
    near = [0]
    for bit in orders[0][:-2]:
        near = near + [far | bit for far in near]
    whole = [blocks if far == 0 else swap(blocks, "col", far) for far in near]
    (whole,) = beside(0, [jnp.stack(whole)])
    held = [whole[:, i * size : (i + 1) * size] for i in range(len(orders))]
    if len(orders[0]) > 1:
        came = [swap(x, "col", order[-2]) for x, order in zip(held, orders)]
        held = beside(1, [jnp.concatenate([x, y], axis=0) for x, y in zip(held, came)])
    came = [swap(x, "col", order[-1]) for x, order in zip(held, orders)]
    shape = (-1,) + blocks.shape[1:]
    return [[x.reshape(shape), y.reshape(shape)] for x, y in zip(held, came)]


def piece_index(per, far, block, rho=0, n_row=1):
    orders = part_orders(per)
    size = per // len(orders)
    half = lax.axis_size("col") // 2
    result = 0
    for i, order in enumerate(orders):
        spot = sum(((far & bit) > 0).astype(jnp.int32) << t for t, bit in enumerate(order))
        piece = (i * n_row + rho) * 2 + spot // half
        here = (piece * half + spot % half) * size + block % size
        result = jnp.where(block // size == i, here, result)
    return result


def split_rows(x):
    n, mine = lax.axis_size("row"), lax.axis_index("row")
    size = -(-x.shape[0] // (8 * n)) * 8
    x = jnp.pad(x, ((0, n * size - x.shape[0]), (0, 0)))
    parts = [lax.dynamic_slice_in_dim(x, (mine ^ k) * size, size, 0) for k in range(n)]
    return scatter_sum(jnp.stack(parts), "row")


def join_rows(x):
    n, mine = lax.axis_size("row"), lax.axis_index("row")
    parts = [x]
    for bit in bits_of("row"):
        parts = parts + [swap(part, "row", bit) for part in parts]
    parts = jnp.stack(parts)
    return jnp.concatenate(
        [lax.dynamic_index_in_dim(parts, mine ^ k, 0, keepdims=False) for k in range(n)]
    )


GROUP = 8
TURN = 4 * GROUP
DEPTH = 5
ROOM = 64
SPARE = 8
FIELD = 1 << 16
UNIT = 2.0**-14
COLS = 32


def tile_rows():
    shape = (8, 16, 128)
    rows = 16 * lax.broadcasted_iota(jnp.int32, shape, 0) + lax.broadcasted_iota(jnp.int32, shape, 1)
    return rows.astype(jnp.float32).astype(jnp.bfloat16)


def blocks_of(lines, rows):
    zero = jnp.zeros((), jnp.bfloat16)
    one = jnp.ones((), jnp.bfloat16)
    empty = jnp.zeros((128, 128), jnp.bfloat16)

    def tile(x):
        return jnp.broadcast_to(x.astype(jnp.float32), (16, 128)).astype(jnp.bfloat16)[None]

    def factors(code):
        o = code >> 16
        w = tile((code & (FIELD - 1)).astype(jnp.float32) * UNIT)
        left = jnp.where(rows == tile(o >> 7), w, zero).reshape(128, 128)
        right = jnp.where(rows == tile(o & 127), one, zero).reshape(128, 128)
        return left, right

    blocks = []
    for u in range(0, len(lines), 2):
        (left, right), (left_too, right_too) = factors(lines[u]), factors(lines[u + 1])
        both = lax.dot_general(
            jnp.concatenate([left, left_too], axis=1),
            jnp.concatenate(
                [
                    jnp.concatenate([right, empty], axis=1),
                    jnp.concatenate([empty, right_too], axis=1),
                ],
                axis=0,
            ),
            (((1,), (1,)), ((), ())),
            preferred_element_type=jnp.float32,
        ).astype(jnp.bfloat16)
        blocks += [both[:, :128], both[:, 128:]]
    return blocks


def column(row):
    return jnp.broadcast_to(row, (8, row.shape[1])).T[:, :1]


def ranks(key):
    n = key.shape[1]
    key_column = column(key)
    lanes = lax.broadcasted_iota(jnp.int32, (128, n), 1)
    lines = lax.broadcasted_iota(jnp.int32, (128, n), 0)
    rank = jnp.zeros((1, n), jnp.float32)
    for t in range(0, n, 128):
        before = (key_column[t : t + 128] == key) & (lines + t < lanes)
        rank += jnp.sum(jnp.where(before, 1.0, 0.0), axis=0, keepdims=True)
    return rank


def pack_kernel(per, owners, count, brow, bcol, offs, wts, out, codes, pos_row, pos, sem):
    slots, width = offs.shape
    stride = ROOM + SPARE
    lanes = lax.broadcasted_iota(jnp.int32, (1, slots), 1)
    live = lanes < count[0, 0]
    row = brow[...].astype(jnp.float32)
    home = jnp.floor((row + 0.5) * (1.0 / per))
    key = jnp.where(live, home, float(owners))
    rank = ranks(key)
    fits = live & (rank < ROOM)
    trash = float(ROOM + SPARE - 1)
    pos_row[...] = jnp.where(fits, home * stride + rank, trash).astype(jnp.int32)
    copy = pltpu.make_async_copy(pos_row, pos, sem)
    copy.start()

    out[...] = jnp.zeros_like(out)
    codes[pl.ds(0, slots), :] = offs[...] * FIELD + (
        wts[...].astype(jnp.float32) * (1.0 / UNIT)
    ).astype(jnp.int32)
    codes[pl.ds(slots, 8), :] = jnp.zeros((8, width), jnp.int32)

    label = 1.0 + (row - per * home) * COLS + bcol[...].astype(jnp.float32)
    names = lax.broadcasted_iota(jnp.int32, (owners, slots), 0).astype(jnp.float32)
    chosen = jnp.where((names == key) & fits, label, 0.0).astype(jnp.bfloat16)
    spots = lax.broadcasted_iota(jnp.int32, (1, 128), 1)
    placed = jnp.where(column(rank) == spots.astype(jnp.float32), 1.0, 0.0).astype(jnp.bfloat16)
    labels = jnp.dot(chosen, placed, preferred_element_type=jnp.float32)
    over = jnp.max(jnp.where(live, rank, 0.0), axis=1, keepdims=True)
    labels = jnp.where(spots < ROOM, labels, jnp.where(over < ROOM, 0.0, 1.0)).astype(jnp.int32)
    for k in range(owners):
        out[pl.ds(k * stride + ROOM, 1), :] = labels[k : k + 1]
    copy.wait()

    def turn(i, _):
        for u in range(GROUP):
            s = i * GROUP + u
            out[pl.ds(pos[0, s], 1), :] = codes[pl.ds(s, 1), :]
        return 0

    lax.fori_loop(0, (count[0, 0] + GROUP - 1) // GROUP, turn, 0)


def build_kernel(span, marks, lists, codes, *refs):
    dense, dbuf, sems = refs[-3:]
    start, turns = marks[0, span[0]], marks[0, span[1]]
    rows = tile_rows()

    def out_copy(i):
        slot = lax.rem(i, DEPTH)
        return pltpu.make_async_copy(
            dbuf.at[slot], dense.at[pl.ds(i * TURN, TURN)], sems.at[slot]
        )

    def turn(i, _):
        slot = lax.rem(i, DEPTH)

        @pl.when(i >= start + DEPTH)
        def _():
            out_copy(i - DEPTH).wait()

        lines = [codes[pl.ds(lists[0, i * TURN + u], 1), :] for u in range(TURN)]
        for u in range(0, TURN, GROUP):
            blocks = blocks_of(lines[u : u + GROUP], rows)
            for k, block in enumerate(blocks):
                dbuf[slot, u + k] = block
        out_copy(i).start()
        return 0

    lax.fori_loop(start, turns, turn, 0)

    def finish(i, _):
        out_copy(i).wait()
        return 0

    lax.fori_loop(jnp.maximum(turns - DEPTH, start), turns, finish, 0)


def fetch(pieces, into, sems):
    size = pieces[0].shape[0]
    copies = [
        pltpu.make_async_copy(piece, into.at[pl.ds(i * size, size)], sems.at[i])
        for i, piece in enumerate(pieces)
    ]
    for copy in copies:
        copy.start()
    return copies


def read_dense(start, turns, dense, dbuf, sems, product, prepare):
    def in_copy(i):
        slot = lax.rem(i, DEPTH)
        return pltpu.make_async_copy(
            dense.at[pl.ds(i * TURN, TURN)], dbuf.at[slot], sems.at[slot]
        )

    def begin(i, _):
        in_copy(i).start()
        return 0

    lax.fori_loop(start, jnp.minimum(turns, start + DEPTH - 1), begin, 0)
    prepare()

    def turn(i, _):
        @pl.when(i + DEPTH - 1 < turns)
        def _():
            in_copy(i + DEPTH - 1).start()

        in_copy(i).wait()
        product(i, lax.rem(i, DEPTH))
        return 0

    lax.fori_loop(start, turns, turn, 0)


def add_pairs(i, owner, one, into):
    groups = TURN // GROUP
    for g in range(0, groups, 2):
        added = [one(g), one(g + 1)]
        for k in range(2):
            into[owner[0, i * groups + g + k]] += added[k]


def forward_kernel(n, scale, span, marks, lists, owner, weight, bias, cotangent, dense, *refs):
    pieces, refs = refs[:n], refs[n:]
    output, turned, local, totals, feat, proj, dbuf, piece_sems, sems = refs
    copies = fetch(pieces, feat, piece_sems)
    size, _, width = pieces[0].shape
    batch = 8 if size % 8 == 0 else 1

    def project(t, _):
        spot = pl.ds(t * batch, batch)
        held = feat[spot].reshape(batch * 128, width)
        low = jnp.dot(held, weight[...], preferred_element_type=jnp.float32)
        proj[spot] = low.astype(jnp.bfloat16).reshape(batch, 128, width)
        return 0

    def prepare():
        totals[...] = jnp.zeros_like(totals)
        for i, copy in enumerate(copies):
            copy.wait()
            lax.fori_loop(i * size // batch, (i + 1) * size // batch, project, 0)

    def product(i, slot):
        def one(g):
            spots = [lists[1, i * TURN + g * GROUP + u] for u in range(GROUP)]
            left = jnp.concatenate([dbuf[slot, g * GROUP + u] for u in range(GROUP)], axis=1)
            right = jnp.concatenate(
                [jnp.concatenate([proj[c], feat[c]], axis=1) for c in spots], axis=0
            )
            return jnp.dot(left, right, preferred_element_type=jnp.float32)

        add_pairs(i, owner, one, totals)

    read_dense(marks[0, span[0]], marks[0, span[1]], dense, dbuf, sems, product, prepare)

    weight_sum, bias_sum = 0.0, 0.0
    for q in range(totals.shape[0]):
        lines = pl.ds(q * 128, 128)
        pre = totals[q, :, :width] + bias[...]
        output[lines, :] = jnp.maximum(pre, 0.0).astype(jnp.bfloat16)
        grad = jnp.where(pre > 0, cotangent[lines, :].astype(jnp.float32), 0.0)
        turned[q] = grad.T.astype(jnp.bfloat16)
        weight_sum += lax.dot_general(
            totals[q, :, width:].astype(jnp.bfloat16),
            grad.astype(jnp.bfloat16),
            (((0,), (0,)), ((), ())),
            preferred_element_type=jnp.float32,
        )
        bias_sum += jnp.sum(grad, axis=0, keepdims=True)
    local[pl.ds(0, width), :] = weight_sum * scale
    local[pl.ds(width, 8), :] = jnp.broadcast_to(bias_sum * scale, (8, width))


def tile_kernel(meta, order, dst, col, codes, panel, totals):
    rows = tile_rows()
    totals[...] = jnp.zeros_like(totals)

    def turn(i, _):
        lines = [codes[pl.ds(order[i * GROUP + u], 1), :] for u in range(GROUP)]
        for u, block in enumerate(blocks_of(lines, rows)):
            p = i * GROUP + u
            totals[dst[p]] += jnp.dot(block, panel[col[p]], preferred_element_type=jnp.float32)
        return 0

    lax.fori_loop(0, meta[0], turn, 0)


def backward_kernel(n, span, marks, lists, owner, before, dense, *refs):
    pieces, (acc, grad, dbuf, piece_sems, sems) = refs[:n], refs[n:]
    copies = fetch(pieces, grad, piece_sems)

    def prepare():
        acc[...] = before[...]
        for copy in copies:
            copy.wait()

    def product(i, slot):
        def one(g):
            spots = [lists[1, i * TURN + g * GROUP + u] for u in range(GROUP)]
            left = jnp.concatenate([grad[c] for c in spots], axis=1)
            right = dbuf[slot, pl.ds(g * GROUP, GROUP)].reshape(GROUP * 128, 128)
            return jnp.dot(left, right, preferred_element_type=jnp.float32)

        add_pairs(i, owner, one, acc)

    read_dense(marks[0, span[0]], marks[0, span[1]], dense, dbuf, sems, product, prepare)


SMEM = pl.BlockSpec(memory_space=pltpu.SMEM)
VMEM = pl.BlockSpec(memory_space=pltpu.VMEM)
HBM = pl.BlockSpec(memory_space=pl.ANY)
PARAMS = pltpu.CompilerParams(vmem_limit_bytes=48 * 1024 * 1024)


def cost(slots, products):
    flops = 2 * slots * products * 128**3
    return pl.CostEstimate(flops=flops, bytes_accessed=slots * 128 * 128 * 2, transcendentals=0)


def run_tile(meta, order, dst, col, codes, panel, row_blocks):
    return pl.pallas_call(
        tile_kernel,
        out_shape=jax.ShapeDtypeStruct((row_blocks, 128, panel.shape[-1]), jnp.float32),
        in_specs=[SMEM] * 4 + [VMEM] * 2,
        out_specs=VMEM,
        compiler_params=PARAMS,
    )(meta, order, dst, col, codes, panel)


def run_pack(per, owners, count, brow, bcol, offs, wts):
    slots = brow.shape[1]
    return pl.pallas_call(
        functools.partial(pack_kernel, per, owners),
        out_shape=(
            jax.ShapeDtypeStruct((owners * (ROOM + SPARE), 128), jnp.int32),
            jax.ShapeDtypeStruct((slots + 8, 128), jnp.int32),
        ),
        in_specs=[SMEM] + [VMEM] * 4,
        out_specs=[VMEM] * 2,
        scratch_shapes=[
            pltpu.VMEM((1, slots), jnp.int32),
            pltpu.SMEM((1, slots), jnp.int32),
            pltpu.SemaphoreType.DMA,
        ],
        compiler_params=PARAMS,
    )(count, brow, bcol, offs, wts)


def run_build(span, listed, codes, after, dense):
    lists, _, marks = listed
    others = after if dense is None else after + [dense]
    return pl.pallas_call(
        functools.partial(build_kernel, span),
        out_shape=jax.ShapeDtypeStruct((lists.shape[1], 128, 128), jnp.bfloat16),
        in_specs=[SMEM] * 2 + [VMEM] + [HBM] * len(others),
        out_specs=HBM,
        scratch_shapes=[
            pltpu.VMEM((DEPTH, TURN, 128, 128), jnp.bfloat16),
            pltpu.SemaphoreType.DMA((DEPTH,)),
        ],
        input_output_aliases={} if dense is None else {2 + len(others): 0},
        compiler_params=PARAMS,
        cost_estimate=cost(lists.shape[1], 2),
    )(marks, lists, codes, *others)


def run_forward(scale, span, listed, weight, bias, cotangent, dense, feat):
    lists, owner, marks = listed
    n = len(feat)
    size, _, width = feat[0].shape
    row_blocks = cotangent.shape[0] // 128
    return pl.pallas_call(
        functools.partial(forward_kernel, n, scale, span),
        out_shape=(
            jax.ShapeDtypeStruct(cotangent.shape, jnp.bfloat16),
            jax.ShapeDtypeStruct((row_blocks, width, 128), jnp.bfloat16),
            jax.ShapeDtypeStruct((width + 8, width), jnp.float32),
        ),
        in_specs=[SMEM] * 3 + [VMEM] * 3 + [HBM] * (n + 1),
        out_specs=[VMEM] * 3,
        scratch_shapes=[
            pltpu.VMEM((row_blocks, 128, 2 * width), jnp.float32),
            pltpu.VMEM((n * size, 128, width), jnp.bfloat16),
            pltpu.VMEM((n * size, 128, width), jnp.bfloat16),
            pltpu.VMEM((DEPTH, TURN, 128, 128), jnp.bfloat16),
            pltpu.SemaphoreType.DMA((n,)),
            pltpu.SemaphoreType.DMA((DEPTH,)),
        ],
        compiler_params=PARAMS,
        cost_estimate=cost(lists.shape[1], 4),
    )(marks, lists, owner, weight, bias, cotangent, dense, *feat)


def run_backward(span, listed, before, dense, pieces):
    lists, owner, marks = listed
    n = len(pieces)
    size, width, _ = pieces[0].shape
    return pl.pallas_call(
        functools.partial(backward_kernel, n, span),
        out_shape=jax.ShapeDtypeStruct(before.shape, jnp.float32),
        in_specs=[SMEM] * 3 + [VMEM] + [HBM] * (n + 1),
        out_specs=VMEM,
        scratch_shapes=[
            pltpu.VMEM((n * size, width, 128), jnp.bfloat16),
            pltpu.VMEM((DEPTH, TURN, 128, 128), jnp.bfloat16),
            pltpu.SemaphoreType.DMA((n,)),
            pltpu.SemaphoreType.DMA((DEPTH,)),
        ],
        compiler_params=PARAMS,
        cost_estimate=cost(lists.shape[1], 4),
    )(marks, lists, owner, before, dense, *pieces)


def list_kernel(keys, split, fills, key_ref, *refs):
    value_refs, (lists, owner_ref, marks_ref) = refs[: len(fills)], refs[len(fills) :]
    n, length = key_ref.shape[1], lists.shape[1]
    key = key_ref[...].astype(jnp.float32)
    rank = ranks(key)

    rows = -(-keys // 8) * 8
    names = lax.broadcasted_iota(jnp.int32, (rows, n), 0).astype(jnp.float32)
    name = lax.broadcasted_iota(jnp.int32, (rows, 1), 0).astype(jnp.float32)
    counts = jnp.sum(jnp.where(names == key, 1.0, 0.0), axis=1, keepdims=True)
    filled = jnp.where(name < keys, jnp.floor((counts + (GROUP - 1)) * (1.0 / GROUP)) * GROUP, 0.0)
    below = jnp.sum(jnp.where(name < split, filled, 0.0), axis=0, keepdims=True)
    first = jnp.floor((below + (TURN - 1)) * (1.0 / TURN))
    filled = filled + jnp.where(name == split - 1, first * TURN - below, 0.0)
    turns = jnp.floor((jnp.sum(filled, axis=0, keepdims=True) + (TURN - 1)) * (1.0 / TURN))
    base = jnp.sum(jnp.where(names < key, filled, 0.0), axis=0, keepdims=True)
    pos_column = column(jnp.where(key < keys, base + rank, -1.0))

    spots = lax.broadcasted_iota(jnp.int32, (1, length), 1).astype(jnp.float32)
    columns = [column(ref[...].astype(jnp.float32)) for ref in value_refs]
    sums = [jnp.zeros((1, length), jnp.float32) for _ in fills]
    for t in range(0, n, 128):
        hit = pos_column[t : t + 128] == spots
        for k, fill in enumerate(fills):
            value = columns[k][t : t + 128] - fill
            sums[k] += jnp.sum(jnp.where(hit, value, 0.0), axis=0, keepdims=True)
    for k, fill in enumerate(fills):
        lists[pl.ds(k, 1), :] = (sums[k] + fill).astype(jnp.int32)

    other = lax.broadcasted_iota(jnp.int32, (rows, 128), 1).astype(jnp.float32)
    ends = column(jnp.sum(jnp.where(name <= other, filled, 0.0), axis=0, keepdims=True))[:rows]
    starts = lax.broadcasted_iota(jnp.int32, owner_ref.shape, 1).astype(jnp.float32) * GROUP
    passed = (ends <= starts) & (name < keys)
    owner = jnp.sum(jnp.where(passed, 1.0, 0.0), axis=0, keepdims=True)
    owner = jnp.minimum(owner, keys - 1.0)
    owner_ref[...] = jnp.where(owner >= split, owner - split, owner).astype(jnp.int32)

    spot = lax.broadcasted_iota(jnp.int32, (1, 128), 1)
    marks = jnp.where(spot == FIRST, first, 0.0)
    for k in range(1, 5):
        marks = jnp.where(spot == FIRST + k, jnp.floor(turns * (k / 4)), marks)
    marks_ref[...] = marks.astype(jnp.int32)


FIRST = 1
QUARTERS = [0, 2, 3, 4, 5]


def make_lists(key, values, fills, keys, split):
    n = key.size
    length = (-(-(n + keys * GROUP) // TURN) + 1) * TURN
    groups = -(-length // GROUP // 128) * 128
    lists, owner, marks = pl.pallas_call(
        functools.partial(list_kernel, keys, split, fills),
        out_shape=(
            jax.ShapeDtypeStruct((len(fills), length), jnp.int32),
            jax.ShapeDtypeStruct((1, groups), jnp.int32),
            jax.ShapeDtypeStruct((1, 128), jnp.int32),
        ),
        in_specs=[VMEM] * (1 + len(fills)),
        out_specs=[VMEM] * 3,
        compiler_params=PARAMS,
        cost_estimate=cost(32, 2),
    )(key.reshape(1, n), *[value.reshape(1, n) for value in values])
    return lists, owner, marks


def place(pos, value, length, fill):
    spots = jnp.arange(length, dtype=jnp.int32)
    hit = pos[:, None] == spots[None, :]
    return jnp.sum(jnp.where(hit, value[:, None] - fill, 0), axis=0) + fill


def shards(
    features,
    weight,
    bias,
    cotangent,
    block_count,
    block_rows,
    block_cols,
    edge_offsets,
    edge_weight,
):
    node_dev, width = features.shape
    n_row = lax.axis_size("row")
    n_col = lax.axis_size("col")
    slots = block_rows.shape[2]
    count = block_count[0, 0]
    mine = lax.axis_index("col")
    mine_row = lax.axis_index("row")
    per = node_dev // 128
    row_blocks = per * n_col
    col_blocks = per * n_row
    scale = (node_dev * n_row * n_col) ** (-0.5)
    by_owner = n_row * n_col * node_dev * width * 2 <= 8 * 1024 * 1024
    by_owner = by_owner and col_blocks <= COLS and per * COLS < 256 and n_col % 8 == 0

    brow = block_rows[0, 0]
    bcol = block_cols[0, 0]
    ids = jnp.arange(slots, dtype=jnp.int32)
    live = ids < count
    packed, codes = run_pack(
        per, n_col, block_count, block_rows[0], block_cols[0], edge_offsets[0, 0], edge_weight[0, 0]
    )
    home = brow // per
    turns_plain = ((count + GROUP - 1) // GROUP).reshape(1)

    def tile_plan():
        wide = lax.all_gather(features, "row", axis=0, tiled=True)
        low = jnp.dot(wide, weight, preferred_element_type=jnp.float32).astype(jnp.bfloat16)
        panel = jnp.concatenate([low, wide], axis=1).reshape(col_blocks, 128, 2 * width)
        order = jnp.where(live, ids, slots)
        dst = jnp.where(live, (home ^ mine) * per + brow % per, 0)
        totals = run_tile(turns_plain, order, dst, bcol, codes, panel, row_blocks)
        own = scatter_sum(totals.reshape(n_col, node_dev, 2 * width), "col")
        pre = own[:, :width] + bias
        output = jnp.maximum(pre, 0.0).astype(jnp.bfloat16)
        grad = jnp.where(pre > 0, cotangent.astype(jnp.float32), 0.0)
        turned = jnp.swapaxes(grad.astype(jnp.bfloat16).reshape(per, 128, width), 1, 2)
        weight_sum = lax.dot_general(
            own[:, width:].astype(jnp.bfloat16),
            grad.astype(jnp.bfloat16),
            (((0,), (0,)), ((), ())),
            preferred_element_type=jnp.float32,
        )
        bias_sum = jnp.broadcast_to(jnp.sum(grad, axis=0), (8, width))
        return output, turned, jnp.concatenate([weight_sum, bias_sum], axis=0) * scale

    source = piece_index(per, home ^ mine, brow % per)
    unit = row_blocks // (2 * len(part_orders(per)))
    late = source // unit % 2
    source = source // (2 * unit) * unit + source % unit
    back_key = jnp.where(live, late * col_blocks + bcol, 2 * col_blocks)
    state = {"dense": None}

    def list_backward(key, value):
        return make_lists(key, [ids, value], [slots, 0], 2 * col_blocks, col_blocks)

    def build(held, start, end):
        span = (QUARTERS[start], QUARTERS[end])
        state["dense"] = run_build(span, state["back"], codes, held, state["dense"])

    if by_owner:
        stride = ROOM + SPARE
        came = lax.all_to_all(
            packed.reshape(n_col, stride, 128), "col", split_axis=0, concat_axis=0, tiled=True
        )
        spread = jnp.max(came[:, ROOM, ROOM:], axis=0)[None]
        for bit in bits_of("row"):
            spread = spread + swap(spread, "row", bit)
        any_over = jnp.max(spread, axis=1)

        got = came[:, ROOM, :ROOM]
        sources = jnp.arange(n_col, dtype=jnp.int32)[:, None]
        places = jnp.arange(ROOM, dtype=jnp.int32)[None, :]
        row_here = ((got - 1) // COLS).reshape(-1)
        col_there = (got - 1) % COLS
        col_there = piece_index(
            per, sources ^ mine, col_there % per, (col_there // per) ^ mine_row, n_row
        )
        line = sources * stride + places
        listed = make_lists(
            jnp.where(got > 0, row_here.reshape(got.shape), per),
            [jnp.broadcast_to(line, got.shape), col_there],
            [ROOM + 1, 0],
            per,
            per,
        )

        def prepare(step, held):
            if step == 0:
                held, inputs = lax.optimization_barrier((held, (back_key, source)))
                state["back"] = list_backward(*inputs)
                build(held, 0, 2)
            if step == 1:
                held, state["dense"] = lax.optimization_barrier((held, state["dense"]))
            return held

        pairs = gather_pieces(features.reshape(per, 128, width), prepare)
        lines = came.reshape(n_col * stride, 128)
        here = run_build((0, QUARTERS[4]), listed, lines, [], None)
        last, here = lax.optimization_barrier(([pair[1] for pair in pairs], here))
        feat = []
        for pair in [[pair[0], x] for pair, x in zip(pairs, last)]:
            rows = [pair]
            for bit in bits_of("row"):
                rows = rows + [[swap(x, "row", bit) for x in pair] for pair in rows]
            feat += [x for pair in rows for x in pair]
        done = run_forward(
            scale, (0, QUARTERS[4]), listed, weight, bias[None], cotangent, here, feat
        )
        done = lax.cond(any_over[0] > 0, tile_plan, lambda: tuple(done))
    else:
        state["back"] = list_backward(back_key, source)
        build([features], 0, 2)
        done = tile_plan()

    output, turned, total = done
    turned = with_layout_constraint(turned, Layout(major_to_minor=(0, 1, 2)))
    steps = bits_of("col")

    def add_total():
        state["total"] = state["total"] + swap(state["total"], "col", steps.pop(0))

    def beside(step, held):
        held, state["total"], state["dense"] = lax.optimization_barrier(
            (held, state["total"], state["dense"])
        )
        if steps:
            add_total()
        if step == 1:
            add_products(0, held)
        return held

    def add_products(half, pieces):
        pieces = [x.reshape((-1,) + x.shape[2:]) if x.ndim == 4 else x for x in pieces]
        state["acc"] = run_backward(
            [(0, FIRST), (FIRST, QUARTERS[4])][half], state["back"], state["acc"], state["dense"], pieces
        )

    state["acc"] = jnp.zeros((col_blocks, width, 128), jnp.float32)
    state["total"] = split_rows(total)
    while len(steps) > 3:
        add_total()
    build([turned], 2, 4)
    if len(steps) > 2:
        state["dense"], state["total"] = lax.optimization_barrier(
            (state["dense"], state["total"])
        )
        add_total()
    grad = gather_pieces(turned, beside)
    late_pieces, state["total"] = lax.optimization_barrier(
        ([pair[1] for pair in grad], state["total"])
    )
    while steps:
        add_total()
    total = join_rows(state["total"])
    add_products(1, late_pieces)
    acc = state["acc"]
    back = jnp.swapaxes(acc, 1, 2).reshape(col_blocks * 128, width)
    grad_proj = scatter_sum(
        jnp.stack(
            [
                lax.dynamic_slice_in_dim(back, (mine_row ^ k) * node_dev, node_dev, 0)
                for k in range(n_row)
            ]
        ),
        "row",
    ).astype(jnp.bfloat16)
    grad_features = lax.dot_general(
        grad_proj, weight, (((1,), (1,)), ((), ())), preferred_element_type=jnp.float32
    ).astype(jnp.bfloat16)
    return (
        output,
        grad_features,
        total[: weight.shape[0]],
        total[weight.shape[0]],
    )


def solution(mesh):
    return jax.shard_map(
        shards,
        mesh=mesh,
        in_specs=(
            P(("row", "col"), None),
            P(),
            P(),
            P(("row", "col"), None),
            P("row", "col"),
            P("row", "col", None),
            P("row", "col", None),
            P("row", "col", None, None),
            P("row", "col", None, None),
        ),
        out_specs=(P(("row", "col"), None), P(("row", "col"), None), P(), P()),
        check_vma=False,
    )
```

```python
import functools
import functools
import jax
import jax.numpy as jnp
from jax import lax
from jax.experimental import pallas as pl
from jax.experimental.pallas import tpu as pltpu
from jax.experimental.layout import Layout, with_layout_constraint
from jax.sharding import PartitionSpec as P


def swap(x, axis, bit):
    n = lax.axis_size(axis)
    return lax.ppermute(x, axis, [(i, i ^ bit) for i in range(n)])


def bits_of(axis):
    n = lax.axis_size(axis)
    return [1 << k for k in range(n.bit_length() - 1)]


def scatter_sum(x, axis):
    for bit in bits_of(axis):
        pairs = x.reshape((x.shape[0] // 2, 2) + x.shape[1:])
        x = pairs[:, 0] + swap(pairs[:, 1], axis, bit)
    return x[0]


def part_orders(per):
    bits = bits_of("col")[::-1]
    turned = bits[:-2] + bits[-1:] + bits[-2:-1]
    return [bits, turned] if per % 2 == 0 and len(bits) > 1 else [bits]


def gather_pieces(blocks, beside):
    orders = part_orders(blocks.shape[0])
    size = blocks.shape[0] // len(orders)
    near = [0]
    for bit in orders[0][:-2]:
        near = near + [far | bit for far in near]
    whole = [blocks if far == 0 else swap(blocks, "col", far) for far in near]
    (whole,) = beside(0, [jnp.stack(whole)])
    held = [whole[:, i * size : (i + 1) * size] for i in range(len(orders))]
    if len(orders[0]) > 1:
        came = [swap(x, "col", order[-2]) for x, order in zip(held, orders)]
        held = beside(1, [jnp.concatenate([x, y], axis=0) for x, y in zip(held, came)])
    came = [swap(x, "col", order[-1]) for x, order in zip(held, orders)]
    shape = (-1,) + blocks.shape[1:]
    return [[x.reshape(shape), y.reshape(shape)] for x, y in zip(held, came)]


def piece_index(per, far, block, rho=0, n_row=1):
    orders = part_orders(per)
    size = per // len(orders)
    half = lax.axis_size("col") // 2
    result = 0
    for i, order in enumerate(orders):
        spot = sum(((far & bit) > 0).astype(jnp.int32) << t for t, bit in enumerate(order))
        piece = (i * n_row + rho) * 2 + spot // half
        here = (piece * half + spot % half) * size + block % size
        result = jnp.where(block // size == i, here, result)
    return result


def split_rows(x):
    n, mine = lax.axis_size("row"), lax.axis_index("row")
    size = -(-x.shape[0] // (8 * n)) * 8
    x = jnp.pad(x, ((0, n * size - x.shape[0]), (0, 0)))
    parts = [lax.dynamic_slice_in_dim(x, (mine ^ k) * size, size, 0) for k in range(n)]
    return scatter_sum(jnp.stack(parts), "row")


def join_rows(x):
    n, mine = lax.axis_size("row"), lax.axis_index("row")
    parts = [x]
    for bit in bits_of("row"):
        parts = parts + [swap(part, "row", bit) for part in parts]
    parts = jnp.stack(parts)
    return jnp.concatenate(
        [lax.dynamic_index_in_dim(parts, mine ^ k, 0, keepdims=False) for k in range(n)]
    )


GROUP = 8
TURN = 4 * GROUP
DEPTH = 5
ROOM = 64
SPARE = 8
FIELD = 1 << 16
UNIT = 2.0**-14
COLS = 32


def tile_rows():
    shape = (8, 16, 128)
    rows = 16 * lax.broadcasted_iota(jnp.int32, shape, 0) + lax.broadcasted_iota(jnp.int32, shape, 1)
    return rows.astype(jnp.float32).astype(jnp.bfloat16)


def blocks_of(lines, rows):
    zero = jnp.zeros((), jnp.bfloat16)
    one = jnp.ones((), jnp.bfloat16)
    empty = jnp.zeros((128, 128), jnp.bfloat16)

    def tile(x):
        return jnp.broadcast_to(x.astype(jnp.float32), (16, 128)).astype(jnp.bfloat16)[None]

    def factors(code):
        o = code >> 16
        w = tile((code & (FIELD - 1)).astype(jnp.float32) * UNIT)
        left = jnp.where(rows == tile(o >> 7), w, zero).reshape(128, 128)
        right = jnp.where(rows == tile(o & 127), one, zero).reshape(128, 128)
        return left, right

    blocks = []
    for u in range(0, len(lines), 2):
        (left, right), (left_too, right_too) = factors(lines[u]), factors(lines[u + 1])
        both = lax.dot_general(
            jnp.concatenate([left, left_too], axis=1),
            jnp.concatenate(
                [
                    jnp.concatenate([right, empty], axis=1),
                    jnp.concatenate([empty, right_too], axis=1),
                ],
                axis=0,
            ),
            (((1,), (1,)), ((), ())),
            preferred_element_type=jnp.float32,
        ).astype(jnp.bfloat16)
        blocks += [both[:, :128], both[:, 128:]]
    return blocks


def column(row):
    return jnp.broadcast_to(row, (8, row.shape[1])).T[:, :1]


def ranks(key):
    n = key.shape[1]
    key_column = column(key)
    lanes = lax.broadcasted_iota(jnp.int32, (128, n), 1)
    lines = lax.broadcasted_iota(jnp.int32, (128, n), 0)
    rank = jnp.zeros((1, n), jnp.float32)
    for t in range(0, n, 128):
        before = (key_column[t : t + 128] == key) & (lines + t < lanes)
        rank += jnp.sum(jnp.where(before, 1.0, 0.0), axis=0, keepdims=True)
    return rank


def pack_kernel(
    per, owners, count, brow, bcol, offs_in, wts_in, out, codes, offs, wts, pos_row, pos, sems
):
    slots, width = offs.shape
    reads = [
        pltpu.make_async_copy(offs_in, offs, sems.at[0]),
        pltpu.make_async_copy(wts_in, wts, sems.at[1]),
    ]
    for read in reads:
        read.start()
    stride = ROOM + SPARE
    lanes = lax.broadcasted_iota(jnp.int32, (1, slots), 1)
    live = lanes < count[0, 0]
    row = brow[...].astype(jnp.float32)
    home = jnp.floor((row + 0.5) * (1.0 / per))
    key = jnp.where(live, home, float(owners))
    rank = ranks(key)
    fits = live & (rank < ROOM)
    trash = float(ROOM + SPARE - 1)
    pos_row[...] = jnp.where(fits, home * stride + rank, trash).astype(jnp.int32)
    copy = pltpu.make_async_copy(pos_row, pos, sems.at[2])
    copy.start()

    out[...] = jnp.zeros_like(out)
    label = 1.0 + (row - per * home) * COLS + bcol[...].astype(jnp.float32)
    names = lax.broadcasted_iota(jnp.int32, (owners, slots), 0).astype(jnp.float32)
    chosen = jnp.where((names == key) & fits, label, 0.0).astype(jnp.bfloat16)
    spots = lax.broadcasted_iota(jnp.int32, (1, 128), 1)
    placed = jnp.where(column(rank) == spots.astype(jnp.float32), 1.0, 0.0).astype(jnp.bfloat16)
    labels = jnp.dot(chosen, placed, preferred_element_type=jnp.float32)
    over = jnp.max(jnp.where(live, rank, 0.0), axis=1, keepdims=True)
    labels = jnp.where(spots < ROOM, labels, jnp.where(over < ROOM, 0.0, 1.0)).astype(jnp.int32)
    for k in range(owners):
        out[pl.ds(k * stride + ROOM, 1), :] = labels[k : k + 1]
    for read in reads:
        read.wait()
    codes[pl.ds(0, slots), :] = offs[...] * FIELD + (
        wts[...].astype(jnp.float32) * (1.0 / UNIT)
    ).astype(jnp.int32)
    codes[pl.ds(slots, 8), :] = jnp.zeros((8, width), jnp.int32)
    copy.wait()

    def turn(i, _):
        for u in range(GROUP):
            s = i * GROUP + u
            out[pl.ds(pos[0, s], 1), :] = codes[pl.ds(s, 1), :]
        return 0

    lax.fori_loop(0, (count[0, 0] + GROUP - 1) // GROUP, turn, 0)


def build_kernel(span, marks, lists, codes, *refs):
    dense, dbuf, sems = refs[-3:]
    start, turns = marks[0, span[0]], marks[0, span[1]]
    rows = tile_rows()

    def out_copy(i):
        slot = lax.rem(i, DEPTH)
        return pltpu.make_async_copy(
            dbuf.at[slot], dense.at[pl.ds(i * TURN, TURN)], sems.at[slot]
        )

    def turn(i, _):
        slot = lax.rem(i, DEPTH)

        @pl.when(i >= start + DEPTH)
        def _():
            out_copy(i - DEPTH).wait()

        lines = [codes[pl.ds(lists[0, i * TURN + u], 1), :] for u in range(TURN)]
        for u in range(0, TURN, GROUP):
            blocks = blocks_of(lines[u : u + GROUP], rows)
            for k, block in enumerate(blocks):
                dbuf[slot, u + k] = block
        out_copy(i).start()
        return 0

    lax.fori_loop(start, turns, turn, 0)

    def finish(i, _):
        out_copy(i).wait()
        return 0

    lax.fori_loop(jnp.maximum(turns - DEPTH, start), turns, finish, 0)


def fetch(pieces, into, sems):
    size = pieces[0].shape[0]
    copies = [
        pltpu.make_async_copy(piece, into.at[pl.ds(i * size, size)], sems.at[i])
        for i, piece in enumerate(pieces)
    ]
    for copy in copies:
        copy.start()
    return copies


def read_dense(start, turns, dense, dbuf, sems, product, prepare):
    def in_copy(i):
        slot = lax.rem(i, DEPTH)
        return pltpu.make_async_copy(
            dense.at[pl.ds(i * TURN, TURN)], dbuf.at[slot], sems.at[slot]
        )

    def begin(i, _):
        in_copy(i).start()
        return 0

    lax.fori_loop(start, jnp.minimum(turns, start + DEPTH - 1), begin, 0)
    prepare()

    def turn(i, _):
        @pl.when(i + DEPTH - 1 < turns)
        def _():
            in_copy(i + DEPTH - 1).start()

        in_copy(i).wait()
        product(i, lax.rem(i, DEPTH))
        return 0

    lax.fori_loop(start, turns, turn, 0)


def add_pairs(i, owner, one, into):
    groups = TURN // GROUP
    for g in range(0, groups, 2):
        added = [one(g), one(g + 1)]
        for k in range(2):
            into[owner[0, i * groups + g + k]] += added[k]


def forward_kernel(n, scale, span, marks, lists, owner, weight, bias, cotangent, dense, *refs):
    pieces, refs = refs[:n], refs[n:]
    output, turned, local, totals, feat, proj, dbuf, piece_sems, sems = refs
    copies = fetch(pieces, feat, piece_sems)
    size, _, width = pieces[0].shape
    batch = 8 if size % 8 == 0 else 1

    def project(t, _):
        spot = pl.ds(t * batch, batch)
        held = feat[spot].reshape(batch * 128, width)
        low = jnp.dot(held, weight[...], preferred_element_type=jnp.float32)
        proj[spot] = low.astype(jnp.bfloat16).reshape(batch, 128, width)
        return 0

    def prepare():
        totals[...] = jnp.zeros_like(totals)
        for i, copy in enumerate(copies):
            copy.wait()
            lax.fori_loop(i * size // batch, (i + 1) * size // batch, project, 0)

    def product(i, slot):
        def one(g):
            spots = [lists[1, i * TURN + g * GROUP + u] for u in range(GROUP)]
            left = jnp.concatenate([dbuf[slot, g * GROUP + u] for u in range(GROUP)], axis=1)
            right = jnp.concatenate(
                [jnp.concatenate([proj[c], feat[c]], axis=1) for c in spots], axis=0
            )
            return jnp.dot(left, right, preferred_element_type=jnp.float32)

        add_pairs(i, owner, one, totals)

    read_dense(marks[0, span[0]], marks[0, span[1]], dense, dbuf, sems, product, prepare)

    weight_sum, bias_sum = 0.0, 0.0
    for q in range(totals.shape[0]):
        lines = pl.ds(q * 128, 128)
        pre = totals[q, :, :width] + bias[...]
        output[lines, :] = jnp.maximum(pre, 0.0).astype(jnp.bfloat16)
        grad = jnp.where(pre > 0, cotangent[lines, :].astype(jnp.float32), 0.0)
        turned[q] = grad.T.astype(jnp.bfloat16)
        weight_sum += lax.dot_general(
            totals[q, :, width:].astype(jnp.bfloat16),
            grad.astype(jnp.bfloat16),
            (((0,), (0,)), ((), ())),
            preferred_element_type=jnp.float32,
        )
        bias_sum += jnp.sum(grad, axis=0, keepdims=True)
    local[pl.ds(0, width), :] = weight_sum * scale
    local[pl.ds(width, 8), :] = jnp.broadcast_to(bias_sum * scale, (8, width))


def tile_kernel(meta, order, dst, col, codes, panel, totals):
    rows = tile_rows()
    totals[...] = jnp.zeros_like(totals)

    def turn(i, _):
        lines = [codes[pl.ds(order[i * GROUP + u], 1), :] for u in range(GROUP)]
        for u, block in enumerate(blocks_of(lines, rows)):
            p = i * GROUP + u
            totals[dst[p]] += jnp.dot(block, panel[col[p]], preferred_element_type=jnp.float32)
        return 0

    lax.fori_loop(0, meta[0], turn, 0)


def backward_kernel(n, span, marks, lists, owner, before, dense, *refs):
    pieces, (acc, grad, dbuf, piece_sems, sems) = refs[:n], refs[n:]
    copies = fetch(pieces, grad, piece_sems)

    def prepare():
        acc[...] = before[...]
        for copy in copies:
            copy.wait()

    def product(i, slot):
        def one(g):
            spots = [lists[1, i * TURN + g * GROUP + u] for u in range(GROUP)]
            left = jnp.concatenate([grad[c] for c in spots], axis=1)
            right = dbuf[slot, pl.ds(g * GROUP, GROUP)].reshape(GROUP * 128, 128)
            return jnp.dot(left, right, preferred_element_type=jnp.float32)

        add_pairs(i, owner, one, acc)

    read_dense(marks[0, span[0]], marks[0, span[1]], dense, dbuf, sems, product, prepare)


SMEM = pl.BlockSpec(memory_space=pltpu.SMEM)
VMEM = pl.BlockSpec(memory_space=pltpu.VMEM)
HBM = pl.BlockSpec(memory_space=pl.ANY)
PARAMS = pltpu.CompilerParams(vmem_limit_bytes=48 * 1024 * 1024)


def cost(slots, products):
    flops = 2 * slots * products * 128**3
    return pl.CostEstimate(flops=flops, bytes_accessed=slots * 128 * 128 * 2, transcendentals=0)


def run_tile(meta, order, dst, col, codes, panel, row_blocks):
    return pl.pallas_call(
        tile_kernel,
        out_shape=jax.ShapeDtypeStruct((row_blocks, 128, panel.shape[-1]), jnp.float32),
        in_specs=[SMEM] * 4 + [VMEM] * 2,
        out_specs=VMEM,
        compiler_params=PARAMS,
    )(meta, order, dst, col, codes, panel)


def run_pack(per, owners, count, brow, bcol, offs, wts):
    slots = brow.shape[1]
    return pl.pallas_call(
        functools.partial(pack_kernel, per, owners),
        out_shape=(
            jax.ShapeDtypeStruct((owners * (ROOM + SPARE), 128), jnp.int32),
            jax.ShapeDtypeStruct((slots + 8, 128), jnp.int32),
        ),
        in_specs=[SMEM] + [VMEM] * 2 + [HBM] * 2,
        out_specs=[VMEM] * 2,
        scratch_shapes=[
            pltpu.VMEM(offs.shape, offs.dtype),
            pltpu.VMEM(wts.shape, wts.dtype),
            pltpu.VMEM((1, slots), jnp.int32),
            pltpu.SMEM((1, slots), jnp.int32),
            pltpu.SemaphoreType.DMA((3,)),
        ],
        compiler_params=PARAMS,
    )(count, brow, bcol, offs, wts)


def run_build(span, listed, codes, after, dense):
    lists, _, marks = listed
    others = after if dense is None else after + [dense]
    return pl.pallas_call(
        functools.partial(build_kernel, span),
        out_shape=jax.ShapeDtypeStruct((lists.shape[1], 128, 128), jnp.bfloat16),
        in_specs=[SMEM] * 2 + [VMEM] + [HBM] * len(others),
        out_specs=HBM,
        scratch_shapes=[
            pltpu.VMEM((DEPTH, TURN, 128, 128), jnp.bfloat16),
            pltpu.SemaphoreType.DMA((DEPTH,)),
        ],
        input_output_aliases={} if dense is None else {2 + len(others): 0},
        compiler_params=PARAMS,
        cost_estimate=cost(lists.shape[1], 2),
    )(marks, lists, codes, *others)


def run_forward(scale, span, listed, weight, bias, cotangent, dense, feat):
    lists, owner, marks = listed
    n = len(feat)
    size, _, width = feat[0].shape
    row_blocks = cotangent.shape[0] // 128
    return pl.pallas_call(
        functools.partial(forward_kernel, n, scale, span),
        out_shape=(
            jax.ShapeDtypeStruct(cotangent.shape, jnp.bfloat16),
            jax.ShapeDtypeStruct((row_blocks, width, 128), jnp.bfloat16),
            jax.ShapeDtypeStruct((width + 8, width), jnp.float32),
        ),
        in_specs=[SMEM] * 3 + [VMEM] * 3 + [HBM] * (n + 1),
        out_specs=[VMEM] * 3,
        scratch_shapes=[
            pltpu.VMEM((row_blocks, 128, 2 * width), jnp.float32),
            pltpu.VMEM((n * size, 128, width), jnp.bfloat16),
            pltpu.VMEM((n * size, 128, width), jnp.bfloat16),
            pltpu.VMEM((DEPTH, TURN, 128, 128), jnp.bfloat16),
            pltpu.SemaphoreType.DMA((n,)),
            pltpu.SemaphoreType.DMA((DEPTH,)),
        ],
        compiler_params=PARAMS,
        cost_estimate=cost(lists.shape[1], 4),
    )(marks, lists, owner, weight, bias, cotangent, dense, *feat)


def run_backward(span, listed, before, dense, pieces):
    lists, owner, marks = listed
    n = len(pieces)
    size, width, _ = pieces[0].shape
    return pl.pallas_call(
        functools.partial(backward_kernel, n, span),
        out_shape=jax.ShapeDtypeStruct(before.shape, jnp.float32),
        in_specs=[SMEM] * 3 + [VMEM] + [HBM] * (n + 1),
        out_specs=VMEM,
        scratch_shapes=[
            pltpu.VMEM((n * size, width, 128), jnp.bfloat16),
            pltpu.VMEM((DEPTH, TURN, 128, 128), jnp.bfloat16),
            pltpu.SemaphoreType.DMA((n,)),
            pltpu.SemaphoreType.DMA((DEPTH,)),
        ],
        compiler_params=PARAMS,
        cost_estimate=cost(lists.shape[1], 4),
    )(marks, lists, owner, before, dense, *pieces)


def list_kernel(keys, split, fills, key_ref, *refs):
    value_refs, (lists, owner_ref, marks_ref) = refs[: len(fills)], refs[len(fills) :]
    n, length = key_ref.shape[1], lists.shape[1]
    key = key_ref[...].astype(jnp.float32)
    rank = ranks(key)

    rows = -(-keys // 8) * 8
    names = lax.broadcasted_iota(jnp.int32, (rows, n), 0).astype(jnp.float32)
    name = lax.broadcasted_iota(jnp.int32, (rows, 1), 0).astype(jnp.float32)
    counts = jnp.sum(jnp.where(names == key, 1.0, 0.0), axis=1, keepdims=True)
    filled = jnp.where(name < keys, jnp.floor((counts + (GROUP - 1)) * (1.0 / GROUP)) * GROUP, 0.0)
    below = jnp.sum(jnp.where(name < split, filled, 0.0), axis=0, keepdims=True)
    first = jnp.floor((below + (TURN - 1)) * (1.0 / TURN))
    filled = filled + jnp.where(name == split - 1, first * TURN - below, 0.0)
    turns = jnp.floor((jnp.sum(filled, axis=0, keepdims=True) + (TURN - 1)) * (1.0 / TURN))
    base = jnp.sum(jnp.where(names < key, filled, 0.0), axis=0, keepdims=True)
    pos_column = column(jnp.where(key < keys, base + rank, -1.0))

    spots = lax.broadcasted_iota(jnp.int32, (1, length), 1).astype(jnp.float32)
    columns = [column(ref[...].astype(jnp.float32)) for ref in value_refs]
    sums = [jnp.zeros((1, length), jnp.float32) for _ in fills]
    for t in range(0, n, 128):
        hit = pos_column[t : t + 128] == spots
        for k, fill in enumerate(fills):
            value = columns[k][t : t + 128] - fill
            sums[k] += jnp.sum(jnp.where(hit, value, 0.0), axis=0, keepdims=True)
    for k, fill in enumerate(fills):
        lists[pl.ds(k, 1), :] = (sums[k] + fill).astype(jnp.int32)

    other = lax.broadcasted_iota(jnp.int32, (rows, 128), 1).astype(jnp.float32)
    ends = column(jnp.sum(jnp.where(name <= other, filled, 0.0), axis=0, keepdims=True))[:rows]
    starts = lax.broadcasted_iota(jnp.int32, owner_ref.shape, 1).astype(jnp.float32) * GROUP
    passed = (ends <= starts) & (name < keys)
    owner = jnp.sum(jnp.where(passed, 1.0, 0.0), axis=0, keepdims=True)
    owner = jnp.minimum(owner, keys - 1.0)
    owner_ref[...] = jnp.where(owner >= split, owner - split, owner).astype(jnp.int32)

    spot = lax.broadcasted_iota(jnp.int32, (1, 128), 1)
    marks = jnp.where(spot == FIRST, first, 0.0)
    for k in range(1, 5):
        marks = jnp.where(spot == FIRST + k, jnp.floor(turns * (k / 4)), marks)
    marks_ref[...] = marks.astype(jnp.int32)


FIRST = 1
QUARTERS = [0, 2, 3, 4, 5]


def make_lists(key, values, fills, keys, split):
    n = key.size
    length = (-(-(n + keys * GROUP) // TURN) + 1) * TURN
    groups = -(-length // GROUP // 128) * 128
    lists, owner, marks = pl.pallas_call(
        functools.partial(list_kernel, keys, split, fills),
        out_shape=(
            jax.ShapeDtypeStruct((len(fills), length), jnp.int32),
            jax.ShapeDtypeStruct((1, groups), jnp.int32),
            jax.ShapeDtypeStruct((1, 128), jnp.int32),
        ),
        in_specs=[VMEM] * (1 + len(fills)),
        out_specs=[VMEM] * 3,
        compiler_params=PARAMS,
        cost_estimate=cost(32, 2),
    )(key.reshape(1, n), *[value.reshape(1, n) for value in values])
    return lists, owner, marks


def place(pos, value, length, fill):
    spots = jnp.arange(length, dtype=jnp.int32)
    hit = pos[:, None] == spots[None, :]
    return jnp.sum(jnp.where(hit, value[:, None] - fill, 0), axis=0) + fill


def shards(
    features,
    weight,
    bias,
    cotangent,
    block_count,
    block_rows,
    block_cols,
    edge_offsets,
    edge_weight,
):
    node_dev, width = features.shape
    n_row = lax.axis_size("row")
    n_col = lax.axis_size("col")
    slots = block_rows.shape[2]
    count = block_count[0, 0]
    mine = lax.axis_index("col")
    mine_row = lax.axis_index("row")
    per = node_dev // 128
    row_blocks = per * n_col
    col_blocks = per * n_row
    scale = (node_dev * n_row * n_col) ** (-0.5)
    by_owner = n_row * n_col * node_dev * width * 2 <= 8 * 1024 * 1024
    by_owner = by_owner and col_blocks <= COLS and per * COLS < 256 and n_col % 8 == 0

    packed, codes = run_pack(
        per, n_col, block_count, block_rows[0], block_cols[0], edge_offsets[0, 0], edge_weight[0, 0]
    )

    def tile_plan():
        ids = jnp.arange(slots, dtype=jnp.int32)
        live = ids < count
        brow, bcol = block_rows[0, 0], block_cols[0, 0]
        home = brow // per
        turns_plain = ((count + GROUP - 1) // GROUP).reshape(1)
        wide = lax.all_gather(features, "row", axis=0, tiled=True)
        low = jnp.dot(wide, weight, preferred_element_type=jnp.float32).astype(jnp.bfloat16)
        panel = jnp.concatenate([low, wide], axis=1).reshape(col_blocks, 128, 2 * width)
        order = jnp.where(live, ids, slots)
        dst = jnp.where(live, (home ^ mine) * per + brow % per, 0)
        totals = run_tile(turns_plain, order, dst, bcol, codes, panel, row_blocks)
        own = scatter_sum(totals.reshape(n_col, node_dev, 2 * width), "col")
        pre = own[:, :width] + bias
        output = jnp.maximum(pre, 0.0).astype(jnp.bfloat16)
        grad = jnp.where(pre > 0, cotangent.astype(jnp.float32), 0.0)
        turned = jnp.swapaxes(grad.astype(jnp.bfloat16).reshape(per, 128, width), 1, 2)
        weight_sum = lax.dot_general(
            own[:, width:].astype(jnp.bfloat16),
            grad.astype(jnp.bfloat16),
            (((0,), (0,)), ((), ())),
            preferred_element_type=jnp.float32,
        )
        bias_sum = jnp.broadcast_to(jnp.sum(grad, axis=0), (8, width))
        return output, turned, jnp.concatenate([weight_sum, bias_sum], axis=0) * scale

    state = {"dense": None}

    def list_backward(count, brow, bcol):
        ids = jnp.arange(slots, dtype=jnp.int32)
        source = piece_index(per, (brow // per) ^ mine, brow % per)
        unit = row_blocks // (2 * len(part_orders(per)))
        late = source // unit % 2
        source = source // (2 * unit) * unit + source % unit
        key = jnp.where(ids < count, late * col_blocks + bcol, 2 * col_blocks)
        return make_lists(key, [ids, source], [slots, 0], 2 * col_blocks, col_blocks)

    slot_inputs = (count, block_rows[0, 0], block_cols[0, 0])

    def build(held, start, end):
        span = (QUARTERS[start], QUARTERS[end])
        state["dense"] = run_build(span, state["back"], codes, held, state["dense"])

    if by_owner:
        stride = ROOM + SPARE
        came = lax.all_to_all(
            packed.reshape(n_col, stride, 128), "col", split_axis=0, concat_axis=0, tiled=True
        )
        spread = jnp.max(came[:, ROOM, ROOM:], axis=0)[None]
        for bit in bits_of("row"):
            spread = spread + swap(spread, "row", bit)
        any_over = jnp.max(spread, axis=1)

        got = came[:, ROOM, :ROOM]
        sources = jnp.arange(n_col, dtype=jnp.int32)[:, None]
        places = jnp.arange(ROOM, dtype=jnp.int32)[None, :]
        row_here = ((got - 1) // COLS).reshape(-1)
        col_there = (got - 1) % COLS
        col_there = piece_index(
            per, sources ^ mine, col_there % per, (col_there // per) ^ mine_row, n_row
        )
        line = sources * stride + places
        listed = make_lists(
            jnp.where(got > 0, row_here.reshape(got.shape), per),
            [jnp.broadcast_to(line, got.shape), col_there],
            [ROOM + 1, 0],
            per,
            per,
        )

        def prepare(step, held):
            if step == 0:
                held, inputs = lax.optimization_barrier((held, slot_inputs))
                state["back"] = list_backward(*inputs)
                build(held, 0, 2)
            if step == 1:
                held, state["dense"] = lax.optimization_barrier((held, state["dense"]))
            return held

        pairs = gather_pieces(features.reshape(per, 128, width), prepare)
        lines = came.reshape(n_col * stride, 128)
        here = run_build((0, QUARTERS[4]), listed, lines, [], None)
        last, here = lax.optimization_barrier(([pair[1] for pair in pairs], here))
        feat = []
        for pair in [[pair[0], x] for pair, x in zip(pairs, last)]:
            rows = [pair]
            for bit in bits_of("row"):
                rows = rows + [[swap(x, "row", bit) for x in pair] for pair in rows]
            feat += [x for pair in rows for x in pair]
        done = run_forward(
            scale, (0, QUARTERS[4]), listed, weight, bias[None], cotangent, here, feat
        )
        done = lax.cond(any_over[0] > 0, tile_plan, lambda: tuple(done))
    else:
        state["back"] = list_backward(*slot_inputs)
        build([features], 0, 2)
        done = tile_plan()

    output, turned, total = done
    turned = with_layout_constraint(turned, Layout(major_to_minor=(0, 1, 2)))
    steps = bits_of("col")

    def add_total():
        state["total"] = state["total"] + swap(state["total"], "col", steps.pop(0))

    def beside(step, held):
        held, state["total"], state["dense"] = lax.optimization_barrier(
            (held, state["total"], state["dense"])
        )
        if steps:
            add_total()
        if step == 1:
            add_products(0, held)
        return held

    def add_products(half, pieces):
        pieces = [x.reshape((-1,) + x.shape[2:]) if x.ndim == 4 else x for x in pieces]
        state["acc"] = run_backward(
            [(0, FIRST), (FIRST, QUARTERS[4])][half], state["back"], state["acc"], state["dense"], pieces
        )

    state["acc"] = jnp.zeros((col_blocks, width, 128), jnp.float32)
    state["total"] = split_rows(total)
    while len(steps) > 3:
        add_total()
    build([turned], 2, 4)
    if len(steps) > 2:
        state["dense"], state["total"] = lax.optimization_barrier(
            (state["dense"], state["total"])
        )
        add_total()
    grad = gather_pieces(turned, beside)
    late_pieces, state["total"] = lax.optimization_barrier(
        ([pair[1] for pair in grad], state["total"])
    )
    while steps:
        add_total()
    total = join_rows(state["total"])
    add_products(1, late_pieces)
    acc = state["acc"]
    back = jnp.swapaxes(acc, 1, 2).reshape(col_blocks * 128, width)
    grad_proj = scatter_sum(
        jnp.stack(
            [
                lax.dynamic_slice_in_dim(back, (mine_row ^ k) * node_dev, node_dev, 0)
                for k in range(n_row)
            ]
        ),
        "row",
    ).astype(jnp.bfloat16)
    grad_features = lax.dot_general(
        grad_proj, weight, (((1,), (1,)), ((), ())), preferred_element_type=jnp.float32
    ).astype(jnp.bfloat16)
    return (
        output,
        grad_features,
        total[: weight.shape[0]],
        total[weight.shape[0]],
    )


def solution(mesh):
    return jax.shard_map(
        shards,
        mesh=mesh,
        in_specs=(
            P(("row", "col"), None),
            P(),
            P(),
            P(("row", "col"), None),
            P("row", "col"),
            P("row", "col", None),
            P("row", "col", None),
            P("row", "col", None, None),
            P("row", "col", None, None),
        ),
        out_specs=(P(("row", "col"), None), P(("row", "col"), None), P(), P()),
        check_vma=False,
    )
```

```python
import functools
import functools
import jax
import jax.numpy as jnp
from jax import lax
from jax.experimental import pallas as pl
from jax.experimental.pallas import tpu as pltpu
from jax.experimental.layout import Layout, with_layout_constraint
from jax.sharding import PartitionSpec as P


def swap(x, axis, bit):
    n = lax.axis_size(axis)
    return lax.ppermute(x, axis, [(i, i ^ bit) for i in range(n)])


def bits_of(axis):
    n = lax.axis_size(axis)
    return [1 << k for k in range(n.bit_length() - 1)]


def scatter_sum(x, axis):
    for bit in bits_of(axis):
        pairs = x.reshape((x.shape[0] // 2, 2) + x.shape[1:])
        x = pairs[:, 0] + swap(pairs[:, 1], axis, bit)
    return x[0]


def part_orders(per):
    bits = bits_of("col")[::-1]
    turned = bits[:-2] + bits[-1:] + bits[-2:-1]
    return [bits, turned] if per % 2 == 0 and len(bits) > 1 else [bits]


def gather_pieces(blocks, beside):
    orders = part_orders(blocks.shape[0])
    size = blocks.shape[0] // len(orders)
    near = [0]
    for bit in orders[0][:-2]:
        near = near + [far | bit for far in near]
    whole = [blocks if far == 0 else swap(blocks, "col", far) for far in near]
    (whole,) = beside(0, [jnp.stack(whole)])
    held = [whole[:, i * size : (i + 1) * size] for i in range(len(orders))]
    if len(orders[0]) > 1:
        came = [swap(x, "col", order[-2]) for x, order in zip(held, orders)]
        held = beside(1, [jnp.concatenate([x, y], axis=0) for x, y in zip(held, came)])
    came = [swap(x, "col", order[-1]) for x, order in zip(held, orders)]
    shape = (-1,) + blocks.shape[1:]
    return [[x.reshape(shape), y.reshape(shape)] for x, y in zip(held, came)]


def piece_index(per, far, block, rho=0, n_row=1):
    orders = part_orders(per)
    size = per // len(orders)
    half = lax.axis_size("col") // 2
    result = 0
    for i, order in enumerate(orders):
        spot = sum(((far & bit) > 0).astype(jnp.int32) << t for t, bit in enumerate(order))
        piece = (i * n_row + rho) * 2 + spot // half
        here = (piece * half + spot % half) * size + block % size
        result = jnp.where(block // size == i, here, result)
    return result


def split_rows(x):
    n, mine = lax.axis_size("row"), lax.axis_index("row")
    size = -(-x.shape[0] // (8 * n)) * 8
    x = jnp.pad(x, ((0, n * size - x.shape[0]), (0, 0)))
    parts = [lax.dynamic_slice_in_dim(x, (mine ^ k) * size, size, 0) for k in range(n)]
    return scatter_sum(jnp.stack(parts), "row")


def join_rows(x):
    n, mine = lax.axis_size("row"), lax.axis_index("row")
    parts = [x]
    for bit in bits_of("row"):
        parts = parts + [swap(part, "row", bit) for part in parts]
    parts = jnp.stack(parts)
    return jnp.concatenate(
        [lax.dynamic_index_in_dim(parts, mine ^ k, 0, keepdims=False) for k in range(n)]
    )


GROUP = 8
TURN = 4 * GROUP
DEPTH = 5
ROOM = 64
SPARE = 8
FIELD = 1 << 16
UNIT = 2.0**-14
COLS = 32


def tile_rows():
    shape = (8, 16, 128)
    rows = 16 * lax.broadcasted_iota(jnp.int32, shape, 0) + lax.broadcasted_iota(jnp.int32, shape, 1)
    return rows.astype(jnp.float32).astype(jnp.bfloat16)


def blocks_of(lines, rows):
    zero = jnp.zeros((), jnp.bfloat16)
    one = jnp.ones((), jnp.bfloat16)
    empty = jnp.zeros((128, 128), jnp.bfloat16)

    def tile(x):
        return jnp.broadcast_to(x.astype(jnp.float32), (16, 128)).astype(jnp.bfloat16)[None]

    def factors(code):
        o = code >> 16
        w = tile((code & (FIELD - 1)).astype(jnp.float32) * UNIT)
        left = jnp.where(rows == tile(o >> 7), w, zero).reshape(128, 128)
        right = jnp.where(rows == tile(o & 127), one, zero).reshape(128, 128)
        return left, right

    blocks = []
    for u in range(0, len(lines), 2):
        (left, right), (left_too, right_too) = factors(lines[u]), factors(lines[u + 1])
        both = lax.dot_general(
            jnp.concatenate([left, left_too], axis=1),
            jnp.concatenate(
                [
                    jnp.concatenate([right, empty], axis=1),
                    jnp.concatenate([empty, right_too], axis=1),
                ],
                axis=0,
            ),
            (((1,), (1,)), ((), ())),
            preferred_element_type=jnp.float32,
        ).astype(jnp.bfloat16)
        blocks += [both[:, :128], both[:, 128:]]
    return blocks


def column(row):
    return jnp.broadcast_to(row, (8, row.shape[1])).T[:, :1]


def ranks(key):
    n = key.shape[1]
    key_column = column(key)
    lanes = lax.broadcasted_iota(jnp.int32, (128, n), 1)
    lines = lax.broadcasted_iota(jnp.int32, (128, n), 0)
    rank = jnp.zeros((1, n), jnp.float32)
    for t in range(0, n, 128):
        before = (key_column[t : t + 128] == key) & (lines + t < lanes)
        rank += jnp.sum(jnp.where(before, 1.0, 0.0), axis=0, keepdims=True)
    return rank


def pack_kernel(
    per, owners, count, brow, bcol, offs_in, wts_in, out, codes, offs, wts, pos_row, pos, sems
):
    slots, width = offs.shape
    reads = [
        pltpu.make_async_copy(offs_in, offs, sems.at[0]),
        pltpu.make_async_copy(wts_in, wts, sems.at[1]),
    ]
    for read in reads:
        read.start()
    stride = ROOM + SPARE
    lanes = lax.broadcasted_iota(jnp.int32, (1, slots), 1)
    live = lanes < count[0, 0]
    row = brow[...].astype(jnp.float32)
    home = jnp.floor((row + 0.5) * (1.0 / per))
    key = jnp.where(live, home, float(owners))
    rank = ranks(key)
    fits = live & (rank < ROOM)
    trash = float(ROOM + SPARE - 1)
    pos_row[...] = jnp.where(fits, home * stride + rank, trash).astype(jnp.int32)
    copy = pltpu.make_async_copy(pos_row, pos, sems.at[2])
    copy.start()

    out[...] = jnp.zeros_like(out)
    label = 1.0 + (row - per * home) * COLS + bcol[...].astype(jnp.float32)
    names = lax.broadcasted_iota(jnp.int32, (owners, slots), 0).astype(jnp.float32)
    chosen = jnp.where((names == key) & fits, label, 0.0).astype(jnp.bfloat16)
    spots = lax.broadcasted_iota(jnp.int32, (1, 128), 1)
    placed = jnp.where(column(rank) == spots.astype(jnp.float32), 1.0, 0.0).astype(jnp.bfloat16)
    labels = jnp.dot(chosen, placed, preferred_element_type=jnp.float32)
    over = jnp.max(jnp.where(live, rank, 0.0), axis=1, keepdims=True)
    labels = jnp.where(spots < ROOM, labels, jnp.where(over < ROOM, 0.0, 1.0)).astype(jnp.int32)
    for k in range(owners):
        out[pl.ds(k * stride + ROOM, 1), :] = labels[k : k + 1]
    for read in reads:
        read.wait()
    codes[pl.ds(0, slots), :] = offs[...] * FIELD + (
        wts[...].astype(jnp.float32) * (1.0 / UNIT)
    ).astype(jnp.int32)
    codes[pl.ds(slots, 8), :] = jnp.zeros((8, width), jnp.int32)
    copy.wait()

    def turn(i, _):
        for u in range(GROUP):
            s = i * GROUP + u
            out[pl.ds(pos[0, s], 1), :] = codes[pl.ds(s, 1), :]
        return 0

    lax.fori_loop(0, (count[0, 0] + GROUP - 1) // GROUP, turn, 0)


def build_kernel(span, marks, lists, codes, *refs):
    dense, dbuf, sems = refs[-3:]
    start, turns = marks[0, span[0]], marks[0, span[1]]
    rows = tile_rows()

    def out_copy(i):
        slot = lax.rem(i, DEPTH)
        return pltpu.make_async_copy(
            dbuf.at[slot], dense.at[pl.ds(i * TURN, TURN)], sems.at[slot]
        )

    def turn(i, _):
        slot = lax.rem(i, DEPTH)

        @pl.when(i >= start + DEPTH)
        def _():
            out_copy(i - DEPTH).wait()

        lines = [codes[pl.ds(lists[0, i * TURN + u], 1), :] for u in range(TURN)]
        for u in range(0, TURN, GROUP):
            blocks = blocks_of(lines[u : u + GROUP], rows)
            for k, block in enumerate(blocks):
                dbuf[slot, u + k] = block
        out_copy(i).start()
        return 0

    lax.fori_loop(start, turns, turn, 0)

    def finish(i, _):
        out_copy(i).wait()
        return 0

    lax.fori_loop(jnp.maximum(turns - DEPTH, start), turns, finish, 0)


def fetch(pieces, into, sems):
    size = pieces[0].shape[0]
    copies = [
        pltpu.make_async_copy(piece, into.at[pl.ds(i * size, size)], sems.at[i])
        for i, piece in enumerate(pieces)
    ]
    for copy in copies:
        copy.start()
    return copies


def read_dense(start, turns, dense, dbuf, sems, product, prepare):
    def in_copy(i):
        slot = lax.rem(i, DEPTH)
        return pltpu.make_async_copy(
            dense.at[pl.ds(i * TURN, TURN)], dbuf.at[slot], sems.at[slot]
        )

    def begin(i, _):
        in_copy(i).start()
        return 0

    lax.fori_loop(start, jnp.minimum(turns, start + DEPTH - 1), begin, 0)
    prepare()

    def turn(i, _):
        @pl.when(i + DEPTH - 1 < turns)
        def _():
            in_copy(i + DEPTH - 1).start()

        in_copy(i).wait()
        product(i, lax.rem(i, DEPTH))
        return 0

    lax.fori_loop(start, turns, turn, 0)


def add_pairs(i, owner, one, into):
    groups = TURN // GROUP
    for g in range(0, groups, 2):
        added = [one(g), one(g + 1)]
        for k in range(2):
            into[owner[0, i * groups + g + k]] += added[k]


def forward_kernel(n, scale, span, marks, lists, owner, weight, bias, cotangent, dense, *refs):
    pieces, refs = refs[:n], refs[n:]
    output, turned, local, totals, feat, proj, dbuf, piece_sems, sems = refs
    copies = fetch(pieces, feat, piece_sems)
    size, _, width = pieces[0].shape
    batch = 8 if size % 8 == 0 else 1

    def project(t, _):
        spot = pl.ds(t * batch, batch)
        held = feat[spot].reshape(batch * 128, width)
        low = jnp.dot(held, weight[...], preferred_element_type=jnp.float32)
        proj[spot] = low.astype(jnp.bfloat16).reshape(batch, 128, width)
        return 0

    def prepare():
        totals[...] = jnp.zeros_like(totals)
        for i, copy in enumerate(copies):
            copy.wait()
            lax.fori_loop(i * size // batch, (i + 1) * size // batch, project, 0)

    def product(i, slot):
        def one(g):
            spots = [lists[1, i * TURN + g * GROUP + u] for u in range(GROUP)]
            left = jnp.concatenate([dbuf[slot, g * GROUP + u] for u in range(GROUP)], axis=1)
            right = jnp.concatenate(
                [jnp.concatenate([proj[c], feat[c]], axis=1) for c in spots], axis=0
            )
            return jnp.dot(left, right, preferred_element_type=jnp.float32)

        add_pairs(i, owner, one, totals)

    read_dense(marks[0, span[0]], marks[0, span[1]], dense, dbuf, sems, product, prepare)

    weight_sum, bias_sum = 0.0, 0.0
    for q in range(totals.shape[0]):
        lines = pl.ds(q * 128, 128)
        pre = totals[q, :, :width] + bias[...]
        output[lines, :] = jnp.maximum(pre, 0.0).astype(jnp.bfloat16)
        grad = jnp.where(pre > 0, cotangent[lines, :].astype(jnp.float32), 0.0)
        turned[q] = grad.T.astype(jnp.bfloat16)
        weight_sum += lax.dot_general(
            totals[q, :, width:].astype(jnp.bfloat16),
            grad.astype(jnp.bfloat16),
            (((0,), (0,)), ((), ())),
            preferred_element_type=jnp.float32,
        )
        bias_sum += jnp.sum(grad, axis=0, keepdims=True)
    local[pl.ds(0, width), :] = weight_sum * scale
    local[pl.ds(width, 8), :] = jnp.broadcast_to(bias_sum * scale, (8, width))


def tile_kernel(meta, order, dst, col, codes, panel, totals):
    rows = tile_rows()
    totals[...] = jnp.zeros_like(totals)

    def turn(i, _):
        lines = [codes[pl.ds(order[i * GROUP + u], 1), :] for u in range(GROUP)]
        for u, block in enumerate(blocks_of(lines, rows)):
            p = i * GROUP + u
            totals[dst[p]] += jnp.dot(block, panel[col[p]], preferred_element_type=jnp.float32)
        return 0

    lax.fori_loop(0, meta[0], turn, 0)


def backward_kernel(n, span, marks, lists, owner, before, dense, *refs):
    pieces, (acc, grad, dbuf, piece_sems, sems) = refs[:n], refs[n:]
    copies = fetch(pieces, grad, piece_sems)

    def prepare():
        acc[...] = before[...]
        for copy in copies:
            copy.wait()

    def product(i, slot):
        def one(g):
            spots = [lists[1, i * TURN + g * GROUP + u] for u in range(GROUP)]
            left = jnp.concatenate([grad[c] for c in spots], axis=1)
            right = dbuf[slot, pl.ds(g * GROUP, GROUP)].reshape(GROUP * 128, 128)
            return jnp.dot(left, right, preferred_element_type=jnp.float32)

        add_pairs(i, owner, one, acc)

    read_dense(marks[0, span[0]], marks[0, span[1]], dense, dbuf, sems, product, prepare)


SMEM = pl.BlockSpec(memory_space=pltpu.SMEM)
VMEM = pl.BlockSpec(memory_space=pltpu.VMEM)
HBM = pl.BlockSpec(memory_space=pl.ANY)
PARAMS = pltpu.CompilerParams(vmem_limit_bytes=48 * 1024 * 1024)


def cost(slots, products):
    flops = 2 * slots * products * 128**3
    return pl.CostEstimate(flops=flops, bytes_accessed=slots * 128 * 128 * 2, transcendentals=0)


def run_tile(meta, order, dst, col, codes, panel, row_blocks):
    return pl.pallas_call(
        tile_kernel,
        out_shape=jax.ShapeDtypeStruct((row_blocks, 128, panel.shape[-1]), jnp.float32),
        in_specs=[SMEM] * 4 + [VMEM] * 2,
        out_specs=VMEM,
        compiler_params=PARAMS,
    )(meta, order, dst, col, codes, panel)


def run_pack(per, owners, count, brow, bcol, offs, wts):
    slots = brow.shape[1]
    return pl.pallas_call(
        functools.partial(pack_kernel, per, owners),
        out_shape=(
            jax.ShapeDtypeStruct((owners * (ROOM + SPARE), 128), jnp.int32),
            jax.ShapeDtypeStruct((slots + 8, 128), jnp.int32),
        ),
        in_specs=[SMEM] + [VMEM] * 2 + [HBM] * 2,
        out_specs=[VMEM] * 2,
        scratch_shapes=[
            pltpu.VMEM(offs.shape, offs.dtype),
            pltpu.VMEM(wts.shape, wts.dtype),
            pltpu.VMEM((1, slots), jnp.int32),
            pltpu.SMEM((1, slots), jnp.int32),
            pltpu.SemaphoreType.DMA((3,)),
        ],
        compiler_params=PARAMS,
    )(count, brow, bcol, offs, wts)


def run_build(span, listed, codes, after, dense):
    lists, _, marks = listed
    others = after if dense is None else after + [dense]
    return pl.pallas_call(
        functools.partial(build_kernel, span),
        out_shape=jax.ShapeDtypeStruct((lists.shape[1], 128, 128), jnp.bfloat16),
        in_specs=[SMEM] * 2 + [VMEM] + [HBM] * len(others),
        out_specs=HBM,
        scratch_shapes=[
            pltpu.VMEM((DEPTH, TURN, 128, 128), jnp.bfloat16),
            pltpu.SemaphoreType.DMA((DEPTH,)),
        ],
        input_output_aliases={} if dense is None else {2 + len(others): 0},
        compiler_params=PARAMS,
        cost_estimate=cost(lists.shape[1], 2),
    )(marks, lists, codes, *others)


def run_forward(scale, span, listed, weight, bias, cotangent, dense, feat):
    lists, owner, marks = listed
    n = len(feat)
    size, _, width = feat[0].shape
    row_blocks = cotangent.shape[0] // 128
    return pl.pallas_call(
        functools.partial(forward_kernel, n, scale, span),
        out_shape=(
            jax.ShapeDtypeStruct(cotangent.shape, jnp.bfloat16),
            jax.ShapeDtypeStruct((row_blocks, width, 128), jnp.bfloat16),
            jax.ShapeDtypeStruct((width + 8, width), jnp.float32),
        ),
        in_specs=[SMEM] * 3 + [VMEM] * 3 + [HBM] * (n + 1),
        out_specs=[VMEM] * 3,
        scratch_shapes=[
            pltpu.VMEM((row_blocks, 128, 2 * width), jnp.float32),
            pltpu.VMEM((n * size, 128, width), jnp.bfloat16),
            pltpu.VMEM((n * size, 128, width), jnp.bfloat16),
            pltpu.VMEM((DEPTH, TURN, 128, 128), jnp.bfloat16),
            pltpu.SemaphoreType.DMA((n,)),
            pltpu.SemaphoreType.DMA((DEPTH,)),
        ],
        compiler_params=PARAMS,
        cost_estimate=cost(lists.shape[1], 4),
    )(marks, lists, owner, weight, bias, cotangent, dense, *feat)


def run_backward(span, listed, before, dense, pieces):
    lists, owner, marks = listed
    n = len(pieces)
    size, width, _ = pieces[0].shape
    return pl.pallas_call(
        functools.partial(backward_kernel, n, span),
        out_shape=jax.ShapeDtypeStruct(before.shape, jnp.float32),
        in_specs=[SMEM] * 3 + [VMEM] + [HBM] * (n + 1),
        out_specs=VMEM,
        scratch_shapes=[
            pltpu.VMEM((n * size, width, 128), jnp.bfloat16),
            pltpu.VMEM((DEPTH, TURN, 128, 128), jnp.bfloat16),
            pltpu.SemaphoreType.DMA((n,)),
            pltpu.SemaphoreType.DMA((DEPTH,)),
        ],
        compiler_params=PARAMS,
        cost_estimate=cost(lists.shape[1], 4),
    )(marks, lists, owner, before, dense, *pieces)


def list_kernel(keys, split, fills, key_ref, *refs):
    value_refs, (lists, owner_ref, marks_ref) = refs[: len(fills)], refs[len(fills) :]
    n, length = key_ref.shape[1], lists.shape[1]
    key = key_ref[...].astype(jnp.float32)
    rank = ranks(key)

    rows = -(-keys // 8) * 8
    names = lax.broadcasted_iota(jnp.int32, (rows, n), 0).astype(jnp.float32)
    name = lax.broadcasted_iota(jnp.int32, (rows, 1), 0).astype(jnp.float32)
    counts = jnp.sum(jnp.where(names == key, 1.0, 0.0), axis=1, keepdims=True)
    filled = jnp.where(name < keys, jnp.floor((counts + (GROUP - 1)) * (1.0 / GROUP)) * GROUP, 0.0)
    below = jnp.sum(jnp.where(name < split, filled, 0.0), axis=0, keepdims=True)
    first = jnp.floor((below + (TURN - 1)) * (1.0 / TURN))
    filled = filled + jnp.where(name == split - 1, first * TURN - below, 0.0)
    turns = jnp.floor((jnp.sum(filled, axis=0, keepdims=True) + (TURN - 1)) * (1.0 / TURN))
    base = jnp.sum(jnp.where(names < key, filled, 0.0), axis=0, keepdims=True)
    pos_column = column(jnp.where(key < keys, base + rank, -1.0))

    spots = lax.broadcasted_iota(jnp.int32, (1, length), 1).astype(jnp.float32)
    columns = [column(ref[...].astype(jnp.float32)) for ref in value_refs]
    sums = [jnp.zeros((1, length), jnp.float32) for _ in fills]
    for t in range(0, n, 128):
        hit = pos_column[t : t + 128] == spots
        for k, fill in enumerate(fills):
            value = columns[k][t : t + 128] - fill
            sums[k] += jnp.sum(jnp.where(hit, value, 0.0), axis=0, keepdims=True)
    for k, fill in enumerate(fills):
        lists[pl.ds(k, 1), :] = (sums[k] + fill).astype(jnp.int32)

    other = lax.broadcasted_iota(jnp.int32, (rows, 128), 1).astype(jnp.float32)
    ends = column(jnp.sum(jnp.where(name <= other, filled, 0.0), axis=0, keepdims=True))[:rows]
    starts = lax.broadcasted_iota(jnp.int32, owner_ref.shape, 1).astype(jnp.float32) * GROUP
    passed = (ends <= starts) & (name < keys)
    owner = jnp.sum(jnp.where(passed, 1.0, 0.0), axis=0, keepdims=True)
    owner = jnp.minimum(owner, keys - 1.0)
    owner_ref[...] = jnp.where(owner >= split, owner - split, owner).astype(jnp.int32)

    spot = lax.broadcasted_iota(jnp.int32, (1, 128), 1)
    marks = jnp.where(spot == FIRST, first, 0.0)
    for k in range(1, 5):
        marks = jnp.where(spot == FIRST + k, jnp.floor(turns * (k / 4)), marks)
    marks_ref[...] = marks.astype(jnp.int32)


FIRST = 1
QUARTERS = [0, 2, 3, 4, 5]


def make_lists(key, values, fills, keys, split):
    n = key.size
    length = (-(-(n + keys * GROUP) // TURN) + 1) * TURN
    groups = -(-length // GROUP // 128) * 128
    lists, owner, marks = pl.pallas_call(
        functools.partial(list_kernel, keys, split, fills),
        out_shape=(
            jax.ShapeDtypeStruct((len(fills), length), jnp.int32),
            jax.ShapeDtypeStruct((1, groups), jnp.int32),
            jax.ShapeDtypeStruct((1, 128), jnp.int32),
        ),
        in_specs=[VMEM] * (1 + len(fills)),
        out_specs=[VMEM] * 3,
        compiler_params=PARAMS,
        cost_estimate=cost(32, 2),
    )(key.reshape(1, n), *[value.reshape(1, n) for value in values])
    return lists, owner, marks


def place(pos, value, length, fill):
    spots = jnp.arange(length, dtype=jnp.int32)
    hit = pos[:, None] == spots[None, :]
    return jnp.sum(jnp.where(hit, value[:, None] - fill, 0), axis=0) + fill


def shards(
    features,
    weight,
    bias,
    cotangent,
    block_count,
    block_rows,
    block_cols,
    edge_offsets,
    edge_weight,
):
    node_dev, width = features.shape
    n_row = lax.axis_size("row")
    n_col = lax.axis_size("col")
    slots = block_rows.shape[2]
    count = block_count[0, 0]
    mine = lax.axis_index("col")
    mine_row = lax.axis_index("row")
    per = node_dev // 128
    row_blocks = per * n_col
    col_blocks = per * n_row
    scale = (node_dev * n_row * n_col) ** (-0.5)
    by_owner = n_row * n_col * node_dev * width * 2 <= 8 * 1024 * 1024
    by_owner = by_owner and col_blocks <= COLS and per * COLS < 256 and n_col % 8 == 0

    packed, codes = run_pack(
        per, n_col, block_count, block_rows[0], block_cols[0], edge_offsets[0, 0], edge_weight[0, 0]
    )

    def tile_plan():
        ids = jnp.arange(slots, dtype=jnp.int32)
        live = ids < count
        brow, bcol = block_rows[0, 0], block_cols[0, 0]
        home = brow // per
        turns_plain = ((count + GROUP - 1) // GROUP).reshape(1)
        wide = lax.all_gather(features, "row", axis=0, tiled=True)
        low = jnp.dot(wide, weight, preferred_element_type=jnp.float32).astype(jnp.bfloat16)
        panel = jnp.concatenate([low, wide], axis=1).reshape(col_blocks, 128, 2 * width)
        order = jnp.where(live, ids, slots)
        dst = jnp.where(live, (home ^ mine) * per + brow % per, 0)
        totals = run_tile(turns_plain, order, dst, bcol, codes, panel, row_blocks)
        own = scatter_sum(totals.reshape(n_col, node_dev, 2 * width), "col")
        pre = own[:, :width] + bias
        output = jnp.maximum(pre, 0.0).astype(jnp.bfloat16)
        grad = jnp.where(pre > 0, cotangent.astype(jnp.float32), 0.0)
        turned = jnp.swapaxes(grad.astype(jnp.bfloat16).reshape(per, 128, width), 1, 2)
        weight_sum = lax.dot_general(
            own[:, width:].astype(jnp.bfloat16),
            grad.astype(jnp.bfloat16),
            (((0,), (0,)), ((), ())),
            preferred_element_type=jnp.float32,
        )
        bias_sum = jnp.broadcast_to(jnp.sum(grad, axis=0), (8, width))
        return output, turned, jnp.concatenate([weight_sum, bias_sum], axis=0) * scale

    state = {"dense": None}

    def list_backward(count, brow, bcol):
        ids = jnp.arange(slots, dtype=jnp.int32)
        source = piece_index(per, (brow // per) ^ mine, brow % per)
        unit = row_blocks // (2 * len(part_orders(per)))
        late = source // unit % 2
        source = source // (2 * unit) * unit + source % unit
        key = jnp.where(ids < count, late * col_blocks + bcol, 2 * col_blocks)
        return make_lists(key, [ids, source], [slots, 0], 2 * col_blocks, col_blocks)

    slot_inputs = (count, block_rows[0, 0], block_cols[0, 0])

    def build(held, start, end):
        span = (QUARTERS[start], QUARTERS[end])
        state["dense"] = run_build(span, state["back"], codes, held, state["dense"])

    if by_owner:
        stride = ROOM + SPARE
        came = lax.all_to_all(
            packed.reshape(n_col, stride, 128), "col", split_axis=0, concat_axis=0, tiled=True
        )
        spread = jnp.max(came[:, ROOM, ROOM:], axis=0)[None]
        for bit in bits_of("row"):
            spread = spread + swap(spread, "row", bit)
        any_over = jnp.max(spread, axis=1)

        got = came[:, ROOM, :ROOM]
        sources = jnp.arange(n_col, dtype=jnp.int32)[:, None]
        places = jnp.arange(ROOM, dtype=jnp.int32)[None, :]
        row_here = ((got - 1) // COLS).reshape(-1)
        col_there = (got - 1) % COLS
        col_there = piece_index(
            per, sources ^ mine, col_there % per, (col_there // per) ^ mine_row, n_row
        )
        line = sources * stride + places
        listed = make_lists(
            jnp.where(got > 0, row_here.reshape(got.shape), per),
            [jnp.broadcast_to(line, got.shape), col_there],
            [ROOM + 1, 0],
            per,
            per,
        )

        def prepare(step, held):
            if step == 0:
                held, inputs = lax.optimization_barrier((held, slot_inputs))
                state["back"] = list_backward(*inputs)
                build(held, 0, 2)
            if step == 1:
                held, state["dense"] = lax.optimization_barrier((held, state["dense"]))
            return held

        pairs = gather_pieces(features.reshape(per, 128, width), prepare)
        lines = came.reshape(n_col * stride, 128)
        here = run_build((0, QUARTERS[4]), listed, lines, [], None)
        last, here = lax.optimization_barrier(([pair[1] for pair in pairs], here))
        feat = []
        for pair in [[pair[0], x] for pair, x in zip(pairs, last)]:
            rows = [pair]
            for bit in bits_of("row"):
                rows = rows + [[swap(x, "row", bit) for x in pair] for pair in rows]
            feat += [x for pair in rows for x in pair]
        done = run_forward(
            scale, (0, QUARTERS[4]), listed, weight, bias[None], cotangent, here, feat
        )
        done = lax.cond(any_over[0] > 0, tile_plan, lambda: tuple(done))
    else:
        state["back"] = list_backward(*slot_inputs)
        build([features], 0, 2)
        done = tile_plan()

    output, turned, total = done
    turned = with_layout_constraint(turned, Layout(major_to_minor=(0, 1, 2)))
    steps = bits_of("col")

    def add_total():
        state["total"] = state["total"] + swap(state["total"], "col", steps.pop(0))

    def beside(step, held):
        held, state["total"], state["dense"] = lax.optimization_barrier(
            (held, state["total"], state["dense"])
        )
        if step == 1:
            add_products(0, held)
            state["acc"], state["total"] = lax.optimization_barrier(
                (state["acc"], state["total"])
            )
        if steps:
            add_total()
        return held

    def add_products(half, pieces):
        pieces = [x.reshape((-1,) + x.shape[2:]) if x.ndim == 4 else x for x in pieces]
        state["acc"] = run_backward(
            [(0, FIRST), (FIRST, QUARTERS[4])][half], state["back"], state["acc"], state["dense"], pieces
        )

    state["acc"] = jnp.zeros((col_blocks, width, 128), jnp.float32)
    state["total"] = split_rows(total)
    while len(steps) > 3:
        add_total()
    build([turned], 2, 4)
    if len(steps) > 2:
        state["dense"], state["total"] = lax.optimization_barrier(
            (state["dense"], state["total"])
        )
        add_total()
    grad = gather_pieces(turned, beside)
    late_pieces, state["total"] = lax.optimization_barrier(
        ([pair[1] for pair in grad], state["total"])
    )
    while steps:
        add_total()
    total = join_rows(state["total"])
    add_products(1, late_pieces)
    acc = state["acc"]
    back = jnp.swapaxes(acc, 1, 2).reshape(col_blocks * 128, width)
    grad_proj = scatter_sum(
        jnp.stack(
            [
                lax.dynamic_slice_in_dim(back, (mine_row ^ k) * node_dev, node_dev, 0)
                for k in range(n_row)
            ]
        ),
        "row",
    ).astype(jnp.bfloat16)
    grad_features = lax.dot_general(
        grad_proj, weight, (((1,), (1,)), ((), ())), preferred_element_type=jnp.float32
    ).astype(jnp.bfloat16)
    return (
        output,
        grad_features,
        total[: weight.shape[0]],
        total[weight.shape[0]],
    )


def solution(mesh):
    return jax.shard_map(
        shards,
        mesh=mesh,
        in_specs=(
            P(("row", "col"), None),
            P(),
            P(),
            P(("row", "col"), None),
            P("row", "col"),
            P("row", "col", None),
            P("row", "col", None),
            P("row", "col", None, None),
            P("row", "col", None, None),
        ),
        out_specs=(P(("row", "col"), None), P(("row", "col"), None), P(), P()),
        check_vma=False,
    )
```
